32 devices in a mesh: row: 4 (over x, core), col: 8 (over z, y).
Axes of the slice: x: 2, y: 2, z: 4, core: 2. Of those that a mesh axis runs over, the one named last changes fastest.
Arguments:
- tokens: bfloat16 [1024, 2, 2560], P('col'), may hold values from -6 to 6
- segments: int32 [1024, 2], P('col'), may hold values from 0 to 3, as said below
- routes: int32 [1024, 2, 6], P('col'), may hold values from 0 to 15, all different within a row; in each aligned block of 256 rows (0 to 255, 256 to 511, ..., all dimensions but the last counted through in order) at most 128 rows name the same one
- attn_gain: bfloat16 [2560], P('col'), may hold values from 0.5 to 1.5
- query_matrix: bfloat16 [2560, 2560], P('col', 'row'), may hold values from -0.125 to 0.125
- key_matrix: bfloat16 [2560, 512], P('col', 'row'), may hold values from -0.125 to 0.125
- value_matrix: bfloat16 [2560, 512], P('col', 'row'), may hold values from -0.125 to 0.125
- attention_output_matrix: bfloat16 [2560, 2560], P('row', 'col'), may hold values from -0.5 to 0.5
- mlp_gain: bfloat16 [2560], P('col'), may hold values from 0.5 to 1.5
- w_router: bfloat16 [2560, 16], P('col'), may hold values from -0.0625 to 0.0625
- shared_gate_matrix: bfloat16 [2560, 3072], P('col', 'row'), may hold values from -0.125 to 0.125
- shared_up_matrix: bfloat16 [2560, 3072], P('col', 'row'), may hold values from -0.125 to 0.125
- shared_down_matrix: bfloat16 [3072, 2560], P('row', 'col'), may hold values from -0.109375 to 0.109375
- expert_gate: bfloat16 [16, 2560, 1536], P('col', None, 'row'), may hold values from -0.125 to 0.125
- expert_up: bfloat16 [16, 2560, 1536], P('col', None, 'row'), may hold values from -0.125 to 0.125
- expert_down: bfloat16 [16, 1536, 2560], P('col', 'row'), may hold values from -0.15625 to 0.15625
- cotangent: float32 [1024, 2, 2560], P('col', None, 'row'), may hold values from -6 to 6
Outputs:
- block_out: bfloat16 [1024, 2, 2560], P('col', None, 'row')
- d_tokens: float32 [1024, 2, 2560], P('col')
- d_attn_gain: float32 [2560], P('col')
- d_query: float32 [2560, 2560], P('col', 'row')
- d_key: float32 [2560, 512], P('col', 'row')
- d_value: float32 [2560, 512], P('col', 'row')
- d_out: float32 [2560, 2560], P('row', 'col')
- d_mlp_gain: float32 [2560], P('col')
- d_router: float32 [2560, 16], P('col')
- d_shared_gate: float32 [2560, 3072], P('col', 'row')
- d_shared_up: float32 [2560, 3072], P('col', 'row')
- d_shared_down: float32 [3072, 2560], P('row', 'col')
- d_expert_gate: float32 [16, 2560, 1536], P('col', None, 'row')
- d_expert_up: float32 [16, 2560, 1536], P('col', None, 'row')
- d_expert_down: float32 [16, 1536, 2560], P('col', 'row')
The draws below stay inside these ranges and needn't reach their ends.
Inputs may be any that keep to these rules, and one draw needn't show every extreme that they name: `segments`: document numbers start at 0 in every sequence and never fall along it; at least one sequence is a single document. `routes`: each token names 6 different experts. Among the 256 tokens of one index of col, no expert is named more than 128 times.
All inputs are finite; a program needn't handle non-finite values.
Results may differ from the reference program's by a relative error of at most 0.015.
Values may be sent and summed in bfloat16 or wider, within the bound.
A program may use at most 384 MiB of HBM per device.

```python
import math
from functools import partial
import jax
import jax.numpy as jnp
import numpy as np
from jax import lax

MODEL_DIM = 2560
QUERY_HEADS = 20
KEY_VALUE_HEADS = 4
HEAD_DIM = 128
EH = 1536
TOP = 6
CUTS = 3
LCOL = 128
SEQUENCE_COUNT = 2
EXPERTS = 16
SHW = 3072
SEQUENCE_LENGTH = 1024
TOKENS = 2048
CAP = 128
N_COL = 8


def draw_segments(key, part):
    key = jax.random.fold_in(key, 7)
    cut_key, whole_key = jax.random.split(key)
    cut_points = jax.random.randint(cut_key, (SEQUENCE_COUNT, CUTS), 1, SEQUENCE_LENGTH)
    whole_seq = jax.random.randint(whole_key, (), 0, SEQUENCE_COUNT)
    keep_cut = jnp.arange(SEQUENCE_COUNT)[:, None] != whole_seq
    cut_points = jnp.where(keep_cut, cut_points, SEQUENCE_LENGTH)
    places = jnp.arange(SEQUENCE_LENGTH)
    doc_ids = jnp.sum((cut_points[None, :, :] <= places[:, None, None]).astype(jnp.int32), axis=2)
    return doc_ids.astype(jnp.int32)


def shard_levels(key, dims, shards, least, largest):
    level, own = 1.0, jax.random.fold_in(key, 6)
    for axis_at, blocks in shards:
        steps = jnp.exp(jax.random.uniform(jax.random.fold_in(own, axis_at), (blocks,), jnp.float32, least / len(shards), largest / len(shards)))
        level = level * jnp.repeat(steps, dims[axis_at] // blocks).reshape([-1 if axis == axis_at else 1 for axis in range(len(dims))])
    return level


def shared_out(own_key, own, number, rows, number_of, top, reach, slope):
    sequence = jax.random.permutation(own_key, number_of)
    packed, common = load_shares(number_of, rows * top, reach, slope, True), load_shares(number_of, rows * top, reach, slope, False)
    places = jnp.arange(number_of)

    def named(tallies, turn):
        used = int((tallies > 0).sum())
        fixed = max(1, used // 4)
        moved = fixed + (places - fixed + turn * (used - fixed)) % max(1, number_of - fixed)
        return jnp.zeros((number_of,), jnp.int32).at[sequence[jnp.where(places < fixed, places, moved)]].set(jnp.asarray(tallies, jnp.int32))

    tallies = jnp.where(number % 4 == 0, named(packed, number // 4), named(common, number - number // 4 - 1))
    mixed = jax.random.permutation(jax.random.fold_in(own, 3), number_of)
    source_of, receiver = mixed[0:number_of // 2 * 2:2], mixed[1:number_of // 2 * 2:2]
    margin = jnp.minimum(tallies[source_of] - 1, reach - tallies[receiver]) // 2
    margin = jnp.where((source_of == sequence[0]) | (receiver == sequence[0]) | (tallies[receiver] == 0), 0, jnp.maximum(margin, 0))
    moved = jax.random.randint(jax.random.fold_in(own, 4), (number_of // 2,), 0, 1 << 20) % (margin + 1)
    tallies = tallies.at[source_of].add(-moved).at[receiver].add(moved)
    items = jnp.searchsorted(jnp.cumsum(tallies), jnp.arange(rows * top), side="right").astype(jnp.int32)
    listing = items.reshape(top, rows).T
    listing = listing[jax.random.permutation(jax.random.fold_in(own, 1), rows)]
    turn = jax.random.randint(jax.random.fold_in(own, 2), (rows, 1), 0, top)
    return jnp.take_along_axis(listing, (jnp.arange(top)[None, :] + turn) % top, axis=1)


def load_shares(number_of, total, limit, skew, full):
    portions = [(1 << 20) // math.isqrt(rank ** skew) + 1 for rank in range(1, number_of + 1)]
    largest = limit if full else min(limit, max(-(-total // number_of), total * portions[0] // sum(portions)))
    least = 1 if total - largest >= number_of - 1 else 0
    given, rest = [largest] + [least] * (number_of - 1), total - largest - least * (number_of - 1)
    while rest > 0:
        candidates = [i for i in range(1, number_of) if given[i] < largest] or [i for i in range(1, number_of) if given[i] < limit]
        whole, left = sum([portions[i] for i in candidates]), rest
        for i in candidates:
            more = min(limit - given[i], max(1, left * portions[i] // whole), rest)
            given[i] = given[i] + more
            rest = rest - more
    return np.array(given)


def noise(rng, dims, width, bound, pieces=(), held_as=jnp.bfloat16):
    entries = jax.random.normal(rng, dims, jnp.float32) * width
    if len(pieces) > 0:
        entries = shard_levels(rng, dims, pieces, -0.22, 0.18) * entries
    return jnp.clip(entries, min=-bound, max=bound).astype(held_as)


def setup_inputs(seed: int = 0) -> dict:
    seeds = jax.random.split(jax.random.key(seed), 18)
    tokens = noise(seeds[0], (SEQUENCE_LENGTH, SEQUENCE_COUNT, MODEL_DIM), 1.0, 6.0, ((0, 8),))
    segments = draw_segments(jax.random.fold_in(seeds[17], 71), 0)
    routes_keys = jax.random.split(jax.random.fold_in(seeds[2], 1), SEQUENCE_LENGTH * SEQUENCE_COUNT // (LCOL * SEQUENCE_COUNT))
    routes_turns = jax.random.permutation(jax.random.fold_in(seeds[2], 3), SEQUENCE_LENGTH * SEQUENCE_COUNT // (LCOL * SEQUENCE_COUNT))
    routes = jax.vmap(lambda own, number: shared_out(jax.random.fold_in(seeds[2], 2), own, number, LCOL * SEQUENCE_COUNT, EXPERTS, TOP, CAP, 1))(routes_keys, routes_turns).reshape((SEQUENCE_LENGTH, SEQUENCE_COUNT, TOP))
    attn_gain = jnp.clip(1.0 + 0.1 * jax.random.normal(seeds[3], (MODEL_DIM,), jnp.float32), 0.5, 1.5).astype(jnp.bfloat16)
    query_matrix = noise(seeds[4], (MODEL_DIM, QUERY_HEADS * HEAD_DIM), MODEL_DIM ** -0.5, 0.125, ((0, 8), (1, 4)))
    key_matrix = noise(seeds[5], (MODEL_DIM, KEY_VALUE_HEADS * HEAD_DIM), MODEL_DIM ** -0.5, 0.125, ((0, 8), (1, 4)))
    value_matrix = noise(seeds[6], (MODEL_DIM, KEY_VALUE_HEADS * HEAD_DIM), MODEL_DIM ** -0.5, 0.125, ((0, 8), (1, 4)))
    attention_output_matrix = noise(seeds[7], (QUERY_HEADS * HEAD_DIM, MODEL_DIM), (QUERY_HEADS * HEAD_DIM // 16) ** -0.5, 0.5, ((0, 4), (1, 8)))
    mlp_gain = jnp.clip(1.0 + 0.1 * jax.random.normal(seeds[8], (MODEL_DIM,), jnp.float32), 0.5, 1.5).astype(jnp.bfloat16)
    w_router = noise(seeds[9], (MODEL_DIM, EXPERTS), (4 * MODEL_DIM) ** -0.5, 0.0625, ((0, 8),))
    shared_gate_matrix = noise(seeds[10], (MODEL_DIM, SHW), MODEL_DIM ** -0.5, 0.125, ((0, 8), (1, 4)))
    shared_up_matrix = noise(seeds[11], (MODEL_DIM, SHW), MODEL_DIM ** -0.5, 0.125, ((0, 8), (1, 4)))
    shared_down_matrix = noise(seeds[12], (SHW, MODEL_DIM), SHW ** -0.5, 0.109375, ((0, 4), (1, 8)))
    expert_gate = noise(seeds[13], (EXPERTS, MODEL_DIM, EH), MODEL_DIM ** -0.5, 0.125, ((0, 8), (2, 4)))
    expert_up = noise(seeds[14], (EXPERTS, MODEL_DIM, EH), MODEL_DIM ** -0.5, 0.125, ((0, 8), (2, 4)))
    expert_down = noise(seeds[15], (EXPERTS, EH, MODEL_DIM), EH ** -0.5, 0.15625, ((0, 8), (1, 4)))
    cotangent = noise(seeds[16], (SEQUENCE_LENGTH, SEQUENCE_COUNT, MODEL_DIM), 1.0, 6.0, ((0, 8), (2, 4)), jnp.float32)
    return {"tokens": tokens, "segments": segments, "routes": routes, "attn_gain": attn_gain, "query_matrix": query_matrix, "key_matrix": key_matrix, "value_matrix": value_matrix, "attention_output_matrix": attention_output_matrix, "mlp_gain": mlp_gain, "w_router": w_router, "shared_gate_matrix": shared_gate_matrix, "shared_up_matrix": shared_up_matrix, "shared_down_matrix": shared_down_matrix, "expert_gate": expert_gate, "expert_up": expert_up, "expert_down": expert_down, "cotangent": cotangent}


norm_eps = 1e-05
rope_base = 500000.0
masked_score = -1e+30

@jax.custom_vjp
def reduced_part(v):
    return lax.optimization_barrier(v.astype(jnp.bfloat16)).astype(jnp.float32)

@jax.custom_vjp
def reduced_backward(v):
    return v

def low_keep(v):
    return (reduced_part(v), None)

def low_pass(kept, grad):
    return (grad,)

def back_keep(v):
    return (v, None)

def back_low(kept, grad):
    return (reduced_part(grad),)
reduced_part.defvjp(low_keep, low_pass)
reduced_backward.defvjp(back_keep, back_low)

def precise_einsum(form, left, right):
    return jnp.einsum(form, left, right, precision=lax.Precision.HIGHEST)

def rope_tables(length):
    places = jnp.arange(length, dtype=jnp.int32).astype(jnp.float32)
    frequency = jnp.power(rope_base, -jnp.arange(0, HEAD_DIM, 2, dtype=jnp.int32).astype(jnp.float32) / HEAD_DIM)
    angles = places[:, None] * frequency[None, :]
    return (jnp.cos(angles), jnp.sin(angles))

def apply_rotation(field_in, cosine_lookup, sine_lookup):
    half_size = field_in.shape[-1] // 2
    front_half = field_in[..., :half_size]
    back_half = field_in[..., half_size:]
    cosine_grid = cosine_lookup[:, None, None, :]
    sine_grid = sine_lookup[:, None, None, :]
    return jnp.concatenate([front_half * cosine_grid - back_half * sine_grid, back_half * cosine_grid + front_half * sine_grid], axis=-1)

def attend_block(inputs):
    query_grid, key_grid, value_grid, doc_ids = inputs
    score_scale = 1.0 / math.sqrt(HEAD_DIM)
    scores = reduced_backward(precise_einsum('gqd,kd->gqk', query_grid, key_grid) * score_scale)
    places = jnp.arange(SEQUENCE_LENGTH, dtype=jnp.int32)
    allowed = (doc_ids[:, None] == doc_ids[None, :]) & (places[None, :] <= places[:, None])
    scores = jnp.where(allowed[None, :, :], scores, masked_score)
    row_top = lax.optimization_barrier(jnp.max(scores, axis=-1, keepdims=True))
    weights = jnp.exp(scores - row_top)
    probs_all = weights / lax.optimization_barrier(jnp.sum(weights, axis=-1, keepdims=True))
    return precise_einsum('gqk,kd->gqd', reduced_part(probs_all), value_grid)

def expert_block(padded, inputs):
    gate_weight, up_weight, down_weight, row_index = inputs
    rows_in = padded[row_index]
    gate_pre = reduced_backward(precise_einsum('rd,df->rf', rows_in, gate_weight))
    up_pre = reduced_backward(precise_einsum('rd,df->rf', rows_in, up_weight))
    hidden = reduced_part(jax.nn.silu(gate_pre) * up_pre)
    return reduced_part(reduced_backward(precise_einsum('rf,fd->rd', hidden, down_weight)))

def dispatch_tables(routes):
    rows_block = LCOL * SEQUENCE_COUNT
    block_routes = routes.reshape(N_COL, rows_block, TOP)
    route_int = (block_routes[..., None] == jnp.arange(EXPERTS, dtype=jnp.int32)).astype(jnp.int32)
    counts = lax.optimization_barrier(jnp.sum(route_int, axis=2))
    before = jnp.cumsum(counts, axis=1) - counts
    slot_rank = lax.optimization_barrier(jnp.sum(route_int * before[:, :, None, :], axis=3))
    block_ids = jnp.arange(N_COL, dtype=jnp.int32)[:, None, None]
    place_index = block_routes * (N_COL * CAP) + block_ids * CAP + slot_rank
    token_ids = block_ids * rows_block + jnp.arange(rows_block, dtype=jnp.int32)[None, :, None]
    token_ids = jnp.broadcast_to(token_ids, place_index.shape)
    slot_table = jnp.full((EXPERTS * N_COL * CAP,), TOKENS, jnp.int32)
    slot_table = slot_table.at[place_index.reshape(-1)].set(token_ids.reshape(-1))
    return (place_index.reshape(TOKENS, TOP), slot_table.reshape(EXPERTS, N_COL * CAP))

def forward(params, segments, routes_hot, place_index, slot_table):
    tokens, attn_gain, query_matrix, key_matrix, value_matrix, attention_output_matrix, mlp_gain, w_router, shared_gate_matrix, shared_up_matrix, shared_down_matrix, expert_gate, expert_up, expert_down = params
    query_group_width = QUERY_HEADS // KEY_VALUE_HEADS
    inv_first = lax.rsqrt(lax.optimization_barrier(jnp.mean(tokens * tokens, axis=-1, keepdims=True)) + norm_eps)
    input_normalized = reduced_part(tokens * inv_first * attn_gain)
    query_rows_projected = reduced_backward(precise_einsum('cjb,bk->cjk', input_normalized, query_matrix))
    keys_projected = reduced_backward(precise_einsum('cjb,bk->cjk', input_normalized, key_matrix))
    value_rows = reduced_part(reduced_backward(precise_einsum('cjb,bk->cjk', input_normalized, value_matrix)))
    cosine_lookup, sine_lookup = rope_tables(SEQUENCE_LENGTH)
    query_rotated = reduced_part(apply_rotation(query_rows_projected.reshape(SEQUENCE_LENGTH, SEQUENCE_COUNT, QUERY_HEADS, HEAD_DIM), cosine_lookup, sine_lookup))
    key_rotated = reduced_part(apply_rotation(keys_projected.reshape(SEQUENCE_LENGTH, SEQUENCE_COUNT, KEY_VALUE_HEADS, HEAD_DIM), cosine_lookup, sine_lookup))
    query_stacked = query_rotated.reshape(SEQUENCE_LENGTH, SEQUENCE_COUNT, KEY_VALUE_HEADS, query_group_width, HEAD_DIM).transpose(1, 2, 3, 0, 4).reshape(SEQUENCE_COUNT * KEY_VALUE_HEADS, query_group_width, SEQUENCE_LENGTH, HEAD_DIM)
    key_stacked = key_rotated.transpose(1, 2, 0, 3).reshape(SEQUENCE_COUNT * KEY_VALUE_HEADS, SEQUENCE_LENGTH, HEAD_DIM)
    value_stacked = value_rows.reshape(SEQUENCE_LENGTH, SEQUENCE_COUNT, KEY_VALUE_HEADS, HEAD_DIM).transpose(1, 2, 0, 3).reshape(SEQUENCE_COUNT * KEY_VALUE_HEADS, SEQUENCE_LENGTH, HEAD_DIM)
    document_stacked = jnp.repeat(jnp.transpose(segments), KEY_VALUE_HEADS, axis=0)
    attention_result = lax.map(jax.checkpoint(attend_block), (query_stacked, key_stacked, value_stacked, document_stacked))
    expert_mixed = attention_result.reshape(SEQUENCE_COUNT, KEY_VALUE_HEADS, query_group_width, SEQUENCE_LENGTH, HEAD_DIM).transpose(3, 0, 1, 2, 4).reshape(SEQUENCE_LENGTH, SEQUENCE_COUNT, QUERY_HEADS * HEAD_DIM)
    heads_reduced = reduced_part(reduced_backward(expert_mixed))
    residual_middle = tokens + reduced_backward(precise_einsum('eov,vh->eoh', heads_reduced, attention_output_matrix))
    inv_second = lax.rsqrt(lax.optimization_barrier(jnp.mean(residual_middle * residual_middle, axis=-1, keepdims=True)) + norm_eps)
    middle_normalized = reduced_part(residual_middle * inv_second * mlp_gain)
    logits = reduced_backward(precise_einsum('lsd,de->lse', middle_normalized, w_router))
    probs_all = jax.nn.softmax(logits, axis=-1)
    picked = lax.optimization_barrier(jnp.sum(routes_hot * probs_all[:, :, None, :], axis=-1))
    gate_weights = picked / lax.optimization_barrier(jnp.sum(picked, axis=-1, keepdims=True))
    padded = jnp.concatenate([middle_normalized.reshape(TOKENS, MODEL_DIM), jnp.zeros((1, MODEL_DIM), jnp.float32)], axis=0)
    expert_rows = lax.map(jax.checkpoint(partial(expert_block, padded)), (expert_gate, expert_up, expert_down, slot_table))
    chosen = expert_rows.reshape(EXPERTS * N_COL * CAP, MODEL_DIM)[place_index]
    routed = lax.optimization_barrier(jnp.sum(gate_weights.reshape(TOKENS, TOP, 1) * chosen, axis=1)).reshape(SEQUENCE_LENGTH, SEQUENCE_COUNT, MODEL_DIM)
    shared_gate_preactivation = reduced_backward(precise_einsum('cjb,bk->cjk', middle_normalized, shared_gate_matrix))
    shared_up_preactivation = reduced_backward(precise_einsum('cjb,bk->cjk', middle_normalized, shared_up_matrix))
    shared_hidden_state = reduced_part(jax.nn.silu(shared_gate_preactivation) * shared_up_preactivation)
    shared_output = reduced_backward(precise_einsum('eov,vh->eoh', shared_hidden_state, shared_down_matrix))
    return residual_middle + routed + shared_output

def reference(tokens, segments, routes, attn_gain, query_matrix, key_matrix, value_matrix, attention_output_matrix, mlp_gain, w_router, shared_gate_matrix, shared_up_matrix, shared_down_matrix, expert_gate, expert_up, expert_down, cotangent):
    place_index, slot_table = dispatch_tables(routes)
    routes_hot = (routes[..., None] == jnp.arange(EXPERTS, dtype=jnp.int32)).astype(jnp.float32)
    floats = (tokens.astype(jnp.float32), attn_gain.astype(jnp.float32), query_matrix.astype(jnp.float32), key_matrix.astype(jnp.float32), value_matrix.astype(jnp.float32), attention_output_matrix.astype(jnp.float32), mlp_gain.astype(jnp.float32), w_router.astype(jnp.float32), shared_gate_matrix.astype(jnp.float32), shared_up_matrix.astype(jnp.float32), shared_down_matrix.astype(jnp.float32), expert_gate.astype(jnp.float32), expert_up.astype(jnp.float32), expert_down.astype(jnp.float32))

    def run_layer(params):
        return forward(params, segments, routes_hot, place_index, slot_table)
    result, pullback = jax.vjp(run_layer, floats)
    gradients = pullback(cotangent.astype(jnp.float32))[0]
    return (result.astype(jnp.bfloat16), gradients[0], gradients[1], gradients[2], gradients[3], gradients[4], gradients[5], gradients[6], gradients[7], gradients[8], gradients[9], gradients[10], gradients[11], gradients[12], gradients[13])
```

```python
import functools
import math

import jax
import jax.numpy as jnp
from jax import lax
from jax.experimental import pallas as pl
from jax.experimental.pallas import tpu as pltpu
from jax.sharding import PartitionSpec as P

HEAD_DIM = 128
LANES = 128


norm_eps = 1e-05
rope_base = 500000.0
masked_score = -1e30

f32 = jnp.float32
bf16 = jnp.bfloat16
MESH = pl.DeviceIdType.MESH


def dot(form, left, right):
    return jnp.einsum(form, left, right, preferred_element_type=f32)


def rope_tables(start_place, local_len, head_size):
    places = (start_place + jnp.arange(local_len, dtype=jnp.int32)).astype(f32)
    frequency = jnp.power(
        rope_base, -jnp.arange(0, head_size, 2, dtype=jnp.int32).astype(f32) / head_size
    )
    angles = places[:, None] * frequency[None, :]
    return (jnp.cos(angles), jnp.sin(angles))


def rotate(field, cosine, sine):
    half = cosine.shape[1]
    parts = []
    for start in range(0, field.shape[1], 2 * half):
        front = field[:, start : start + half]
        back = field[:, start + half : start + 2 * half]
        parts.append(front * cosine - back * sine)
        parts.append(back * cosine + front * sine)
    return jnp.concatenate(parts, axis=1)


def rms_scale(values_in):
    return lax.rsqrt(jnp.mean(values_in * values_in, axis=-1, keepdims=True) + norm_eps)


def silu_parts(pre_gate):
    sigmoid_gate = jax.nn.sigmoid(pre_gate)
    silu_gate = pre_gate * sigmoid_gate
    slope_gate = sigmoid_gate * (1.0 + pre_gate * (1.0 - sigmoid_gate))
    return (silu_gate, slope_gate)


def gather_col(part):
    return lax.all_gather(part, "col", axis=0, tiled=False)


def scatter_col(blocks):
    flat = blocks.reshape(-1, blocks.shape[-1])
    return lax.psum_scatter(flat, "col", scatter_dimension=0, tiled=True)


def gather_all(part):
    got = lax.all_gather(part, ("col", "row"), axis=0, tiled=False)
    cols, rows = lax.axis_size("col"), lax.axis_size("row")
    got = got.reshape(cols, rows, *part.shape).transpose(0, 2, 1, 3)
    return got.reshape(cols, part.shape[0], rows * part.shape[1])


def scatter_all(blocks):
    flat = blocks.reshape(-1, blocks.shape[-1])
    part = lax.psum_scatter(flat, "row", scatter_dimension=1, tiled=True)
    return lax.psum_scatter(part, "col", scatter_dimension=0, tiled=True)


def swap_col(blocks):
    return lax.all_to_all(blocks, "col", split_axis=0, concat_axis=0, tiled=True)


class Net:
    def __init__(self, cols, send_sems, recv_sems):
        self.send_sems, self.recv_sems, self.used, self.sent = send_sems, recv_sems, 0, []
        self.cols, self.high_count = cols, cols // 2
        self.me = lax.axis_index("col")
        self.high, self.low = self.me // 2, self.me % 2
        self.row = lax.axis_index("row")
        self.outer, self.core = self.row // 2, self.row % 2

    def block(self, step, other=False):
        high = lax.rem(self.high + self.high_count - step, self.high_count)
        return 2 * high + (1 - self.low if other else self.low)

    def block_ahead(self, step, other=False):
        high = lax.rem(self.high + step, self.high_count)
        return 2 * high + (1 - self.low if other else self.low)

    def z_peer(self, step):
        return {"col": self.block_ahead(step)}

    def y_peer(self):
        return {"col": 2 * self.high + 1 - self.low}

    def x_peer(self):
        return {"row": 2 * (1 - self.outer) + self.core}

    def core_peer(self):
        return {"row": 2 * self.outer + 1 - self.core}

    def col_peer(self, step):
        return {"col": lax.rem(self.me + step, self.cols)}

    def greet(self, peers):
        barrier = pltpu.get_barrier_semaphore()
        for peer in peers:
            pl.semaphore_signal(barrier, inc=1, device_id=peer, device_id_type=MESH)
        pl.semaphore_wait(barrier, len(peers))

    def send(self, source, target, peer):
        copy = pltpu.make_async_remote_copy(
            src_ref=source,
            dst_ref=target,
            send_sem=self.send_sems.at[self.used],
            recv_sem=self.recv_sems.at[self.used],
            device_id=peer,
            device_id_type=MESH,
        )
        self.used += 1
        copy.start()
        self.sent.append(copy)
        return copy

    def finish(self):
        for copy in self.sent:
            copy.wait_send()


def col_peers(net):
    return [net.z_peer(step) for step in range(1, net.high_count)] + [net.y_peer()]


def row_peers(net):
    return [net.x_peer(), net.core_peer()]


def gather_kernel(cols, kinds, *refs):
    count = len(kinds)
    ins, outs = refs[:count], refs[count : 2 * count]
    send_sems, recv_sems, local_sems = refs[2 * count :]
    net = Net(cols, send_sems, recv_sems)
    swaps = "swap" in kinds
    if swaps:
        peers = [net.col_peer(step) for step in range(1, cols)]
    else:
        peers = col_peers(net)
    net.greet(peers + (row_peers(net) if "all" in kinds else []))

    def place(i, block):
        if kinds[i] == "all":
            part = ins[i].shape[1]
            return outs[i].at[block, :, pl.ds(pl.multiple_of(net.row * part, LANES), part)]
        return outs[i].at[block]

    def other_place(i, block):
        part = ins[i].shape[1]
        row = 2 * (1 - net.outer) + net.core
        return outs[i].at[block, :, pl.ds(pl.multiple_of(row * part, LANES), part)]

    locals_ = []
    steps = range(1, net.high_count)
    along_z, along_y, along_x, crossed = {}, {}, {}, []

    def spread(i, source, block, key):
        along_x[i, key] = net.send(source, place(i, block), net.x_peer())
        crossed.append(net.send(source, place(i, block), net.core_peer()))

    for i, kind in enumerate(kinds):
        own = ins[i].at[net.me] if kind == "swap" else ins[i]
        local = pltpu.make_async_copy(own, place(i, net.me), local_sems.at[i])
        local.start()
        locals_.append(local)
        if kind == "swap":
            for step in range(1, cols):
                block = lax.rem(net.me + step, cols)
                crossed.append(net.send(ins[i].at[block], outs[i].at[net.me], net.col_peer(step)))
            continue
        for step in reversed(steps):
            along_z[i, step] = net.send(ins[i], place(i, net.me), net.z_peer(step))
        along_y[i, 0] = net.send(ins[i], place(i, net.me), net.y_peer())
        if kind == "all":
            spread(i, ins[i], net.me, (0, False))
    for step in steps:
        for i, kind in enumerate(kinds):
            if kind == "swap":
                continue
            block = net.block(step)
            along_z[i, step].wait_recv()
            along_y[i, step] = net.send(place(i, block), place(i, block), net.y_peer())
            if kind == "all":
                spread(i, place(i, block), block, (step, False))
    for step in range(net.high_count):
        for i, kind in enumerate(kinds):
            if kind == "swap":
                continue
            block = net.block(step, True)
            along_y[i, step].wait_recv()
            if kind == "all":
                spread(i, place(i, block), block, (step, True))
    for other in (False, True):
        for step in range(net.high_count):
            for i, kind in enumerate(kinds):
                if kind == "all":
                    block = net.block(step, other)
                    along_x[i, (step, other)].wait_recv()
                    slot = other_place(i, block)
                    crossed.append(net.send(slot, slot, net.core_peer()))
    for copy in crossed:
        copy.wait_recv()
    for local in locals_:
        local.wait()
    net.finish()


def gather(cols, collective_id, *pairs):
    kinds = [kind for kind, _ in pairs]
    arrays = [array for _, array in pairs]
    copies = 0
    shapes = []
    for kind, array in pairs:
        if kind == "swap":
            shapes.append(jax.ShapeDtypeStruct(array.shape, array.dtype))
            copies += cols
        elif kind == "col":
            shapes.append(jax.ShapeDtypeStruct((cols, *array.shape), array.dtype))
            copies += cols
        else:
            rows = lax.axis_size("row")
            shape = (cols, array.shape[0], rows * array.shape[1])
            shapes.append(jax.ShapeDtypeStruct(shape, array.dtype))
            copies += 4 * cols
    return pl.pallas_call(
        functools.partial(gather_kernel, cols, kinds),
        out_shape=shapes,
        in_specs=[pl.BlockSpec(memory_space=pl.ANY)] * len(pairs),
        out_specs=[pl.BlockSpec(memory_space=pl.ANY)] * len(pairs),
        scratch_shapes=[
            pltpu.SemaphoreType.DMA((copies,)),
            pltpu.SemaphoreType.DMA((copies,)),
            pltpu.SemaphoreType.DMA((len(pairs),)),
        ],
        compiler_params=pltpu.CompilerParams(collective_id=collective_id, has_side_effects=True),
        name=f"gather_{collective_id}",
    )(*arrays)


def add_rows(target, terms):
    rows = target.shape[0]
    piece = 32 if rows % 32 == 0 else rows

    def body(index, carry):
        at = pl.ds(pl.multiple_of(index * piece, piece), piece)
        total = terms[0][at, :].astype(f32)
        for term in terms[1:]:
            total = total + term[at, :].astype(f32)
        target[at, :] = total.astype(target.dtype)
        return carry

    lax.fori_loop(0, rows // piece, body, 0)


def scatter_col_steps(net, part, from_y, to_y, from_z, to_z, out, ready):
    along_y, along_z = {}, {}
    order = [*range(1, net.high_count), 0]
    for step in order:
        block = net.block_ahead(step, True)
        ready(block)
        if to_y is None:
            source = part.at[block]
        else:
            source = to_y.at[step]
            add_rows(source, [part.at[block]])
        along_y[step] = net.send(source, from_y.at[step], net.y_peer())
    for step in order:
        block = net.block_ahead(step)
        ready(block)
        along_y[step].wait_recv()
        if step:
            add_rows(to_z.at[step - 1], [part.at[block], from_y.at[step]])
            along_z[step] = net.send(to_z.at[step - 1], from_z.at[step - 1], net.z_peer(step))
    for step in range(1, net.high_count):
        along_z[step].wait_recv()
    terms = [from_z.at[step - 1] for step in range(1, net.high_count)]
    add_rows(out, [part.at[net.me], from_y.at[0], *terms])


def scatter_col_kernel(cols, count, *refs):
    parts, outs, scratch = refs[:count], refs[count : 2 * count], refs[2 * count :]
    send_sems, recv_sems = scratch[-2:]
    net = Net(cols, send_sems, recv_sems)
    net.greet(col_peers(net))
    for i in range(count):
        from_y, from_z, to_z = scratch[3 * i : 3 * i + 3]
        scatter_col_steps(
            net, parts[i], from_y, None, from_z, to_z, outs[i], lambda block: None
        )
    net.finish()


def scatter_col_call(cols, collective_id, *parts):
    high_count = cols // 2
    scratch = []
    for part in parts:
        shape = part.shape[1:]
        scratch += [
            pltpu.VMEM((high_count, *shape), bf16),
            pltpu.VMEM((high_count - 1, *shape), bf16),
            pltpu.VMEM((high_count - 1, *shape), bf16),
        ]
    copies = cols * len(parts)
    return pl.pallas_call(
        functools.partial(scatter_col_kernel, cols, len(parts)),
        out_shape=[jax.ShapeDtypeStruct(part.shape[1:], f32) for part in parts],
        in_specs=[pl.BlockSpec(memory_space=pltpu.VMEM)] * len(parts),
        out_specs=[pl.BlockSpec(memory_space=pltpu.VMEM)] * len(parts),
        scratch_shapes=[
            *scratch,
            pltpu.SemaphoreType.DMA((copies,)),
            pltpu.SemaphoreType.DMA((copies,)),
        ],
        compiler_params=pltpu.CompilerParams(
            collective_id=collective_id, has_side_effects=True, vmem_limit_bytes=56 << 20
        ),
        name=f"scatter_col_{collective_id}",
    )(*parts)


def scatter_all_kernel(cols, spread_back, part, out, *scratch):
    if spread_back:
        kept, *scratch = scratch
    from_core, to_x, from_x, total, from_y, to_y, from_z, to_z, send_sems, recv_sems = scratch
    net = Net(cols, send_sems, recv_sems)
    net.greet(col_peers(net) + row_peers(net))
    width = total.shape[2]

    def features(row):
        return pl.ds(pl.multiple_of(row * width, LANES), width)

    order = [*range(1, net.high_count), 0]
    blocks = [net.block_ahead(step, True) for step in order]
    blocks += [net.block_ahead(step) for step in order]
    across, along_x = {}, {}
    for far in (1, 0):
        outer = 1 - net.outer if far else net.outer
        for j, block in enumerate(blocks):
            source = part.at[block, :, features(2 * outer + 1 - net.core)]
            across[j, far] = net.send(source, from_core.at[far, block], net.core_peer())
    for j, block in enumerate(blocks):
        across[j, 1].wait_recv()
        mine = part.at[block, :, features(2 * (1 - net.outer) + net.core)]
        add_rows(to_x.at[block], [mine, from_core.at[1, block]])
        along_x[j] = net.send(to_x.at[block], from_x.at[block], net.x_peer())
    at = iter(range(len(blocks)))

    def ready(block):
        j = next(at)
        across[j, 0].wait_recv()
        along_x[j].wait_recv()
        mine = part.at[block, :, features(net.row)]
        add_rows(total.at[block], [mine, from_core.at[0, block], from_x.at[block]])

    if not spread_back:
        scatter_col_steps(net, total, from_y, to_y, from_z, to_z, out, ready)
        net.finish()
        return
    scatter_col_steps(net, total, from_y, to_y, from_z, to_z, kept, ready)
    own, other = features(net.row), features(2 * (1 - net.outer) + net.core)
    out[:, own] = kept[...].astype(bf16)
    far = net.send(out.at[:, own], out.at[:, own], net.x_peer())
    near = net.send(out.at[:, own], out.at[:, own], net.core_peer())
    far.wait_recv()
    last = net.send(out.at[:, other], out.at[:, other], net.core_peer())
    near.wait_recv()
    last.wait_recv()
    net.finish()


def scatter_all_call(cols, collective_id, part, spread_back=False):
    high_count = cols // 2
    rows, width = part.shape[1], part.shape[2] // lax.axis_size("row")
    piece = (rows, width)
    copies = 4 * cols + 4
    out = jax.ShapeDtypeStruct(piece, f32)
    if spread_back:
        out = jax.ShapeDtypeStruct((rows, part.shape[2]), bf16)
    return pl.pallas_call(
        functools.partial(scatter_all_kernel, cols, spread_back),
        out_shape=out,
        in_specs=[pl.BlockSpec(memory_space=pltpu.VMEM)],
        out_specs=pl.BlockSpec(memory_space=pltpu.VMEM),
        scratch_shapes=[
            *([pltpu.VMEM(piece, f32)] if spread_back else []),
            pltpu.VMEM((2, cols, *piece), bf16),
            pltpu.VMEM((cols, *piece), bf16),
            pltpu.VMEM((cols, *piece), bf16),
            pltpu.VMEM((cols, *piece), f32),
            pltpu.VMEM((high_count, *piece), bf16),
            pltpu.VMEM((high_count, *piece), bf16),
            pltpu.VMEM((high_count - 1, *piece), bf16),
            pltpu.VMEM((high_count - 1, *piece), bf16),
            pltpu.SemaphoreType.DMA((copies,)),
            pltpu.SemaphoreType.DMA((copies,)),
        ],
        compiler_params=pltpu.CompilerParams(
            collective_id=collective_id, has_side_effects=True, vmem_limit_bytes=56 << 20
        ),
        name=f"scatter_all_{collective_id}",
    )(part)


def sum_row_kernel(part, out, from_core, to_x, from_x, send_sems, recv_sems):
    net = Net(2, send_sems, recv_sems)
    net.greet(row_peers(net))
    pieces = from_core.shape[0]
    rows = from_core.shape[1]

    def piece(core, i):
        start = (core * pieces + i) * rows
        return pl.ds(pl.multiple_of(start, rows), rows)

    across = [
        net.send(part.at[piece(1 - net.core, i)], from_core.at[i], net.core_peer())
        for i in range(pieces)
    ]
    along, back = [], []
    for i in range(pieces):
        across[i].wait_recv()
        add_rows(to_x.at[i], [part.at[piece(net.core, i)], from_core.at[i]])
        along.append(net.send(to_x.at[i], from_x.at[i], net.x_peer()))
    for i in range(pieces):
        along[i].wait_recv()
        mine = piece(net.core, i)
        add_rows(out.at[mine], [to_x.at[i], from_x.at[i]])
        back.append(net.send(out.at[mine], out.at[mine], net.core_peer()))
    for copy in back:
        copy.wait_recv()
    net.finish()


def sum_row_call(collective_id, part):
    pieces = 4
    rows = part.shape[0] // 2 // pieces
    piece = (pieces, rows, part.shape[1])
    return pl.pallas_call(
        sum_row_kernel,
        out_shape=jax.ShapeDtypeStruct(part.shape, bf16),
        in_specs=[pl.BlockSpec(memory_space=pltpu.VMEM)],
        out_specs=pl.BlockSpec(memory_space=pltpu.VMEM),
        scratch_shapes=[
            pltpu.VMEM(piece, bf16),
            pltpu.VMEM(piece, bf16),
            pltpu.VMEM(piece, bf16),
            pltpu.SemaphoreType.DMA((3 * pieces,)),
            pltpu.SemaphoreType.DMA((3 * pieces,)),
        ],
        compiler_params=pltpu.CompilerParams(
            collective_id=collective_id, has_side_effects=True, vmem_limit_bytes=32 << 20
        ),
        name=f"sum_row_{collective_id}",
    )(part)


def fits(cols, rows, width):
    return cols % 2 == 0 and cols * rows * width * 2 <= 12 << 20


def gather_parts(kernels, cols, collective_id, *pairs):
    if kernels:
        return gather(cols, collective_id, *pairs)
    ways = {"col": gather_col, "all": gather_all, "swap": swap_col}
    return [ways[kind](array) for kind, array in pairs]


def scatter_col_parts(kernels, cols, collective_id, *parts):
    if kernels:
        return scatter_col_call(cols, collective_id, *parts)
    return [scatter_col(part).astype(f32) for part in parts]


def scatter_all_part(kernels, cols, collective_id, part):
    if kernels:
        return scatter_all_call(cols, collective_id, part)
    return scatter_all(part).astype(f32)


def scatter_all_back(kernels, cols, collective_id, part):
    if kernels:
        return scatter_all_call(cols, collective_id, part, True)
    return lax.all_gather(scatter_all(part), "row", axis=1, tiled=True)


def sum_row(kernels, collective_id, part):
    if kernels:
        return sum_row_call(collective_id, part)
    return lax.psum(part, "row")


def on_device(
    tokens,
    segments,
    routes,
    attn_gain,
    query_matrix,
    key_matrix,
    value_matrix,
    attention_output_matrix,
    mlp_gain,
    w_router,
    shared_gate_matrix,
    shared_up_matrix,
    shared_down_matrix,
    expert_gate,
    expert_up,
    expert_down,
    cotangent,
):
    local_len, seqs, width = tokens.shape
    cols = lax.axis_size("col")
    col_index = lax.axis_index("col")
    rows_w = query_matrix.shape[0]
    full_len = local_len * cols
    size = HEAD_DIM
    q_width = query_matrix.shape[1]
    kv_width = key_matrix.shape[1]
    kv_local = kv_width // size
    group = q_width // kv_width
    row_width = cotangent.shape[2]
    toks = local_len * seqs
    top = routes.shape[2]
    experts = w_router.shape[1]
    exp_local = expert_gate.shape[0]
    hidden_local = expert_gate.shape[2]
    capacity = max(2, toks * top * 4 // (3 * experts))
    shared_part = shared_gate_matrix.shape[1] // cols
    scale = 1.0 / math.sqrt(size)
    kernels = fits(cols, toks, width)

    def seq_major(a):
        return jnp.swapaxes(a, 0, 1).reshape(toks, a.shape[2])

    misc = jnp.concatenate(
        [
            w_router,
            attn_gain[:, None],
            mlp_gain[:, None],
            jnp.zeros((rows_w, LANES - experts - 2), bf16),
        ],
        axis=1,
    )
    first_weights = jnp.concatenate([query_matrix, key_matrix, value_matrix, misc], axis=1)
    shared_weights = jnp.concatenate(
        [
            shared_gate_matrix.reshape(rows_w, cols, shared_part),
            shared_up_matrix.reshape(rows_w, cols, shared_part),
            shared_down_matrix.T.reshape(rows_w, cols, shared_part),
        ],
        axis=2,
    )
    first_weights, out_weights, shared_weights, grad_all = gather_parts(
        kernels,
        cols,
        0,
        ("col", first_weights),
        ("col", attention_output_matrix.T),
        ("swap", jnp.swapaxes(shared_weights, 0, 1)),
        ("all", seq_major(cotangent).astype(bf16)),
    )
    first_weights = first_weights.reshape(width, -1)
    out_weights = out_weights.reshape(width, q_width)
    shared_weights = shared_weights.reshape(width, 3 * shared_part)
    qkv_width = q_width + 2 * kv_width
    qkv_weights = first_weights[:, :qkv_width]
    router = first_weights[:, qkv_width : qkv_width + experts]
    gain_one = first_weights[:, qkv_width + experts].astype(f32)
    gain_two = first_weights[:, qkv_width + experts + 1].astype(f32)
    shared_in_weights = shared_weights[:, : 2 * shared_part]
    shared_down = shared_weights[:, 2 * shared_part :]


    x = seq_major(tokens).astype(f32)
    inv_first = rms_scale(x)
    base_first = x * inv_first
    h1 = (base_first * gain_one).astype(bf16)
    qkv = dot("tb,bk->tk", h1, qkv_weights)
    cosine, sine = rope_tables(col_index * local_len, local_len, size)
    cosine, sine = jnp.tile(cosine, (seqs, 1)), jnp.tile(sine, (seqs, 1))
    qk = rotate(qkv[:, : q_width + kv_width], cosine, sine).astype(bf16)
    value_low = qkv[:, q_width + kv_width :].astype(bf16)

    flat_routes = seq_major(routes)
    named = flat_routes[:, :, None] == jnp.arange(experts, dtype=jnp.int32)
    mask = jnp.any(named, axis=1)
    order = jnp.arange(toks, dtype=jnp.int32)
    upto = (order[None, :] <= order[:, None]).astype(bf16)
    rank = jnp.where(mask, dot("ij,je->ie", upto, mask.astype(bf16)), 0.0)

    doc = jnp.transpose(segments)
    side = jnp.concatenate(
        [
            rank.astype(bf16),
            doc.reshape(toks, 1).astype(bf16),
            jnp.zeros((toks, LANES - experts - 1), bf16),
        ],
        axis=1,
    )
    (kv_all,) = gather_parts(
        kernels, cols, 1, ("col", jnp.concatenate([qk[:, q_width:], value_low, side], axis=1))
    )
    rank_all = kv_all[:, :, 2 * kv_width : 2 * kv_width + experts]
    kv_seq = jnp.swapaxes(kv_all.reshape(cols, seqs, local_len, -1), 0, 1)
    kv_seq = kv_seq.reshape(seqs, full_len, -1)
    key_all = kv_seq[:, :, :kv_width].reshape(seqs, full_len, kv_local, size)
    value_all = kv_seq[:, :, kv_width : 2 * kv_width].reshape(seqs, full_len, kv_local, size)
    doc_all = kv_seq[:, :, 2 * kv_width + experts]

    def to_grid(flat):
        shaped = flat.reshape(seqs, local_len, kv_local, group, size)
        return shaped.transpose(0, 2, 3, 1, 4).reshape(seqs, kv_local, group * local_len, size)

    def from_grid(grid):
        shaped = grid.reshape(seqs, kv_local, group, local_len, size)
        return shaped.transpose(0, 3, 1, 2, 4).reshape(toks, q_width)

    query_grid = to_grid(qk[:, :q_width])
    place = col_index * local_len + jnp.arange(local_len, dtype=jnp.int32)
    same = doc.astype(bf16)[:, :, None] == doc_all[:, None, :]
    causal = jnp.arange(full_len, dtype=jnp.int32)[None, :] <= place[:, None]
    allowed = jnp.tile(same & causal[None], (1, group, 1))[:, None]
    scores = dot("shrd,skhd->shrk", query_grid, key_all) * scale
    scores = jnp.where(allowed, scores, masked_score)
    weights = jnp.exp(scores - jnp.max(scores, axis=-1, keepdims=True))
    weights = jnp.where(allowed, weights, 0.0)
    probs = (weights / jnp.sum(weights, axis=-1, keepdims=True)).astype(bf16)
    heads = from_grid(dot("shrk,skhd->shrd", probs, value_all)).astype(bf16)
    attn = sum_row(kernels, 2, dot("tk,bk->tb", heads, out_weights).astype(bf16))
    middle = x + attn.astype(f32)

    inv_second = rms_scale(middle)
    base_second = middle * inv_second
    h2 = (base_second * gain_two).astype(bf16)
    row_index = lax.axis_index("row")
    h2_slice = lax.dynamic_slice_in_dim(h2, row_index * row_width, row_width, 1)
    (h2_all,) = gather_parts(kernels, cols, 3, ("all", h2_slice))

    all_mask = (rank_all > 0).astype(f32)
    all_probs = jax.nn.softmax(dot("ctd,de->cte", h2_all, router), axis=-1)
    all_picked = all_probs * all_mask
    all_gate = all_picked / jnp.sum(all_picked, axis=-1, keepdims=True)
    own = col_index * exp_local
    own_gate = lax.dynamic_slice_in_dim(all_gate, own, exp_local, 2)
    own_rank = lax.dynamic_slice_in_dim(rank_all, own, exp_local, 2).astype(jnp.int32)
    slots = jnp.arange(1, capacity + 1, dtype=jnp.int32)
    pick = jnp.swapaxes(own_rank, 1, 2)[:, :, None, :] == slots[:, None]
    slot_gate = jnp.sum(
        jnp.where(pick, jnp.swapaxes(own_gate, 1, 2)[:, :, None, :], 0.0), axis=3
    )[..., None]
    pick_low = pick.astype(bf16).reshape(cols, exp_local * capacity, toks)
    slot_shape = (cols, exp_local, capacity, width)
    slot_rows = dot("cut,ctd->cud", pick_low, h2_all).astype(bf16).reshape(slot_shape)
    slot_grad = dot("cut,ctd->cud", pick_low, grad_all).astype(bf16).reshape(slot_shape)
    gate_pre = dot("necd,edf->necf", slot_rows, expert_gate)
    up_pre = dot("necd,edf->necf", slot_rows, expert_up)
    silu_gate, slope_gate = silu_parts(gate_pre)
    hidden = silu_gate * up_pre
    gated = (hidden * slot_gate).astype(bf16)
    slot_out = dot("necf,efd->necd", gated, expert_down).astype(bf16)
    hidden_grad = dot("necd,efd->necf", slot_grad, expert_down)
    slot_dots = jnp.sum(hidden * hidden_grad, axis=-1)
    hidden_grad = hidden_grad * slot_gate
    gate_grad = (hidden_grad * up_pre * slope_gate).astype(bf16)
    up_grad = (hidden_grad * silu_gate).astype(bf16)
    slot_back = dot("necf,edf->necd", gate_grad, expert_gate)
    slot_back = (slot_back + dot("necf,edf->necd", up_grad, expert_up)).astype(bf16)
    grad_expert_down = dot("necf,necd->efd", gated, slot_grad)
    grad_expert_gate = dot("necd,necf->edf", slot_rows, gate_grad)
    grad_expert_up = dot("necd,necf->edf", slot_rows, up_grad)
    pick_flat = pick_low.reshape(cols, exp_local * capacity, toks)
    slot_out = slot_out.reshape(cols, exp_local * capacity, width)
    slot_back = slot_back.reshape(cols, exp_local * capacity, width)

    shared_pre = dot("ctd,dk->ctk", h2_all, shared_in_weights)
    sgate_pre, sup_pre = shared_pre[:, :, :shared_part], shared_pre[:, :, shared_part:]
    shared_silu, shared_slope = silu_parts(sgate_pre)
    shared_hidden = (shared_silu * sup_pre).astype(bf16)
    part_out = dot("cut,cud->ctd", pick_flat, slot_out) + dot(
        "ctk,dk->ctd", shared_hidden, shared_down
    )
    shared_hgrad = dot("ctd,dk->ctk", grad_all, shared_down)
    shared_grads = jnp.concatenate(
        [shared_hgrad * sup_pre * shared_slope, shared_hgrad * shared_silu], axis=2
    ).astype(bf16)
    part_back = dot("cut,cud->ctd", pick_flat, slot_back) + dot(
        "ctk,dk->ctd", shared_grads, shared_in_weights
    )
    token_dots = jnp.einsum(
        "ceu,ceut->cte", slot_dots, pick.astype(f32), precision=lax.Precision.HIGHEST
    )
    gate_dots = lax.psum(swap_col(token_dots), "row")
    gate_dots = jnp.swapaxes(gate_dots, 0, 1).reshape(toks, experts)

    back_full = scatter_all_back(kernels, cols, 4, part_back.astype(bf16)).astype(f32)
    out_slice = scatter_all_part(kernels, cols, 5, part_out.astype(bf16))
    middle_slice = lax.dynamic_slice_in_dim(middle, row_index * row_width, row_width, 1)
    block_out = (middle_slice + out_slice).astype(bf16)

    shared_share = jnp.concatenate(
        [dot("ctd,ctk->dk", h2_all, shared_grads), dot("ctd,ctk->dk", grad_all, shared_hidden)],
        axis=1,
    ).astype(bf16)
    shared_share = swap_col(shared_share.reshape(cols, rows_w, 3 * shared_part))
    shared_share = jnp.swapaxes(shared_share, 0, 1).astype(f32)
    share_sgate, share_sup, share_sdown = (
        shared_share[:, :, i * shared_part : (i + 1) * shared_part].reshape(rows_w, -1)
        for i in range(3)
    )

    logits = dot("td,de->te", h2, router)
    probs_router = jax.nn.softmax(logits, axis=-1)
    picked = jnp.where(mask, probs_router, 0.0)
    pick_total = jnp.sum(picked, axis=-1, keepdims=True)
    gate = picked / pick_total
    pick_grad = gate_dots - jnp.sum(gate * gate_dots, axis=-1, keepdims=True)
    prob_grad = jnp.where(mask, pick_grad / pick_total, 0.0)
    logit_grad = probs_router * (
        prob_grad - jnp.sum(probs_router * prob_grad, axis=-1, keepdims=True)
    )
    logit_low = logit_grad.astype(bf16)
    grad_router = dot("td,te->de", h2, logit_low)

    back_full = back_full + dot("te,de->td", logit_low, router)
    grad_own = lax.dynamic_slice_in_dim(grad_all, col_index, 1, 0)[0].astype(f32)
    grad_gain_two = jnp.sum(back_full * base_second, axis=0)
    scaled_two = back_full * gain_two
    middle_grad = (
        inv_second
        * (scaled_two - base_second * jnp.mean(scaled_two * base_second, axis=-1, keepdims=True))
        + grad_own
    )
    attn_grad = middle_grad.astype(bf16)
    grad_out = dot("td,tk->dk", attn_grad, heads).astype(bf16)

    heads_grad = to_grid(dot("td,dk->tk", attn_grad, out_weights).astype(bf16))
    value_grad = dot("shrk,shrd->skhd", probs, heads_grad)
    weight_grad = dot("shrd,skhd->shrk", heads_grad, value_all)
    probs_wide = probs.astype(f32)
    delta = jnp.sum(probs_wide * weight_grad, axis=-1, keepdims=True)
    score_grad = (probs_wide * (weight_grad - delta)).astype(bf16)
    query_grad = from_grid(dot("shrk,skhd->shrd", score_grad, key_all)) * scale
    key_grad = dot("shrk,shrd->skhd", score_grad, query_grid) * scale
    kv_grad = jnp.concatenate(
        [key_grad.reshape(seqs, full_len, kv_width), value_grad.reshape(seqs, full_len, kv_width)],
        axis=2,
    ).astype(bf16)
    kv_grad = jnp.swapaxes(kv_grad.reshape(seqs, cols, local_len, 2 * kv_width), 0, 1)
    (kv_share,) = scatter_col_parts(kernels, cols, 6, kv_grad.reshape(cols, toks, 2 * kv_width))
    qk_grad = rotate(
        jnp.concatenate([query_grad, kv_share[:, :kv_width]], axis=1), cosine, -sine
    )
    qkv_grad = jnp.concatenate([qk_grad, kv_share[:, kv_width:]], axis=1).astype(bf16)
    first_grad = dot("tk,bk->tb", qkv_grad, qkv_weights).astype(bf16)
    first_grad = sum_row(kernels, 7, first_grad).astype(f32)
    grad_gain_one = jnp.sum(first_grad * base_first, axis=0)
    scaled_one = first_grad * gain_one
    token_grad = (
        inv_first
        * (scaled_one - base_first * jnp.mean(scaled_one * base_first, axis=-1, keepdims=True))
        + middle_grad
    )
    grad_first = jnp.concatenate(
        [
            dot("tb,tk->bk", h1, qkv_grad),
            grad_router,
            grad_gain_one[:, None],
            grad_gain_two[:, None],
            jnp.zeros((width, LANES - experts - 2), f32),
        ],
        axis=1,
    ).astype(bf16)
    share_out, share_first = scatter_col_parts(
        kernels,
        cols,
        8,
        grad_out.reshape(cols, rows_w, q_width),
        grad_first.reshape(cols, rows_w, -1),
    )

    def tokens_first(a):
        return jnp.swapaxes(a.reshape(seqs, local_len, a.shape[1]), 0, 1)

    return (
        tokens_first(block_out),
        tokens_first(token_grad),
        share_first[:, qkv_width + experts],
        share_first[:, :q_width],
        share_first[:, q_width : q_width + kv_width],
        share_first[:, q_width + kv_width : qkv_width],
        share_out.T,
        share_first[:, qkv_width + experts + 1],
        share_first[:, qkv_width : qkv_width + experts],
        share_sgate,
        share_sup,
        share_sdown.T,
        grad_expert_gate,
        grad_expert_up,
        grad_expert_down,
    )


def solution(mesh):
    in_specs = (
        P("col", None, None),
        P("col", None),
        P("col", None, None),
        P("col"),
        P("col", "row"),
        P("col", "row"),
        P("col", "row"),
        P("row", "col"),
        P("col"),
        P("col", None),
        P("col", "row"),
        P("col", "row"),
        P("row", "col"),
        P("col", None, "row"),
        P("col", None, "row"),
        P("col", "row", None),
        P("col", None, "row"),
    )
    out_specs = (
        P("col", None, "row"),
        P("col", None, None),
        P("col"),
        P("col", "row"),
        P("col", "row"),
        P("col", "row"),
        P("row", "col"),
        P("col"),
        P("col", None),
        P("col", "row"),
        P("col", "row"),
        P("row", "col"),
        P("col", None, "row"),
        P("col", None, "row"),
        P("col", "row", None),
    )
    return jax.shard_map(
        on_device, mesh=mesh, in_specs=in_specs, out_specs=out_specs, check_vma=False
    )
```

```python
import functools
import math

import jax
import jax.numpy as jnp
from jax import lax
from jax.experimental import pallas as pl
from jax.experimental.pallas import tpu as pltpu
from jax.sharding import PartitionSpec as P

HEAD_DIM = 128
LANES = 128


norm_eps = 1e-05
rope_base = 500000.0
masked_score = -1e30

f32 = jnp.float32
bf16 = jnp.bfloat16
MESH = pl.DeviceIdType.MESH


def dot(form, left, right):
    return jnp.einsum(form, left, right, preferred_element_type=f32)


def rope_tables(start_place, local_len, head_size):
    places = (start_place + jnp.arange(local_len, dtype=jnp.int32)).astype(f32)
    frequency = jnp.power(
        rope_base, -jnp.arange(0, head_size, 2, dtype=jnp.int32).astype(f32) / head_size
    )
    angles = places[:, None] * frequency[None, :]
    return (jnp.cos(angles), jnp.sin(angles))


def rotate(field, cosine, sine):
    half = cosine.shape[1]
    parts = []
    for start in range(0, field.shape[1], 2 * half):
        front = field[:, start : start + half]
        back = field[:, start + half : start + 2 * half]
        parts.append(front * cosine - back * sine)
        parts.append(back * cosine + front * sine)
    return jnp.concatenate(parts, axis=1)


def rms_scale(values_in):
    return lax.rsqrt(jnp.mean(values_in * values_in, axis=-1, keepdims=True) + norm_eps)


def silu_parts(pre_gate):
    sigmoid_gate = jax.nn.sigmoid(pre_gate)
    silu_gate = pre_gate * sigmoid_gate
    slope_gate = sigmoid_gate * (1.0 + pre_gate * (1.0 - sigmoid_gate))
    return (silu_gate, slope_gate)


def gather_col(part):
    return lax.all_gather(part, "col", axis=0, tiled=False)


def scatter_col(blocks):
    flat = blocks.reshape(-1, blocks.shape[-1])
    return lax.psum_scatter(flat, "col", scatter_dimension=0, tiled=True)


def gather_all(part):
    got = lax.all_gather(part, ("col", "row"), axis=0, tiled=False)
    cols, rows = lax.axis_size("col"), lax.axis_size("row")
    got = got.reshape(cols, rows, *part.shape).transpose(0, 2, 1, 3)
    return got.reshape(cols, part.shape[0], rows * part.shape[1])


def scatter_all(blocks):
    flat = blocks.reshape(-1, blocks.shape[-1])
    part = lax.psum_scatter(flat, "row", scatter_dimension=1, tiled=True)
    return lax.psum_scatter(part, "col", scatter_dimension=0, tiled=True)


def swap_col(blocks):
    return lax.all_to_all(blocks, "col", split_axis=0, concat_axis=0, tiled=True)


class Net:
    def __init__(self, cols, send_sems, recv_sems):
        self.send_sems, self.recv_sems, self.used, self.sent = send_sems, recv_sems, 0, []
        self.cols, self.high_count = cols, cols // 2
        self.me = lax.axis_index("col")
        self.high, self.low = self.me // 2, self.me % 2
        self.row = lax.axis_index("row")
        self.outer, self.core = self.row // 2, self.row % 2

    def block(self, step, other=False):
        high = lax.rem(self.high + self.high_count - step, self.high_count)
        return 2 * high + (1 - self.low if other else self.low)

    def block_ahead(self, step, other=False):
        high = lax.rem(self.high + step, self.high_count)
        return 2 * high + (1 - self.low if other else self.low)

    def z_peer(self, step):
        return {"col": self.block_ahead(step)}

    def y_peer(self):
        return {"col": 2 * self.high + 1 - self.low}

    def x_peer(self):
        return {"row": 2 * (1 - self.outer) + self.core}

    def core_peer(self):
        return {"row": 2 * self.outer + 1 - self.core}

    def col_peer(self, step):
        return {"col": lax.rem(self.me + step, self.cols)}

    def greet(self, peers):
        barrier = pltpu.get_barrier_semaphore()
        for peer in peers:
            pl.semaphore_signal(barrier, inc=1, device_id=peer, device_id_type=MESH)
        pl.semaphore_wait(barrier, len(peers))

    def send(self, source, target, peer):
        copy = pltpu.make_async_remote_copy(
            src_ref=source,
            dst_ref=target,
            send_sem=self.send_sems.at[self.used],
            recv_sem=self.recv_sems.at[self.used],
            device_id=peer,
            device_id_type=MESH,
        )
        self.used += 1
        copy.start()
        self.sent.append(copy)
        return copy

    def left(self, copy):
        copy.wait_send()
        self.sent = [other for other in self.sent if other is not copy]

    def finish(self):
        for copy in self.sent:
            copy.wait_send()


def col_peers(net):
    return [net.z_peer(step) for step in range(1, net.high_count)] + [net.y_peer()]


def row_peers(net):
    return [net.x_peer(), net.core_peer()]


def gather_kernel(cols, kinds, pieces, *refs):
    count = len(kinds)
    ins, outs = refs[:count], refs[count : 2 * count]
    send_sems, recv_sems, local_sems = refs[2 * count :]
    net = Net(cols, send_sems, recv_sems)
    swaps = [i for i, kind in enumerate(kinds) if kind == "swap"]
    peers = [net.col_peer(step) for step in range(1, cols)] if swaps else col_peers(net)
    net.greet(peers + (row_peers(net) if "all" in kinds else []))
    other_row = 2 * (1 - net.outer) + net.core

    def place(i, block, rows, row):
        if kinds[i] == "all":
            part = ins[i].shape[1]
            return outs[i].at[block, rows, pl.ds(pl.multiple_of(row * part, LANES), part)]
        return outs[i].at[block, rows]

    order = []
    for i in sorted(range(count), key=lambda i: kinds[i] != "all"):
        if kinds[i] != "swap":
            rows = ins[i].shape[0] // pieces[i]
            order += [(i, pl.ds(q * rows, rows)) for q in range(pieces[i])]
    swap_sends = [(i, step) for i in swaps for step in range(1, cols)]
    steps = range(net.high_count)
    along_z, along_y, along_x, to_core, moved = {}, {}, {}, {}, []
    locals_ = []
    for i, kind in enumerate(kinds):
        own = ins[i].at[net.me] if kind == "swap" else ins[i]
        slot = outs[i].at[net.me] if kind == "swap" else place(
            i, net.me, pl.ds(0, ins[i].shape[0]), net.row
        )
        local = pltpu.make_async_copy(own, slot, local_sems.at[i])
        local.start()
        locals_.append(local)

    def swap_next():
        if swap_sends:
            i, step = swap_sends.pop(0)
            block = lax.rem(net.me + step, cols)
            moved.append(net.send(ins[i].at[block], outs[i].at[net.me], net.col_peer(step)))

    def in_chip(q, step, other, source, slot):
        if kinds[order[q][0]] == "all":
            along_x[q, step, other] = net.send(source, slot, net.x_peer())
            to_core[q, step, other] = net.send(source, slot, net.core_peer())

    def start(q):
        i, rows = order[q]
        source, slot = ins[i].at[rows], place(i, net.me, rows, net.row)
        for step in reversed(range(1, net.high_count)):
            along_z[q, step] = net.send(source, slot, net.z_peer(step))
        along_y[q, 0] = net.send(source, slot, net.y_peer())
        in_chip(q, 0, False, source, slot)

    def after_z(q):
        i, rows = order[q]
        for step in reversed(range(1, net.high_count)):
            along_z[q, step].wait_recv()
            slot = place(i, net.block(step), rows, net.row)
            along_y[q, step] = net.send(slot, slot, net.y_peer())
            in_chip(q, step, False, slot, slot)

    def after_y(q):
        i, rows = order[q]
        for step in steps:
            along_y[q, step].wait_recv()
            slot = place(i, net.block(step, True), rows, net.row)
            in_chip(q, step, True, slot, slot)

    def after_x(q):
        i, rows = order[q]
        if kinds[i] == "all":
            for other in (False, True):
                for step in steps:
                    along_x[q, step, other].wait_recv()
                    slot = place(i, net.block(step, other), rows, other_row)
                    moved.append(net.send(slot, slot, net.core_peer()))

    for tick in range(len(order) + 3):
        if tick < len(order):
            if tick >= 2:
                for step in range(1, net.high_count):
                    net.left(along_z[tick - 2, step])
            start(tick)
        if tick % 2:
            swap_next()
        for stage, lag in ((after_z, 1), (after_y, 2), (after_x, 3)):
            if 0 <= tick - lag < len(order):
                stage(tick - lag)
    while swap_sends:
        swap_next()
    for copy in [*moved, *to_core.values()]:
        copy.wait_recv()
    for local in locals_:
        local.wait()
    net.finish()


def gather(cols, collective_id, *triples):
    kinds = [kind for kind, _, _ in triples]
    pieces = [piece for _, piece, _ in triples]
    arrays = [array for _, _, array in triples]
    copies = 0
    shapes = []
    for kind, piece, array in triples:
        if kind == "swap":
            shapes.append(jax.ShapeDtypeStruct(array.shape, array.dtype))
            copies += cols
        elif kind == "col":
            shapes.append(jax.ShapeDtypeStruct((cols, *array.shape), array.dtype))
            copies += cols * piece
        else:
            rows = lax.axis_size("row")
            shape = (cols, array.shape[0], rows * array.shape[1])
            shapes.append(jax.ShapeDtypeStruct(shape, array.dtype))
            copies += 4 * cols * piece
    return pl.pallas_call(
        functools.partial(gather_kernel, cols, kinds, pieces),
        out_shape=shapes,
        in_specs=[pl.BlockSpec(memory_space=pl.ANY)] * len(triples),
        out_specs=[pl.BlockSpec(memory_space=pl.ANY)] * len(triples),
        scratch_shapes=[
            pltpu.SemaphoreType.DMA((copies,)),
            pltpu.SemaphoreType.DMA((copies,)),
            pltpu.SemaphoreType.DMA((len(triples),)),
        ],
        compiler_params=pltpu.CompilerParams(collective_id=collective_id, has_side_effects=True),
        name=f"gather_{collective_id}",
    )(*arrays)


def add_rows(target, terms):
    rows = target.shape[0]
    piece = 32 if rows % 32 == 0 else 16

    def body(index, carry):
        at = pl.ds(pl.multiple_of(index * piece, piece), piece)
        total = terms[0][at, :].astype(f32)
        for term in terms[1:]:
            total = total + term[at, :].astype(f32)
        target[at, :] = total.astype(target.dtype)
        return carry

    lax.fori_loop(0, rows // piece, body, 0)


class ScatterCol:
    def __init__(self, net, part, rows, from_y, from_z, out):
        self.net, self.part, self.rows = net, part, rows
        self.from_y, self.from_z, self.out = from_y, from_z, out
        self.order = [*range(1, net.high_count), 0]
        self.along_y, self.along_z = {}, {}
        self.stages = [self.send_y, self.send_z, self.last]

    def send_y(self):
        for step in self.order:
            source = self.part.at[self.net.block_ahead(step, True), self.rows]
            self.along_y[step] = self.net.send(
                source, self.from_y.at[step, self.rows], self.net.y_peer()
            )

    def send_z(self):
        for step in self.order:
            self.along_y[step].wait_recv()
            mine = self.part.at[self.net.block_ahead(step), self.rows]
            slot = self.from_y.at[step, self.rows]
            if step:
                add_rows(slot, [mine, slot])
                self.along_z[step] = self.net.send(
                    slot, self.from_z.at[step - 1, self.rows], self.net.z_peer(step)
                )

    def last(self):
        for step in range(1, self.net.high_count):
            self.along_z[step].wait_recv()
        terms = [
            self.from_z.at[step - 1, self.rows] for step in range(1, self.net.high_count)
        ]
        mine = self.part.at[self.net.me, self.rows]
        add_rows(self.out.at[self.rows], [mine, self.from_y.at[0, self.rows], *terms])

    def clear_y(self):
        for step in self.order:
            self.net.left(self.along_y[step])


class ScatterAll:
    def __init__(self, net, part, rows, from_core, from_x, from_y, from_z, out):
        self.net, self.part, self.rows, self.out = net, part, rows, out
        self.from_core, self.from_x, self.from_y, self.from_z = from_core, from_x, from_y, from_z
        self.order = [*range(1, net.high_count), 0]
        self.blocks = [(step, True) for step in self.order]
        self.blocks += [(step, False) for step in self.order]
        self.across, self.onward, self.along_y, self.along_z = {}, {}, {}, {}
        self.other_row = 2 * (1 - net.outer) + net.core
        self.stages = [self.send_core, self.send_x, self.send_y, self.send_z, self.last]

    def features(self, row):
        width = self.out.shape[1]
        return pl.ds(pl.multiple_of(row * width, LANES), width)

    def block(self, key):
        return self.net.block_ahead(*key)

    def send_core(self):
        net = self.net
        for far in (1, 0):
            outer = 1 - net.outer if far else net.outer
            for key in self.blocks:
                block = self.block(key)
                features = self.features(2 * outer + 1 - net.core)
                self.across[far, key] = net.send(
                    self.part.at[block, self.rows, features],
                    self.from_core.at[far, block, self.rows],
                    net.core_peer(),
                )

    def send_x(self):
        for key in self.blocks:
            self.across[1, key].wait_recv()
            block = self.block(key)
            slot = self.from_core.at[1, block, self.rows]
            mine = self.part.at[block, self.rows, self.features(self.other_row)]
            add_rows(slot, [mine, slot])
            self.onward[key] = self.net.send(
                slot, self.from_x.at[block, self.rows], self.net.x_peer()
            )

    def send_y(self):
        for key in self.blocks:
            self.across[0, key].wait_recv()
            self.onward[key].wait_recv()
            block = self.block(key)
            slot = self.from_core.at[0, block, self.rows]
            mine = self.part.at[block, self.rows, self.features(self.net.row)]
            add_rows(slot, [mine, slot, self.from_x.at[block, self.rows]])
            step, other = key
            if other:
                self.along_y[step] = self.net.send(
                    slot, self.from_y.at[step, self.rows], self.net.y_peer()
                )

    def send_z(self):
        for step in self.order:
            self.along_y[step].wait_recv()
            slot = self.from_core.at[0, self.block((step, False)), self.rows]
            add_rows(slot, [slot, self.from_y.at[step, self.rows]])
            if step:
                self.along_z[step] = self.net.send(
                    slot, self.from_z.at[step - 1, self.rows], self.net.z_peer(step)
                )

    def last(self):
        for step in range(1, self.net.high_count):
            self.along_z[step].wait_recv()
        terms = [
            self.from_z.at[step - 1, self.rows] for step in range(1, self.net.high_count)
        ]
        mine = self.from_core.at[0, self.net.me, self.rows]
        add_rows(self.out.at[self.rows], [mine, *terms])


def scatter_kernel(cols, kinds, pieces, *refs):
    count = len(kinds)
    parts, outs, scratch = refs[:count], refs[count : 2 * count], list(refs[2 * count :])
    send_sems, recv_sems = scratch[-2:]
    net = Net(cols, send_sems, recv_sems)
    net.greet(col_peers(net) + (row_peers(net) if "all" in kinds else []))
    lines = {"all": [], "col": []}
    for i, kind in enumerate(kinds):
        buffers = [scratch.pop(0) for _ in range(4 if kind == "all" else 2)]
        rows = outs[i].shape[0] // pieces[i]
        make = ScatterAll if kind == "all" else ScatterCol
        lines[kind] += [
            make(net, parts[i], pl.ds(q * rows, rows), *buffers, outs[i])
            for q in range(pieces[i])
        ]
    ticks = max(len(lines["all"]) + 4, len(lines["col"]) + 2)
    for tick in range(ticks):
        for kind in ("col", "all"):
            line = lines[kind]
            if kind == "col" and 2 <= tick < len(line):
                line[tick - 2].clear_y()
            depth = 5 if kind == "all" else 3
            for stage in range(depth):
                if 0 <= tick - stage < len(line):
                    line[tick - stage].stages[stage]()
    net.finish()


def scatter(cols, collective_id, *triples):
    high = cols // 2
    scratch, outs, copies = [], [], 0
    for kind, piece, array in triples:
        rows, width = array.shape[1:]
        if kind == "all":
            width = width // lax.axis_size("row")
            scratch += [
                pltpu.VMEM((2, cols, rows, width), bf16),
                pltpu.VMEM((cols, rows, width), bf16),
            ]
            copies += 3 * cols * piece
        copies += cols * piece
        scratch += [pltpu.VMEM((high, rows, width), bf16), pltpu.VMEM((high - 1, rows, width), bf16)]
        outs.append(jax.ShapeDtypeStruct((rows, width), f32))
    vmem = pl.BlockSpec(memory_space=pltpu.VMEM)
    return pl.pallas_call(
        functools.partial(
            scatter_kernel, cols, [kind for kind, _, _ in triples], [p for _, p, _ in triples]
        ),
        out_shape=outs,
        in_specs=[vmem] * len(triples),
        out_specs=[vmem] * len(triples),
        scratch_shapes=[
            *scratch,
            pltpu.SemaphoreType.DMA((copies,)),
            pltpu.SemaphoreType.DMA((copies,)),
        ],
        compiler_params=pltpu.CompilerParams(
            collective_id=collective_id, has_side_effects=True, vmem_limit_bytes=60 << 20
        ),
        name=f"scatter_{collective_id}",
    )(*[array for _, _, array in triples])


def sum_row_kernel(part, out, from_core, to_x, from_x, send_sems, recv_sems):
    net = Net(2, send_sems, recv_sems)
    net.greet(row_peers(net))
    pieces = from_core.shape[0]
    rows = from_core.shape[1]

    def piece(core, i):
        start = (core * pieces + i) * rows
        return pl.ds(pl.multiple_of(start, rows), rows)

    across = [
        net.send(part.at[piece(1 - net.core, i)], from_core.at[i], net.core_peer())
        for i in range(pieces)
    ]
    along, back = [], []
    for i in range(pieces):
        across[i].wait_recv()
        add_rows(to_x.at[i], [part.at[piece(net.core, i)], from_core.at[i]])
        along.append(net.send(to_x.at[i], from_x.at[i], net.x_peer()))
    for i in range(pieces):
        along[i].wait_recv()
        mine = piece(net.core, i)
        add_rows(out.at[mine], [to_x.at[i], from_x.at[i]])
        back.append(net.send(out.at[mine], out.at[mine], net.core_peer()))
    for copy in back:
        copy.wait_recv()
    net.finish()


def sum_row_call(collective_id, part):
    pieces = 4
    rows = part.shape[0] // 2 // pieces
    piece = (pieces, rows, part.shape[1])
    return pl.pallas_call(
        sum_row_kernel,
        out_shape=jax.ShapeDtypeStruct(part.shape, bf16),
        in_specs=[pl.BlockSpec(memory_space=pltpu.VMEM)],
        out_specs=pl.BlockSpec(memory_space=pltpu.VMEM),
        scratch_shapes=[
            pltpu.VMEM(piece, bf16),
            pltpu.VMEM(piece, bf16),
            pltpu.VMEM(piece, bf16),
            pltpu.SemaphoreType.DMA((3 * pieces,)),
            pltpu.SemaphoreType.DMA((3 * pieces,)),
        ],
        compiler_params=pltpu.CompilerParams(
            collective_id=collective_id, has_side_effects=True, vmem_limit_bytes=32 << 20
        ),
        name=f"sum_row_{collective_id}",
    )(part)


def dot_nn(left, right):
    return lax.dot_general(left, right, (((1,), (0,)), ((), ())), preferred_element_type=f32)


def dot_nt(left, right):
    return lax.dot_general(left, right, (((1,), (1,)), ((), ())), preferred_element_type=f32)


def dot_tn(left, right):
    return lax.dot_general(left, right, (((0,), (0,)), ((), ())), preferred_element_type=f32)


def each_tile(count, body):
    def step(index, carry):
        body(index)
        return carry

    lax.fori_loop(0, count, step, 0)


TILE = 512


def tile_at(index, tile=TILE):
    if isinstance(index, int):
        return pl.ds(index * tile, tile)
    return pl.ds(pl.multiple_of(index * tile, tile), tile)


def experts_kernel(
    cols,
    capacity,
    h2,
    grads,
    w_gate,
    w_up,
    w_down,
    w_shared,
    rank_row,
    rank_col,
    gate_own,
    out_part,
    back,
    g_gate,
    g_up,
    g_down,
    g_shared,
    gate_dots,
    h2_all,
    xs_all,
    cs_all,
    wgu,
    wd,
    ws,
    gates,
    hb,
    xbuf,
    ybuf,
    obuf,
    part,
    pre,
    gcol,
    dcol,
    dz_all,
    zg_all,
    dgu_all,
    sdz_all,
    sz_all,
    sgu_all,
    from_core,
    from_x,
    from_y,
    from_z,
    kept,
    dots,
    dots_core,
    dots_x,
    tiles,
    tiles_all,
    stage,
    stage_low,
    send_sems,
    recv_sems,
    local_sems,
):
    net = Net(cols, send_sems, recv_sems)
    toks, width = h2.shape
    exp_local, _, hidden = w_gate.shape
    high = net.high_count
    pad = ws.shape[1] // 3
    slots = exp_local * capacity
    pair = 2 * capacity
    piece = width // lax.axis_size("row")
    share = width // LANES // 5 * LANES
    rest = (width - 4 * share) // 2
    wide = width // TILE
    net.greet([net.col_peer(step) for step in range(1, cols)] + row_peers(net))

    def local_copy(source, target, index):
        copy = pltpu.make_async_copy(source, target, local_sems.at[index])
        copy.start()
        return copy

    gate_copies = [
        net.send(gate_own, gates.at[net.me], net.col_peer(step)) for step in range(1, cols)
    ]
    gates[net.me] = gate_own[...]

    def feature_e(row):
        return pl.ds(pl.multiple_of(row * share, LANES), share)

    def feature_r(core):
        return pl.ds(pl.multiple_of(4 * share + core * rest, LANES), rest)

    own_e, own_r = feature_e(net.row), feature_r(net.core)
    far_e = feature_e(2 * (1 - net.outer) + net.core)

    def pass_on(source, block, features, peer):
        return net.send(source.at[..., features], h2_all.at[block, :, features], peer)

    along_z, along_y, along_x, to_core = {}, {}, {}, {}
    for step in range(high - 1, 0, -1):
        along_z[high - step] = [
            pass_on(h2, net.me, own_e, net.z_peer(step)),
            pass_on(h2, net.me, own_r, net.z_peer(step)),
        ]
    along_y[0] = [
        pass_on(h2, net.me, own_e, net.y_peer()),
        pass_on(h2, net.me, own_r, net.y_peer()),
    ]

    def block_of(step, other):
        return net.block_ahead(step, other)

    def share_in_chip(step, other):
        block = block_of(step, other)
        source = h2_all.at[block]
        along_x[step, other] = pass_on(source, block, own_e, net.x_peer())
        to_core[step, other] = [
            pass_on(source, block, own_e, net.core_peer()),
            pass_on(source, block, own_r, net.core_peer()),
        ]

    def arrived_y(step):
        for copy in along_y[step]:
            copy.wait_recv()
        share_in_chip(step, True)

    def arrived_z(step):
        for copy in along_z[step]:
            copy.wait_recv()
        block = block_of(step, False)
        along_y[step] = [
            pass_on(h2_all.at[block], block, own_e, net.y_peer()),
            pass_on(h2_all.at[block], block, own_r, net.y_peer()),
        ]
        share_in_chip(step, False)

    def arrived_x(step, other):
        along_x[step, other].wait_recv()
        block = block_of(step, other)
        to_core[step, other].append(pass_on(h2_all.at[block], block, far_e, net.core_peer()))

    def whole(step, other):
        for copy in to_core[step, other]:
            copy.wait_recv()

    events = [functools.partial(arrived_y, 0)]
    for step in range(1, high):
        events.append(functools.partial(arrived_z, step))
        events.append(functools.partial(arrived_x, step - 1, True))
        events.append(functools.partial(arrived_y, step))
        events.append(functools.partial(arrived_x, step, False))
    events.append(functools.partial(arrived_x, high - 1, True))
    events = iter(events)

    def pump(count=1):
        for _ in range(count):
            event = next(events, None)
            if event is not None:
                event()

    loads = []
    for e in range(exp_local):
        loads.append(local_copy(w_down.at[e], wd.at[e], 3 * e))
        loads.append(local_copy(w_gate.at[e], wgu.at[e, :, pl.ds(0, hidden)], 3 * e + 1))
        loads.append(local_copy(w_up.at[e], wgu.at[e, :, pl.ds(hidden, hidden)], 3 * e + 2))
    base = 3 * exp_local
    loads.append(local_copy(w_shared, ws, base))
    keep_own = local_copy(h2, h2_all.at[net.me], base + 1)
    base += 2

    def load_pair(source, step):
        first = local_copy(source.at[block_of(step, False)], hb.at[0], base)
        second = local_copy(source.at[block_of(step, True)], hb.at[1], base + 1)
        first.wait()
        second.wait()

    slot_row = lax.broadcasted_iota(jnp.int32, (capacity, toks), 0).astype(f32) + 1.0
    slot_lane = lax.broadcasted_iota(jnp.int32, (toks, capacity), 1).astype(f32) + 1.0

    def chosen(block, e):
        return rank_row[block, e : e + 1, :] == slot_row

    def picks(block):
        rows = [
            jnp.where(chosen(block, e), 1.0, 0.0).astype(bf16) for e in range(exp_local)
        ]
        return jnp.concatenate(rows, axis=0)

    def picks_back(block):
        lanes = [
            jnp.where(rank_col[block, :, e : e + 1] == slot_lane, 1.0, 0.0).astype(bf16)
            for e in range(exp_local)
        ]
        return jnp.concatenate(lanes, axis=1)

    def dispatch(step):
        for b in (0, 1):
            table = picks(block_of(step, b == 1))

            def tile(index, b=b, table=table):
                at = tile_at(index)
                rows = dot_nn(table, hb[b, :, at]).astype(bf16)
                for e in range(exp_local):
                    xbuf[e, pl.ds(b * capacity, capacity), at] = rows[
                        e * capacity : (e + 1) * capacity
                    ]

            each_tile(wide, tile)

    def save_rows(target, step):
        return [
            local_copy(
                xbuf.at[e], target.at[e, pl.ds(step * pair, pair)], base + 2 + e
            )
            for e in range(exp_local)
        ]

    saved = []
    for step in range(high):
        load_pair(grads, step)
        if step == 0:
            for copy in loads:
                copy.wait()
        for copy in saved:
            copy.wait()
        dispatch(step)
        saved = save_rows(cs_all, step)
        for e in range(exp_local):
            dz_all[e, pl.ds(step * pair, pair), :] = dot_nt(xbuf[e], wd[e]).astype(bf16)
        for b in (0, 1):
            sdz_all[block_of(step, b == 1)] = dot_nn(hb[b], ws[:, 2 * pad :]).astype(bf16)
        pump()
    for copy in gate_copies:
        copy.wait_recv()
    keep_own.wait()

    across, onward, upward, far_z = {}, {}, {}, {}

    def features(row):
        return pl.ds(pl.multiple_of(row * piece, LANES), piece)

    other_row = 2 * (1 - net.outer) + net.core

    def hand_over(step):
        for b in (1, 0):
            for far in (1, 0):
                outer = 1 - net.outer if far else net.outer
                source = part.at[b, :, features(2 * outer + 1 - net.core)]
                across[step, b, far] = net.send(
                    source, from_core.at[far, step, b], net.core_peer()
                )

    def sum_cores(step):
        for b in (1, 0):
            for far, row in ((1, other_row), (0, net.row)):
                across[step, b, far].wait_recv()
                slot = from_core.at[far, step, b]
                add_rows(slot, [part.at[b, :, features(row)], slot])
                if far:
                    onward[step, b] = net.send(slot, from_x.at[step, b], net.x_peer())
        for b in (1, 0):
            for far in (1, 0):
                net.left(across[step, b, far])

    def sum_chips(step):
        for b in (1, 0):
            onward[step, b].wait_recv()
            slot = from_core.at[0, step, b]
            add_rows(slot, [slot, from_x.at[step, b]])
            if b:
                upward[step] = net.send(slot, from_y.at[step], net.y_peer())

    def sum_plane(step):
        upward[step].wait_recv()
        slot = from_core.at[0, step, 0]
        add_rows(slot, [slot, from_y.at[step]])
        if step:
            far_z[step] = net.send(slot, from_z.at[step - 1], net.z_peer(step))

    own_expert = lax.rem(net.me, cols) * exp_local
    gate_rows = gates.shape[1]
    gate_row = lax.broadcasted_iota(jnp.int32, (gate_rows, toks), 0)
    dots[...] = jnp.zeros_like(dots)
    for step in range(high):
        if step:
            whole(step, False)
        whole(step, True)
        load_pair(h2_all, step)
        for copy in saved:
            copy.wait()
        dispatch(step)
        saved = save_rows(xs_all, step)
        pump()
        for b in (0, 1):
            block = block_of(step, b == 1)
            inner = dot_nn(hb[b], ws[:, : 2 * pad])
            sa, su = inner[:, :pad], inner[:, pad:]
            sig = 1.0 / (1.0 + jnp.exp(-sa))
            silu = sa * sig
            slope = sig * (1.0 + sa * (1.0 - sig))
            sz_all[block] = (silu * su).astype(bf16)
            sdz = sdz_all[block].astype(f32)
            sgu_all[block, :, :pad] = (sdz * su * slope).astype(bf16)
            sgu_all[block, :, pad:] = (sdz * silu).astype(bf16)
        if step:
            sum_cores(step - 1)
        rows = pl.ds(step * pair, pair)
        for e in range(exp_local):

            def inner_tile(index, e=e):
                at = tile_at(index, 256)
                pre[:, at] = dot_nn(xbuf[e], wgu[e, :, at])

            each_tile(2 * hidden // 256, inner_tile)
            for b in (0, 1):
                block = block_of(step, b == 1)
                gate = jnp.sum(
                    jnp.where(gate_row == own_expert + e, gates[block], 0.0), axis=0, keepdims=True
                )
                gate = jnp.sum(jnp.where(chosen(block, e), gate, 0.0), axis=1, keepdims=True)
                gcol[pl.ds(b * capacity, capacity), :] = jnp.broadcast_to(gate, (capacity, LANES))

            def gating(index, e=e, step=step):
                at = pl.ds(pl.multiple_of(index * 32, 32), 32)
                saved_at = pl.ds(pl.multiple_of(step * pair + index * 32, 32), 32)
                a, u = pre[at, :hidden], pre[at, hidden:]
                gate = jnp.concatenate([gcol[at, :]] * (hidden // LANES), axis=1)
                dz = dz_all[e, saved_at, :].astype(f32)
                sig = 1.0 / (1.0 + jnp.exp(-a))
                silu = a * sig
                slope = sig * (1.0 + a * (1.0 - sig))
                z = silu * u
                dcol[at, :] = jnp.broadcast_to(
                    jnp.sum(z * dz, axis=1, keepdims=True), (32, LANES)
                )
                zg_all[e, saved_at, :] = (z * gate).astype(bf16)
                dz = dz * gate
                dgu_all[e, saved_at, :hidden] = (dz * u * slope).astype(bf16)
                dgu_all[e, saved_at, hidden:] = (dz * silu).astype(bf16)

            each_tile(pair // 32, gating)
            for b in (0, 1):
                block = block_of(step, b == 1)
                col = dcol[pl.ds(b * capacity, capacity), :]
                col = jnp.concatenate([col] * (toks // LANES), axis=1)
                dots[block, e : e + 1, :] = jnp.sum(
                    jnp.where(chosen(block, e), col, 0.0), axis=0, keepdims=True
                )

            def out_tile(index, e=e):
                at = tile_at(index)
                y = dot_nn(zg_all[e, rows, :], wd[e, :, at]).astype(bf16)
                for b in (0, 1):
                    ybuf[b, pl.ds(e * capacity, capacity), at] = y[b * capacity : (b + 1) * capacity]

            each_tile(wide, out_tile)
            pump()
        if step:
            for copy in out_copies:
                copy.wait()
        out_copies = []
        for b in (0, 1):
            block = block_of(step, b == 1)
            table = picks_back(block)

            def join_tile(index, b=b, table=table, block=block):
                at = tile_at(index)
                total = dot_nn(table, ybuf[b, :, at])
                total = total + dot_nt(sz_all[block], ws[at, 2 * pad :])
                obuf[b, :, at] = total.astype(bf16)

            each_tile(wide, join_tile)
            out_copies.append(
                local_copy(obuf.at[b], out_part.at[block], base + 2 + exp_local + b)
            )
        pump()
        if step:
            sum_chips(step - 1)
        for e in range(exp_local):

            def back_tile(index, e=e):
                at = tile_at(index)
                y = dot_nt(dgu_all[e, rows, :], wgu[e, at, :]).astype(bf16)
                for b in (0, 1):
                    ybuf[b, pl.ds(e * capacity, capacity), at] = y[b * capacity : (b + 1) * capacity]

            each_tile(wide, back_tile)
        pump()
        for b in (1, 0):
            block = block_of(step, b == 1)
            table = picks_back(block)

            def back_join(index, b=b, table=table, block=block):
                at = tile_at(index)
                total = dot_nn(table, ybuf[b, :, at])
                total = total + dot_nt(sgu_all[block], ws[at, : 2 * pad])
                part[b, :, at] = total.astype(bf16)

            each_tile(wide, back_join)
        hand_over(step)
        if step:
            sum_plane(step - 1)
    pump(64)
    last = high - 1
    for copy in saved + out_copies:
        copy.wait()

    load_sem, store_sem = base + 4 + exp_local, base + 6 + exp_local

    def passes(count, load, work, stores):
        def load_copy(j, slot):
            source, target = load(j, slot)
            return pltpu.make_async_copy(source, target, local_sems.at[load_sem + slot])

        def store_copies(j, slot):
            return [
                pltpu.make_async_copy(
                    source, target, local_sems.at[store_sem + 2 * slot + i]
                )
                for i, (source, target) in enumerate(stores(j, slot))
            ]

        load_copy(0, 0).start()

        def body(j):
            slot = lax.rem(j, 2)

            @pl.when(j + 1 < count)
            def _():
                load_copy(j + 1, 1 - slot).start()

            load_copy(j, slot).wait()

            @pl.when(j >= 2)
            def _():
                for copy in store_copies(j - 2, slot):
                    copy.wait()

            work(j, slot)
            for copy in store_copies(j, slot):
                copy.start()

        each_tile(count, body)
        for j in range(max(0, count - 2), count):
            for copy in store_copies(j, j % 2):
                copy.wait()

    def inner_grads(e):
        passes(
            wide,
            lambda j, slot: (
                xs_all.at[e, :, tile_at(j)],
                tiles.at[slot],
            ),
            lambda j, slot: put(stage.at[slot], dot_tn(tiles[slot], dgu_all[e])),
            lambda j, slot: [
                (stage.at[slot, :, pl.ds(0, hidden)], g_gate.at[e, tile_at(j)]),
                (stage.at[slot, :, pl.ds(hidden, hidden)], g_up.at[e, tile_at(j)]),
            ],
        )

    def put(target, value):
        target[...] = value

    def down_grads(e):
        passes(
            wide,
            lambda j, slot: (
                cs_all.at[e, :, tile_at(j)],
                tiles.at[slot],
            ),
            lambda j, slot: put(
                stage.at[slot, pl.ds(0, hidden), pl.ds(0, TILE)],
                dot_tn(zg_all[e], tiles[slot]),
            ),
            lambda j, slot: [
                (
                    stage.at[slot, pl.ds(0, hidden), pl.ds(0, TILE)],
                    g_down.at[e, :, tile_at(j)],
                ),
            ],
        )

    def shared_grads(source, others, start, size):
        def work(j, slot):
            total = dot_tn(tiles_all[slot, 0], others[0])
            for c in range(1, cols):
                total = total + dot_tn(tiles_all[slot, c], others[c])
            stage_low[slot, :, :size] = total.astype(bf16)

        def load(j, slot):
            return (source.at[:, :, tile_at(j)], tiles_all.at[slot])

        passes(
            wide,
            lambda j, slot: load(j, slot),
            work,
            lambda j, slot: [
                (
                    stage_low.at[slot, :, pl.ds(0, size)],
                    g_shared.at[tile_at(j), pl.ds(start, size)],
                ),
            ],
        )

    first_dots = net.send(dots, dots_core, net.core_peer())
    inner_grads(0)
    sum_cores(last)
    first_dots.wait_recv()
    net.left(first_dots)
    dots[...] = dots[...] + dots_core[...]
    second_dots = net.send(dots, dots_x, net.x_peer())
    inner_grads(1)
    sum_chips(last)
    second_dots.wait_recv()
    dots_core[...] = dots[...] + dots_x[...]
    third_dots = []
    for step in range(1, cols):
        block = lax.rem(net.me + step, cols)
        third_dots.append(
            net.send(dots_core.at[block], gate_dots.at[net.me], net.col_peer(step))
        )
    gate_dots[net.me] = dots_core[net.me]
    down_grads(0)
    sum_plane(last)
    down_grads(1)
    for step in range(1, high):
        far_z[step].wait_recv()
    add_rows(kept, [from_core.at[0, 0, 0], *[from_z.at[step - 1] for step in range(1, high)]])
    own, other = features(net.row), features(other_row)
    back[:, own] = kept[...].astype(bf16)
    far = net.send(back.at[:, own], back.at[:, own], net.x_peer())
    near = net.send(back.at[:, own], back.at[:, own], net.core_peer())
    shared_grads(h2_all, sgu_all, 0, 2 * pad)
    far.wait_recv()
    crossed = net.send(back.at[:, other], back.at[:, other], net.core_peer())
    shared_grads(grads, sz_all, 2 * pad, pad)
    near.wait_recv()
    crossed.wait_recv()
    for copy in third_dots:
        copy.wait_recv()
    net.finish()


def experts_call(
    cols, collective_id, capacity, h2, grads, w_gate, w_up, w_down, w_shared, rank_row, rank_col, gate
):
    toks, width = h2.shape
    exp_local, _, hidden = w_gate.shape
    high = cols // 2
    pad = w_shared.shape[1] // 3
    piece = width // lax.axis_size("row")
    pair = 2 * capacity
    any_space = pl.BlockSpec(memory_space=pl.ANY)
    vmem = pl.BlockSpec(memory_space=pltpu.VMEM)
    copies = 160

    def shape(*dims, dtype=bf16):
        return jax.ShapeDtypeStruct(dims, dtype)

    return pl.pallas_call(
        functools.partial(experts_kernel, cols, capacity),
        out_shape=[
            shape(cols, toks, width),
            shape(toks, width),
            shape(exp_local, width, hidden, dtype=f32),
            shape(exp_local, width, hidden, dtype=f32),
            shape(exp_local, hidden, width, dtype=f32),
            shape(width, 3 * pad),
            shape(cols, 8, toks, dtype=f32),
            shape(cols, toks, width),
            shape(exp_local, cols * capacity, width),
            shape(exp_local, cols * capacity, width),
        ],
        in_specs=[any_space] * 6 + [vmem] * 3,
        out_specs=[
            any_space,
            vmem,
            any_space,
            any_space,
            any_space,
            any_space,
            vmem,
            any_space,
            any_space,
            any_space,
        ],
        scratch_shapes=[
            pltpu.VMEM((exp_local, width, 2 * hidden), bf16),
            pltpu.VMEM((exp_local, hidden, width), bf16),
            pltpu.VMEM((width, 3 * pad), bf16),
            pltpu.VMEM((cols, *gate.shape), f32),
            pltpu.VMEM((2, toks, width), bf16),
            pltpu.VMEM((exp_local, pair, width), bf16),
            pltpu.VMEM((2, exp_local * capacity, width), bf16),
            pltpu.VMEM((2, toks, width), bf16),
            pltpu.VMEM((2, toks, width), bf16),
            pltpu.VMEM((pair, 2 * hidden), f32),
            pltpu.VMEM((pair, LANES), f32),
            pltpu.VMEM((pair, LANES), f32),
            pltpu.VMEM((exp_local, cols * capacity, hidden), bf16),
            pltpu.VMEM((exp_local, cols * capacity, hidden), bf16),
            pltpu.VMEM((exp_local, cols * capacity, 2 * hidden), bf16),
            pltpu.VMEM((cols, toks, pad), bf16),
            pltpu.VMEM((cols, toks, pad), bf16),
            pltpu.VMEM((cols, toks, 2 * pad), bf16),
            pltpu.VMEM((2, high, 2, toks, piece), bf16),
            pltpu.VMEM((high, 2, toks, piece), bf16),
            pltpu.VMEM((high, toks, piece), bf16),
            pltpu.VMEM((high - 1, toks, piece), bf16),
            pltpu.VMEM((toks, piece), f32),
            pltpu.VMEM((cols, 8, toks), f32),
            pltpu.VMEM((cols, 8, toks), f32),
            pltpu.VMEM((cols, 8, toks), f32),
            pltpu.VMEM((2, cols * capacity, TILE), bf16),
            pltpu.VMEM((2, cols, toks, TILE), bf16),
            pltpu.VMEM((2, TILE, 2 * hidden), f32),
            pltpu.VMEM((2, TILE, 2 * pad), bf16),
            pltpu.SemaphoreType.DMA((copies,)),
            pltpu.SemaphoreType.DMA((copies,)),
            pltpu.SemaphoreType.DMA((24,)),
        ],
        compiler_params=pltpu.CompilerParams(
            collective_id=collective_id, has_side_effects=True, vmem_limit_bytes=62 << 20
        ),
        name=f"experts_{collective_id}",
    )(h2, grads, w_gate, w_up, w_down, w_shared, rank_row, rank_col, gate)


def experts_kernels(
    cols, collective_id, capacity, h2, grad_all, w_gate, w_up, w_down, shared_weights, *tables
):
    width, shared_part = shared_weights.shape[0], shared_weights.shape[1] // 3
    pad = -shared_part % LANES
    padded = jnp.pad(shared_weights.reshape(width, 3, shared_part), ((0, 0), (0, 0), (0, pad)))
    padded = padded.reshape(width, -1)
    out_part, back, g_gate, g_up, g_down, g_shared, gate_dots, *_ = experts_call(
        cols, collective_id, capacity, h2, grad_all, w_gate, w_up, w_down, padded, *tables
    )
    gate_dots = gate_dots[:, : w_gate.shape[0]].reshape(-1, h2.shape[0]).T
    g_shared = g_shared.reshape(width, 3, -1)[:, :, :shared_part].reshape(width, -1)
    return (out_part, back, gate_dots, g_shared, g_gate, g_up, g_down)


def fits(cols, rows, width):
    return cols % 2 == 0 and cols * rows * width * 2 <= 12 << 20


def gather_parts(kernels, cols, collective_id, *triples):
    if kernels:
        return gather(cols, collective_id, *triples)
    ways = {"col": gather_col, "all": gather_all, "swap": swap_col}
    return [ways[kind](array) for kind, _, array in triples]


def scatter_parts(kernels, cols, collective_id, *triples):
    if kernels:
        return scatter(cols, collective_id, *triples)
    ways = {"col": scatter_col, "all": scatter_all}
    return [ways[kind](array).astype(f32) for kind, _, array in triples]


def sum_row(kernels, collective_id, part):
    if kernels:
        return sum_row_call(collective_id, part)
    return lax.psum(part, "row")


def experts_plain(
    h2, grad_all, w_gate, w_up, w_down, shared_weights, router, rank_all, capacity, row_width
):
    cols = lax.axis_size("col")
    col_index, row_index = lax.axis_index("col"), lax.axis_index("row")
    toks, width = h2.shape
    exp_local = w_gate.shape[0]
    experts = rank_all.shape[2]
    shared_part = shared_weights.shape[1] // 3
    shared_in_weights = shared_weights[:, : 2 * shared_part]
    shared_down = shared_weights[:, 2 * shared_part :]
    h2_slice = lax.dynamic_slice_in_dim(h2, row_index * row_width, row_width, 1)
    h2_all = gather_all(h2_slice)

    all_mask = (rank_all > 0).astype(f32)
    all_probs = jax.nn.softmax(dot("ctd,de->cte", h2_all, router), axis=-1)
    all_picked = all_probs * all_mask
    all_gate = all_picked / jnp.sum(all_picked, axis=-1, keepdims=True)
    own = col_index * exp_local
    own_gate = lax.dynamic_slice_in_dim(all_gate, own, exp_local, 2)
    own_rank = lax.dynamic_slice_in_dim(rank_all, own, exp_local, 2).astype(jnp.int32)
    slots = jnp.arange(1, capacity + 1, dtype=jnp.int32)
    pick = jnp.swapaxes(own_rank, 1, 2)[:, :, None, :] == slots[:, None]
    slot_gate = jnp.sum(
        jnp.where(pick, jnp.swapaxes(own_gate, 1, 2)[:, :, None, :], 0.0), axis=3
    )[..., None]
    pick_low = pick.astype(bf16).reshape(cols, exp_local * capacity, toks)
    slot_shape = (cols, exp_local, capacity, width)
    slot_rows = dot("cut,ctd->cud", pick_low, h2_all).astype(bf16).reshape(slot_shape)
    slot_grad = dot("cut,ctd->cud", pick_low, grad_all).astype(bf16).reshape(slot_shape)
    gate_pre = dot("necd,edf->necf", slot_rows, w_gate)
    up_pre = dot("necd,edf->necf", slot_rows, w_up)
    silu_gate, slope_gate = silu_parts(gate_pre)
    hidden = silu_gate * up_pre
    gated = (hidden * slot_gate).astype(bf16)
    slot_out = dot("necf,efd->necd", gated, w_down).astype(bf16)
    hidden_grad = dot("necd,efd->necf", slot_grad, w_down)
    slot_dots = jnp.sum(hidden * hidden_grad, axis=-1)
    hidden_grad = hidden_grad * slot_gate
    gate_grad = (hidden_grad * up_pre * slope_gate).astype(bf16)
    up_grad = (hidden_grad * silu_gate).astype(bf16)
    slot_back = dot("necf,edf->necd", gate_grad, w_gate)
    slot_back = (slot_back + dot("necf,edf->necd", up_grad, w_up)).astype(bf16)
    grad_expert_down = dot("necf,necd->efd", gated, slot_grad)
    grad_expert_gate = dot("necd,necf->edf", slot_rows, gate_grad)
    grad_expert_up = dot("necd,necf->edf", slot_rows, up_grad)
    pick_flat = pick_low.reshape(cols, exp_local * capacity, toks)
    slot_out = slot_out.reshape(cols, exp_local * capacity, width)
    slot_back = slot_back.reshape(cols, exp_local * capacity, width)

    shared_pre = dot("ctd,dk->ctk", h2_all, shared_in_weights)
    sgate_pre, sup_pre = shared_pre[:, :, :shared_part], shared_pre[:, :, shared_part:]
    shared_silu, shared_slope = silu_parts(sgate_pre)
    shared_hidden = (shared_silu * sup_pre).astype(bf16)
    part_out = dot("cut,cud->ctd", pick_flat, slot_out) + dot(
        "ctk,dk->ctd", shared_hidden, shared_down
    )
    shared_hgrad = dot("ctd,dk->ctk", grad_all, shared_down)
    shared_grads = jnp.concatenate(
        [shared_hgrad * sup_pre * shared_slope, shared_hgrad * shared_silu], axis=2
    ).astype(bf16)
    part_back = dot("cut,cud->ctd", pick_flat, slot_back) + dot(
        "ctk,dk->ctd", shared_grads, shared_in_weights
    )
    token_dots = jnp.einsum(
        "ceu,ceut->cte", slot_dots, pick.astype(f32), precision=lax.Precision.HIGHEST
    )
    gate_dots = lax.psum(swap_col(token_dots), "row")
    gate_dots = jnp.swapaxes(gate_dots, 0, 1).reshape(toks, experts)

    shared_share = jnp.concatenate(
        [dot("ctd,ctk->dk", h2_all, shared_grads), dot("ctd,ctk->dk", grad_all, shared_hidden)],
        axis=1,
    ).astype(bf16)
    back_full = lax.all_gather(scatter_all(part_back.astype(bf16)), "row", axis=1, tiled=True)
    return (
        part_out.astype(bf16),
        back_full,
        gate_dots,
        shared_share,
        grad_expert_gate,
        grad_expert_up,
        grad_expert_down,
    )


def on_device(
    tokens,
    segments,
    routes,
    attn_gain,
    query_matrix,
    key_matrix,
    value_matrix,
    attention_output_matrix,
    mlp_gain,
    w_router,
    shared_gate_matrix,
    shared_up_matrix,
    shared_down_matrix,
    expert_gate,
    expert_up,
    expert_down,
    cotangent,
):
    local_len, seqs, width = tokens.shape
    cols = lax.axis_size("col")
    col_index = lax.axis_index("col")
    rows_w = query_matrix.shape[0]
    full_len = local_len * cols
    size = HEAD_DIM
    q_width = query_matrix.shape[1]
    kv_width = key_matrix.shape[1]
    kv_local = kv_width // size
    group = q_width // kv_width
    row_width = cotangent.shape[2]
    toks = local_len * seqs
    top = routes.shape[2]
    experts = w_router.shape[1]
    exp_local = expert_gate.shape[0]
    hidden_local = expert_gate.shape[2]
    capacity = max(2, toks * top * 4 // (3 * experts))
    shared_part = shared_gate_matrix.shape[1] // cols
    scale = 1.0 / math.sqrt(size)
    kernels = fits(cols, toks, width)

    def seq_major(a):
        return jnp.swapaxes(a, 0, 1).reshape(toks, a.shape[2])

    misc = jnp.concatenate(
        [
            w_router,
            attn_gain[:, None],
            mlp_gain[:, None],
            jnp.zeros((rows_w, LANES - experts - 2), bf16),
        ],
        axis=1,
    )
    first_weights = jnp.concatenate([query_matrix, key_matrix, value_matrix, misc], axis=1)
    shared_weights = jnp.concatenate(
        [
            shared_gate_matrix.reshape(rows_w, cols, shared_part),
            shared_up_matrix.reshape(rows_w, cols, shared_part),
            shared_down_matrix.T.reshape(rows_w, cols, shared_part),
        ],
        axis=2,
    )
    first_weights, out_weights, shared_weights, grad_all = gather_parts(
        kernels,
        cols,
        0,
        ("col", 5, first_weights),
        ("col", 4, attention_output_matrix.T),
        ("swap", 1, jnp.swapaxes(shared_weights, 0, 1)),
        ("all", 4, seq_major(cotangent).astype(bf16)),
    )
    first_weights = first_weights.reshape(width, -1)
    out_weights = out_weights.reshape(width, q_width)
    shared_weights = shared_weights.reshape(width, 3 * shared_part)
    qkv_width = q_width + 2 * kv_width
    qkv_weights = first_weights[:, :qkv_width]
    router = first_weights[:, qkv_width : qkv_width + experts]
    gain_one = first_weights[:, qkv_width + experts].astype(f32)
    gain_two = first_weights[:, qkv_width + experts + 1].astype(f32)


    x = seq_major(tokens).astype(f32)
    inv_first = rms_scale(x)
    base_first = x * inv_first
    h1 = (base_first * gain_one).astype(bf16)
    qkv = dot("tb,bk->tk", h1, qkv_weights)
    cosine, sine = rope_tables(col_index * local_len, local_len, size)
    cosine, sine = jnp.tile(cosine, (seqs, 1)), jnp.tile(sine, (seqs, 1))
    qk = rotate(qkv[:, : q_width + kv_width], cosine, sine).astype(bf16)
    value_low = qkv[:, q_width + kv_width :].astype(bf16)

    flat_routes = seq_major(routes)
    named = flat_routes[:, :, None] == jnp.arange(experts, dtype=jnp.int32)
    mask = jnp.any(named, axis=1)
    order = jnp.arange(toks, dtype=jnp.int32)
    upto = (order[None, :] <= order[:, None]).astype(bf16)
    rank = jnp.where(mask, dot("ij,je->ie", upto, mask.astype(bf16)), 0.0)

    doc = jnp.transpose(segments)
    side = jnp.concatenate(
        [
            rank.astype(bf16),
            doc.reshape(toks, 1).astype(bf16),
            jnp.zeros((toks, LANES - experts - 1), bf16),
        ],
        axis=1,
    )
    (kv_all,) = gather_parts(
        kernels, cols, 1, ("col", 4, jnp.concatenate([qk[:, q_width:], value_low, side], axis=1))
    )
    rank_all = kv_all[:, :, 2 * kv_width : 2 * kv_width + experts]
    kv_seq = jnp.swapaxes(kv_all.reshape(cols, seqs, local_len, -1), 0, 1)
    kv_seq = kv_seq.reshape(seqs, full_len, -1)
    key_all = kv_seq[:, :, :kv_width].reshape(seqs, full_len, kv_local, size)
    value_all = kv_seq[:, :, kv_width : 2 * kv_width].reshape(seqs, full_len, kv_local, size)
    doc_all = kv_seq[:, :, 2 * kv_width + experts]

    def to_grid(flat):
        shaped = flat.reshape(seqs, local_len, kv_local, group, size)
        return shaped.transpose(0, 2, 3, 1, 4).reshape(seqs, kv_local, group * local_len, size)

    def from_grid(grid):
        shaped = grid.reshape(seqs, kv_local, group, local_len, size)
        return shaped.transpose(0, 3, 1, 2, 4).reshape(toks, q_width)

    query_grid = to_grid(qk[:, :q_width])
    place = col_index * local_len + jnp.arange(local_len, dtype=jnp.int32)
    same = doc.astype(bf16)[:, :, None] == doc_all[:, None, :]
    causal = jnp.arange(full_len, dtype=jnp.int32)[None, :] <= place[:, None]
    allowed = jnp.tile(same & causal[None], (1, group, 1))[:, None]
    scores = dot("shrd,skhd->shrk", query_grid, key_all) * scale
    scores = jnp.where(allowed, scores, masked_score)
    weights = jnp.exp(scores - jnp.max(scores, axis=-1, keepdims=True))
    weights = jnp.where(allowed, weights, 0.0)
    probs = (weights / jnp.sum(weights, axis=-1, keepdims=True)).astype(bf16)
    heads = from_grid(dot("shrk,skhd->shrd", probs, value_all)).astype(bf16)
    attn = sum_row(kernels, 2, dot("tk,bk->tb", heads, out_weights).astype(bf16))
    middle = x + attn.astype(f32)

    inv_second = rms_scale(middle)
    base_second = middle * inv_second
    h2 = (base_second * gain_two).astype(bf16)
    row_index = lax.axis_index("row")
    probs_router = jax.nn.softmax(dot("td,de->te", h2, router), axis=-1)
    picked = jnp.where(mask, probs_router, 0.0)
    pick_total = jnp.sum(picked, axis=-1, keepdims=True)
    gate = picked / pick_total
    if kernels:
        rank_own = lax.dynamic_slice_in_dim(rank_all, col_index * exp_local, exp_local, 2)
        rank_own = rank_own.astype(f32)
        part_out, back_full, gate_dots, shared_share, *expert_grads = experts_kernels(
            cols,
            3,
            capacity,
            h2,
            grad_all,
            expert_gate,
            expert_up,
            expert_down,
            shared_weights,
            jnp.swapaxes(rank_own, 1, 2),
            rank_own,
            gate.T,
        )
    else:
        part_out, back_full, gate_dots, shared_share, *expert_grads = experts_plain(
            h2,
            grad_all,
            expert_gate,
            expert_up,
            expert_down,
            shared_weights,
            router,
            rank_all,
            capacity,
            row_width,
        )
    back_full = back_full.astype(f32)
    shared_share = swap_col(shared_share.reshape(cols, rows_w, 3 * shared_part))
    shared_share = jnp.swapaxes(shared_share, 0, 1).astype(f32)
    share_sgate, share_sup, share_sdown = (
        shared_share[:, :, i * shared_part : (i + 1) * shared_part].reshape(rows_w, -1)
        for i in range(3)
    )

    pick_grad = gate_dots - jnp.sum(gate * gate_dots, axis=-1, keepdims=True)
    prob_grad = jnp.where(mask, pick_grad / pick_total, 0.0)
    logit_grad = probs_router * (
        prob_grad - jnp.sum(probs_router * prob_grad, axis=-1, keepdims=True)
    )
    logit_low = logit_grad.astype(bf16)
    grad_router = dot("td,te->de", h2, logit_low)

    back_full = back_full + dot("te,de->td", logit_low, router)
    grad_own = lax.dynamic_slice_in_dim(grad_all, col_index, 1, 0)[0].astype(f32)
    grad_gain_two = jnp.sum(back_full * base_second, axis=0)
    scaled_two = back_full * gain_two
    middle_grad = (
        inv_second
        * (scaled_two - base_second * jnp.mean(scaled_two * base_second, axis=-1, keepdims=True))
        + grad_own
    )
    attn_grad = middle_grad.astype(bf16)
    grad_out = dot("td,tk->dk", attn_grad, heads).astype(bf16)

    heads_grad = to_grid(dot("td,dk->tk", attn_grad, out_weights).astype(bf16))
    value_grad = dot("shrk,shrd->skhd", probs, heads_grad)
    weight_grad = dot("shrd,skhd->shrk", heads_grad, value_all)
    probs_wide = probs.astype(f32)
    delta = jnp.sum(probs_wide * weight_grad, axis=-1, keepdims=True)
    score_grad = (probs_wide * (weight_grad - delta)).astype(bf16)
    query_grad = from_grid(dot("shrk,skhd->shrd", score_grad, key_all)) * scale
    key_grad = dot("shrk,shrd->skhd", score_grad, query_grid) * scale
    kv_grad = jnp.concatenate(
        [key_grad.reshape(seqs, full_len, kv_width), value_grad.reshape(seqs, full_len, kv_width)],
        axis=2,
    ).astype(bf16)
    kv_grad = jnp.swapaxes(kv_grad.reshape(seqs, cols, local_len, 2 * kv_width), 0, 1)
    (kv_share,) = scatter_parts(
        kernels, cols, 6, ("col", 4, kv_grad.reshape(cols, toks, 2 * kv_width))
    )
    qk_grad = rotate(
        jnp.concatenate([query_grad, kv_share[:, :kv_width]], axis=1), cosine, -sine
    )
    qkv_grad = jnp.concatenate([qk_grad, kv_share[:, kv_width:]], axis=1).astype(bf16)
    first_grad = dot("tk,bk->tb", qkv_grad, qkv_weights).astype(bf16)
    first_grad = sum_row(kernels, 7, first_grad).astype(f32)
    grad_gain_one = jnp.sum(first_grad * base_first, axis=0)
    scaled_one = first_grad * gain_one
    token_grad = (
        inv_first
        * (scaled_one - base_first * jnp.mean(scaled_one * base_first, axis=-1, keepdims=True))
        + middle_grad
    )
    grad_first = jnp.concatenate(
        [
            dot("tb,tk->bk", h1, qkv_grad),
            grad_router,
            grad_gain_one[:, None],
            grad_gain_two[:, None],
            jnp.zeros((width, LANES - experts - 2), f32),
        ],
        axis=1,
    ).astype(bf16)
    out_slice, share_out, share_first = scatter_parts(
        kernels,
        cols,
        8,
        ("all", 4, part_out),
        ("col", 4, grad_out.reshape(cols, rows_w, q_width)),
        ("col", 5, grad_first.reshape(cols, rows_w, -1)),
    )
    middle_slice = lax.dynamic_slice_in_dim(middle, row_index * row_width, row_width, 1)
    block_out = (middle_slice + out_slice).astype(bf16)

    def tokens_first(a):
        return jnp.swapaxes(a.reshape(seqs, local_len, a.shape[1]), 0, 1)

    return (
        tokens_first(block_out),
        tokens_first(token_grad),
        share_first[:, qkv_width + experts],
        share_first[:, :q_width],
        share_first[:, q_width : q_width + kv_width],
        share_first[:, q_width + kv_width : qkv_width],
        share_out.T,
        share_first[:, qkv_width + experts + 1],
        share_first[:, qkv_width : qkv_width + experts],
        share_sgate,
        share_sup,
        share_sdown.T,
        *expert_grads,
    )


def solution(mesh):
    in_specs = (
        P("col", None, None),
        P("col", None),
        P("col", None, None),
        P("col"),
        P("col", "row"),
        P("col", "row"),
        P("col", "row"),
        P("row", "col"),
        P("col"),
        P("col", None),
        P("col", "row"),
        P("col", "row"),
        P("row", "col"),
        P("col", None, "row"),
        P("col", None, "row"),
        P("col", "row", None),
        P("col", None, "row"),
    )
    out_specs = (
        P("col", None, "row"),
        P("col", None, None),
        P("col"),
        P("col", "row"),
        P("col", "row"),
        P("col", "row"),
        P("row", "col"),
        P("col"),
        P("col", None),
        P("col", "row"),
        P("col", "row"),
        P("row", "col"),
        P("col", None, "row"),
        P("col", None, "row"),
        P("col", "row", None),
    )
    return jax.shard_map(
        on_device, mesh=mesh, in_specs=in_specs, out_specs=out_specs, check_vma=False
    )
```

```python
import functools
import math

import jax
import jax.numpy as jnp
from jax import lax
from jax.experimental import pallas as pl
from jax.experimental.pallas import tpu as pltpu
from jax.sharding import PartitionSpec as P

HEAD_DIM = 128
LANES = 128


norm_eps = 1e-05
rope_base = 500000.0
masked_score = -1e30

f32 = jnp.float32
bf16 = jnp.bfloat16
MESH = pl.DeviceIdType.MESH


def dot(form, left, right):
    return jnp.einsum(form, left, right, preferred_element_type=f32)


def rope_tables(start_place, local_len, head_size):
    places = (start_place + jnp.arange(local_len, dtype=jnp.int32)).astype(f32)
    frequency = jnp.power(
        rope_base, -jnp.arange(0, head_size, 2, dtype=jnp.int32).astype(f32) / head_size
    )
    angles = places[:, None] * frequency[None, :]
    return (jnp.cos(angles), jnp.sin(angles))


def rotate(field, cosine, sine):
    half = cosine.shape[1]
    parts = []
    for start in range(0, field.shape[1], 2 * half):
        front = field[:, start : start + half]
        back = field[:, start + half : start + 2 * half]
        parts.append(front * cosine - back * sine)
        parts.append(back * cosine + front * sine)
    return jnp.concatenate(parts, axis=1)


def rms_scale(values_in):
    return lax.rsqrt(jnp.mean(values_in * values_in, axis=-1, keepdims=True) + norm_eps)


def silu_parts(pre_gate):
    sigmoid_gate = jax.nn.sigmoid(pre_gate)
    silu_gate = pre_gate * sigmoid_gate
    slope_gate = sigmoid_gate * (1.0 + pre_gate * (1.0 - sigmoid_gate))
    return (silu_gate, slope_gate)


def gather_col(part):
    return lax.all_gather(part, "col", axis=0, tiled=False)


def scatter_col(blocks):
    flat = blocks.reshape(-1, blocks.shape[-1])
    return lax.psum_scatter(flat, "col", scatter_dimension=0, tiled=True)


def gather_all(part):
    got = lax.all_gather(part, ("col", "row"), axis=0, tiled=False)
    cols, rows = lax.axis_size("col"), lax.axis_size("row")
    got = got.reshape(cols, rows, *part.shape).transpose(0, 2, 1, 3)
    return got.reshape(cols, part.shape[0], rows * part.shape[1])


def scatter_all(blocks):
    flat = blocks.reshape(-1, blocks.shape[-1])
    part = lax.psum_scatter(flat, "row", scatter_dimension=1, tiled=True)
    return lax.psum_scatter(part, "col", scatter_dimension=0, tiled=True)


def swap_col(blocks):
    return lax.all_to_all(blocks, "col", split_axis=0, concat_axis=0, tiled=True)


class Net:
    def __init__(self, cols, send_sems, recv_sems):
        self.send_sems, self.recv_sems, self.used, self.sent = send_sems, recv_sems, 0, []
        self.cols, self.high_count = cols, cols // 2
        self.me = lax.axis_index("col")
        self.high, self.low = self.me // 2, self.me % 2
        self.row = lax.axis_index("row")
        self.outer, self.core = self.row // 2, self.row % 2

    def block(self, step, other=False):
        high = lax.rem(self.high + self.high_count - step, self.high_count)
        return 2 * high + (1 - self.low if other else self.low)

    def block_ahead(self, step, other=False):
        high = lax.rem(self.high + step, self.high_count)
        return 2 * high + (1 - self.low if other else self.low)

    def z_peer(self, step):
        return {"col": self.block_ahead(step)}

    def y_peer(self):
        return {"col": 2 * self.high + 1 - self.low}

    def x_peer(self):
        return {"row": 2 * (1 - self.outer) + self.core}

    def core_peer(self):
        return {"row": 2 * self.outer + 1 - self.core}

    def col_peer(self, step):
        return {"col": lax.rem(self.me + step, self.cols)}

    def greet(self, peers):
        barrier = pltpu.get_barrier_semaphore()
        for peer in peers:
            pl.semaphore_signal(barrier, inc=1, device_id=peer, device_id_type=MESH)
        pl.semaphore_wait(barrier, len(peers))

    def send(self, source, target, peer):
        copy = pltpu.make_async_remote_copy(
            src_ref=source,
            dst_ref=target,
            send_sem=self.send_sems.at[self.used],
            recv_sem=self.recv_sems.at[self.used],
            device_id=peer,
            device_id_type=MESH,
        )
        self.used += 1
        copy.start()
        self.sent.append(copy)
        return copy

    def left(self, copy):
        copy.wait_send()
        self.sent = [other for other in self.sent if other is not copy]

    def finish(self):
        for copy in self.sent:
            copy.wait_send()


def col_peers(net):
    return [net.z_peer(step) for step in range(1, net.high_count)] + [net.y_peer()]


def row_peers(net):
    return [net.x_peer(), net.core_peer()]


def gather_kernel(cols, kinds, pieces, *refs):
    count = len(kinds)
    ins, outs = refs[:count], refs[count : 2 * count]
    send_sems, recv_sems, local_sems = refs[2 * count :]
    net = Net(cols, send_sems, recv_sems)
    swaps = [i for i, kind in enumerate(kinds) if kind == "swap"]
    peers = [net.col_peer(step) for step in range(1, cols)] if swaps else col_peers(net)
    net.greet(peers + (row_peers(net) if "all" in kinds else []))
    other_row = 2 * (1 - net.outer) + net.core

    def place(i, block, rows, row):
        if kinds[i] == "all":
            part = ins[i].shape[1]
            return outs[i].at[block, rows, pl.ds(pl.multiple_of(row * part, LANES), part)]
        return outs[i].at[block, rows]

    order = []
    for i in sorted(range(count), key=lambda i: kinds[i] != "all"):
        if kinds[i] != "swap":
            rows = ins[i].shape[0] // pieces[i]
            order += [(i, pl.ds(q * rows, rows)) for q in range(pieces[i])]
    swap_sends = [(i, step) for i in swaps for step in range(1, cols)]
    steps = range(net.high_count)
    along_z, along_y, along_x, to_core, moved = {}, {}, {}, {}, []
    locals_ = []
    for i, kind in enumerate(kinds):
        own = ins[i].at[net.me] if kind == "swap" else ins[i]
        slot = outs[i].at[net.me] if kind == "swap" else place(
            i, net.me, pl.ds(0, ins[i].shape[0]), net.row
        )
        local = pltpu.make_async_copy(own, slot, local_sems.at[i])
        local.start()
        locals_.append(local)

    def swap_next():
        if swap_sends:
            i, step = swap_sends.pop(0)
            block = lax.rem(net.me + step, cols)
            moved.append(net.send(ins[i].at[block], outs[i].at[net.me], net.col_peer(step)))

    def in_chip(q, step, other, source, slot):
        if kinds[order[q][0]] == "all":
            along_x[q, step, other] = net.send(source, slot, net.x_peer())
            to_core[q, step, other] = net.send(source, slot, net.core_peer())

    def start(q):
        i, rows = order[q]
        source, slot = ins[i].at[rows], place(i, net.me, rows, net.row)
        for step in reversed(range(1, net.high_count)):
            along_z[q, step] = net.send(source, slot, net.z_peer(step))
        along_y[q, 0] = net.send(source, slot, net.y_peer())
        in_chip(q, 0, False, source, slot)

    def after_z(q):
        i, rows = order[q]
        for step in reversed(range(1, net.high_count)):
            along_z[q, step].wait_recv()
            slot = place(i, net.block(step), rows, net.row)
            along_y[q, step] = net.send(slot, slot, net.y_peer())
            in_chip(q, step, False, slot, slot)

    def after_y(q):
        i, rows = order[q]
        for step in steps:
            along_y[q, step].wait_recv()
            slot = place(i, net.block(step, True), rows, net.row)
            in_chip(q, step, True, slot, slot)

    def after_x(q):
        i, rows = order[q]
        if kinds[i] == "all":
            for other in (False, True):
                for step in steps:
                    along_x[q, step, other].wait_recv()
                    slot = place(i, net.block(step, other), rows, other_row)
                    moved.append(net.send(slot, slot, net.core_peer()))

    for tick in range(len(order) + 3):
        if tick < len(order):
            if tick >= 2:
                for step in range(1, net.high_count):
                    net.left(along_z[tick - 2, step])
            start(tick)
        if tick % 2:
            swap_next()
        for stage, lag in ((after_z, 1), (after_y, 2), (after_x, 3)):
            if 0 <= tick - lag < len(order):
                stage(tick - lag)
    while swap_sends:
        swap_next()
    for copy in [*moved, *to_core.values()]:
        copy.wait_recv()
    for local in locals_:
        local.wait()
    net.finish()


def gather(cols, collective_id, *triples):
    kinds = [kind for kind, _, _ in triples]
    pieces = [piece for _, piece, _ in triples]
    arrays = [array for _, _, array in triples]
    copies = 0
    shapes = []
    for kind, piece, array in triples:
        if kind == "swap":
            shapes.append(jax.ShapeDtypeStruct(array.shape, array.dtype))
            copies += cols
        elif kind == "col":
            shapes.append(jax.ShapeDtypeStruct((cols, *array.shape), array.dtype))
            copies += cols * piece
        else:
            rows = lax.axis_size("row")
            shape = (cols, array.shape[0], rows * array.shape[1])
            shapes.append(jax.ShapeDtypeStruct(shape, array.dtype))
            copies += 4 * cols * piece
    return pl.pallas_call(
        functools.partial(gather_kernel, cols, kinds, pieces),
        out_shape=shapes,
        in_specs=[pl.BlockSpec(memory_space=pl.ANY)] * len(triples),
        out_specs=[pl.BlockSpec(memory_space=pl.ANY)] * len(triples),
        scratch_shapes=[
            pltpu.SemaphoreType.DMA((copies,)),
            pltpu.SemaphoreType.DMA((copies,)),
            pltpu.SemaphoreType.DMA((len(triples),)),
        ],
        compiler_params=pltpu.CompilerParams(collective_id=collective_id, has_side_effects=True),
        name=f"gather_{collective_id}",
    )(*arrays)


def add_rows(target, terms):
    rows = target.shape[0]
    piece = 32 if rows % 32 == 0 else 16

    def body(index, carry):
        at = pl.ds(pl.multiple_of(index * piece, piece), piece)
        total = terms[0][at, :].astype(f32)
        for term in terms[1:]:
            total = total + term[at, :].astype(f32)
        target[at, :] = total.astype(target.dtype)
        return carry

    lax.fori_loop(0, rows // piece, body, 0)


class ScatterCol:
    def __init__(self, net, part, rows, from_y, from_z, out):
        self.net, self.part, self.rows = net, part, rows
        self.from_y, self.from_z, self.out = from_y, from_z, out
        self.order = [*range(1, net.high_count), 0]
        self.along_y, self.along_z = {}, {}
        self.stages = [self.send_y, self.send_z, self.last]

    def send_y(self):
        for step in self.order:
            source = self.part.at[self.net.block_ahead(step, True), self.rows]
            self.along_y[step] = self.net.send(
                source, self.from_y.at[step, self.rows], self.net.y_peer()
            )

    def send_z(self):
        for step in self.order:
            self.along_y[step].wait_recv()
            mine = self.part.at[self.net.block_ahead(step), self.rows]
            slot = self.from_y.at[step, self.rows]
            if step:
                add_rows(slot, [mine, slot])
                self.along_z[step] = self.net.send(
                    slot, self.from_z.at[step - 1, self.rows], self.net.z_peer(step)
                )

    def last(self):
        for step in range(1, self.net.high_count):
            self.along_z[step].wait_recv()
        terms = [
            self.from_z.at[step - 1, self.rows] for step in range(1, self.net.high_count)
        ]
        mine = self.part.at[self.net.me, self.rows]
        add_rows(self.out.at[self.rows], [mine, self.from_y.at[0, self.rows], *terms])

    def clear_y(self):
        for step in self.order:
            self.net.left(self.along_y[step])


class ScatterAll:
    def __init__(self, net, part, rows, from_core, from_x, from_y, from_z, out):
        self.net, self.part, self.rows, self.out = net, part, rows, out
        self.from_core, self.from_x, self.from_y, self.from_z = from_core, from_x, from_y, from_z
        self.order = [*range(1, net.high_count), 0]
        self.blocks = [(step, True) for step in self.order]
        self.blocks += [(step, False) for step in self.order]
        self.across, self.onward, self.along_y, self.along_z = {}, {}, {}, {}
        self.other_row = 2 * (1 - net.outer) + net.core
        self.stages = [self.send_core, self.send_x, self.send_y, self.send_z, self.last]

    def features(self, row):
        width = self.out.shape[1]
        return pl.ds(pl.multiple_of(row * width, LANES), width)

    def block(self, key):
        return self.net.block_ahead(*key)

    def send_core(self):
        net = self.net
        for far in (1, 0):
            outer = 1 - net.outer if far else net.outer
            for key in self.blocks:
                block = self.block(key)
                features = self.features(2 * outer + 1 - net.core)
                self.across[far, key] = net.send(
                    self.part.at[block, self.rows, features],
                    self.from_core.at[far, block, self.rows],
                    net.core_peer(),
                )

    def send_x(self):
        for key in self.blocks:
            self.across[1, key].wait_recv()
            block = self.block(key)
            slot = self.from_core.at[1, block, self.rows]
            mine = self.part.at[block, self.rows, self.features(self.other_row)]
            add_rows(slot, [mine, slot])
            self.onward[key] = self.net.send(
                slot, self.from_x.at[block, self.rows], self.net.x_peer()
            )

    def send_y(self):
        for key in self.blocks:
            self.across[0, key].wait_recv()
            self.onward[key].wait_recv()
            block = self.block(key)
            slot = self.from_core.at[0, block, self.rows]
            mine = self.part.at[block, self.rows, self.features(self.net.row)]
            add_rows(slot, [mine, slot, self.from_x.at[block, self.rows]])
            step, other = key
            if other:
                self.along_y[step] = self.net.send(
                    slot, self.from_y.at[step, self.rows], self.net.y_peer()
                )

    def send_z(self):
        for step in self.order:
            self.along_y[step].wait_recv()
            slot = self.from_core.at[0, self.block((step, False)), self.rows]
            add_rows(slot, [slot, self.from_y.at[step, self.rows]])
            if step:
                self.along_z[step] = self.net.send(
                    slot, self.from_z.at[step - 1, self.rows], self.net.z_peer(step)
                )

    def last(self):
        for step in range(1, self.net.high_count):
            self.along_z[step].wait_recv()
        terms = [
            self.from_z.at[step - 1, self.rows] for step in range(1, self.net.high_count)
        ]
        mine = self.from_core.at[0, self.net.me, self.rows]
        add_rows(self.out.at[self.rows], [mine, *terms])


def scatter_kernel(cols, kinds, pieces, *refs):
    count = len(kinds)
    parts, outs, scratch = refs[:count], refs[count : 2 * count], list(refs[2 * count :])
    send_sems, recv_sems = scratch[-2:]
    net = Net(cols, send_sems, recv_sems)
    net.greet(col_peers(net) + (row_peers(net) if "all" in kinds else []))
    lines = {"all": [], "col": []}
    for i, kind in enumerate(kinds):
        buffers = [scratch.pop(0) for _ in range(4 if kind == "all" else 2)]
        rows = outs[i].shape[0] // pieces[i]
        make = ScatterAll if kind == "all" else ScatterCol
        lines[kind] += [
            make(net, parts[i], pl.ds(q * rows, rows), *buffers, outs[i])
            for q in range(pieces[i])
        ]
    ticks = max(len(lines["all"]) + 4, len(lines["col"]) + 2)
    for tick in range(ticks):
        for kind in ("col", "all"):
            line = lines[kind]
            if kind == "col" and 2 <= tick < len(line):
                line[tick - 2].clear_y()
            depth = 5 if kind == "all" else 3
            for stage in range(depth):
                if 0 <= tick - stage < len(line):
                    line[tick - stage].stages[stage]()
    net.finish()


def scatter(cols, collective_id, *triples):
    high = cols // 2
    scratch, outs, copies = [], [], 0
    for kind, piece, array in triples:
        rows, width = array.shape[1:]
        if kind == "all":
            width = width // lax.axis_size("row")
            scratch += [
                pltpu.VMEM((2, cols, rows, width), bf16),
                pltpu.VMEM((cols, rows, width), bf16),
            ]
            copies += 3 * cols * piece
        copies += cols * piece
        scratch += [pltpu.VMEM((high, rows, width), bf16), pltpu.VMEM((high - 1, rows, width), bf16)]
        outs.append(jax.ShapeDtypeStruct((rows, width), f32))
    vmem = pl.BlockSpec(memory_space=pltpu.VMEM)
    return pl.pallas_call(
        functools.partial(
            scatter_kernel, cols, [kind for kind, _, _ in triples], [p for _, p, _ in triples]
        ),
        out_shape=outs,
        in_specs=[vmem] * len(triples),
        out_specs=[vmem] * len(triples),
        scratch_shapes=[
            *scratch,
            pltpu.SemaphoreType.DMA((copies,)),
            pltpu.SemaphoreType.DMA((copies,)),
        ],
        compiler_params=pltpu.CompilerParams(
            collective_id=collective_id, has_side_effects=True, vmem_limit_bytes=60 << 20
        ),
        name=f"scatter_{collective_id}",
    )(*[array for _, _, array in triples])


def sum_row_kernel(part, out, from_core, to_x, from_x, send_sems, recv_sems):
    net = Net(2, send_sems, recv_sems)
    net.greet(row_peers(net))
    pieces = from_core.shape[0]
    rows = from_core.shape[1]

    def piece(core, i):
        start = (core * pieces + i) * rows
        return pl.ds(pl.multiple_of(start, rows), rows)

    across = [
        net.send(part.at[piece(1 - net.core, i)], from_core.at[i], net.core_peer())
        for i in range(pieces)
    ]
    along, back = [], []
    for i in range(pieces):
        across[i].wait_recv()
        add_rows(to_x.at[i], [part.at[piece(net.core, i)], from_core.at[i]])
        along.append(net.send(to_x.at[i], from_x.at[i], net.x_peer()))
    for i in range(pieces):
        along[i].wait_recv()
        mine = piece(net.core, i)
        add_rows(out.at[mine], [to_x.at[i], from_x.at[i]])
        back.append(net.send(out.at[mine], out.at[mine], net.core_peer()))
    for copy in back:
        copy.wait_recv()
    net.finish()


def sum_row_call(collective_id, part):
    pieces = 4
    rows = part.shape[0] // 2 // pieces
    piece = (pieces, rows, part.shape[1])
    return pl.pallas_call(
        sum_row_kernel,
        out_shape=jax.ShapeDtypeStruct(part.shape, bf16),
        in_specs=[pl.BlockSpec(memory_space=pltpu.VMEM)],
        out_specs=pl.BlockSpec(memory_space=pltpu.VMEM),
        scratch_shapes=[
            pltpu.VMEM(piece, bf16),
            pltpu.VMEM(piece, bf16),
            pltpu.VMEM(piece, bf16),
            pltpu.SemaphoreType.DMA((3 * pieces,)),
            pltpu.SemaphoreType.DMA((3 * pieces,)),
        ],
        compiler_params=pltpu.CompilerParams(
            collective_id=collective_id, has_side_effects=True, vmem_limit_bytes=32 << 20
        ),
        name=f"sum_row_{collective_id}",
    )(part)


def dot_nn(left, right):
    return lax.dot_general(left, right, (((1,), (0,)), ((), ())), preferred_element_type=f32)


def dot_nt(left, right):
    return lax.dot_general(left, right, (((1,), (1,)), ((), ())), preferred_element_type=f32)


def dot_tn(left, right):
    return lax.dot_general(left, right, (((0,), (0,)), ((), ())), preferred_element_type=f32)


def each_tile(count, body):
    def step(index, carry):
        body(index)
        return carry

    lax.fori_loop(0, count, step, 0)


TILE = 512


def tile_at(index, tile=TILE):
    if isinstance(index, int):
        return pl.ds(index * tile, tile)
    return pl.ds(pl.multiple_of(index * tile, tile), tile)


class Line:
    def __init__(self, net, items, direct=(), direct_from=0):
        self.net, self.items, self.direct, self.direct_from = net, items, list(direct), direct_from
        self.other_row = 2 * (1 - net.outer) + net.core
        self.along_z, self.along_y, self.along_x, self.to_core = {}, {}, {}, {}
        self.moved = []
        self.now = 0

    def in_chip(self, q, step, other, source, slot):
        if self.items[q][2]:
            self.along_x[q, step, other] = self.net.send(source, slot, self.net.x_peer())
            self.to_core[q, step, other] = self.net.send(source, slot, self.net.core_peer())

    def start(self, q):
        net = self.net
        source, slot_of, _ = self.items[q]
        slot = slot_of(net.me, net.row)
        for step in reversed(range(1, net.high_count)):
            self.along_z[q, step] = net.send(source, slot, net.z_peer(step))
        self.along_y[q, 0] = net.send(source, slot, net.y_peer())
        self.in_chip(q, 0, False, source, slot)

    def after_z(self, q):
        net = self.net
        for step in reversed(range(1, net.high_count)):
            self.along_z[q, step].wait_recv()
            slot = self.items[q][1](net.block(step), net.row)
            self.along_y[q, step] = net.send(slot, slot, net.y_peer())
            self.in_chip(q, step, False, slot, slot)

    def after_y(self, q):
        net = self.net
        for step in range(net.high_count):
            self.along_y[q, step].wait_recv()
            slot = self.items[q][1](net.block(step, True), net.row)
            self.in_chip(q, step, True, slot, slot)

    def after_x(self, q):
        net = self.net
        if self.items[q][2]:
            for other in (False, True):
                for step in range(net.high_count):
                    self.along_x[q, step, other].wait_recv()
                    slot = self.items[q][1](net.block(step, other), self.other_row)
                    self.moved.append(net.send(slot, slot, net.core_peer()))

    def tick(self, count=1):
        net = self.net
        for _ in range(count):
            now, self.now = self.now, self.now + 1
            if now < len(self.items):
                if now >= 2:
                    for step in range(1, net.high_count):
                        net.left(self.along_z[now - 2, step])
                self.start(now)
            if now >= self.direct_from and self.direct:
                self.moved.append(net.send(*self.direct.pop(0)))
            for stage, lag in ((self.after_z, 1), (self.after_y, 2), (self.after_x, 3)):
                if 0 <= now - lag < len(self.items):
                    stage(now - lag)

    def drain(self):
        while self.now < len(self.items) + 3 or self.direct:
            self.tick()
        for copy in [*self.moved, *self.to_core.values()]:
            copy.wait_recv()


def front_kernel(
    cols,
    experts,
    tokens,
    query,
    key,
    value,
    misc,
    out_own,
    shared_own,
    grad_own,
    table_row,
    table_col,
    doc_col,
    cosine,
    sine,
    weights,
    out_weights,
    shared_all,
    grad_all,
    rows_all,
    cols_all,
    h1,
    q_low,
    kv_all,
    probs,
    heads,
    attn,
    h2,
    gate,
    router_probs,
    gains,
    inverse,
    kv_low,
    keys,
    values,
    bias,
    partial,
    from_core,
    to_x,
    from_x,
    send_sems,
    recv_sems,
    local_sems,
):
    net = Net(cols, send_sems, recv_sems)
    toks, width = tokens.shape
    size = HEAD_DIM
    q_width = q_low.shape[1]
    group = q_width // size
    rows_w = query.shape[0]
    seqs = probs.shape[0]
    local_len = toks // seqs
    full_len = local_len * cols
    scale = 1.0 / math.sqrt(size)
    mine = pl.ds(pl.multiple_of(net.me * rows_w, 16), rows_w)

    copies = []

    def local_copy(source, target):
        copy = pltpu.make_async_copy(source, target, local_sems.at[len(copies)])
        copy.start()
        copies.append(copy)

    local_copy(query, weights.at[mine, pl.ds(0, q_width)])
    local_copy(key, weights.at[mine, pl.ds(q_width, size)])
    local_copy(value, weights.at[mine, pl.ds(q_width + size, size)])
    local_copy(misc, weights.at[mine, pl.ds(q_width + 2 * size, LANES)])
    first = len(copies)
    local_copy(out_own, out_weights.at[mine])
    local_copy(shared_own.at[net.me], shared_all.at[net.me])
    part = grad_own.shape[1]
    local_copy(
        grad_own, grad_all.at[net.me, :, pl.ds(pl.multiple_of(net.row * part, LANES), part)]
    )
    local_copy(table_row, rows_all.at[net.me])
    local_copy(table_col, cols_all.at[net.me])
    net.greet([net.col_peer(step) for step in range(1, cols)] + row_peers(net))
    for copy in copies[:first]:
        copy.wait()

    def weight_slot(target, start, count):
        def slot(block, row):
            return target.at[pl.ds(pl.multiple_of(block * rows_w + start, 16), count)]

        return slot

    def grad_slot(start, count):
        def slot(block, row):
            return grad_all.at[
                block, pl.ds(start, count), pl.ds(pl.multiple_of(row * part, LANES), part)
            ]

        return slot

    items = [(table_row, lambda block, row: rows_all.at[block], False)]
    pieces, out_pieces, grad_pieces = 5, 4, 4
    count = rows_w // pieces
    for q in range(pieces):
        slot = weight_slot(weights, q * count, count)
        items.append((slot(net.me, net.row), slot, False))
    ready_weights = len(items) + 2
    out_items, grad_items = [], []
    count = rows_w // out_pieces
    for q in range(out_pieces):
        slot = weight_slot(out_weights, q * count, count)
        out_items.append((out_own.at[pl.ds(q * count, count)], slot, False))
    count = toks // grad_pieces
    for q in range(grad_pieces):
        grad_items.append((grad_own.at[pl.ds(q * count, count)], grad_slot(q * count, count), True))
    items += out_items[:2]
    for q in range(2, out_pieces):
        items += [grad_items[q - 2], out_items[q]]
    ready_out = len(items) + 2
    items += grad_items[out_pieces - 2 :]
    items.append((table_col, lambda block, row: cols_all.at[block], False))
    direct = []
    for step in range(1, cols):
        block = lax.rem(net.me + step, cols)
        direct.append((shared_own.at[block], shared_all.at[net.me], net.col_peer(step)))
    line = Line(net, items, direct, ready_weights - 2)

    line.tick(2)
    copies[first + 3].wait()

    def chunks(body, rows=32):
        def step(index, carry):
            body(pl.ds(pl.multiple_of(index * rows, rows), rows))
            return carry

        lax.fori_loop(0, toks // rows, step, 0)

    def measure_first(at):
        x = tokens[at, :].astype(f32)
        total = jnp.sum(x * x, axis=1, keepdims=True)
        inverse[at, :] = jnp.broadcast_to(lax.rsqrt(total / width + norm_eps), (32, LANES))

    chunks(measure_first)
    line.tick(ready_weights - line.now)

    start = q_width + 2 * size
    for tile in range(width // TILE):
        at = pl.ds(tile * TILE, TILE)
        turned = jnp.transpose(weights[at, start : start + LANES].astype(f32))
        gains[:, at] = turned[experts : experts + 8]

    def norm_first(at):
        x = tokens[at, :].astype(f32) * inverse[at, 0:1]
        h1[at, :] = (x * gains[0:1, :]).astype(bf16)

    chunks(norm_first)
    line.tick()
    heads_all = group + 2
    for head in range(heads_all - 1, -1, -1):
        raw = dot_nn(h1[...], weights[:, head * size : (head + 1) * size])
        if head <= group:
            raw = raw * cosine[...] + pltpu.roll(raw, size // 2, 1) * sine[...]
        if head < group:
            q_low[:, head * size : (head + 1) * size] = raw.astype(bf16)
        else:
            kv_low[:, (head - group) * size : (head - group + 1) * size] = raw.astype(bf16)
        if head == group:
            kv_all[net.me] = kv_low[...]

            def kv_slot(s):
                rows = pl.ds(s * local_len, local_len)
                return lambda block, row: kv_all.at[block, rows]

            kv_line = Line(
                net,
                [
                    (kv_low.at[pl.ds(s * local_len, local_len)], kv_slot(s), False)
                    for s in range(seqs)
                ],
            )
            kv_line.tick()
        if head == group // 2:
            kv_line.tick()
    line.tick()
    kv_line.tick()

    for s in range(seqs):
        if s:
            kv_line.tick()
        rows = pl.ds(s * local_len, local_len)
        place = lax.broadcasted_iota(jnp.int32, (local_len, local_len), 0)
        lane = lax.broadcasted_iota(jnp.int32, (local_len, local_len), 1)
        for c in range(cols):
            at = pl.ds(c * local_len, local_len)
            keys[at, :] = kv_all[c, rows, :size]
            values[at, :] = kv_all[c, rows, size:]
            same = doc_col[rows, :] == rows_all[c, experts : experts + 1, rows]
            ahead = (c - net.me) * local_len
            allowed = same & (lane + ahead <= place)
            bias[:, at] = jnp.where(allowed, 0.0, masked_score)

        def attend(g, carry, s=s, rows=rows):
            at = pl.ds(pl.multiple_of(g * size, size), size)
            scores = dot_nt(q_low[rows, at], keys[...]) * scale + bias[...]
            weight = jnp.exp(scores - jnp.max(scores, axis=1, keepdims=True))
            p = (weight / jnp.sum(weight, axis=1, keepdims=True)).astype(bf16)
            probs[s, g] = p
            heads[rows, at] = dot_nn(p, values[...]).astype(bf16)
            return carry

        lax.fori_loop(0, group, attend, 0)
        if line.now < ready_out:
            line.tick()
    line.tick(max(0, ready_out - line.now))
    copies[first].wait()

    pieces = from_core.shape[0]
    piece_rows = from_core.shape[1]

    def row_piece(core, i):
        return pl.ds(
            pl.multiple_of((core * pieces + i) * piece_rows, piece_rows), piece_rows
        )

    half = pieces * piece_rows
    across = []
    for core in (1 - net.core, net.core):
        at_rows = pl.ds(pl.multiple_of(core * half, half), half)
        for tile in range(width // TILE):
            at = pl.ds(tile * TILE, TILE)
            partial[at_rows, at] = dot_nt(heads[at_rows, :], out_weights[at, :]).astype(bf16)
        if not across:
            across = [
                net.send(partial.at[row_piece(1 - net.core, i)], from_core.at[i], net.core_peer())
                for i in range(pieces)
            ]
    along, back = [], []
    for i in range(pieces):
        across[i].wait_recv()
        add_rows(to_x.at[i], [partial.at[row_piece(net.core, i)], from_core.at[i]])
        along.append(net.send(to_x.at[i], from_x.at[i], net.x_peer()))
    line.tick()
    for i in range(pieces):
        along[i].wait_recv()
        at = row_piece(net.core, i)
        add_rows(attn.at[at], [to_x.at[i], from_x.at[i]])
        back.append(net.send(attn.at[at], attn.at[at], net.core_peer()))
    line.tick()
    for copy in back:
        copy.wait_recv()

    def norm_second(at):
        x = tokens[at, :].astype(f32) + attn[at, :].astype(f32)
        total = jnp.sum(x * x, axis=1, keepdims=True)
        h2[at, :] = (x * lax.rsqrt(total / width + norm_eps) * gains[1:2, :]).astype(bf16)

    chunks(norm_second)
    line.tick()
    logits = dot_nn(h2[...], weights[:, start : start + LANES])
    lane = lax.broadcasted_iota(jnp.int32, (toks, LANES), 1)
    logits = jnp.where(lane < experts, logits, masked_score)
    weight = jnp.exp(logits - jnp.max(logits, axis=1, keepdims=True))
    chance = weight / jnp.sum(weight, axis=1, keepdims=True)
    router_probs[...] = chance
    picked = jnp.where((table_col[...] > 0) & (lane < experts), chance, 0.0)
    gate[...] = picked / jnp.sum(picked, axis=1, keepdims=True)
    line.drain()
    kv_line.drain()
    for copy in [*copies[first + 1 : first + 3], copies[first + 4]]:
        copy.wait()
    net.finish()


def front_call(
    cols, collective_id, experts, tokens, query, key, value, misc, out_own, shared_own, grad_own,
    table_row, table_col, doc_col, cosine, sine, seqs,
):
    toks, width = tokens.shape
    q_width = query.shape[1]
    size = HEAD_DIM
    local_len = toks // seqs
    vmem, any_space = pl.BlockSpec(memory_space=pltpu.VMEM), pl.BlockSpec(memory_space=pl.ANY)

    def shape(*dims, dtype=bf16):
        return jax.ShapeDtypeStruct(dims, dtype)

    pieces = 4
    piece = (pieces, toks // 2 // pieces, width)
    copies = 320
    return pl.pallas_call(
        functools.partial(front_kernel, cols, experts),
        out_shape=[
            shape(width, q_width + 2 * size + LANES),
            shape(width, q_width),
            shape(*shared_own.shape),
            shape(cols, toks, width),
            shape(cols, *table_row.shape, dtype=f32),
            shape(cols, *table_col.shape),
            shape(toks, width),
            shape(toks, q_width),
            shape(cols, toks, 2 * size),
            shape(seqs, q_width // size, local_len, cols * local_len),
            shape(toks, q_width),
            shape(toks, width),
            shape(toks, width),
            shape(toks, LANES, dtype=f32),
            shape(toks, LANES, dtype=f32),
        ],
        in_specs=[vmem] + [any_space] * 7 + [vmem] * 5,
        out_specs=[vmem, vmem, any_space, any_space] + [vmem] * 11,
        scratch_shapes=[
            pltpu.VMEM((8, width), f32),
            pltpu.VMEM((toks, LANES), f32),
            pltpu.VMEM((toks, 2 * size), bf16),
            pltpu.VMEM((cols * local_len, size), bf16),
            pltpu.VMEM((cols * local_len, size), bf16),
            pltpu.VMEM((local_len, cols * local_len), f32),
            pltpu.VMEM((toks, width), bf16),
            pltpu.VMEM(piece, bf16),
            pltpu.VMEM(piece, bf16),
            pltpu.VMEM(piece, bf16),
            pltpu.SemaphoreType.DMA((copies,)),
            pltpu.SemaphoreType.DMA((copies,)),
            pltpu.SemaphoreType.DMA((16,)),
        ],
        compiler_params=pltpu.CompilerParams(
            collective_id=collective_id, has_side_effects=True, vmem_limit_bytes=48 << 20
        ),
        name=f"front_{collective_id}",
    )(
        tokens, query, key, value, misc, out_own, shared_own, grad_own,
        table_row, table_col, doc_col, cosine, sine,
    )


def experts_kernel(
    cols,
    capacity,
    h2,
    grads,
    w_gate,
    w_up,
    w_down,
    w_shared,
    rank_row,
    rank_col,
    gate_own,
    out_part,
    back,
    g_gate,
    g_up,
    g_down,
    g_shared,
    gate_dots,
    h2_all,
    xs_all,
    cs_all,
    wgu,
    wd,
    ws,
    gates,
    hb,
    xbuf,
    ybuf,
    obuf,
    part,
    pre,
    gcol,
    dcol,
    dz_all,
    zg_all,
    dgu_all,
    sdz_all,
    sz_all,
    sgu_all,
    from_core,
    from_x,
    from_y,
    from_z,
    kept,
    dots,
    dots_core,
    dots_x,
    tiles,
    tiles_all,
    stage,
    stage_low,
    send_sems,
    recv_sems,
    local_sems,
):
    net = Net(cols, send_sems, recv_sems)
    toks, width = h2.shape
    exp_local, _, hidden = w_gate.shape
    high = net.high_count
    pad = ws.shape[1] // 3
    slots = exp_local * capacity
    pair = 2 * capacity
    piece = width // lax.axis_size("row")
    share = width // LANES // 5 * LANES
    rest = (width - 4 * share) // 2
    wide = width // TILE
    net.greet([net.col_peer(step) for step in range(1, cols)] + row_peers(net))

    def local_copy(source, target, index):
        copy = pltpu.make_async_copy(source, target, local_sems.at[index])
        copy.start()
        return copy

    gate_copies = [
        net.send(gate_own, gates.at[net.me], net.col_peer(step)) for step in range(1, cols)
    ]
    gates[net.me] = gate_own[...]

    def feature_e(row):
        return pl.ds(pl.multiple_of(row * share, LANES), share)

    def feature_r(core):
        return pl.ds(pl.multiple_of(4 * share + core * rest, LANES), rest)

    own_e, own_r = feature_e(net.row), feature_r(net.core)
    far_e = feature_e(2 * (1 - net.outer) + net.core)

    def pass_on(source, block, features, peer):
        return net.send(source.at[..., features], h2_all.at[block, :, features], peer)

    along_z, along_y, along_x, to_core = {}, {}, {}, {}
    for step in range(high - 1, 0, -1):
        along_z[high - step] = [
            pass_on(h2, net.me, own_e, net.z_peer(step)),
            pass_on(h2, net.me, own_r, net.z_peer(step)),
        ]
    along_y[0] = [
        pass_on(h2, net.me, own_e, net.y_peer()),
        pass_on(h2, net.me, own_r, net.y_peer()),
    ]

    def block_of(step, other):
        return net.block_ahead(step, other)

    def share_in_chip(step, other):
        block = block_of(step, other)
        source = h2_all.at[block]
        along_x[step, other] = pass_on(source, block, own_e, net.x_peer())
        to_core[step, other] = [
            pass_on(source, block, own_e, net.core_peer()),
            pass_on(source, block, own_r, net.core_peer()),
        ]

    def arrived_y(step):
        for copy in along_y[step]:
            copy.wait_recv()
        share_in_chip(step, True)

    def arrived_z(step):
        for copy in along_z[step]:
            copy.wait_recv()
        block = block_of(step, False)
        along_y[step] = [
            pass_on(h2_all.at[block], block, own_e, net.y_peer()),
            pass_on(h2_all.at[block], block, own_r, net.y_peer()),
        ]
        share_in_chip(step, False)

    def arrived_x(step, other):
        along_x[step, other].wait_recv()
        block = block_of(step, other)
        to_core[step, other].append(pass_on(h2_all.at[block], block, far_e, net.core_peer()))

    def whole(step, other):
        for copy in to_core[step, other]:
            copy.wait_recv()

    events = [functools.partial(arrived_y, 0)]
    for step in range(1, high):
        events.append(functools.partial(arrived_z, step))
        events.append(functools.partial(arrived_x, step - 1, True))
        events.append(functools.partial(arrived_y, step))
        events.append(functools.partial(arrived_x, step, False))
    events.append(functools.partial(arrived_x, high - 1, True))
    events = iter(events)

    def pump(count=1):
        for _ in range(count):
            event = next(events, None)
            if event is not None:
                event()

    loads = []
    for e in range(exp_local):
        loads.append(local_copy(w_down.at[e], wd.at[e], 3 * e))
        loads.append(local_copy(w_gate.at[e], wgu.at[e, :, pl.ds(0, hidden)], 3 * e + 1))
        loads.append(local_copy(w_up.at[e], wgu.at[e, :, pl.ds(hidden, hidden)], 3 * e + 2))
    base = 3 * exp_local
    loads.append(local_copy(w_shared, ws, base))
    keep_own = local_copy(h2, h2_all.at[net.me], base + 1)
    base += 2

    def load_pair(source, step):
        first = local_copy(source.at[block_of(step, False)], hb.at[0], base)
        second = local_copy(source.at[block_of(step, True)], hb.at[1], base + 1)
        first.wait()
        second.wait()

    slot_row = lax.broadcasted_iota(jnp.int32, (capacity, toks), 0).astype(f32) + 1.0
    slot_lane = lax.broadcasted_iota(jnp.int32, (toks, capacity), 1).astype(f32) + 1.0

    def chosen(block, e):
        return rank_row[block, e : e + 1, :] == slot_row

    def picks(block):
        rows = [
            jnp.where(chosen(block, e), 1.0, 0.0).astype(bf16) for e in range(exp_local)
        ]
        return jnp.concatenate(rows, axis=0)

    def picks_back(block):
        lanes = [
            jnp.where(rank_col[block, :, e : e + 1] == slot_lane, 1.0, 0.0).astype(bf16)
            for e in range(exp_local)
        ]
        return jnp.concatenate(lanes, axis=1)

    def dispatch(step):
        for b in (0, 1):
            table = picks(block_of(step, b == 1))

            def tile(index, b=b, table=table):
                at = tile_at(index)
                rows = dot_nn(table, hb[b, :, at]).astype(bf16)
                for e in range(exp_local):
                    xbuf[e, pl.ds(b * capacity, capacity), at] = rows[
                        e * capacity : (e + 1) * capacity
                    ]

            each_tile(wide, tile)

    def save_rows(target, step):
        return [
            local_copy(
                xbuf.at[e], target.at[e, pl.ds(step * pair, pair)], base + 2 + e
            )
            for e in range(exp_local)
        ]

    saved = []
    for step in range(high):
        load_pair(grads, step)
        if step == 0:
            for copy in loads:
                copy.wait()
        for copy in saved:
            copy.wait()
        dispatch(step)
        saved = save_rows(cs_all, step)
        for e in range(exp_local):
            dz_all[e, pl.ds(step * pair, pair), :] = dot_nt(xbuf[e], wd[e]).astype(bf16)
        for b in (0, 1):
            sdz_all[block_of(step, b == 1)] = dot_nn(hb[b], ws[:, 2 * pad :]).astype(bf16)
        pump()
    for copy in gate_copies:
        copy.wait_recv()
    keep_own.wait()

    across, onward, upward, far_z = {}, {}, {}, {}

    def features(row):
        return pl.ds(pl.multiple_of(row * piece, LANES), piece)

    other_row = 2 * (1 - net.outer) + net.core

    def hand_over(step):
        for b in (1, 0):
            for far in (1, 0):
                outer = 1 - net.outer if far else net.outer
                source = part.at[b, :, features(2 * outer + 1 - net.core)]
                across[step, b, far] = net.send(
                    source, from_core.at[far, step, b], net.core_peer()
                )

    def sum_cores(step):
        for b in (1, 0):
            for far, row in ((1, other_row), (0, net.row)):
                across[step, b, far].wait_recv()
                slot = from_core.at[far, step, b]
                add_rows(slot, [part.at[b, :, features(row)], slot])
                if far:
                    onward[step, b] = net.send(slot, from_x.at[step, b], net.x_peer())
        for b in (1, 0):
            for far in (1, 0):
                net.left(across[step, b, far])

    def sum_chips(step):
        for b in (1, 0):
            onward[step, b].wait_recv()
            slot = from_core.at[0, step, b]
            add_rows(slot, [slot, from_x.at[step, b]])
            if b:
                upward[step] = net.send(slot, from_y.at[step], net.y_peer())

    def sum_plane(step):
        upward[step].wait_recv()
        slot = from_core.at[0, step, 0]
        add_rows(slot, [slot, from_y.at[step]])
        if step:
            far_z[step] = net.send(slot, from_z.at[step - 1], net.z_peer(step))

    own_expert = lax.rem(net.me, cols) * exp_local
    gate_rows = gates.shape[1]
    gate_row = lax.broadcasted_iota(jnp.int32, (gate_rows, toks), 0)
    dots[...] = jnp.zeros_like(dots)
    for step in range(high):
        if step:
            whole(step, False)
        whole(step, True)
        load_pair(h2_all, step)
        for copy in saved:
            copy.wait()
        dispatch(step)
        saved = save_rows(xs_all, step)
        pump()
        for b in (0, 1):
            block = block_of(step, b == 1)
            inner = dot_nn(hb[b], ws[:, : 2 * pad])
            sa, su = inner[:, :pad], inner[:, pad:]
            sig = 1.0 / (1.0 + jnp.exp(-sa))
            silu = sa * sig
            slope = sig * (1.0 + sa * (1.0 - sig))
            sz_all[block] = (silu * su).astype(bf16)
            sdz = sdz_all[block].astype(f32)
            sgu_all[block, :, :pad] = (sdz * su * slope).astype(bf16)
            sgu_all[block, :, pad:] = (sdz * silu).astype(bf16)
        if step:
            sum_cores(step - 1)
        rows = pl.ds(step * pair, pair)
        for e in range(exp_local):

            def inner_tile(index, e=e):
                at = tile_at(index, 256)
                pre[:, at] = dot_nn(xbuf[e], wgu[e, :, at])

            each_tile(2 * hidden // 256, inner_tile)
            for b in (0, 1):
                block = block_of(step, b == 1)
                gate = jnp.sum(
                    jnp.where(gate_row == own_expert + e, gates[block], 0.0), axis=0, keepdims=True
                )
                gate = jnp.sum(jnp.where(chosen(block, e), gate, 0.0), axis=1, keepdims=True)
                gcol[pl.ds(b * capacity, capacity), :] = jnp.broadcast_to(gate, (capacity, LANES))

            def gating(index, e=e, step=step):
                at = pl.ds(pl.multiple_of(index * 32, 32), 32)
                saved_at = pl.ds(pl.multiple_of(step * pair + index * 32, 32), 32)
                a, u = pre[at, :hidden], pre[at, hidden:]
                gate = jnp.concatenate([gcol[at, :]] * (hidden // LANES), axis=1)
                dz = dz_all[e, saved_at, :].astype(f32)
                sig = 1.0 / (1.0 + jnp.exp(-a))
                silu = a * sig
                slope = sig * (1.0 + a * (1.0 - sig))
                z = silu * u
                dcol[at, :] = jnp.broadcast_to(
                    jnp.sum(z * dz, axis=1, keepdims=True), (32, LANES)
                )
                zg_all[e, saved_at, :] = (z * gate).astype(bf16)
                dz = dz * gate
                dgu_all[e, saved_at, :hidden] = (dz * u * slope).astype(bf16)
                dgu_all[e, saved_at, hidden:] = (dz * silu).astype(bf16)

            each_tile(pair // 32, gating)
            for b in (0, 1):
                block = block_of(step, b == 1)
                col = dcol[pl.ds(b * capacity, capacity), :]
                col = jnp.concatenate([col] * (toks // LANES), axis=1)
                dots[block, e : e + 1, :] = jnp.sum(
                    jnp.where(chosen(block, e), col, 0.0), axis=0, keepdims=True
                )

            def out_tile(index, e=e):
                at = tile_at(index)
                y = dot_nn(zg_all[e, rows, :], wd[e, :, at]).astype(bf16)
                for b in (0, 1):
                    ybuf[b, pl.ds(e * capacity, capacity), at] = y[b * capacity : (b + 1) * capacity]

            each_tile(wide, out_tile)
            pump()
        if step:
            for copy in out_copies:
                copy.wait()
        out_copies = []
        for b in (0, 1):
            block = block_of(step, b == 1)
            table = picks_back(block)

            def join_tile(index, b=b, table=table, block=block):
                at = tile_at(index)
                total = dot_nn(table, ybuf[b, :, at])
                total = total + dot_nt(sz_all[block], ws[at, 2 * pad :])
                obuf[b, :, at] = total.astype(bf16)

            each_tile(wide, join_tile)
            out_copies.append(
                local_copy(obuf.at[b], out_part.at[block], base + 2 + exp_local + b)
            )
        pump()
        if step:
            sum_chips(step - 1)
        for e in range(exp_local):

            def back_tile(index, e=e):
                at = tile_at(index)
                y = dot_nt(dgu_all[e, rows, :], wgu[e, at, :]).astype(bf16)
                for b in (0, 1):
                    ybuf[b, pl.ds(e * capacity, capacity), at] = y[b * capacity : (b + 1) * capacity]

            each_tile(wide, back_tile)
        pump()
        for b in (1, 0):
            block = block_of(step, b == 1)
            table = picks_back(block)

            def back_join(index, b=b, table=table, block=block):
                at = tile_at(index)
                total = dot_nn(table, ybuf[b, :, at])
                total = total + dot_nt(sgu_all[block], ws[at, : 2 * pad])
                part[b, :, at] = total.astype(bf16)

            each_tile(wide, back_join)
        hand_over(step)
        if step:
            sum_plane(step - 1)
    pump(64)
    last = high - 1
    for copy in saved + out_copies:
        copy.wait()

    load_sem, store_sem = base + 4 + exp_local, base + 6 + exp_local

    def passes(count, load, work, stores):
        def load_copy(j, slot):
            source, target = load(j, slot)
            return pltpu.make_async_copy(source, target, local_sems.at[load_sem + slot])

        def store_copies(j, slot):
            return [
                pltpu.make_async_copy(
                    source, target, local_sems.at[store_sem + 2 * slot + i]
                )
                for i, (source, target) in enumerate(stores(j, slot))
            ]

        load_copy(0, 0).start()

        def body(j):
            slot = lax.rem(j, 2)

            @pl.when(j + 1 < count)
            def _():
                load_copy(j + 1, 1 - slot).start()

            load_copy(j, slot).wait()

            @pl.when(j >= 2)
            def _():
                for copy in store_copies(j - 2, slot):
                    copy.wait()

            work(j, slot)
            for copy in store_copies(j, slot):
                copy.start()

        each_tile(count, body)
        for j in range(max(0, count - 2), count):
            for copy in store_copies(j, j % 2):
                copy.wait()

    def inner_grads(e):
        passes(
            wide,
            lambda j, slot: (
                xs_all.at[e, :, tile_at(j)],
                tiles.at[slot],
            ),
            lambda j, slot: put(stage.at[slot], dot_tn(tiles[slot], dgu_all[e])),
            lambda j, slot: [
                (stage.at[slot, :, pl.ds(0, hidden)], g_gate.at[e, tile_at(j)]),
                (stage.at[slot, :, pl.ds(hidden, hidden)], g_up.at[e, tile_at(j)]),
            ],
        )

    def put(target, value):
        target[...] = value

    def down_grads(e):
        passes(
            wide,
            lambda j, slot: (
                cs_all.at[e, :, tile_at(j)],
                tiles.at[slot],
            ),
            lambda j, slot: put(
                stage.at[slot, pl.ds(0, hidden), pl.ds(0, TILE)],
                dot_tn(zg_all[e], tiles[slot]),
            ),
            lambda j, slot: [
                (
                    stage.at[slot, pl.ds(0, hidden), pl.ds(0, TILE)],
                    g_down.at[e, :, tile_at(j)],
                ),
            ],
        )

    def shared_grads(source, others, start, size):
        def work(j, slot):
            total = dot_tn(tiles_all[slot, 0], others[0])
            for c in range(1, cols):
                total = total + dot_tn(tiles_all[slot, c], others[c])
            stage_low[slot, :, :size] = total.astype(bf16)

        def load(j, slot):
            return (source.at[:, :, tile_at(j)], tiles_all.at[slot])

        passes(
            wide,
            lambda j, slot: load(j, slot),
            work,
            lambda j, slot: [
                (
                    stage_low.at[slot, :, pl.ds(0, size)],
                    g_shared.at[tile_at(j), pl.ds(start, size)],
                ),
            ],
        )

    first_dots = net.send(dots, dots_core, net.core_peer())
    inner_grads(0)
    sum_cores(last)
    first_dots.wait_recv()
    net.left(first_dots)
    dots[...] = dots[...] + dots_core[...]
    second_dots = net.send(dots, dots_x, net.x_peer())
    inner_grads(1)
    sum_chips(last)
    second_dots.wait_recv()
    dots_core[...] = dots[...] + dots_x[...]
    third_dots = []
    for step in range(1, cols):
        block = lax.rem(net.me + step, cols)
        third_dots.append(
            net.send(dots_core.at[block], gate_dots.at[net.me], net.col_peer(step))
        )
    gate_dots[net.me] = dots_core[net.me]
    down_grads(0)
    sum_plane(last)
    down_grads(1)
    for step in range(1, high):
        far_z[step].wait_recv()
    add_rows(kept, [from_core.at[0, 0, 0], *[from_z.at[step - 1] for step in range(1, high)]])
    own, other = features(net.row), features(other_row)
    back[:, own] = kept[...].astype(bf16)
    far = net.send(back.at[:, own], back.at[:, own], net.x_peer())
    near = net.send(back.at[:, own], back.at[:, own], net.core_peer())
    shared_grads(h2_all, sgu_all, 0, 2 * pad)
    far.wait_recv()
    crossed = net.send(back.at[:, other], back.at[:, other], net.core_peer())
    shared_grads(grads, sz_all, 2 * pad, pad)
    near.wait_recv()
    crossed.wait_recv()
    for copy in third_dots:
        copy.wait_recv()
    net.finish()


def experts_call(
    cols, collective_id, capacity, h2, grads, w_gate, w_up, w_down, w_shared, rank_row, rank_col, gate
):
    toks, width = h2.shape
    exp_local, _, hidden = w_gate.shape
    high = cols // 2
    pad = w_shared.shape[1] // 3
    piece = width // lax.axis_size("row")
    pair = 2 * capacity
    any_space = pl.BlockSpec(memory_space=pl.ANY)
    vmem = pl.BlockSpec(memory_space=pltpu.VMEM)
    copies = 160

    def shape(*dims, dtype=bf16):
        return jax.ShapeDtypeStruct(dims, dtype)

    return pl.pallas_call(
        functools.partial(experts_kernel, cols, capacity),
        out_shape=[
            shape(cols, toks, width),
            shape(toks, width),
            shape(exp_local, width, hidden, dtype=f32),
            shape(exp_local, width, hidden, dtype=f32),
            shape(exp_local, hidden, width, dtype=f32),
            shape(width, 3 * pad),
            shape(cols, 8, toks, dtype=f32),
            shape(cols, toks, width),
            shape(exp_local, cols * capacity, width),
            shape(exp_local, cols * capacity, width),
        ],
        in_specs=[any_space] * 6 + [vmem] * 3,
        out_specs=[
            any_space,
            vmem,
            any_space,
            any_space,
            any_space,
            any_space,
            vmem,
            any_space,
            any_space,
            any_space,
        ],
        scratch_shapes=[
            pltpu.VMEM((exp_local, width, 2 * hidden), bf16),
            pltpu.VMEM((exp_local, hidden, width), bf16),
            pltpu.VMEM((width, 3 * pad), bf16),
            pltpu.VMEM((cols, *gate.shape), f32),
            pltpu.VMEM((2, toks, width), bf16),
            pltpu.VMEM((exp_local, pair, width), bf16),
            pltpu.VMEM((2, exp_local * capacity, width), bf16),
            pltpu.VMEM((2, toks, width), bf16),
            pltpu.VMEM((2, toks, width), bf16),
            pltpu.VMEM((pair, 2 * hidden), f32),
            pltpu.VMEM((pair, LANES), f32),
            pltpu.VMEM((pair, LANES), f32),
            pltpu.VMEM((exp_local, cols * capacity, hidden), bf16),
            pltpu.VMEM((exp_local, cols * capacity, hidden), bf16),
            pltpu.VMEM((exp_local, cols * capacity, 2 * hidden), bf16),
            pltpu.VMEM((cols, toks, pad), bf16),
            pltpu.VMEM((cols, toks, pad), bf16),
            pltpu.VMEM((cols, toks, 2 * pad), bf16),
            pltpu.VMEM((2, high, 2, toks, piece), bf16),
            pltpu.VMEM((high, 2, toks, piece), bf16),
            pltpu.VMEM((high, toks, piece), bf16),
            pltpu.VMEM((high - 1, toks, piece), bf16),
            pltpu.VMEM((toks, piece), f32),
            pltpu.VMEM((cols, 8, toks), f32),
            pltpu.VMEM((cols, 8, toks), f32),
            pltpu.VMEM((cols, 8, toks), f32),
            pltpu.VMEM((2, cols * capacity, TILE), bf16),
            pltpu.VMEM((2, cols, toks, TILE), bf16),
            pltpu.VMEM((2, TILE, 2 * hidden), f32),
            pltpu.VMEM((2, TILE, 2 * pad), bf16),
            pltpu.SemaphoreType.DMA((copies,)),
            pltpu.SemaphoreType.DMA((copies,)),
            pltpu.SemaphoreType.DMA((24,)),
        ],
        compiler_params=pltpu.CompilerParams(
            collective_id=collective_id, has_side_effects=True, vmem_limit_bytes=62 << 20
        ),
        name=f"experts_{collective_id}",
    )(h2, grads, w_gate, w_up, w_down, w_shared, rank_row, rank_col, gate)


def experts_kernels(
    cols, collective_id, capacity, h2, grad_all, w_gate, w_up, w_down, shared_weights, *tables
):
    width, shared_part = shared_weights.shape[0], shared_weights.shape[1] // 3
    pad = -shared_part % LANES
    padded = jnp.pad(shared_weights.reshape(width, 3, shared_part), ((0, 0), (0, 0), (0, pad)))
    padded = padded.reshape(width, -1)
    out_part, back, g_gate, g_up, g_down, g_shared, gate_dots, *_ = experts_call(
        cols, collective_id, capacity, h2, grad_all, w_gate, w_up, w_down, padded, *tables
    )
    gate_dots = gate_dots[:, : w_gate.shape[0]].reshape(-1, h2.shape[0]).T
    g_shared = g_shared.reshape(width, 3, -1)[:, :, :shared_part].reshape(width, -1)
    return (out_part, back, gate_dots, g_shared, g_gate, g_up, g_down)


def fits(cols, rows, width):
    return cols % 2 == 0 and cols * rows * width * 2 <= 12 << 20


def gather_parts(kernels, cols, collective_id, *triples):
    if kernels:
        return gather(cols, collective_id, *triples)
    ways = {"col": gather_col, "all": gather_all, "swap": swap_col}
    return [ways[kind](array) for kind, _, array in triples]


def scatter_parts(kernels, cols, collective_id, *triples):
    if kernels:
        return scatter(cols, collective_id, *triples)
    ways = {"col": scatter_col, "all": scatter_all}
    return [ways[kind](array).astype(f32) for kind, _, array in triples]


def sum_row(kernels, collective_id, part):
    if kernels:
        return sum_row_call(collective_id, part)
    return lax.psum(part, "row")


def experts_plain(
    h2, grad_all, w_gate, w_up, w_down, shared_weights, router, rank_all, capacity, row_width
):
    cols = lax.axis_size("col")
    col_index, row_index = lax.axis_index("col"), lax.axis_index("row")
    toks, width = h2.shape
    exp_local = w_gate.shape[0]
    experts = rank_all.shape[2]
    shared_part = shared_weights.shape[1] // 3
    shared_in_weights = shared_weights[:, : 2 * shared_part]
    shared_down = shared_weights[:, 2 * shared_part :]
    h2_slice = lax.dynamic_slice_in_dim(h2, row_index * row_width, row_width, 1)
    h2_all = gather_all(h2_slice)

    all_mask = (rank_all > 0).astype(f32)
    all_probs = jax.nn.softmax(dot("ctd,de->cte", h2_all, router), axis=-1)
    all_picked = all_probs * all_mask
    all_gate = all_picked / jnp.sum(all_picked, axis=-1, keepdims=True)
    own = col_index * exp_local
    own_gate = lax.dynamic_slice_in_dim(all_gate, own, exp_local, 2)
    own_rank = lax.dynamic_slice_in_dim(rank_all, own, exp_local, 2).astype(jnp.int32)
    slots = jnp.arange(1, capacity + 1, dtype=jnp.int32)
    pick = jnp.swapaxes(own_rank, 1, 2)[:, :, None, :] == slots[:, None]
    slot_gate = jnp.sum(
        jnp.where(pick, jnp.swapaxes(own_gate, 1, 2)[:, :, None, :], 0.0), axis=3
    )[..., None]
    pick_low = pick.astype(bf16).reshape(cols, exp_local * capacity, toks)
    slot_shape = (cols, exp_local, capacity, width)
    slot_rows = dot("cut,ctd->cud", pick_low, h2_all).astype(bf16).reshape(slot_shape)
    slot_grad = dot("cut,ctd->cud", pick_low, grad_all).astype(bf16).reshape(slot_shape)
    gate_pre = dot("necd,edf->necf", slot_rows, w_gate)
    up_pre = dot("necd,edf->necf", slot_rows, w_up)
    silu_gate, slope_gate = silu_parts(gate_pre)
    hidden = silu_gate * up_pre
    gated = (hidden * slot_gate).astype(bf16)
    slot_out = dot("necf,efd->necd", gated, w_down).astype(bf16)
    hidden_grad = dot("necd,efd->necf", slot_grad, w_down)
    slot_dots = jnp.sum(hidden * hidden_grad, axis=-1)
    hidden_grad = hidden_grad * slot_gate
    gate_grad = (hidden_grad * up_pre * slope_gate).astype(bf16)
    up_grad = (hidden_grad * silu_gate).astype(bf16)
    slot_back = dot("necf,edf->necd", gate_grad, w_gate)
    slot_back = (slot_back + dot("necf,edf->necd", up_grad, w_up)).astype(bf16)
    grad_expert_down = dot("necf,necd->efd", gated, slot_grad)
    grad_expert_gate = dot("necd,necf->edf", slot_rows, gate_grad)
    grad_expert_up = dot("necd,necf->edf", slot_rows, up_grad)
    pick_flat = pick_low.reshape(cols, exp_local * capacity, toks)
    slot_out = slot_out.reshape(cols, exp_local * capacity, width)
    slot_back = slot_back.reshape(cols, exp_local * capacity, width)

    shared_pre = dot("ctd,dk->ctk", h2_all, shared_in_weights)
    sgate_pre, sup_pre = shared_pre[:, :, :shared_part], shared_pre[:, :, shared_part:]
    shared_silu, shared_slope = silu_parts(sgate_pre)
    shared_hidden = (shared_silu * sup_pre).astype(bf16)
    part_out = dot("cut,cud->ctd", pick_flat, slot_out) + dot(
        "ctk,dk->ctd", shared_hidden, shared_down
    )
    shared_hgrad = dot("ctd,dk->ctk", grad_all, shared_down)
    shared_grads = jnp.concatenate(
        [shared_hgrad * sup_pre * shared_slope, shared_hgrad * shared_silu], axis=2
    ).astype(bf16)
    part_back = dot("cut,cud->ctd", pick_flat, slot_back) + dot(
        "ctk,dk->ctd", shared_grads, shared_in_weights
    )
    token_dots = jnp.einsum(
        "ceu,ceut->cte", slot_dots, pick.astype(f32), precision=lax.Precision.HIGHEST
    )
    gate_dots = lax.psum(swap_col(token_dots), "row")
    gate_dots = jnp.swapaxes(gate_dots, 0, 1).reshape(toks, experts)

    shared_share = jnp.concatenate(
        [dot("ctd,ctk->dk", h2_all, shared_grads), dot("ctd,ctk->dk", grad_all, shared_hidden)],
        axis=1,
    ).astype(bf16)
    back_full = lax.all_gather(scatter_all(part_back.astype(bf16)), "row", axis=1, tiled=True)
    return (
        part_out.astype(bf16),
        back_full,
        gate_dots,
        shared_share,
        grad_expert_gate,
        grad_expert_up,
        grad_expert_down,
    )


def on_device(
    tokens,
    segments,
    routes,
    attn_gain,
    query_matrix,
    key_matrix,
    value_matrix,
    attention_output_matrix,
    mlp_gain,
    w_router,
    shared_gate_matrix,
    shared_up_matrix,
    shared_down_matrix,
    expert_gate,
    expert_up,
    expert_down,
    cotangent,
):
    local_len, seqs, width = tokens.shape
    cols = lax.axis_size("col")
    col_index = lax.axis_index("col")
    rows_w = query_matrix.shape[0]
    full_len = local_len * cols
    size = HEAD_DIM
    q_width = query_matrix.shape[1]
    kv_width = key_matrix.shape[1]
    kv_local = kv_width // size
    group = q_width // kv_width
    row_width = cotangent.shape[2]
    toks = local_len * seqs
    top = routes.shape[2]
    experts = w_router.shape[1]
    exp_local = expert_gate.shape[0]
    hidden_local = expert_gate.shape[2]
    capacity = max(2, toks * top * 4 // (3 * experts))
    shared_part = shared_gate_matrix.shape[1] // cols
    scale = 1.0 / math.sqrt(size)
    kernels = fits(cols, toks, width) and kv_local == 1 and exp_local == 2

    def seq_major(a):
        return jnp.swapaxes(a, 0, 1).reshape(toks, a.shape[2])

    misc = jnp.concatenate(
        [
            w_router,
            attn_gain[:, None],
            mlp_gain[:, None],
            jnp.zeros((rows_w, LANES - experts - 2), bf16),
        ],
        axis=1,
    )
    shared_weights = jnp.concatenate(
        [
            shared_gate_matrix.reshape(rows_w, cols, shared_part),
            shared_up_matrix.reshape(rows_w, cols, shared_part),
            shared_down_matrix.T.reshape(rows_w, cols, shared_part),
        ],
        axis=2,
    )
    shared_own = jnp.swapaxes(shared_weights, 0, 1)
    grad_own = seq_major(cotangent).astype(bf16)
    cosine, sine = rope_tables(col_index * local_len, local_len, size)
    cosine, sine = jnp.tile(cosine, (seqs, 1)), jnp.tile(sine, (seqs, 1))
    qkv_width = q_width + 2 * kv_width
    flat_routes = seq_major(routes)
    named = flat_routes[:, :, None] == jnp.arange(experts, dtype=jnp.int32)
    mask = jnp.any(named, axis=1)
    order = jnp.arange(toks, dtype=jnp.int32)
    upto = (order[None, :] <= order[:, None]).astype(bf16)
    rank = jnp.where(mask, dot("ij,je->ie", upto, mask.astype(bf16)), 0.0)

    doc = jnp.transpose(segments)
    def to_grid(flat):
        shaped = flat.reshape(seqs, local_len, kv_local, group, size)
        return shaped.transpose(0, 2, 3, 1, 4).reshape(seqs, kv_local, group * local_len, size)

    def from_grid(grid):
        shaped = grid.reshape(seqs, kv_local, group, local_len, size)
        return shaped.transpose(0, 3, 1, 2, 4).reshape(toks, q_width)

    token_rows = seq_major(tokens)
    x = token_rows.astype(f32)
    inv_first = rms_scale(x)
    base_first = x * inv_first
    if kernels:
        table_row = jnp.concatenate([rank.T, doc.reshape(1, toks).astype(f32)], axis=0)
        table_row = jnp.pad(table_row, ((0, -(experts + 1) % 8), (0, 0)))
        table_col = jnp.pad(rank, ((0, 0), (0, LANES - experts))).astype(bf16)
        (
            first_weights,
            out_weights,
            shared_weights,
            grad_all,
            rows_all,
            rank_all,
            h1,
            q_low,
            kv_all,
            probs,
            heads,
            attn,
            h2,
            gate,
            probs_router,
        ) = front_call(
            cols,
            0,
            experts,
            token_rows,
            query_matrix,
            key_matrix,
            value_matrix,
            misc,
            attention_output_matrix.T,
            shared_own,
            grad_own,
            table_row,
            table_col,
            doc.reshape(toks, 1).astype(f32),
            jnp.concatenate([cosine, cosine], axis=1),
            jnp.concatenate([-sine, sine], axis=1),
            seqs,
        )
        gate, probs_router = gate[:, :experts], probs_router[:, :experts]
    else:
        first_weights = jnp.concatenate([query_matrix, key_matrix, value_matrix, misc], axis=1)
        first_weights = gather_col(first_weights).reshape(width, -1)
        out_weights = gather_col(attention_output_matrix.T).reshape(width, q_width)
        shared_weights, grad_all = swap_col(shared_own), gather_all(grad_own)
        gain_one = first_weights[:, qkv_width + experts].astype(f32)
        h1 = (base_first * gain_one).astype(bf16)
        qkv = dot("tb,bk->tk", h1, first_weights[:, :qkv_width])
        qk = rotate(qkv[:, : q_width + kv_width], cosine, sine).astype(bf16)
        q_low = qk[:, :q_width]
        value_low = qkv[:, q_width + kv_width :].astype(bf16)
        side = jnp.concatenate(
            [
                rank.astype(bf16),
                doc.reshape(toks, 1).astype(bf16),
                jnp.zeros((toks, LANES - experts - 1), bf16),
            ],
            axis=1,
        )
        kv_all = gather_col(jnp.concatenate([qk[:, q_width:], value_low, side], axis=1))
        rank_all = kv_all[:, :, 2 * kv_width : 2 * kv_width + experts]
    shared_weights = shared_weights.reshape(width, 3 * shared_part)
    qkv_weights = first_weights[:, :qkv_width]
    router = first_weights[:, qkv_width : qkv_width + experts]
    gain_one = first_weights[:, qkv_width + experts].astype(f32)
    gain_two = first_weights[:, qkv_width + experts + 1].astype(f32)
    kv_seq = jnp.swapaxes(kv_all.reshape(cols, seqs, local_len, -1), 0, 1)
    kv_seq = kv_seq.reshape(seqs, full_len, -1)
    key_all = kv_seq[:, :, :kv_width].reshape(seqs, full_len, kv_local, size)
    value_all = kv_seq[:, :, kv_width : 2 * kv_width].reshape(seqs, full_len, kv_local, size)
    query_grid = to_grid(q_low)
    if kernels:
        probs = probs.reshape(seqs, kv_local, group * local_len, full_len)
    else:
        doc_all = kv_seq[:, :, 2 * kv_width + experts]
        place = col_index * local_len + jnp.arange(local_len, dtype=jnp.int32)
        same = doc.astype(bf16)[:, :, None] == doc_all[:, None, :]
        causal = jnp.arange(full_len, dtype=jnp.int32)[None, :] <= place[:, None]
        allowed = jnp.tile(same & causal[None], (1, group, 1))[:, None]
        scores = dot("shrd,skhd->shrk", query_grid, key_all) * scale
        scores = jnp.where(allowed, scores, masked_score)
        weights = jnp.exp(scores - jnp.max(scores, axis=-1, keepdims=True))
        weights = jnp.where(allowed, weights, 0.0)
        probs = (weights / jnp.sum(weights, axis=-1, keepdims=True)).astype(bf16)
        heads = from_grid(dot("shrk,skhd->shrd", probs, value_all)).astype(bf16)
        attn = lax.psum(dot("tk,bk->tb", heads, out_weights).astype(bf16), "row")
    middle = x + attn.astype(f32)

    inv_second = rms_scale(middle)
    base_second = middle * inv_second
    row_index = lax.axis_index("row")
    if not kernels:
        h2 = (base_second * gain_two).astype(bf16)
        probs_router = jax.nn.softmax(dot("td,de->te", h2, router), axis=-1)
    picked = jnp.where(mask, probs_router, 0.0)
    pick_total = jnp.sum(picked, axis=-1, keepdims=True)
    if not kernels:
        gate = picked / pick_total
    if kernels:
        rank_own = lax.dynamic_slice_in_dim(rank_all, col_index * exp_local, exp_local, 2)
        rank_own = rank_own.astype(f32)
        part_out, back_full, gate_dots, shared_share, *expert_grads = experts_kernels(
            cols,
            3,
            capacity,
            h2,
            grad_all,
            expert_gate,
            expert_up,
            expert_down,
            shared_weights,
            lax.dynamic_slice_in_dim(rows_all, col_index * exp_local, exp_local, 1),
            rank_own,
            gate.T,
        )
    else:
        part_out, back_full, gate_dots, shared_share, *expert_grads = experts_plain(
            h2,
            grad_all,
            expert_gate,
            expert_up,
            expert_down,
            shared_weights,
            router,
            rank_all,
            capacity,
            row_width,
        )
    back_full = back_full.astype(f32)
    shared_share = swap_col(shared_share.reshape(cols, rows_w, 3 * shared_part))
    shared_share = jnp.swapaxes(shared_share, 0, 1).astype(f32)
    share_sgate, share_sup, share_sdown = (
        shared_share[:, :, i * shared_part : (i + 1) * shared_part].reshape(rows_w, -1)
        for i in range(3)
    )

    pick_grad = gate_dots - jnp.sum(gate * gate_dots, axis=-1, keepdims=True)
    prob_grad = jnp.where(mask, pick_grad / pick_total, 0.0)
    logit_grad = probs_router * (
        prob_grad - jnp.sum(probs_router * prob_grad, axis=-1, keepdims=True)
    )
    logit_low = logit_grad.astype(bf16)
    grad_router = dot("td,te->de", h2, logit_low)

    back_full = back_full + dot("te,de->td", logit_low, router)
    grad_own = lax.dynamic_slice_in_dim(grad_all, col_index, 1, 0)[0].astype(f32)
    grad_gain_two = jnp.sum(back_full * base_second, axis=0)
    scaled_two = back_full * gain_two
    middle_grad = (
        inv_second
        * (scaled_two - base_second * jnp.mean(scaled_two * base_second, axis=-1, keepdims=True))
        + grad_own
    )
    attn_grad = middle_grad.astype(bf16)
    grad_out = dot("td,tk->dk", attn_grad, heads).astype(bf16)

    heads_grad = to_grid(dot("td,dk->tk", attn_grad, out_weights).astype(bf16))
    value_grad = dot("shrk,shrd->skhd", probs, heads_grad)
    weight_grad = dot("shrd,skhd->shrk", heads_grad, value_all)
    probs_wide = probs.astype(f32)
    delta = jnp.sum(probs_wide * weight_grad, axis=-1, keepdims=True)
    score_grad = (probs_wide * (weight_grad - delta)).astype(bf16)
    query_grad = from_grid(dot("shrk,skhd->shrd", score_grad, key_all)) * scale
    key_grad = dot("shrk,shrd->skhd", score_grad, query_grid) * scale
    kv_grad = jnp.concatenate(
        [key_grad.reshape(seqs, full_len, kv_width), value_grad.reshape(seqs, full_len, kv_width)],
        axis=2,
    ).astype(bf16)
    kv_grad = jnp.swapaxes(kv_grad.reshape(seqs, cols, local_len, 2 * kv_width), 0, 1)
    (kv_share,) = scatter_parts(
        kernels, cols, 6, ("col", 4, kv_grad.reshape(cols, toks, 2 * kv_width))
    )
    qk_grad = rotate(
        jnp.concatenate([query_grad, kv_share[:, :kv_width]], axis=1), cosine, -sine
    )
    qkv_grad = jnp.concatenate([qk_grad, kv_share[:, kv_width:]], axis=1).astype(bf16)
    first_grad = dot("tk,bk->tb", qkv_grad, qkv_weights).astype(bf16)
    first_grad = sum_row(kernels, 7, first_grad).astype(f32)
    grad_gain_one = jnp.sum(first_grad * base_first, axis=0)
    scaled_one = first_grad * gain_one
    token_grad = (
        inv_first
        * (scaled_one - base_first * jnp.mean(scaled_one * base_first, axis=-1, keepdims=True))
        + middle_grad
    )
    grad_first = jnp.concatenate(
        [
            dot("tb,tk->bk", h1, qkv_grad),
            grad_router,
            grad_gain_one[:, None],
            grad_gain_two[:, None],
            jnp.zeros((width, LANES - experts - 2), f32),
        ],
        axis=1,
    ).astype(bf16)
    out_slice, share_out, share_first = scatter_parts(
        kernels,
        cols,
        8,
        ("all", 4, part_out),
        ("col", 4, grad_out.reshape(cols, rows_w, q_width)),
        ("col", 5, grad_first.reshape(cols, rows_w, -1)),
    )
    middle_slice = lax.dynamic_slice_in_dim(middle, row_index * row_width, row_width, 1)
    block_out = (middle_slice + out_slice).astype(bf16)

    def tokens_first(a):
        return jnp.swapaxes(a.reshape(seqs, local_len, a.shape[1]), 0, 1)

    return (
        tokens_first(block_out),
        tokens_first(token_grad),
        share_first[:, qkv_width + experts],
        share_first[:, :q_width],
        share_first[:, q_width : q_width + kv_width],
        share_first[:, q_width + kv_width : qkv_width],
        share_out.T,
        share_first[:, qkv_width + experts + 1],
        share_first[:, qkv_width : qkv_width + experts],
        share_sgate,
        share_sup,
        share_sdown.T,
        *expert_grads,
    )


def solution(mesh):
    in_specs = (
        P("col", None, None),
        P("col", None),
        P("col", None, None),
        P("col"),
        P("col", "row"),
        P("col", "row"),
        P("col", "row"),
        P("row", "col"),
        P("col"),
        P("col", None),
        P("col", "row"),
        P("col", "row"),
        P("row", "col"),
        P("col", None, "row"),
        P("col", None, "row"),
        P("col", "row", None),
        P("col", None, "row"),
    )
    out_specs = (
        P("col", None, "row"),
        P("col", None, None),
        P("col"),
        P("col", "row"),
        P("col", "row"),
        P("col", "row"),
        P("row", "col"),
        P("col"),
        P("col", None),
        P("col", "row"),
        P("col", "row"),
        P("row", "col"),
        P("col", None, "row"),
        P("col", None, "row"),
        P("col", "row", None),
    )
    return jax.shard_map(
        on_device, mesh=mesh, in_specs=in_specs, out_specs=out_specs, check_vma=False
    )
```

```python
import functools
import math

import jax
import jax.numpy as jnp
from jax import lax
from jax.experimental import pallas as pl
from jax.experimental.pallas import tpu as pltpu
from jax.sharding import PartitionSpec as P

HEAD_DIM = 128
LANES = 128


norm_eps = 1e-05
rope_base = 500000.0
masked_score = -1e30

f32 = jnp.float32
bf16 = jnp.bfloat16
MESH = pl.DeviceIdType.MESH


def dot(form, left, right):
    return jnp.einsum(form, left, right, preferred_element_type=f32)


def rope_tables(start_place, local_len, head_size):
    places = (start_place + jnp.arange(local_len, dtype=jnp.int32)).astype(f32)
    frequency = jnp.power(
        rope_base, -jnp.arange(0, head_size, 2, dtype=jnp.int32).astype(f32) / head_size
    )
    angles = places[:, None] * frequency[None, :]
    return (jnp.cos(angles), jnp.sin(angles))


def rotate(field, cosine, sine):
    half = cosine.shape[1]
    parts = []
    for start in range(0, field.shape[1], 2 * half):
        front = field[:, start : start + half]
        back = field[:, start + half : start + 2 * half]
        parts.append(front * cosine - back * sine)
        parts.append(back * cosine + front * sine)
    return jnp.concatenate(parts, axis=1)


def rms_scale(values_in):
    return lax.rsqrt(jnp.mean(values_in * values_in, axis=-1, keepdims=True) + norm_eps)


def silu_parts(pre_gate):
    sigmoid_gate = jax.nn.sigmoid(pre_gate)
    silu_gate = pre_gate * sigmoid_gate
    slope_gate = sigmoid_gate * (1.0 + pre_gate * (1.0 - sigmoid_gate))
    return (silu_gate, slope_gate)


def gather_col(part):
    return lax.all_gather(part, "col", axis=0, tiled=False)


def scatter_col(blocks):
    flat = blocks.reshape(-1, blocks.shape[-1])
    return lax.psum_scatter(flat, "col", scatter_dimension=0, tiled=True)


def gather_all(part):
    got = lax.all_gather(part, ("col", "row"), axis=0, tiled=False)
    cols, rows = lax.axis_size("col"), lax.axis_size("row")
    got = got.reshape(cols, rows, *part.shape).transpose(0, 2, 1, 3)
    return got.reshape(cols, part.shape[0], rows * part.shape[1])


def scatter_all(blocks):
    flat = blocks.reshape(-1, blocks.shape[-1])
    part = lax.psum_scatter(flat, "row", scatter_dimension=1, tiled=True)
    return lax.psum_scatter(part, "col", scatter_dimension=0, tiled=True)


def swap_col(blocks):
    return lax.all_to_all(blocks, "col", split_axis=0, concat_axis=0, tiled=True)


class Net:
    def __init__(self, cols, send_sems, recv_sems):
        self.send_sems, self.recv_sems, self.used, self.sent = send_sems, recv_sems, 0, []
        self.cols, self.high_count = cols, cols // 2
        self.me = lax.axis_index("col")
        self.high, self.low = self.me // 2, self.me % 2
        self.row = lax.axis_index("row")
        self.outer, self.core = self.row // 2, self.row % 2

    def block(self, step, other=False):
        high = lax.rem(self.high + self.high_count - step, self.high_count)
        return 2 * high + (1 - self.low if other else self.low)

    def block_ahead(self, step, other=False):
        high = lax.rem(self.high + step, self.high_count)
        return 2 * high + (1 - self.low if other else self.low)

    def z_peer(self, step):
        return {"col": self.block_ahead(step)}

    def y_peer(self):
        return {"col": 2 * self.high + 1 - self.low}

    def x_peer(self):
        return {"row": 2 * (1 - self.outer) + self.core}

    def core_peer(self):
        return {"row": 2 * self.outer + 1 - self.core}

    def col_peer(self, step):
        return {"col": lax.rem(self.me + step, self.cols)}

    def greet(self, peers):
        barrier = pltpu.get_barrier_semaphore()
        for peer in peers:
            pl.semaphore_signal(barrier, inc=1, device_id=peer, device_id_type=MESH)
        pl.semaphore_wait(barrier, len(peers))

    def send(self, source, target, peer):
        copy = pltpu.make_async_remote_copy(
            src_ref=source,
            dst_ref=target,
            send_sem=self.send_sems.at[self.used],
            recv_sem=self.recv_sems.at[self.used],
            device_id=peer,
            device_id_type=MESH,
        )
        self.used += 1
        copy.start()
        self.sent.append(copy)
        return copy

    def left(self, copy):
        copy.wait_send()
        self.sent = [other for other in self.sent if other is not copy]

    def finish(self):
        for copy in self.sent:
            copy.wait_send()


def col_peers(net):
    return [net.z_peer(step) for step in range(1, net.high_count)] + [net.y_peer()]


def row_peers(net):
    return [net.x_peer(), net.core_peer()]


def add_rows(target, terms):
    rows = target.shape[0]
    piece = 32 if rows % 32 == 0 else 16

    def body(index, carry):
        at = pl.ds(pl.multiple_of(index * piece, piece), piece)
        total = terms[0][at, :].astype(f32)
        for term in terms[1:]:
            total = total + term[at, :].astype(f32)
        target[at, :] = total.astype(target.dtype)
        return carry

    lax.fori_loop(0, rows // piece, body, 0)


def dot_nn(left, right):
    return lax.dot_general(left, right, (((1,), (0,)), ((), ())), preferred_element_type=f32)


def dot_nt(left, right):
    return lax.dot_general(left, right, (((1,), (1,)), ((), ())), preferred_element_type=f32)


def dot_tn(left, right):
    return lax.dot_general(left, right, (((0,), (0,)), ((), ())), preferred_element_type=f32)


def each_tile(count, body):
    def step(index, carry):
        body(index)
        return carry

    lax.fori_loop(0, count, step, 0)


TILE = 512


def tile_at(index, tile=TILE):
    if isinstance(index, int):
        return pl.ds(index * tile, tile)
    return pl.ds(pl.multiple_of(index * tile, tile), tile)


class Line:
    def __init__(self, net, items, direct=(), direct_from=0):
        self.net, self.items, self.direct, self.direct_from = net, items, list(direct), direct_from
        self.other_row = 2 * (1 - net.outer) + net.core
        self.along_z, self.along_y, self.along_x, self.to_core = {}, {}, {}, {}
        self.moved = []
        self.now = 0

    def in_chip(self, q, step, other, source, slot):
        if self.items[q][2]:
            self.along_x[q, step, other] = self.net.send(source, slot, self.net.x_peer())
            self.to_core[q, step, other] = self.net.send(source, slot, self.net.core_peer())

    def start(self, q):
        net = self.net
        source, slot_of, _ = self.items[q]
        slot = slot_of(net.me, net.row)
        for step in reversed(range(1, net.high_count)):
            self.along_z[q, step] = net.send(source, slot, net.z_peer(step))
        self.along_y[q, 0] = net.send(source, slot, net.y_peer())
        self.in_chip(q, 0, False, source, slot)

    def after_z(self, q):
        net = self.net
        for step in reversed(range(1, net.high_count)):
            self.along_z[q, step].wait_recv()
            slot = self.items[q][1](net.block(step), net.row)
            self.along_y[q, step] = net.send(slot, slot, net.y_peer())
            self.in_chip(q, step, False, slot, slot)

    def after_y(self, q):
        net = self.net
        for step in range(net.high_count):
            self.along_y[q, step].wait_recv()
            slot = self.items[q][1](net.block(step, True), net.row)
            self.in_chip(q, step, True, slot, slot)

    def after_x(self, q):
        net = self.net
        if self.items[q][2]:
            for other in (False, True):
                for step in range(net.high_count):
                    self.along_x[q, step, other].wait_recv()
                    slot = self.items[q][1](net.block(step, other), self.other_row)
                    self.moved.append(net.send(slot, slot, net.core_peer()))

    def tick(self, count=1):
        net = self.net
        for _ in range(count):
            now, self.now = self.now, self.now + 1
            if now < len(self.items):
                if now >= 2:
                    for step in range(1, net.high_count):
                        net.left(self.along_z[now - 2, step])
                self.start(now)
            if now >= self.direct_from and self.direct:
                self.moved.append(net.send(*self.direct.pop(0)))
            for stage, lag in ((self.after_z, 1), (self.after_y, 2), (self.after_x, 3)):
                if 0 <= now - lag < len(self.items):
                    stage(now - lag)

    def drain(self):
        while self.now < len(self.items) + 3 or self.direct:
            self.tick()
        for copy in [*self.moved, *self.to_core.values()]:
            copy.wait_recv()


def front_kernel(
    cols,
    experts,
    tokens,
    query,
    key,
    value,
    misc,
    out_own,
    shared_own,
    grad_own,
    table_row,
    table_col,
    doc_col,
    cosine,
    sine,
    weights,
    out_weights,
    shared_all,
    grad_all,
    rows_all,
    cols_all,
    h1,
    q_low,
    kv_all,
    probs,
    heads,
    attn,
    h2,
    gate,
    router_probs,
    gains,
    inverse,
    kv_low,
    keys,
    values,
    bias,
    partial,
    from_core,
    to_x,
    from_x,
    send_sems,
    recv_sems,
    local_sems,
):
    net = Net(cols, send_sems, recv_sems)
    toks, width = tokens.shape
    size = HEAD_DIM
    q_width = q_low.shape[1]
    group = q_width // size
    rows_w = query.shape[0]
    seqs = probs.shape[0]
    local_len = toks // seqs
    full_len = local_len * cols
    scale = 1.0 / math.sqrt(size)
    mine = pl.ds(pl.multiple_of(net.me * rows_w, 16), rows_w)

    copies = []

    def local_copy(source, target):
        copy = pltpu.make_async_copy(source, target, local_sems.at[len(copies)])
        copy.start()
        copies.append(copy)

    local_copy(query, weights.at[mine, pl.ds(0, q_width)])
    local_copy(key, weights.at[mine, pl.ds(q_width, size)])
    local_copy(value, weights.at[mine, pl.ds(q_width + size, size)])
    local_copy(misc, weights.at[mine, pl.ds(q_width + 2 * size, LANES)])
    first = len(copies)
    local_copy(out_own, out_weights.at[mine])
    local_copy(shared_own.at[net.me], shared_all.at[net.me])
    part = grad_own.shape[1]
    local_copy(
        grad_own, grad_all.at[net.me, :, pl.ds(pl.multiple_of(net.row * part, LANES), part)]
    )
    local_copy(table_row, rows_all.at[net.me])
    local_copy(table_col, cols_all.at[net.me])
    net.greet([net.col_peer(step) for step in range(1, cols)] + row_peers(net))
    for copy in copies[:first]:
        copy.wait()

    def weight_slot(target, start, count):
        def slot(block, row):
            return target.at[pl.ds(pl.multiple_of(block * rows_w + start, 16), count)]

        return slot

    def grad_slot(start, count):
        def slot(block, row):
            return grad_all.at[
                block, pl.ds(start, count), pl.ds(pl.multiple_of(row * part, LANES), part)
            ]

        return slot

    items = [(table_row, lambda block, row: rows_all.at[block], False)]
    pieces, out_pieces, grad_pieces = 5, 4, 4
    count = rows_w // pieces
    for q in range(pieces):
        slot = weight_slot(weights, q * count, count)
        items.append((slot(net.me, net.row), slot, False))
    ready_weights = len(items) + 2
    out_items, grad_items = [], []
    count = rows_w // out_pieces
    for q in range(out_pieces):
        slot = weight_slot(out_weights, q * count, count)
        out_items.append((out_own.at[pl.ds(q * count, count)], slot, False))
    count = toks // grad_pieces
    for q in range(grad_pieces):
        grad_items.append((grad_own.at[pl.ds(q * count, count)], grad_slot(q * count, count), True))
    items += out_items[:2]
    for q in range(2, out_pieces):
        items += [grad_items[q - 2], out_items[q]]
    ready_out = len(items) + 2
    items += grad_items[out_pieces - 2 :]
    items.append((table_col, lambda block, row: cols_all.at[block], False))
    direct = []
    for step in range(1, cols):
        block = lax.rem(net.me + step, cols)
        direct.append((shared_own.at[block], shared_all.at[net.me], net.col_peer(step)))
    line = Line(net, items, direct, ready_weights - 2)

    line.tick(2)
    copies[first + 3].wait()

    def chunks(body, rows=32):
        def step(index, carry):
            body(pl.ds(pl.multiple_of(index * rows, rows), rows))
            return carry

        lax.fori_loop(0, toks // rows, step, 0)

    def measure_first(at):
        x = tokens[at, :].astype(f32)
        total = jnp.sum(x * x, axis=1, keepdims=True)
        inverse[at, :] = jnp.broadcast_to(lax.rsqrt(total / width + norm_eps), (32, LANES))

    chunks(measure_first)
    line.tick(ready_weights - line.now)

    start = q_width + 2 * size
    for tile in range(width // TILE):
        at = pl.ds(tile * TILE, TILE)
        turned = jnp.transpose(weights[at, start : start + LANES].astype(f32))
        gains[:, at] = turned[experts : experts + 8]

    def norm_first(at):
        x = tokens[at, :].astype(f32) * inverse[at, 0:1]
        h1[at, :] = (x * gains[0:1, :]).astype(bf16)

    chunks(norm_first)
    line.tick()
    heads_all = group + 2
    for head in range(heads_all - 1, -1, -1):
        raw = dot_nn(h1[...], weights[:, head * size : (head + 1) * size])
        if head <= group:
            raw = raw * cosine[...] + pltpu.roll(raw, size // 2, 1) * sine[...]
        if head < group:
            q_low[:, head * size : (head + 1) * size] = raw.astype(bf16)
        else:
            kv_low[:, (head - group) * size : (head - group + 1) * size] = raw.astype(bf16)
        if head == group:
            kv_all[net.me] = kv_low[...]

            def kv_slot(s):
                rows = pl.ds(s * local_len, local_len)
                return lambda block, row: kv_all.at[block, rows]

            kv_line = Line(
                net,
                [
                    (kv_low.at[pl.ds(s * local_len, local_len)], kv_slot(s), False)
                    for s in range(seqs)
                ],
            )
            kv_line.tick()
        if head == group // 2:
            kv_line.tick()
    line.tick()
    kv_line.tick()

    for s in range(seqs):
        if s:
            kv_line.tick()
        rows = pl.ds(s * local_len, local_len)
        place = lax.broadcasted_iota(jnp.int32, (local_len, local_len), 0)
        lane = lax.broadcasted_iota(jnp.int32, (local_len, local_len), 1)
        for c in range(cols):
            at = pl.ds(c * local_len, local_len)
            keys[at, :] = kv_all[c, rows, :size]
            values[at, :] = kv_all[c, rows, size:]
            same = doc_col[rows, :] == rows_all[c, experts : experts + 1, rows]
            ahead = (c - net.me) * local_len
            allowed = same & (lane + ahead <= place)
            bias[:, at] = jnp.where(allowed, 0.0, masked_score)

        def attend(g, carry, s=s, rows=rows):
            at = pl.ds(pl.multiple_of(g * size, size), size)
            scores = dot_nt(q_low[rows, at], keys[...]) * scale + bias[...]
            weight = jnp.exp(scores - jnp.max(scores, axis=1, keepdims=True))
            p = (weight / jnp.sum(weight, axis=1, keepdims=True)).astype(bf16)
            probs[s, g] = p
            heads[rows, at] = dot_nn(p, values[...]).astype(bf16)
            return carry

        lax.fori_loop(0, group, attend, 0)
        if line.now < ready_out:
            line.tick()
    line.tick(max(0, ready_out - line.now))
    copies[first].wait()

    pieces = from_core.shape[0]
    piece_rows = from_core.shape[1]

    def row_piece(core, i):
        return pl.ds(
            pl.multiple_of((core * pieces + i) * piece_rows, piece_rows), piece_rows
        )

    half = pieces * piece_rows
    across = []
    for core in (1 - net.core, net.core):
        at_rows = pl.ds(pl.multiple_of(core * half, half), half)
        for tile in range(width // TILE):
            at = pl.ds(tile * TILE, TILE)
            partial[at_rows, at] = dot_nt(heads[at_rows, :], out_weights[at, :]).astype(bf16)
        if not across:
            across = [
                net.send(partial.at[row_piece(1 - net.core, i)], from_core.at[i], net.core_peer())
                for i in range(pieces)
            ]
    along, back = [], []
    for i in range(pieces):
        across[i].wait_recv()
        add_rows(to_x.at[i], [partial.at[row_piece(net.core, i)], from_core.at[i]])
        along.append(net.send(to_x.at[i], from_x.at[i], net.x_peer()))
    line.tick()
    for i in range(pieces):
        along[i].wait_recv()
        at = row_piece(net.core, i)
        add_rows(attn.at[at], [to_x.at[i], from_x.at[i]])
        back.append(net.send(attn.at[at], attn.at[at], net.core_peer()))
    line.tick()
    for copy in back:
        copy.wait_recv()

    def norm_second(at):
        x = tokens[at, :].astype(f32) + attn[at, :].astype(f32)
        total = jnp.sum(x * x, axis=1, keepdims=True)
        h2[at, :] = (x * lax.rsqrt(total / width + norm_eps) * gains[1:2, :]).astype(bf16)

    chunks(norm_second)
    line.tick()
    logits = dot_nn(h2[...], weights[:, start : start + LANES])
    lane = lax.broadcasted_iota(jnp.int32, (toks, LANES), 1)
    logits = jnp.where(lane < experts, logits, masked_score)
    weight = jnp.exp(logits - jnp.max(logits, axis=1, keepdims=True))
    chance = weight / jnp.sum(weight, axis=1, keepdims=True)
    router_probs[...] = chance
    picked = jnp.where((table_col[...] > 0) & (lane < experts), chance, 0.0)
    gate[...] = picked / jnp.sum(picked, axis=1, keepdims=True)
    line.drain()
    kv_line.drain()
    for copy in [*copies[first + 1 : first + 3], copies[first + 4]]:
        copy.wait()
    net.finish()


def front_call(
    cols, collective_id, experts, tokens, query, key, value, misc, out_own, shared_own, grad_own,
    table_row, table_col, doc_col, cosine, sine, seqs,
):
    toks, width = tokens.shape
    q_width = query.shape[1]
    size = HEAD_DIM
    local_len = toks // seqs
    vmem, any_space = pl.BlockSpec(memory_space=pltpu.VMEM), pl.BlockSpec(memory_space=pl.ANY)

    def shape(*dims, dtype=bf16):
        return jax.ShapeDtypeStruct(dims, dtype)

    pieces = 4
    piece = (pieces, toks // 2 // pieces, width)
    copies = 320
    return pl.pallas_call(
        functools.partial(front_kernel, cols, experts),
        out_shape=[
            shape(width, q_width + 2 * size + LANES),
            shape(width, q_width),
            shape(*shared_own.shape),
            shape(cols, toks, width),
            shape(cols, *table_row.shape, dtype=f32),
            shape(cols, *table_col.shape),
            shape(toks, width),
            shape(toks, q_width),
            shape(cols, toks, 2 * size),
            shape(seqs, q_width // size, local_len, cols * local_len),
            shape(toks, q_width),
            shape(toks, width),
            shape(toks, width),
            shape(toks, LANES, dtype=f32),
            shape(toks, LANES, dtype=f32),
        ],
        in_specs=[vmem] + [any_space] * 7 + [vmem] * 5,
        out_specs=[vmem, vmem, any_space, any_space] + [vmem] * 11,
        scratch_shapes=[
            pltpu.VMEM((8, width), f32),
            pltpu.VMEM((toks, LANES), f32),
            pltpu.VMEM((toks, 2 * size), bf16),
            pltpu.VMEM((cols * local_len, size), bf16),
            pltpu.VMEM((cols * local_len, size), bf16),
            pltpu.VMEM((local_len, cols * local_len), f32),
            pltpu.VMEM((toks, width), bf16),
            pltpu.VMEM(piece, bf16),
            pltpu.VMEM(piece, bf16),
            pltpu.VMEM(piece, bf16),
            pltpu.SemaphoreType.DMA((copies,)),
            pltpu.SemaphoreType.DMA((copies,)),
            pltpu.SemaphoreType.DMA((16,)),
        ],
        compiler_params=pltpu.CompilerParams(
            collective_id=collective_id, has_side_effects=True, vmem_limit_bytes=48 << 20
        ),
        name=f"front_{collective_id}",
    )(
        tokens, query, key, value, misc, out_own, shared_own, grad_own,
        table_row, table_col, doc_col, cosine, sine,
    )


def experts_kernel(
    cols,
    capacity,
    h2,
    grads,
    w_gate,
    w_up,
    w_down,
    w_shared,
    rank_row,
    rank_col,
    gate_own,
    out_part,
    back,
    g_gate,
    g_up,
    g_down,
    g_shared,
    gate_dots,
    h2_all,
    xs_all,
    cs_all,
    wgu,
    wd,
    ws,
    gates,
    hb,
    xbuf,
    ybuf,
    obuf,
    part,
    pre,
    gcol,
    dcol,
    dz_all,
    zg_all,
    dgu_all,
    sdz_all,
    sz_all,
    sgu_all,
    from_core,
    from_x,
    from_y,
    from_z,
    kept,
    dots,
    dots_core,
    dots_x,
    tiles,
    tiles_all,
    stage,
    stage_low,
    send_sems,
    recv_sems,
    local_sems,
):
    net = Net(cols, send_sems, recv_sems)
    toks, width = h2.shape
    exp_local, _, hidden = w_gate.shape
    high = net.high_count
    pad = ws.shape[1] // 3
    slots = exp_local * capacity
    pair = 2 * capacity
    piece = width // lax.axis_size("row")
    share = width // LANES // 5 * LANES
    rest = (width - 4 * share) // 2
    wide = width // TILE
    net.greet([net.col_peer(step) for step in range(1, cols)] + row_peers(net))

    def local_copy(source, target, index):
        copy = pltpu.make_async_copy(source, target, local_sems.at[index])
        copy.start()
        return copy

    gate_copies = [
        net.send(gate_own, gates.at[net.me], net.col_peer(step)) for step in range(1, cols)
    ]
    gates[net.me] = gate_own[...]

    def feature_e(row):
        return pl.ds(pl.multiple_of(row * share, LANES), share)

    def feature_r(core):
        return pl.ds(pl.multiple_of(4 * share + core * rest, LANES), rest)

    own_e, own_r = feature_e(net.row), feature_r(net.core)
    far_e = feature_e(2 * (1 - net.outer) + net.core)

    def pass_on(source, block, features, peer):
        return net.send(source.at[..., features], h2_all.at[block, :, features], peer)

    along_z, along_y, along_x, to_core = {}, {}, {}, {}
    for step in range(high - 1, 0, -1):
        along_z[high - step] = [
            pass_on(h2, net.me, own_e, net.z_peer(step)),
            pass_on(h2, net.me, own_r, net.z_peer(step)),
        ]
    along_y[0] = [
        pass_on(h2, net.me, own_e, net.y_peer()),
        pass_on(h2, net.me, own_r, net.y_peer()),
    ]

    def block_of(step, other):
        return net.block_ahead(step, other)

    def share_in_chip(step, other):
        block = block_of(step, other)
        source = h2_all.at[block]
        along_x[step, other] = pass_on(source, block, own_e, net.x_peer())
        to_core[step, other] = [
            pass_on(source, block, own_e, net.core_peer()),
            pass_on(source, block, own_r, net.core_peer()),
        ]

    def arrived_y(step):
        for copy in along_y[step]:
            copy.wait_recv()
        share_in_chip(step, True)

    def arrived_z(step):
        for copy in along_z[step]:
            copy.wait_recv()
        block = block_of(step, False)
        along_y[step] = [
            pass_on(h2_all.at[block], block, own_e, net.y_peer()),
            pass_on(h2_all.at[block], block, own_r, net.y_peer()),
        ]
        share_in_chip(step, False)

    def arrived_x(step, other):
        along_x[step, other].wait_recv()
        block = block_of(step, other)
        to_core[step, other].append(pass_on(h2_all.at[block], block, far_e, net.core_peer()))

    def whole(step, other):
        for copy in to_core[step, other]:
            copy.wait_recv()

    events = [functools.partial(arrived_y, 0)]
    for step in range(1, high):
        events.append(functools.partial(arrived_z, step))
        events.append(functools.partial(arrived_x, step - 1, True))
        events.append(functools.partial(arrived_y, step))
        events.append(functools.partial(arrived_x, step, False))
    events.append(functools.partial(arrived_x, high - 1, True))
    events = iter(events)

    def pump(count=1):
        for _ in range(count):
            event = next(events, None)
            if event is not None:
                event()

    loads = []
    for e in range(exp_local):
        loads.append(local_copy(w_down.at[e], wd.at[e], 3 * e))
        loads.append(local_copy(w_gate.at[e], wgu.at[e, :, pl.ds(0, hidden)], 3 * e + 1))
        loads.append(local_copy(w_up.at[e], wgu.at[e, :, pl.ds(hidden, hidden)], 3 * e + 2))
    base = 3 * exp_local
    loads.append(local_copy(w_shared, ws, base))
    keep_own = local_copy(h2, h2_all.at[net.me], base + 1)
    base += 2

    def load_pair(source, step):
        first = local_copy(source.at[block_of(step, False)], hb.at[0], base)
        second = local_copy(source.at[block_of(step, True)], hb.at[1], base + 1)
        first.wait()
        second.wait()

    slot_row = lax.broadcasted_iota(jnp.int32, (capacity, toks), 0).astype(f32) + 1.0
    slot_lane = lax.broadcasted_iota(jnp.int32, (toks, capacity), 1).astype(f32) + 1.0

    def chosen(block, e):
        return rank_row[block, e : e + 1, :] == slot_row

    def picks(block):
        rows = [
            jnp.where(chosen(block, e), 1.0, 0.0).astype(bf16) for e in range(exp_local)
        ]
        return jnp.concatenate(rows, axis=0)

    def picks_back(block):
        lanes = [
            jnp.where(rank_col[block, :, e : e + 1] == slot_lane, 1.0, 0.0).astype(bf16)
            for e in range(exp_local)
        ]
        return jnp.concatenate(lanes, axis=1)

    def dispatch(step):
        for b in (0, 1):
            table = picks(block_of(step, b == 1))

            def tile(index, b=b, table=table):
                at = tile_at(index)
                rows = dot_nn(table, hb[b, :, at]).astype(bf16)
                for e in range(exp_local):
                    xbuf[e, pl.ds(b * capacity, capacity), at] = rows[
                        e * capacity : (e + 1) * capacity
                    ]

            each_tile(wide, tile)

    def save_rows(target, step):
        return [
            local_copy(
                xbuf.at[e], target.at[e, pl.ds(step * pair, pair)], base + 2 + e
            )
            for e in range(exp_local)
        ]

    saved = []
    for step in range(high):
        load_pair(grads, step)
        if step == 0:
            for copy in loads:
                copy.wait()
        for copy in saved:
            copy.wait()
        dispatch(step)
        saved = save_rows(cs_all, step)
        for e in range(exp_local):
            dz_all[e, pl.ds(step * pair, pair), :] = dot_nt(xbuf[e], wd[e]).astype(bf16)
        for b in (0, 1):
            sdz_all[block_of(step, b == 1)] = dot_nn(hb[b], ws[:, 2 * pad :]).astype(bf16)
        pump()
    for copy in gate_copies:
        copy.wait_recv()
    keep_own.wait()

    across, onward, upward, far_z = {}, {}, {}, {}

    def features(row):
        return pl.ds(pl.multiple_of(row * piece, LANES), piece)

    other_row = 2 * (1 - net.outer) + net.core

    def hand_over(step):
        for b in (1, 0):
            for far in (1, 0):
                outer = 1 - net.outer if far else net.outer
                source = part.at[b, :, features(2 * outer + 1 - net.core)]
                across[step, b, far] = net.send(
                    source, from_core.at[far, step, b], net.core_peer()
                )

    def sum_cores(step):
        for b in (1, 0):
            for far, row in ((1, other_row), (0, net.row)):
                across[step, b, far].wait_recv()
                slot = from_core.at[far, step, b]
                add_rows(slot, [part.at[b, :, features(row)], slot])
                if far:
                    onward[step, b] = net.send(slot, from_x.at[step, b], net.x_peer())
        for b in (1, 0):
            for far in (1, 0):
                net.left(across[step, b, far])

    def sum_chips(step):
        for b in (1, 0):
            onward[step, b].wait_recv()
            slot = from_core.at[0, step, b]
            add_rows(slot, [slot, from_x.at[step, b]])
            if b:
                upward[step] = net.send(slot, from_y.at[step], net.y_peer())

    def sum_plane(step):
        upward[step].wait_recv()
        slot = from_core.at[0, step, 0]
        add_rows(slot, [slot, from_y.at[step]])
        if step:
            far_z[step] = net.send(slot, from_z.at[step - 1], net.z_peer(step))

    own_expert = lax.rem(net.me, cols) * exp_local
    gate_rows = gates.shape[1]
    gate_row = lax.broadcasted_iota(jnp.int32, (gate_rows, toks), 0)
    dots[...] = jnp.zeros_like(dots)
    for step in range(high):
        if step:
            whole(step, False)
        whole(step, True)
        load_pair(h2_all, step)
        for copy in saved:
            copy.wait()
        dispatch(step)
        saved = save_rows(xs_all, step)
        pump()
        for b in (0, 1):
            block = block_of(step, b == 1)
            inner = dot_nn(hb[b], ws[:, : 2 * pad])
            sa, su = inner[:, :pad], inner[:, pad:]
            sig = 1.0 / (1.0 + jnp.exp(-sa))
            silu = sa * sig
            slope = sig * (1.0 + sa * (1.0 - sig))
            sz_all[block] = (silu * su).astype(bf16)
            sdz = sdz_all[block].astype(f32)
            sgu_all[block, :, :pad] = (sdz * su * slope).astype(bf16)
            sgu_all[block, :, pad:] = (sdz * silu).astype(bf16)
        if step:
            sum_cores(step - 1)
        rows = pl.ds(step * pair, pair)
        for e in range(exp_local):

            def inner_tile(index, e=e):
                at = tile_at(index, 256)
                pre[:, at] = dot_nn(xbuf[e], wgu[e, :, at])

            each_tile(2 * hidden // 256, inner_tile)
            for b in (0, 1):
                block = block_of(step, b == 1)
                gate = jnp.sum(
                    jnp.where(gate_row == own_expert + e, gates[block], 0.0), axis=0, keepdims=True
                )
                gate = jnp.sum(jnp.where(chosen(block, e), gate, 0.0), axis=1, keepdims=True)
                gcol[pl.ds(b * capacity, capacity), :] = jnp.broadcast_to(gate, (capacity, LANES))

            def gating(index, e=e, step=step):
                at = pl.ds(pl.multiple_of(index * 32, 32), 32)
                saved_at = pl.ds(pl.multiple_of(step * pair + index * 32, 32), 32)
                a, u = pre[at, :hidden], pre[at, hidden:]
                gate = jnp.concatenate([gcol[at, :]] * (hidden // LANES), axis=1)
                dz = dz_all[e, saved_at, :].astype(f32)
                sig = 1.0 / (1.0 + jnp.exp(-a))
                silu = a * sig
                slope = sig * (1.0 + a * (1.0 - sig))
                z = silu * u
                dcol[at, :] = jnp.broadcast_to(
                    jnp.sum(z * dz, axis=1, keepdims=True), (32, LANES)
                )
                zg_all[e, saved_at, :] = (z * gate).astype(bf16)
                dz = dz * gate
                dgu_all[e, saved_at, :hidden] = (dz * u * slope).astype(bf16)
                dgu_all[e, saved_at, hidden:] = (dz * silu).astype(bf16)

            each_tile(pair // 32, gating)
            for b in (0, 1):
                block = block_of(step, b == 1)
                col = dcol[pl.ds(b * capacity, capacity), :]
                col = jnp.concatenate([col] * (toks // LANES), axis=1)
                dots[block, e : e + 1, :] = jnp.sum(
                    jnp.where(chosen(block, e), col, 0.0), axis=0, keepdims=True
                )

            def out_tile(index, e=e):
                at = tile_at(index)
                y = dot_nn(zg_all[e, rows, :], wd[e, :, at]).astype(bf16)
                for b in (0, 1):
                    ybuf[b, pl.ds(e * capacity, capacity), at] = y[b * capacity : (b + 1) * capacity]

            each_tile(wide, out_tile)
            pump()
        if step:
            for copy in out_copies:
                copy.wait()
        out_copies = []
        for b in (0, 1):
            block = block_of(step, b == 1)
            table = picks_back(block)

            def join_tile(index, b=b, table=table, block=block):
                at = tile_at(index)
                total = dot_nn(table, ybuf[b, :, at])
                total = total + dot_nt(sz_all[block], ws[at, 2 * pad :])
                obuf[b, :, at] = total.astype(bf16)

            each_tile(wide, join_tile)
            out_copies.append(
                local_copy(obuf.at[b], out_part.at[block], base + 2 + exp_local + b)
            )
        pump()
        if step:
            sum_chips(step - 1)
        for e in range(exp_local):

            def back_tile(index, e=e):
                at = tile_at(index)
                y = dot_nt(dgu_all[e, rows, :], wgu[e, at, :]).astype(bf16)
                for b in (0, 1):
                    ybuf[b, pl.ds(e * capacity, capacity), at] = y[b * capacity : (b + 1) * capacity]

            each_tile(wide, back_tile)
        pump()
        for b in (1, 0):
            block = block_of(step, b == 1)
            table = picks_back(block)

            def back_join(index, b=b, table=table, block=block):
                at = tile_at(index)
                total = dot_nn(table, ybuf[b, :, at])
                total = total + dot_nt(sgu_all[block], ws[at, : 2 * pad])
                part[b, :, at] = total.astype(bf16)

            each_tile(wide, back_join)
        hand_over(step)
        if step:
            sum_plane(step - 1)
    pump(64)
    last = high - 1
    for copy in saved + out_copies:
        copy.wait()

    load_sem, store_sem = base + 4 + exp_local, base + 6 + exp_local

    def passes(count, load, work, stores):
        def load_copy(j, slot):
            source, target = load(j, slot)
            return pltpu.make_async_copy(source, target, local_sems.at[load_sem + slot])

        def store_copies(j, slot):
            return [
                pltpu.make_async_copy(
                    source, target, local_sems.at[store_sem + 2 * slot + i]
                )
                for i, (source, target) in enumerate(stores(j, slot))
            ]

        load_copy(0, 0).start()

        def body(j):
            slot = lax.rem(j, 2)

            @pl.when(j + 1 < count)
            def _():
                load_copy(j + 1, 1 - slot).start()

            load_copy(j, slot).wait()

            @pl.when(j >= 2)
            def _():
                for copy in store_copies(j - 2, slot):
                    copy.wait()

            work(j, slot)
            for copy in store_copies(j, slot):
                copy.start()

        each_tile(count, body)
        for j in range(max(0, count - 2), count):
            for copy in store_copies(j, j % 2):
                copy.wait()

    def inner_grads(e):
        passes(
            wide,
            lambda j, slot: (
                xs_all.at[e, :, tile_at(j)],
                tiles.at[slot],
            ),
            lambda j, slot: put(stage.at[slot], dot_tn(tiles[slot], dgu_all[e])),
            lambda j, slot: [
                (stage.at[slot, :, pl.ds(0, hidden)], g_gate.at[e, tile_at(j)]),
                (stage.at[slot, :, pl.ds(hidden, hidden)], g_up.at[e, tile_at(j)]),
            ],
        )

    def put(target, value):
        target[...] = value

    def down_grads(e):
        passes(
            wide,
            lambda j, slot: (
                cs_all.at[e, :, tile_at(j)],
                tiles.at[slot],
            ),
            lambda j, slot: put(
                stage.at[slot, pl.ds(0, hidden), pl.ds(0, TILE)],
                dot_tn(zg_all[e], tiles[slot]),
            ),
            lambda j, slot: [
                (
                    stage.at[slot, pl.ds(0, hidden), pl.ds(0, TILE)],
                    g_down.at[e, :, tile_at(j)],
                ),
            ],
        )

    def shared_grads(source, others, start, size):
        def work(j, slot):
            total = dot_tn(tiles_all[slot, 0], others[0])
            for c in range(1, cols):
                total = total + dot_tn(tiles_all[slot, c], others[c])
            stage_low[slot, :, :size] = total.astype(bf16)

        def load(j, slot):
            return (source.at[:, :, tile_at(j)], tiles_all.at[slot])

        passes(
            wide,
            lambda j, slot: load(j, slot),
            work,
            lambda j, slot: [
                (
                    stage_low.at[slot, :, pl.ds(0, size)],
                    g_shared.at[tile_at(j), pl.ds(start, size)],
                ),
            ],
        )

    first_dots = net.send(dots, dots_core, net.core_peer())
    inner_grads(0)
    sum_cores(last)
    first_dots.wait_recv()
    net.left(first_dots)
    dots[...] = dots[...] + dots_core[...]
    second_dots = net.send(dots, dots_x, net.x_peer())
    inner_grads(1)
    sum_chips(last)
    second_dots.wait_recv()
    dots_core[...] = dots[...] + dots_x[...]
    third_dots = []
    for step in range(1, cols):
        block = lax.rem(net.me + step, cols)
        third_dots.append(
            net.send(dots_core.at[block], gate_dots.at[net.me], net.col_peer(step))
        )
    gate_dots[net.me] = dots_core[net.me]
    down_grads(0)
    sum_plane(last)
    down_grads(1)
    for step in range(1, high):
        far_z[step].wait_recv()
    add_rows(kept, [from_core.at[0, 0, 0], *[from_z.at[step - 1] for step in range(1, high)]])
    own, other = features(net.row), features(other_row)
    back[:, own] = kept[...].astype(bf16)
    far = net.send(back.at[:, own], back.at[:, own], net.x_peer())
    near = net.send(back.at[:, own], back.at[:, own], net.core_peer())
    shared_grads(h2_all, sgu_all, 0, 2 * pad)
    far.wait_recv()
    crossed = net.send(back.at[:, other], back.at[:, other], net.core_peer())
    shared_grads(grads, sz_all, 2 * pad, pad)
    near.wait_recv()
    crossed.wait_recv()
    for copy in third_dots:
        copy.wait_recv()
    net.finish()


def experts_call(
    cols, collective_id, capacity, h2, grads, w_gate, w_up, w_down, w_shared, rank_row, rank_col, gate
):
    toks, width = h2.shape
    exp_local, _, hidden = w_gate.shape
    high = cols // 2
    pad = w_shared.shape[1] // 3
    piece = width // lax.axis_size("row")
    pair = 2 * capacity
    any_space = pl.BlockSpec(memory_space=pl.ANY)
    vmem = pl.BlockSpec(memory_space=pltpu.VMEM)
    copies = 160

    def shape(*dims, dtype=bf16):
        return jax.ShapeDtypeStruct(dims, dtype)

    return pl.pallas_call(
        functools.partial(experts_kernel, cols, capacity),
        out_shape=[
            shape(cols, toks, width),
            shape(toks, width),
            shape(exp_local, width, hidden, dtype=f32),
            shape(exp_local, width, hidden, dtype=f32),
            shape(exp_local, hidden, width, dtype=f32),
            shape(width, 3 * pad),
            shape(cols, 8, toks, dtype=f32),
            shape(cols, toks, width),
            shape(exp_local, cols * capacity, width),
            shape(exp_local, cols * capacity, width),
        ],
        in_specs=[any_space] * 6 + [vmem] * 3,
        out_specs=[
            any_space,
            vmem,
            any_space,
            any_space,
            any_space,
            any_space,
            vmem,
            any_space,
            any_space,
            any_space,
        ],
        scratch_shapes=[
            pltpu.VMEM((exp_local, width, 2 * hidden), bf16),
            pltpu.VMEM((exp_local, hidden, width), bf16),
            pltpu.VMEM((width, 3 * pad), bf16),
            pltpu.VMEM((cols, *gate.shape), f32),
            pltpu.VMEM((2, toks, width), bf16),
            pltpu.VMEM((exp_local, pair, width), bf16),
            pltpu.VMEM((2, exp_local * capacity, width), bf16),
            pltpu.VMEM((2, toks, width), bf16),
            pltpu.VMEM((2, toks, width), bf16),
            pltpu.VMEM((pair, 2 * hidden), f32),
            pltpu.VMEM((pair, LANES), f32),
            pltpu.VMEM((pair, LANES), f32),
            pltpu.VMEM((exp_local, cols * capacity, hidden), bf16),
            pltpu.VMEM((exp_local, cols * capacity, hidden), bf16),
            pltpu.VMEM((exp_local, cols * capacity, 2 * hidden), bf16),
            pltpu.VMEM((cols, toks, pad), bf16),
            pltpu.VMEM((cols, toks, pad), bf16),
            pltpu.VMEM((cols, toks, 2 * pad), bf16),
            pltpu.VMEM((2, high, 2, toks, piece), bf16),
            pltpu.VMEM((high, 2, toks, piece), bf16),
            pltpu.VMEM((high, toks, piece), bf16),
            pltpu.VMEM((high - 1, toks, piece), bf16),
            pltpu.VMEM((toks, piece), f32),
            pltpu.VMEM((cols, 8, toks), f32),
            pltpu.VMEM((cols, 8, toks), f32),
            pltpu.VMEM((cols, 8, toks), f32),
            pltpu.VMEM((2, cols * capacity, TILE), bf16),
            pltpu.VMEM((2, cols, toks, TILE), bf16),
            pltpu.VMEM((2, TILE, 2 * hidden), f32),
            pltpu.VMEM((2, TILE, 2 * pad), bf16),
            pltpu.SemaphoreType.DMA((copies,)),
            pltpu.SemaphoreType.DMA((copies,)),
            pltpu.SemaphoreType.DMA((24,)),
        ],
        compiler_params=pltpu.CompilerParams(
            collective_id=collective_id, has_side_effects=True, vmem_limit_bytes=62 << 20
        ),
        name=f"experts_{collective_id}",
    )(h2, grads, w_gate, w_up, w_down, w_shared, rank_row, rank_col, gate)


def experts_kernels(
    cols, collective_id, capacity, h2, grad_all, w_gate, w_up, w_down, shared_weights, *tables
):
    width, shared_part = shared_weights.shape[0], shared_weights.shape[1] // 3
    pad = -shared_part % LANES
    padded = jnp.pad(shared_weights.reshape(width, 3, shared_part), ((0, 0), (0, 0), (0, pad)))
    padded = padded.reshape(width, -1)
    out_part, back, g_gate, g_up, g_down, g_shared, gate_dots, *_ = experts_call(
        cols, collective_id, capacity, h2, grad_all, w_gate, w_up, w_down, padded, *tables
    )
    g_shared = g_shared.reshape(width, 3, -1)[:, :, :shared_part].reshape(width, -1)
    return (out_part, back, gate_dots, g_shared, g_gate, g_up, g_down)


def fits(cols, rows, width):
    return cols % 2 == 0 and cols * rows * width * 2 <= 12 << 20


class Sum2D:
    def __init__(self, net, source, start, count, from_y, from_z, out):
        self.net, self.source, self.start, self.count = net, source, start, count
        self.from_y, self.from_z, self.out = from_y, from_z, out
        self.rows = pl.ds(start, count)
        self.order = [*range(1, net.high_count), 0]
        self.along_y, self.along_z = {}, {}

    def mine(self, block):
        return self.source(block, self.start, self.count)

    def send_y(self):
        for step in self.order:
            source = self.mine(self.net.block_ahead(step, True))
            self.along_y[step] = self.net.send(
                source, self.from_y.at[step, self.rows], self.net.y_peer()
            )

    def send_z(self):
        for step in self.order:
            self.along_y[step].wait_recv()
            slot = self.from_y.at[step, self.rows]
            if step:
                add_rows(slot, [self.mine(self.net.block_ahead(step)), slot])
                self.along_z[step] = self.net.send(
                    slot, self.from_z.at[step - 1, self.rows], self.net.z_peer(step)
                )

    def last(self):
        for step in range(1, self.net.high_count):
            self.along_z[step].wait_recv()
        terms = [
            self.from_z.at[step - 1, self.rows] for step in range(1, self.net.high_count)
        ]
        mine = self.mine(self.net.me)
        add_rows(self.out.at[self.rows], [mine, self.from_y.at[0, self.rows], *terms])


def rear_kernel(
    cols,
    experts,
    out_part,
    back,
    gate_dots,
    gate,
    router_probs,
    table_col,
    h1,
    h2,
    tokens,
    attn,
    weights_in,
    out_weights_in,
    grads,
    heads,
    q_low,
    kv_all,
    probs,
    cosine,
    sine,
    out_slice,
    d_tokens,
    share_qkv,
    share_misc,
    share_out,
    weights,
    out_weights,
    misc,
    misc_low,
    grad_own,
    gains,
    dots,
    logit_low,
    low,
    dob,
    keys,
    values,
    stacked,
    ds_all,
    kv_grad,
    kv_share,
    dqkv,
    gain_sums,
    own,
    from_core,
    from_x,
    from_y,
    from_z,
    kv_y,
    kv_z,
    out_y,
    out_z,
    qkv_y,
    qkv_z,
    misc_y,
    misc_z,
    row_core,
    row_to,
    row_from,
    send_sems,
    recv_sems,
    local_sems,
):
    net = Net(cols, send_sems, recv_sems)
    toks, width = back.shape
    size = HEAD_DIM
    q_width = q_low.shape[1]
    group = q_width // size
    qkv_width = q_width + 2 * size
    seqs = probs.shape[0]
    local_len = toks // seqs
    rows_w = width // cols
    piece = width // lax.axis_size("row")
    scale = 1.0 / math.sqrt(size)
    other_row = 2 * (1 - net.outer) + net.core

    def local_copy(source, target, index):
        copy = pltpu.make_async_copy(source, target, local_sems.at[index])
        copy.start()
        return copy

    def features(row):
        return pl.ds(pl.multiple_of(row * piece, LANES), piece)

    loads = [
        local_copy(weights_in, weights, 0),
        local_copy(out_weights_in, out_weights, 1),
        local_copy(grads.at[net.me], grad_own, 2),
    ]
    near_load = local_copy(out_part.at[:, :, features(net.row)], own.at[0], 3)
    far_load = local_copy(out_part.at[:, :, features(other_row)], own.at[1], 4)
    net.greet(col_peers(net) + row_peers(net))

    pieces = 4
    count = toks // pieces
    order = [*range(1, net.high_count), 0]
    keys_of = [(step, True) for step in order] + [(step, False) for step in order]
    across, onward, along_y, along_z = {}, {}, {}, {}

    def rows_of(q):
        return pl.ds(q * count, count)

    def out_core(q):
        for far in (1, 0):
            outer = 1 - net.outer if far else net.outer
            for key in keys_of:
                block = net.block_ahead(*key)
                across[q, far, key] = net.send(
                    out_part.at[block, rows_of(q), features(2 * outer + 1 - net.core)],
                    from_core.at[far, block, rows_of(q)],
                    net.core_peer(),
                )

    def out_x(q):
        for key in keys_of:
            across[q, 1, key].wait_recv()
            block = net.block_ahead(*key)
            slot = from_core.at[1, block, rows_of(q)]
            add_rows(slot, [own.at[1, block, rows_of(q)], slot])
            onward[q, key] = net.send(slot, from_x.at[block, rows_of(q)], net.x_peer())

    def out_y_stage(q):
        for key in keys_of:
            across[q, 0, key].wait_recv()
            onward[q, key].wait_recv()
            block = net.block_ahead(*key)
            slot = from_core.at[0, block, rows_of(q)]
            add_rows(slot, [own.at[0, block, rows_of(q)], slot, from_x.at[block, rows_of(q)]])
            if key[1]:
                along_y[q, key[0]] = net.send(
                    slot, from_y.at[key[0], rows_of(q)], net.y_peer()
                )

    def out_z_stage(q):
        for step in order:
            along_y[q, step].wait_recv()
            slot = from_core.at[0, net.block_ahead(step), rows_of(q)]
            add_rows(slot, [slot, from_y.at[step, rows_of(q)]])
            if step:
                along_z[q, step] = net.send(
                    slot, from_z.at[step - 1, rows_of(q)], net.z_peer(step)
                )

    def out_last(q):
        for step in range(1, net.high_count):
            along_z[q, step].wait_recv()
        terms = [from_z.at[step - 1, rows_of(q)] for step in range(1, net.high_count)]
        add_rows(out_slice.at[rows_of(q)], [from_core.at[0, net.me, rows_of(q)], *terms])

    state = {"tick": 0}

    def pump(ticks=1):
        for _ in range(ticks):
            tick = state["tick"]
            state["tick"] += 1
            for lag, stage in enumerate((out_core, out_x, out_y_stage, out_z_stage, out_last)):
                if 0 <= tick - lag < pieces:
                    stage(tick - lag)

    pump()
    for copy in loads:
        copy.wait()

    def chunks(body, rows=32):
        def step(index, carry):
            body(pl.ds(pl.multiple_of(index * rows, rows), rows))
            return carry

        lax.fori_loop(0, toks // rows, step, 0)

    for tile in range(width // TILE):
        at = pl.ds(tile * TILE, TILE)
        turned = jnp.transpose(weights[at, qkv_width : qkv_width + LANES].astype(f32))
        gains[:, at] = turned[experts : experts + 8]
    dots[...] = jnp.zeros_like(dots)
    for c in range(cols):
        dots[2 * c : 2 * c + 2, :] = gate_dots[c, 0:2, :]
    gate_grad = jnp.transpose(dots[...])
    lane = lax.broadcasted_iota(jnp.int32, (toks, LANES), 1)
    mask = (table_col[...] > 0) & (lane < experts)
    chance, gates = router_probs[...], gate[...]
    total = jnp.sum(jnp.where(mask, chance, 0.0), axis=1, keepdims=True)
    gate_grad = jnp.where(mask, gate_grad, 0.0)
    pick_grad = gate_grad - jnp.sum(gates * gate_grad, axis=1, keepdims=True)
    chance_grad = jnp.where(mask, pick_grad / total, 0.0)
    logit_grad = chance * (chance_grad - jnp.sum(chance * chance_grad, axis=1, keepdims=True))
    logit_low[...] = logit_grad.astype(bf16)
    near_load.wait()
    far_load.wait()
    pump()

    for tile in range(width // TILE):
        at = pl.ds(tile * TILE, TILE)
        d_tokens[:, at] = back[:, at].astype(f32) + dot_nt(
            logit_low[...], weights[at, qkv_width : qkv_width + LANES]
        )
    gain_sums[...] = jnp.zeros_like(gain_sums)

    def fold(values, start):
        total = values[0:8]
        for r in range(8, values.shape[0], 8):
            total = total + values[r : r + 8]
        gain_sums[start : start + 8, :] = gain_sums[start : start + 8, :] + total

    def norm_second(at):
        x = tokens[at, :].astype(f32) + attn[at, :].astype(f32)
        inverse = lax.rsqrt(jnp.sum(x * x, axis=1, keepdims=True) / width + norm_eps)
        base = x * inverse
        dh = d_tokens[at, :]
        fold(dh * base, 8)
        scaled = dh * gains[1:2, :]
        mean = jnp.sum(scaled * base, axis=1, keepdims=True) / width
        middle = inverse * (scaled - base * mean) + grad_own[at, :].astype(f32)
        d_tokens[at, :] = middle
        low[at, :] = middle.astype(bf16)

    chunks(norm_second, 16)
    dob[...] = dot_nn(low[...], out_weights[...]).astype(bf16)
    pump()
    for tile in range(width // TILE):
        at = pl.ds(tile * TILE, TILE)
        out_weights[at, :] = dot_tn(low[:, at], heads[...]).astype(bf16)

    def blocks_of(array):
        def source(block, start, count):
            return array.at[pl.ds(pl.multiple_of(block * rows_w + start, 16), count)]

        return source

    out_pieces = 4
    out_count = rows_w // out_pieces
    out_line = [
        Sum2D(net, blocks_of(out_weights), q * out_count, out_count, out_y, out_z, share_out)
        for q in range(out_pieces)
    ]
    out_line[0].send_y()
    out_line[1].send_y()

    kv_line = [
        Sum2D(
            net,
            lambda block, start, count: kv_grad.at[block, pl.ds(start, count)],
            s * local_len,
            local_len,
            kv_y,
            kv_z,
            kv_share,
        )
        for s in range(seqs)
    ]
    for s in range(seqs):
        rows = pl.ds(s * local_len, local_len)
        for c in range(cols):
            at = pl.ds(c * local_len, local_len)
            keys[at, :] = kv_all[c, rows, :size]
            values[at, :] = kv_all[c, rows, size:]

        def attend(g, carry, s=s, rows=rows):
            at = pl.ds(pl.multiple_of(g * size, size), size)
            grow = pl.ds(pl.multiple_of(g * local_len, local_len), local_len)
            dout = dob[rows, at]
            stacked[0, grow, :] = q_low[rows, at]
            stacked[1, grow, :] = dout
            p = probs[s, g]
            p = p.astype(f32)
            dp = dot_nt(dout, values[...])
            delta = jnp.sum(p * dp, axis=1, keepdims=True)
            ds = (p * (dp - delta)).astype(bf16)
            ds_all[grow, :] = ds
            raw = dot_nn(ds, keys[...]) * scale
            dqkv[rows, at] = (
                raw * cosine[rows, :] - pltpu.roll(raw, size // 2, 1) * sine[rows, :]
            ).astype(bf16)
            return carry

        lax.fori_loop(0, group, attend, 0)
        dk = (dot_tn(ds_all[...], stacked[0]) * scale).astype(bf16)
        dv = dot_tn(probs[s].reshape(group * local_len, -1), stacked[1]).astype(bf16)
        for c in range(cols):
            kv_grad[c, rows, :size] = dk[c * local_len : (c + 1) * local_len]
            kv_grad[c, rows, size:] = dv[c * local_len : (c + 1) * local_len]
        kv_line[s].send_y()
        if s == 0:
            out_line[0].send_z()
            pump()
        else:
            kv_line[s - 1].send_z()
    kv_line[seqs - 1].send_z()
    out_line[1].send_z()
    out_line[2].send_y()
    for s in range(seqs):
        kv_line[s].last()
    raw = kv_share[:, :size]
    dqkv[:, q_width : q_width + size] = (
        raw * cosine[...] - pltpu.roll(raw, size // 2, 1) * sine[...]
    ).astype(bf16)
    dqkv[:, q_width + size : qkv_width] = kv_share[:, size:].astype(bf16)

    row_pieces, piece_rows = row_core.shape[0], row_core.shape[1]
    half = row_pieces * piece_rows

    def row_piece(core, i):
        return pl.ds(pl.multiple_of((core * row_pieces + i) * piece_rows, piece_rows), piece_rows)

    over = []
    for core in (1 - net.core, net.core):
        at_rows = pl.ds(pl.multiple_of(core * half, half), half)
        for tile in range(width // TILE):
            at = pl.ds(tile * TILE, TILE)
            low[at_rows, at] = dot_nt(dqkv[at_rows, :], weights[at, :qkv_width]).astype(bf16)
        if not over:
            over = [
                net.send(low.at[row_piece(1 - net.core, i)], row_core.at[i], net.core_peer())
                for i in range(row_pieces)
            ]

    qkv_pieces = 5
    qkv_count = rows_w // qkv_pieces
    for tile in range(width // TILE):
        at = pl.ds(tile * TILE, TILE)
        misc[at, :] = dot_tn(h2[:, at], logit_low[...])
        weights[at, :qkv_width] = dot_tn(h1[:, at], dqkv[...]).astype(bf16)
    qkv_line = [
        Sum2D(
            net,
            lambda block, start, count: weights.at[
                pl.ds(pl.multiple_of(block * rows_w + start, 16), count), pl.ds(0, qkv_width)
            ],
            q * qkv_count,
            qkv_count,
            qkv_y,
            qkv_z,
            share_qkv,
        )
        for q in range(qkv_pieces)
    ]
    qkv_line[0].send_y()
    along, returned = [], []
    for i in range(row_pieces):
        over[i].wait_recv()
        add_rows(row_to.at[i], [low.at[row_piece(net.core, i)], row_core.at[i]])
        along.append(net.send(row_to.at[i], row_from.at[i], net.x_peer()))
    qkv_line[1].send_y()
    for i in range(row_pieces):
        along[i].wait_recv()
        at = row_piece(net.core, i)
        add_rows(grad_own.at[at], [row_to.at[i], row_from.at[i]])
        returned.append(net.send(grad_own.at[at], grad_own.at[at], net.core_peer()))
    qkv_line[0].send_z()
    pump()
    for copy in returned:
        copy.wait_recv()

    def norm_first(at):
        x = tokens[at, :].astype(f32)
        inverse = lax.rsqrt(jnp.sum(x * x, axis=1, keepdims=True) / width + norm_eps)
        base = x * inverse
        dh = grad_own[at, :].astype(f32)
        fold(dh * base, 0)
        scaled = dh * gains[0:1, :]
        mean = jnp.sum(scaled * base, axis=1, keepdims=True) / width
        d_tokens[at, :] = d_tokens[at, :] + inverse * (scaled - base * mean)

    chunks(norm_first, 16)
    total = [jnp.sum(gain_sums[8 * i : 8 * i + 8, :], axis=0, keepdims=True) for i in (0, 1)]
    row_at = lax.broadcasted_iota(jnp.int32, (LANES, TILE), 0)
    for tile in range(width // TILE):
        at = pl.ds(tile * TILE, TILE)
        part = slice(tile * TILE, (tile + 1) * TILE)
        placed = jnp.where(row_at == experts, total[0][:, part], 0.0)
        placed = jnp.where(row_at == experts + 1, total[1][:, part], placed)
        lanes = lax.broadcasted_iota(jnp.int32, (TILE, LANES), 1)
        misc_low[at, :] = jnp.where(lanes < experts, misc[at, :], jnp.transpose(placed)).astype(bf16)
    misc_line = Sum2D(net, blocks_of(misc_low), 0, rows_w, misc_y, misc_z, share_misc)
    misc_line.send_y()
    qkv_line[2].send_y()
    qkv_line[1].send_z()
    out_line[2].send_z()
    out_line[3].send_y()
    pump()
    misc_line.send_z()
    qkv_line[3].send_y()
    qkv_line[2].send_z()
    out_line[3].send_z()
    pump()
    qkv_line[4].send_y()
    qkv_line[3].send_z()
    pump()
    qkv_line[4].send_z()
    pump(8)
    for piece_sum in (*out_line, misc_line, *qkv_line):
        piece_sum.last()
    net.finish()


def rear_call(
    cols, collective_id, experts, out_part, back, gate_dots, gate, router_probs, table_col, h1, h2,
    tokens, attn, weights, out_weights, grads, heads, q_low, kv_all, probs, cosine, sine,
):
    toks, width = back.shape
    q_width = q_low.shape[1]
    size = HEAD_DIM
    qkv_width = q_width + 2 * size
    seqs, group, local_len, full_len = probs.shape
    rows_w, high = width // cols, cols // 2
    piece = width // lax.axis_size("row")
    row_pieces = 4
    row_piece = (row_pieces, toks // 2 // row_pieces, width)
    vmem, any_space = pl.BlockSpec(memory_space=pltpu.VMEM), pl.BlockSpec(memory_space=pl.ANY)

    def shape(*dims, dtype=f32):
        return jax.ShapeDtypeStruct(dims, dtype)

    def sums(rows, columns):
        return [
            pltpu.VMEM((high, rows, columns), bf16),
            pltpu.VMEM((high - 1, rows, columns), bf16),
        ]

    copies = 420
    return pl.pallas_call(
        functools.partial(rear_kernel, cols, experts),
        out_shape=[
            shape(toks, piece),
            shape(toks, width),
            shape(rows_w, qkv_width),
            shape(rows_w, LANES),
            shape(rows_w, q_width),
        ],
        in_specs=[any_space] + [vmem] * 9 + [any_space] * 3 + [vmem] * 6,
        out_specs=[vmem] * 5,
        scratch_shapes=[
            pltpu.VMEM((width, qkv_width + LANES), bf16),
            pltpu.VMEM((width, q_width), bf16),
            pltpu.VMEM((width, LANES), f32),
            pltpu.VMEM((width, LANES), bf16),
            pltpu.VMEM((toks, width), bf16),
            pltpu.VMEM((8, width), f32),
            pltpu.VMEM((LANES, toks), f32),
            pltpu.VMEM((toks, LANES), bf16),
            pltpu.VMEM((toks, width), bf16),
            pltpu.VMEM((toks, q_width), bf16),
            pltpu.VMEM((full_len, size), bf16),
            pltpu.VMEM((full_len, size), bf16),
            pltpu.VMEM((2, group * local_len, size), bf16),
            pltpu.VMEM((group * local_len, full_len), bf16),
            pltpu.VMEM((cols, toks, 2 * size), bf16),
            pltpu.VMEM((toks, 2 * size), f32),
            pltpu.VMEM((toks, qkv_width), bf16),
            pltpu.VMEM((16, width), f32),
            pltpu.VMEM((2, cols, toks, piece), bf16),
            pltpu.VMEM((2, cols, toks, piece), bf16),
            pltpu.VMEM((cols, toks, piece), bf16),
            *sums(toks, piece),
            *sums(toks, 2 * size),
            *sums(rows_w, q_width),
            *sums(rows_w, qkv_width),
            *sums(rows_w, LANES),
            pltpu.VMEM(row_piece, bf16),
            pltpu.VMEM(row_piece, bf16),
            pltpu.VMEM(row_piece, bf16),
            pltpu.SemaphoreType.DMA((copies,)),
            pltpu.SemaphoreType.DMA((copies,)),
            pltpu.SemaphoreType.DMA((8,)),
        ],
        compiler_params=pltpu.CompilerParams(
            collective_id=collective_id, has_side_effects=True, vmem_limit_bytes=62 << 20
        ),
        name=f"rear_{collective_id}",
    )(
        out_part, back, gate_dots, gate, router_probs, table_col, h1, h2, tokens, attn, weights,
        out_weights, grads, heads, q_low, kv_all, probs, cosine, sine,
    )


def experts_plain(
    h2, grad_all, w_gate, w_up, w_down, shared_weights, router, rank_all, capacity, row_width
):
    cols = lax.axis_size("col")
    col_index, row_index = lax.axis_index("col"), lax.axis_index("row")
    toks, width = h2.shape
    exp_local = w_gate.shape[0]
    experts = rank_all.shape[2]
    shared_part = shared_weights.shape[1] // 3
    shared_in_weights = shared_weights[:, : 2 * shared_part]
    shared_down = shared_weights[:, 2 * shared_part :]
    h2_slice = lax.dynamic_slice_in_dim(h2, row_index * row_width, row_width, 1)
    h2_all = gather_all(h2_slice)

    all_mask = (rank_all > 0).astype(f32)
    all_probs = jax.nn.softmax(dot("ctd,de->cte", h2_all, router), axis=-1)
    all_picked = all_probs * all_mask
    all_gate = all_picked / jnp.sum(all_picked, axis=-1, keepdims=True)
    own = col_index * exp_local
    own_gate = lax.dynamic_slice_in_dim(all_gate, own, exp_local, 2)
    own_rank = lax.dynamic_slice_in_dim(rank_all, own, exp_local, 2).astype(jnp.int32)
    slots = jnp.arange(1, capacity + 1, dtype=jnp.int32)
    pick = jnp.swapaxes(own_rank, 1, 2)[:, :, None, :] == slots[:, None]
    slot_gate = jnp.sum(
        jnp.where(pick, jnp.swapaxes(own_gate, 1, 2)[:, :, None, :], 0.0), axis=3
    )[..., None]
    pick_low = pick.astype(bf16).reshape(cols, exp_local * capacity, toks)
    slot_shape = (cols, exp_local, capacity, width)
    slot_rows = dot("cut,ctd->cud", pick_low, h2_all).astype(bf16).reshape(slot_shape)
    slot_grad = dot("cut,ctd->cud", pick_low, grad_all).astype(bf16).reshape(slot_shape)
    gate_pre = dot("necd,edf->necf", slot_rows, w_gate)
    up_pre = dot("necd,edf->necf", slot_rows, w_up)
    silu_gate, slope_gate = silu_parts(gate_pre)
    hidden = silu_gate * up_pre
    gated = (hidden * slot_gate).astype(bf16)
    slot_out = dot("necf,efd->necd", gated, w_down).astype(bf16)
    hidden_grad = dot("necd,efd->necf", slot_grad, w_down)
    slot_dots = jnp.sum(hidden * hidden_grad, axis=-1)
    hidden_grad = hidden_grad * slot_gate
    gate_grad = (hidden_grad * up_pre * slope_gate).astype(bf16)
    up_grad = (hidden_grad * silu_gate).astype(bf16)
    slot_back = dot("necf,edf->necd", gate_grad, w_gate)
    slot_back = (slot_back + dot("necf,edf->necd", up_grad, w_up)).astype(bf16)
    grad_expert_down = dot("necf,necd->efd", gated, slot_grad)
    grad_expert_gate = dot("necd,necf->edf", slot_rows, gate_grad)
    grad_expert_up = dot("necd,necf->edf", slot_rows, up_grad)
    pick_flat = pick_low.reshape(cols, exp_local * capacity, toks)
    slot_out = slot_out.reshape(cols, exp_local * capacity, width)
    slot_back = slot_back.reshape(cols, exp_local * capacity, width)

    shared_pre = dot("ctd,dk->ctk", h2_all, shared_in_weights)
    sgate_pre, sup_pre = shared_pre[:, :, :shared_part], shared_pre[:, :, shared_part:]
    shared_silu, shared_slope = silu_parts(sgate_pre)
    shared_hidden = (shared_silu * sup_pre).astype(bf16)
    part_out = dot("cut,cud->ctd", pick_flat, slot_out) + dot(
        "ctk,dk->ctd", shared_hidden, shared_down
    )
    shared_hgrad = dot("ctd,dk->ctk", grad_all, shared_down)
    shared_grads = jnp.concatenate(
        [shared_hgrad * sup_pre * shared_slope, shared_hgrad * shared_silu], axis=2
    ).astype(bf16)
    part_back = dot("cut,cud->ctd", pick_flat, slot_back) + dot(
        "ctk,dk->ctd", shared_grads, shared_in_weights
    )
    token_dots = jnp.einsum(
        "ceu,ceut->cte", slot_dots, pick.astype(f32), precision=lax.Precision.HIGHEST
    )
    gate_dots = lax.psum(swap_col(token_dots), "row")
    gate_dots = jnp.swapaxes(gate_dots, 0, 1).reshape(toks, experts)

    shared_share = jnp.concatenate(
        [dot("ctd,ctk->dk", h2_all, shared_grads), dot("ctd,ctk->dk", grad_all, shared_hidden)],
        axis=1,
    ).astype(bf16)
    back_full = lax.all_gather(scatter_all(part_back.astype(bf16)), "row", axis=1, tiled=True)
    return (
        part_out.astype(bf16),
        back_full,
        gate_dots,
        shared_share,
        grad_expert_gate,
        grad_expert_up,
        grad_expert_down,
    )


def on_device(
    tokens,
    segments,
    routes,
    attn_gain,
    query_matrix,
    key_matrix,
    value_matrix,
    attention_output_matrix,
    mlp_gain,
    w_router,
    shared_gate_matrix,
    shared_up_matrix,
    shared_down_matrix,
    expert_gate,
    expert_up,
    expert_down,
    cotangent,
):
    local_len, seqs, width = tokens.shape
    cols = lax.axis_size("col")
    col_index = lax.axis_index("col")
    rows_w = query_matrix.shape[0]
    full_len = local_len * cols
    size = HEAD_DIM
    q_width = query_matrix.shape[1]
    kv_width = key_matrix.shape[1]
    kv_local = kv_width // size
    group = q_width // kv_width
    row_width = cotangent.shape[2]
    toks = local_len * seqs
    top = routes.shape[2]
    experts = w_router.shape[1]
    exp_local = expert_gate.shape[0]
    hidden_local = expert_gate.shape[2]
    capacity = max(2, toks * top * 4 // (3 * experts))
    shared_part = shared_gate_matrix.shape[1] // cols
    scale = 1.0 / math.sqrt(size)
    kernels = fits(cols, toks, width) and kv_local == 1 and exp_local == 2

    def seq_major(a):
        return jnp.swapaxes(a, 0, 1).reshape(toks, a.shape[2])

    misc = jnp.concatenate(
        [
            w_router,
            attn_gain[:, None],
            mlp_gain[:, None],
            jnp.zeros((rows_w, LANES - experts - 2), bf16),
        ],
        axis=1,
    )
    shared_weights = jnp.concatenate(
        [
            shared_gate_matrix.reshape(rows_w, cols, shared_part),
            shared_up_matrix.reshape(rows_w, cols, shared_part),
            shared_down_matrix.T.reshape(rows_w, cols, shared_part),
        ],
        axis=2,
    )
    shared_own = jnp.swapaxes(shared_weights, 0, 1)
    grad_own = seq_major(cotangent).astype(bf16)
    cosine, sine = rope_tables(col_index * local_len, local_len, size)
    cosine, sine = jnp.tile(cosine, (seqs, 1)), jnp.tile(sine, (seqs, 1))
    qkv_width = q_width + 2 * kv_width
    flat_routes = seq_major(routes)
    named = flat_routes[:, :, None] == jnp.arange(experts, dtype=jnp.int32)
    mask = jnp.any(named, axis=1)
    order = jnp.arange(toks, dtype=jnp.int32)
    upto = (order[None, :] <= order[:, None]).astype(bf16)
    rank = jnp.where(mask, dot("ij,je->ie", upto, mask.astype(bf16)), 0.0)

    doc = jnp.transpose(segments)
    def to_grid(flat):
        shaped = flat.reshape(seqs, local_len, kv_local, group, size)
        return shaped.transpose(0, 2, 3, 1, 4).reshape(seqs, kv_local, group * local_len, size)

    def from_grid(grid):
        shaped = grid.reshape(seqs, kv_local, group, local_len, size)
        return shaped.transpose(0, 3, 1, 2, 4).reshape(toks, q_width)

    token_rows = seq_major(tokens)
    x = token_rows.astype(f32)
    inv_first = rms_scale(x)
    base_first = x * inv_first
    if kernels:
        table_row = jnp.concatenate([rank.T, doc.reshape(1, toks).astype(f32)], axis=0)
        table_row = jnp.pad(table_row, ((0, -(experts + 1) % 8), (0, 0)))
        table_col = jnp.pad(rank, ((0, 0), (0, LANES - experts))).astype(bf16)
        (
            first_weights,
            out_weights,
            shared_weights,
            grad_all,
            rows_all,
            rank_all,
            h1,
            q_low,
            kv_all,
            probs,
            heads,
            attn,
            h2,
            gate,
            probs_router,
        ) = front_call(
            cols,
            0,
            experts,
            token_rows,
            query_matrix,
            key_matrix,
            value_matrix,
            misc,
            attention_output_matrix.T,
            shared_own,
            grad_own,
            table_row,
            table_col,
            doc.reshape(toks, 1).astype(f32),
            jnp.concatenate([cosine, cosine], axis=1),
            jnp.concatenate([-sine, sine], axis=1),
            seqs,
        )
    else:
        first_weights = jnp.concatenate([query_matrix, key_matrix, value_matrix, misc], axis=1)
        first_weights = gather_col(first_weights).reshape(width, -1)
        out_weights = gather_col(attention_output_matrix.T).reshape(width, q_width)
        shared_weights, grad_all = swap_col(shared_own), gather_all(grad_own)
        gain_one = first_weights[:, qkv_width + experts].astype(f32)
        h1 = (base_first * gain_one).astype(bf16)
        qkv = dot("tb,bk->tk", h1, first_weights[:, :qkv_width])
        qk = rotate(qkv[:, : q_width + kv_width], cosine, sine).astype(bf16)
        q_low = qk[:, :q_width]
        value_low = qkv[:, q_width + kv_width :].astype(bf16)
        side = jnp.concatenate(
            [
                rank.astype(bf16),
                doc.reshape(toks, 1).astype(bf16),
                jnp.zeros((toks, LANES - experts - 1), bf16),
            ],
            axis=1,
        )
        kv_all = gather_col(jnp.concatenate([qk[:, q_width:], value_low, side], axis=1))
        rank_all = kv_all[:, :, 2 * kv_width : 2 * kv_width + experts]
    shared_weights = shared_weights.reshape(width, 3 * shared_part)
    qkv_weights = first_weights[:, :qkv_width]
    router = first_weights[:, qkv_width : qkv_width + experts]
    gain_one = first_weights[:, qkv_width + experts].astype(f32)
    gain_two = first_weights[:, qkv_width + experts + 1].astype(f32)
    kv_seq = jnp.swapaxes(kv_all.reshape(cols, seqs, local_len, -1), 0, 1)
    kv_seq = kv_seq.reshape(seqs, full_len, -1)
    key_all = kv_seq[:, :, :kv_width].reshape(seqs, full_len, kv_local, size)
    value_all = kv_seq[:, :, kv_width : 2 * kv_width].reshape(seqs, full_len, kv_local, size)
    query_grid = to_grid(q_low)
    if not kernels:
        doc_all = kv_seq[:, :, 2 * kv_width + experts]
        place = col_index * local_len + jnp.arange(local_len, dtype=jnp.int32)
        same = doc.astype(bf16)[:, :, None] == doc_all[:, None, :]
        causal = jnp.arange(full_len, dtype=jnp.int32)[None, :] <= place[:, None]
        allowed = jnp.tile(same & causal[None], (1, group, 1))[:, None]
        scores = dot("shrd,skhd->shrk", query_grid, key_all) * scale
        scores = jnp.where(allowed, scores, masked_score)
        weights = jnp.exp(scores - jnp.max(scores, axis=-1, keepdims=True))
        weights = jnp.where(allowed, weights, 0.0)
        probs = (weights / jnp.sum(weights, axis=-1, keepdims=True)).astype(bf16)
        heads = from_grid(dot("shrk,skhd->shrd", probs, value_all)).astype(bf16)
        attn = lax.psum(dot("tk,bk->tb", heads, out_weights).astype(bf16), "row")
    middle = x + attn.astype(f32)

    inv_second = rms_scale(middle)
    base_second = middle * inv_second
    row_index = lax.axis_index("row")
    if not kernels:
        h2 = (base_second * gain_two).astype(bf16)
        probs_router = jax.nn.softmax(dot("td,de->te", h2, router), axis=-1)
        picked = jnp.where(mask, probs_router, 0.0)
        pick_total = jnp.sum(picked, axis=-1, keepdims=True)
        gate = picked / pick_total
    if kernels:
        rank_own = lax.dynamic_slice_in_dim(rank_all, col_index * exp_local, exp_local, 2)
        rank_own = rank_own.astype(f32)
        part_out, back_full, gate_dots, shared_share, *expert_grads = experts_kernels(
            cols,
            3,
            capacity,
            h2,
            grad_all,
            expert_gate,
            expert_up,
            expert_down,
            shared_weights,
            lax.dynamic_slice_in_dim(rows_all, col_index * exp_local, exp_local, 1),
            rank_own,
            gate[:, :experts].T,
        )
    else:
        part_out, back_full, gate_dots, shared_share, *expert_grads = experts_plain(
            h2,
            grad_all,
            expert_gate,
            expert_up,
            expert_down,
            shared_weights,
            router,
            rank_all,
            capacity,
            row_width,
        )
    if not kernels:
        back_full = back_full.astype(f32)
    shared_share = swap_col(shared_share.reshape(cols, rows_w, 3 * shared_part))
    shared_share = jnp.swapaxes(shared_share, 0, 1).astype(f32)
    share_sgate, share_sup, share_sdown = (
        shared_share[:, :, i * shared_part : (i + 1) * shared_part].reshape(rows_w, -1)
        for i in range(3)
    )

    if kernels:
        out_slice, token_grad, share_qkv, share_misc, share_out = rear_call(
            cols,
            5,
            experts,
            part_out,
            back_full,
            gate_dots,
            gate,
            probs_router,
            table_col,
            h1,
            h2,
            token_rows,
            attn,
            first_weights,
            out_weights,
            grad_all,
            heads,
            q_low,
            kv_all,
            probs,
            jnp.concatenate([cosine, cosine], axis=1),
            jnp.concatenate([-sine, sine], axis=1),
        )
    else:
        pick_grad = gate_dots - jnp.sum(gate * gate_dots, axis=-1, keepdims=True)
        prob_grad = jnp.where(mask, pick_grad / pick_total, 0.0)
        logit_grad = probs_router * (
            prob_grad - jnp.sum(probs_router * prob_grad, axis=-1, keepdims=True)
        )
        logit_low = logit_grad.astype(bf16)
        grad_router = dot("td,te->de", h2, logit_low)

        back_full = back_full + dot("te,de->td", logit_low, router)
        grad_own = lax.dynamic_slice_in_dim(grad_all, col_index, 1, 0)[0].astype(f32)
        grad_gain_two = jnp.sum(back_full * base_second, axis=0)
        scaled_two = back_full * gain_two
        middle_grad = (
            inv_second
            * (scaled_two - base_second * jnp.mean(scaled_two * base_second, axis=-1, keepdims=True))
            + grad_own
        )
        attn_grad = middle_grad.astype(bf16)
        grad_out = dot("td,tk->dk", attn_grad, heads).astype(bf16)

        heads_grad = to_grid(dot("td,dk->tk", attn_grad, out_weights).astype(bf16))
        value_grad = dot("shrk,shrd->skhd", probs, heads_grad)
        weight_grad = dot("shrd,skhd->shrk", heads_grad, value_all)
        probs_wide = probs.astype(f32)
        delta = jnp.sum(probs_wide * weight_grad, axis=-1, keepdims=True)
        score_grad = (probs_wide * (weight_grad - delta)).astype(bf16)
        query_grad = from_grid(dot("shrk,skhd->shrd", score_grad, key_all)) * scale
        key_grad = dot("shrk,shrd->skhd", score_grad, query_grid) * scale
        kv_grad = jnp.concatenate(
            [key_grad.reshape(seqs, full_len, kv_width), value_grad.reshape(seqs, full_len, kv_width)],
            axis=2,
        ).astype(bf16)
        kv_grad = jnp.swapaxes(kv_grad.reshape(seqs, cols, local_len, 2 * kv_width), 0, 1)
        kv_share = scatter_col(kv_grad.reshape(cols, toks, 2 * kv_width)).astype(f32)
        qk_grad = rotate(
            jnp.concatenate([query_grad, kv_share[:, :kv_width]], axis=1), cosine, -sine
        )
        qkv_grad = jnp.concatenate([qk_grad, kv_share[:, kv_width:]], axis=1).astype(bf16)
        first_grad = dot("tk,bk->tb", qkv_grad, qkv_weights).astype(bf16)
        first_grad = lax.psum(first_grad, "row").astype(f32)
        grad_gain_one = jnp.sum(first_grad * base_first, axis=0)
        scaled_one = first_grad * gain_one
        token_grad = (
            inv_first
            * (scaled_one - base_first * jnp.mean(scaled_one * base_first, axis=-1, keepdims=True))
            + middle_grad
        )
        grad_first = jnp.concatenate(
            [
                dot("tb,tk->bk", h1, qkv_grad),
                grad_router,
                grad_gain_one[:, None],
                grad_gain_two[:, None],
                jnp.zeros((width, LANES - experts - 2), f32),
            ],
            axis=1,
        ).astype(bf16)
        out_slice = scatter_all(part_out).astype(f32)
        share_out = scatter_col(grad_out.reshape(cols, rows_w, q_width)).astype(f32)
        share_first = scatter_col(grad_first.reshape(cols, rows_w, -1)).astype(f32)
        share_qkv, share_misc = share_first[:, :qkv_width], share_first[:, qkv_width:]
    middle_slice = lax.dynamic_slice_in_dim(middle, row_index * row_width, row_width, 1)
    block_out = (middle_slice + out_slice).astype(bf16)

    def tokens_first(a):
        return jnp.swapaxes(a.reshape(seqs, local_len, a.shape[1]), 0, 1)

    return (
        tokens_first(block_out),
        tokens_first(token_grad),
        share_misc[:, experts],
        share_qkv[:, :q_width],
        share_qkv[:, q_width : q_width + kv_width],
        share_qkv[:, q_width + kv_width :],
        share_out.T,
        share_misc[:, experts + 1],
        share_misc[:, :experts],
        share_sgate,
        share_sup,
        share_sdown.T,
        *expert_grads,
    )


def solution(mesh):
    in_specs = (
        P("col", None, None),
        P("col", None),
        P("col", None, None),
        P("col"),
        P("col", "row"),
        P("col", "row"),
        P("col", "row"),
        P("row", "col"),
        P("col"),
        P("col", None),
        P("col", "row"),
        P("col", "row"),
        P("row", "col"),
        P("col", None, "row"),
        P("col", None, "row"),
        P("col", "row", None),
        P("col", None, "row"),
    )
    out_specs = (
        P("col", None, "row"),
        P("col", None, None),
        P("col"),
        P("col", "row"),
        P("col", "row"),
        P("col", "row"),
        P("row", "col"),
        P("col"),
        P("col", None),
        P("col", "row"),
        P("col", "row"),
        P("row", "col"),
        P("col", None, "row"),
        P("col", None, "row"),
        P("col", "row", None),
    )
    return jax.shard_map(
        on_device, mesh=mesh, in_specs=in_specs, out_specs=out_specs, check_vma=False
    )
```

```python
import functools
import math

import jax
import jax.numpy as jnp
from jax import lax
from jax.experimental import pallas as pl
from jax.experimental.pallas import tpu as pltpu
from jax.sharding import PartitionSpec as P

HEAD_DIM = 128
LANES = 128


norm_eps = 1e-05
rope_base = 500000.0
masked_score = -1e30

f32 = jnp.float32
bf16 = jnp.bfloat16
MESH = pl.DeviceIdType.MESH


def dot(form, left, right):
    return jnp.einsum(form, left, right, preferred_element_type=f32)


def rope_tables(start_place, local_len, head_size):
    places = (start_place + jnp.arange(local_len, dtype=jnp.int32)).astype(f32)
    frequency = jnp.power(
        rope_base, -jnp.arange(0, head_size, 2, dtype=jnp.int32).astype(f32) / head_size
    )
    angles = places[:, None] * frequency[None, :]
    return (jnp.cos(angles), jnp.sin(angles))


def rotate(field, cosine, sine):
    half = cosine.shape[1]
    parts = []
    for start in range(0, field.shape[1], 2 * half):
        front = field[:, start : start + half]
        back = field[:, start + half : start + 2 * half]
        parts.append(front * cosine - back * sine)
        parts.append(back * cosine + front * sine)
    return jnp.concatenate(parts, axis=1)


def rms_scale(values_in):
    return lax.rsqrt(jnp.mean(values_in * values_in, axis=-1, keepdims=True) + norm_eps)


def silu_parts(pre_gate):
    sigmoid_gate = jax.nn.sigmoid(pre_gate)
    silu_gate = pre_gate * sigmoid_gate
    slope_gate = sigmoid_gate * (1.0 + pre_gate * (1.0 - sigmoid_gate))
    return (silu_gate, slope_gate)


def gather_col(part):
    return lax.all_gather(part, "col", axis=0, tiled=False)


def scatter_col(blocks):
    flat = blocks.reshape(-1, blocks.shape[-1])
    return lax.psum_scatter(flat, "col", scatter_dimension=0, tiled=True)


def gather_all(part):
    got = lax.all_gather(part, ("col", "row"), axis=0, tiled=False)
    cols, rows = lax.axis_size("col"), lax.axis_size("row")
    got = got.reshape(cols, rows, *part.shape).transpose(0, 2, 1, 3)
    return got.reshape(cols, part.shape[0], rows * part.shape[1])


def scatter_all(blocks):
    flat = blocks.reshape(-1, blocks.shape[-1])
    part = lax.psum_scatter(flat, "row", scatter_dimension=1, tiled=True)
    return lax.psum_scatter(part, "col", scatter_dimension=0, tiled=True)


def swap_col(blocks):
    return lax.all_to_all(blocks, "col", split_axis=0, concat_axis=0, tiled=True)


class Net:
    def __init__(self, cols, send_sems, recv_sems):
        self.send_sems, self.recv_sems, self.used, self.sent = send_sems, recv_sems, 0, []
        self.cols, self.high_count = cols, cols // 2
        self.me = lax.axis_index("col")
        self.high, self.low = self.me // 2, self.me % 2
        self.row = lax.axis_index("row")
        self.outer, self.core = self.row // 2, self.row % 2

    def block(self, step, other=False):
        high = lax.rem(self.high + self.high_count - step, self.high_count)
        return 2 * high + (1 - self.low if other else self.low)

    def block_ahead(self, step, other=False):
        high = lax.rem(self.high + step, self.high_count)
        return 2 * high + (1 - self.low if other else self.low)

    def z_peer(self, step):
        return {"col": self.block_ahead(step)}

    def y_peer(self):
        return {"col": 2 * self.high + 1 - self.low}

    def x_peer(self):
        return {"row": 2 * (1 - self.outer) + self.core}

    def core_peer(self):
        return {"row": 2 * self.outer + 1 - self.core}

    def col_peer(self, step):
        return {"col": lax.rem(self.me + step, self.cols)}

    def greet(self, peers):
        barrier = pltpu.get_barrier_semaphore()
        for peer in peers:
            pl.semaphore_signal(barrier, inc=1, device_id=peer, device_id_type=MESH)
        pl.semaphore_wait(barrier, len(peers))

    def send(self, source, target, peer):
        copy = pltpu.make_async_remote_copy(
            src_ref=source,
            dst_ref=target,
            send_sem=self.send_sems.at[self.used],
            recv_sem=self.recv_sems.at[self.used],
            device_id=peer,
            device_id_type=MESH,
        )
        self.used += 1
        copy.start()
        self.sent.append(copy)
        return copy

    def left(self, copy):
        copy.wait_send()
        self.sent = [other for other in self.sent if other is not copy]

    def finish(self):
        for copy in self.sent:
            copy.wait_send()


def col_peers(net):
    return [net.z_peer(step) for step in range(1, net.high_count)] + [net.y_peer()]


def row_peers(net):
    return [net.x_peer(), net.core_peer()]


def add_rows(target, terms):
    rows = target.shape[0]
    piece = 32 if rows % 32 == 0 else 16

    def body(index, carry):
        at = pl.ds(pl.multiple_of(index * piece, piece), piece)
        total = terms[0][at, :].astype(f32)
        for term in terms[1:]:
            total = total + term[at, :].astype(f32)
        target[at, :] = total.astype(target.dtype)
        return carry

    lax.fori_loop(0, rows // piece, body, 0)


def dot_nn(left, right):
    return lax.dot_general(left, right, (((1,), (0,)), ((), ())), preferred_element_type=f32)


def dot_nt(left, right):
    return lax.dot_general(left, right, (((1,), (1,)), ((), ())), preferred_element_type=f32)


def dot_tn(left, right):
    return lax.dot_general(left, right, (((0,), (0,)), ((), ())), preferred_element_type=f32)


def each_tile(count, body):
    def step(index, carry):
        body(index)
        return carry

    lax.fori_loop(0, count, step, 0)


TILE = 512


def tile_at(index, tile=TILE):
    if isinstance(index, int):
        return pl.ds(index * tile, tile)
    return pl.ds(pl.multiple_of(index * tile, tile), tile)


class Line:
    def __init__(self, net, items, direct=(), direct_from=0):
        self.net, self.items, self.direct, self.direct_from = net, items, list(direct), direct_from
        self.other_row = 2 * (1 - net.outer) + net.core
        self.along_z, self.along_y, self.along_x, self.to_core = {}, {}, {}, {}
        self.moved = []
        self.now = 0

    def in_chip(self, q, step, other, source, slot):
        if self.items[q][2]:
            self.along_x[q, step, other] = self.net.send(source, slot, self.net.x_peer())
            self.to_core[q, step, other] = self.net.send(source, slot, self.net.core_peer())

    def start(self, q):
        net = self.net
        source, slot_of, _ = self.items[q]
        slot = slot_of(net.me, net.row)
        for step in reversed(range(1, net.high_count)):
            self.along_z[q, step] = net.send(source, slot, net.z_peer(step))
        self.along_y[q, 0] = net.send(source, slot, net.y_peer())
        self.in_chip(q, 0, False, source, slot)

    def after_z(self, q):
        net = self.net
        for step in reversed(range(1, net.high_count)):
            self.along_z[q, step].wait_recv()
            slot = self.items[q][1](net.block(step), net.row)
            self.along_y[q, step] = net.send(slot, slot, net.y_peer())
            self.in_chip(q, step, False, slot, slot)

    def after_y(self, q):
        net = self.net
        for step in range(net.high_count):
            self.along_y[q, step].wait_recv()
            slot = self.items[q][1](net.block(step, True), net.row)
            self.in_chip(q, step, True, slot, slot)

    def after_x(self, q):
        net = self.net
        if self.items[q][2]:
            for other in (False, True):
                for step in range(net.high_count):
                    self.along_x[q, step, other].wait_recv()
                    slot = self.items[q][1](net.block(step, other), self.other_row)
                    self.moved.append(net.send(slot, slot, net.core_peer()))

    def tick(self, count=1):
        net = self.net
        for _ in range(count):
            now, self.now = self.now, self.now + 1
            if now < len(self.items):
                if now >= 2:
                    for step in range(1, net.high_count):
                        net.left(self.along_z[now - 2, step])
                self.start(now)
            if now >= self.direct_from and self.direct:
                self.moved.append(net.send(*self.direct.pop(0)))
            for stage, lag in ((self.after_z, 1), (self.after_y, 2), (self.after_x, 3)):
                if 0 <= now - lag < len(self.items):
                    stage(now - lag)

    def drain(self):
        while self.now < len(self.items) + 3 or self.direct:
            self.tick()
        for copy in [*self.moved, *self.to_core.values()]:
            copy.wait_recv()


def front_kernel(
    cols,
    experts,
    tokens,
    query,
    key,
    value,
    misc,
    out_own,
    shared_own,
    grad_own,
    table_row,
    table_col,
    doc_col,
    cosine,
    sine,
    weights,
    out_weights,
    shared_all,
    grad_all,
    rows_all,
    cols_all,
    h1,
    q_low,
    kv_all,
    probs,
    heads,
    attn,
    h2,
    h2_turned,
    gate,
    router_probs,
    gains,
    inverse,
    kv_low,
    keys,
    values,
    bias,
    partial,
    from_core,
    to_x,
    from_x,
    send_sems,
    recv_sems,
    local_sems,
):
    net = Net(cols, send_sems, recv_sems)
    toks, width = tokens.shape
    size = HEAD_DIM
    q_width = q_low.shape[1]
    group = q_width // size
    rows_w = query.shape[0]
    seqs = probs.shape[0]
    local_len = toks // seqs
    full_len = local_len * cols
    scale = 1.0 / math.sqrt(size)
    mine = pl.ds(pl.multiple_of(net.me * rows_w, 16), rows_w)

    copies = []

    def local_copy(source, target):
        copy = pltpu.make_async_copy(source, target, local_sems.at[len(copies)])
        copy.start()
        copies.append(copy)

    local_copy(query, weights.at[mine, pl.ds(0, q_width)])
    local_copy(key, weights.at[mine, pl.ds(q_width, size)])
    local_copy(value, weights.at[mine, pl.ds(q_width + size, size)])
    local_copy(misc, weights.at[mine, pl.ds(q_width + 2 * size, LANES)])
    first = len(copies)
    local_copy(out_own, out_weights.at[mine])
    local_copy(shared_own.at[net.me], shared_all.at[net.me])
    part = grad_own.shape[0]
    local_copy(
        grad_own, grad_all.at[net.me, pl.ds(pl.multiple_of(net.row * part, LANES), part)]
    )
    local_copy(table_row, rows_all.at[net.me])
    local_copy(table_col, cols_all.at[net.me])
    net.greet([net.col_peer(step) for step in range(1, cols)] + row_peers(net))
    for copy in copies[:first]:
        copy.wait()

    def weight_slot(target, start, count):
        def slot(block, row):
            return target.at[pl.ds(pl.multiple_of(block * rows_w + start, 16), count)]

        return slot

    def grad_slot(start, count):
        def slot(block, row):
            return grad_all.at[block, pl.ds(pl.multiple_of(row * part + start, 16), count)]

        return slot

    items = [(table_row, lambda block, row: rows_all.at[block], False)]
    pieces, out_pieces, grad_pieces = 5, 4, 4
    count = rows_w // pieces
    for q in range(pieces):
        slot = weight_slot(weights, q * count, count)
        items.append((slot(net.me, net.row), slot, False))
    ready_weights = len(items) + 2
    out_items, grad_items = [], []
    count = rows_w // out_pieces
    for q in range(out_pieces):
        slot = weight_slot(out_weights, q * count, count)
        out_items.append((out_own.at[pl.ds(q * count, count)], slot, False))
    count = part // grad_pieces
    for q in range(grad_pieces):
        grad_items.append((grad_own.at[pl.ds(q * count, count)], grad_slot(q * count, count), True))
    items += out_items[:2]
    for q in range(2, out_pieces):
        items += [grad_items[q - 2], out_items[q]]
    ready_out = len(items) + 2
    items += grad_items[out_pieces - 2 :]
    items.append((table_col, lambda block, row: cols_all.at[block], False))
    direct = []
    for step in range(1, cols):
        block = lax.rem(net.me + step, cols)
        direct.append((shared_own.at[block], shared_all.at[net.me], net.col_peer(step)))
    line = Line(net, items, direct, ready_weights - 2)

    line.tick(2)
    copies[first + 3].wait()

    def chunks(body, rows=32):
        def step(index, carry):
            body(pl.ds(pl.multiple_of(index * rows, rows), rows))
            return carry

        lax.fori_loop(0, toks // rows, step, 0)

    def measure_first(at):
        x = tokens[at, :].astype(f32)
        total = jnp.sum(x * x, axis=1, keepdims=True)
        inverse[at, :] = jnp.broadcast_to(lax.rsqrt(total / width + norm_eps), (32, LANES))

    chunks(measure_first)
    line.tick(ready_weights - line.now)

    start = q_width + 2 * size
    for tile in range(width // TILE):
        at = pl.ds(tile * TILE, TILE)
        turned = jnp.transpose(weights[at, start : start + LANES].astype(f32))
        gains[:, at] = turned[experts : experts + 8]

    def norm_first(at):
        x = tokens[at, :].astype(f32) * inverse[at, 0:1]
        h1[at, :] = (x * gains[0:1, :]).astype(bf16)

    chunks(norm_first)
    line.tick()
    heads_all = group + 2
    for head in range(heads_all - 1, -1, -1):
        raw = dot_nn(h1[...], weights[:, head * size : (head + 1) * size])
        if head <= group:
            raw = raw * cosine[...] + pltpu.roll(raw, size // 2, 1) * sine[...]
        if head < group:
            q_low[:, head * size : (head + 1) * size] = raw.astype(bf16)
        else:
            kv_low[:, (head - group) * size : (head - group + 1) * size] = raw.astype(bf16)
        if head == group:
            kv_all[net.me] = kv_low[...]

            def kv_slot(s):
                rows = pl.ds(s * local_len, local_len)
                return lambda block, row: kv_all.at[block, rows]

            kv_line = Line(
                net,
                [
                    (kv_low.at[pl.ds(s * local_len, local_len)], kv_slot(s), False)
                    for s in range(seqs)
                ],
            )
            kv_line.tick()
        if head == group // 2:
            kv_line.tick()
    line.tick()
    kv_line.tick()

    for s in range(seqs):
        if s:
            kv_line.tick()
        rows = pl.ds(s * local_len, local_len)
        place = lax.broadcasted_iota(jnp.int32, (local_len, local_len), 0)
        lane = lax.broadcasted_iota(jnp.int32, (local_len, local_len), 1)
        for c in range(cols):
            at = pl.ds(c * local_len, local_len)
            keys[at, :] = kv_all[c, rows, :size]
            values[at, :] = kv_all[c, rows, size:]
            same = doc_col[rows, :] == rows_all[c, experts : experts + 1, rows]
            ahead = (c - net.me) * local_len
            allowed = same & (lane + ahead <= place)
            bias[:, at] = jnp.where(allowed, 0.0, masked_score)

        def attend(g, carry, s=s, rows=rows):
            at = pl.ds(pl.multiple_of(g * size, size), size)
            scores = dot_nt(q_low[rows, at], keys[...]) * scale + bias[...]
            weight = jnp.exp(scores - jnp.max(scores, axis=1, keepdims=True))
            p = (weight / jnp.sum(weight, axis=1, keepdims=True)).astype(bf16)
            probs[s, g] = p
            heads[rows, at] = dot_nn(p, values[...]).astype(bf16)
            return carry

        lax.fori_loop(0, group, attend, 0)
        if line.now < ready_out:
            line.tick()
    line.tick(max(0, ready_out - line.now))
    copies[first].wait()

    pieces = from_core.shape[0]
    piece_rows = from_core.shape[1]

    def row_piece(core, i):
        return pl.ds(
            pl.multiple_of((core * pieces + i) * piece_rows, piece_rows), piece_rows
        )

    half = pieces * piece_rows
    across = []
    for core in (1 - net.core, net.core):
        at_rows = pl.ds(pl.multiple_of(core * half, half), half)
        for tile in range(width // TILE):
            at = pl.ds(tile * TILE, TILE)
            partial[at_rows, at] = dot_nt(heads[at_rows, :], out_weights[at, :]).astype(bf16)
        if not across:
            across = [
                net.send(partial.at[row_piece(1 - net.core, i)], from_core.at[i], net.core_peer())
                for i in range(pieces)
            ]
    along, back = [], []
    for i in range(pieces):
        across[i].wait_recv()
        add_rows(to_x.at[i], [partial.at[row_piece(net.core, i)], from_core.at[i]])
        along.append(net.send(to_x.at[i], from_x.at[i], net.x_peer()))
    line.tick()
    for i in range(pieces):
        along[i].wait_recv()
        at = row_piece(net.core, i)
        add_rows(attn.at[at], [to_x.at[i], from_x.at[i]])
        back.append(net.send(attn.at[at], attn.at[at], net.core_peer()))
    line.tick()
    for copy in back:
        copy.wait_recv()

    def norm_second(at):
        x = tokens[at, :].astype(f32) + attn[at, :].astype(f32)
        total = jnp.sum(x * x, axis=1, keepdims=True)
        h2[at, :] = (x * lax.rsqrt(total / width + norm_eps) * gains[1:2, :]).astype(bf16)

    chunks(norm_second)
    line.tick()
    for tile in range(width // 256):
        at = slice(tile * 256, (tile + 1) * 256)
        h2_turned[at, :] = turn(h2[:, at])
    logits = dot_nn(h2[...], weights[:, start : start + LANES])
    lane = lax.broadcasted_iota(jnp.int32, (toks, LANES), 1)
    logits = jnp.where(lane < experts, logits, masked_score)
    weight = jnp.exp(logits - jnp.max(logits, axis=1, keepdims=True))
    chance = weight / jnp.sum(weight, axis=1, keepdims=True)
    router_probs[...] = chance
    picked = jnp.where((table_col[...] > 0) & (lane < experts), chance, 0.0)
    gate[...] = picked / jnp.sum(picked, axis=1, keepdims=True)
    line.drain()
    kv_line.drain()
    for copy in [*copies[first + 1 : first + 3], copies[first + 4]]:
        copy.wait()
    net.finish()


def front_call(
    cols, collective_id, experts, tokens, query, key, value, misc, out_own, shared_own, grad_own,
    table_row, table_col, doc_col, cosine, sine, seqs,
):
    toks, width = tokens.shape
    q_width = query.shape[1]
    size = HEAD_DIM
    local_len = toks // seqs
    vmem, any_space = pl.BlockSpec(memory_space=pltpu.VMEM), pl.BlockSpec(memory_space=pl.ANY)

    def shape(*dims, dtype=bf16):
        return jax.ShapeDtypeStruct(dims, dtype)

    pieces = 4
    piece = (pieces, toks // 2 // pieces, width)
    copies = 320
    return pl.pallas_call(
        functools.partial(front_kernel, cols, experts),
        out_shape=[
            shape(width, q_width + 2 * size + LANES),
            shape(width, q_width),
            shape(*shared_own.shape),
            shape(cols, width, toks),
            shape(cols, *table_row.shape, dtype=f32),
            shape(cols, *table_col.shape),
            shape(toks, width),
            shape(toks, q_width),
            shape(cols, toks, 2 * size),
            shape(seqs, q_width // size, local_len, cols * local_len),
            shape(toks, q_width),
            shape(toks, width),
            shape(toks, width),
            shape(width, toks),
            shape(toks, LANES, dtype=f32),
            shape(toks, LANES, dtype=f32),
        ],
        in_specs=[vmem] + [any_space] * 7 + [vmem] * 5,
        out_specs=[vmem, vmem, any_space, any_space] + [vmem] * 12,
        scratch_shapes=[
            pltpu.VMEM((8, width), f32),
            pltpu.VMEM((toks, LANES), f32),
            pltpu.VMEM((toks, 2 * size), bf16),
            pltpu.VMEM((cols * local_len, size), bf16),
            pltpu.VMEM((cols * local_len, size), bf16),
            pltpu.VMEM((local_len, cols * local_len), f32),
            pltpu.VMEM((toks, width), bf16),
            pltpu.VMEM(piece, bf16),
            pltpu.VMEM(piece, bf16),
            pltpu.VMEM(piece, bf16),
            pltpu.SemaphoreType.DMA((copies,)),
            pltpu.SemaphoreType.DMA((copies,)),
            pltpu.SemaphoreType.DMA((16,)),
        ],
        compiler_params=pltpu.CompilerParams(
            collective_id=collective_id, has_side_effects=True, vmem_limit_bytes=48 << 20
        ),
        name=f"front_{collective_id}",
    )(
        tokens, query, key, value, misc, out_own, shared_own, grad_own,
        table_row, table_col, doc_col, cosine, sine,
    )


def one_hot_square(size):
    row = lax.broadcasted_iota(jnp.int32, (size, size), 0)
    lane = lax.broadcasted_iota(jnp.int32, (size, size), 1)
    return jnp.where(row == lane, 1.0, 0.0).astype(bf16)


def turn(values):
    return dot_nt(one_hot_square(values.shape[1]), values).astype(bf16)


WIDE = 1280


def experts_kernel(
    cols,
    capacity,
    h2,
    grads,
    w_gate,
    w_up,
    w_down,
    w_shared,
    rank_row,
    rank_col,
    gate_own,
    out_part,
    back,
    g_gate,
    g_up,
    g_down,
    g_shared,
    gate_dots,
    h2_all,
    xs_all,
    cs_all,
    wgu,
    wgu_t,
    wd,
    wd_t,
    ws,
    ws_t,
    gates,
    hb,
    xbuf,
    ybuf,
    part,
    pre,
    dz_all,
    zg_all,
    dgu_all,
    sdz_all,
    s_all,
    z_all,
    stage_low,
    from_core,
    from_x,
    from_y,
    from_z,
    kept,
    dots,
    dots_core,
    dots_x,
    send_sems,
    recv_sems,
    local_sems,
):
    net = Net(cols, send_sems, recv_sems)
    width, toks = h2.shape
    exp_local, _, hidden = w_gate.shape
    high = net.high_count
    rows_w, packed = w_shared.shape[1:]
    third = packed // 3
    slots = exp_local * capacity
    pair = 2 * capacity
    piece = width // lax.axis_size("row")
    share = width // LANES // 5 * LANES
    rest = (width - 4 * share) // 2
    wide = width // TILE
    net.greet([net.col_peer(step) for step in range(1, cols)] + row_peers(net))

    def local_copy(source, target, index):
        copy = pltpu.make_async_copy(source, target, local_sems.at[index])
        copy.start()
        return copy

    gate_copies = [
        net.send(gate_own, gates.at[net.me], net.col_peer(step)) for step in range(1, cols)
    ]
    gates[net.me] = gate_own[...]

    def feature_e(row):
        return pl.ds(pl.multiple_of(row * share, LANES), share)

    def feature_r(core):
        return pl.ds(pl.multiple_of(4 * share + core * rest, LANES), rest)

    own_e, own_r = feature_e(net.row), feature_r(net.core)
    far_e = feature_e(2 * (1 - net.outer) + net.core)

    def pass_on(source, block, features, peer):
        return net.send(source.at[features], h2_all.at[block, features], peer)

    along_z, along_y, along_x, to_core = {}, {}, {}, {}

    def start_z(step):
        along_z[step] = [
            pass_on(h2, net.me, own_e, net.z_peer(high - step)),
            pass_on(h2, net.me, own_r, net.z_peer(high - step)),
        ]

    def left_z(step):
        for copy in along_z[step]:
            net.left(copy)

    start_z(1)
    along_y[0] = [
        pass_on(h2, net.me, own_e, net.y_peer()),
        pass_on(h2, net.me, own_r, net.y_peer()),
    ]

    def block_of(step, other):
        return net.block_ahead(step, other)

    def share_in_chip(step, other):
        block = block_of(step, other)
        source = h2_all.at[block]
        along_x[step, other] = pass_on(source, block, own_e, net.x_peer())
        to_core[step, other] = [
            pass_on(source, block, own_e, net.core_peer()),
            pass_on(source, block, own_r, net.core_peer()),
        ]

    def arrived_y(step):
        for copy in along_y[step]:
            copy.wait_recv()
        share_in_chip(step, True)

    def arrived_z(step):
        for copy in along_z[step]:
            copy.wait_recv()
        block = block_of(step, False)
        along_y[step] = [
            pass_on(h2_all.at[block], block, own_e, net.y_peer()),
            pass_on(h2_all.at[block], block, own_r, net.y_peer()),
        ]
        share_in_chip(step, False)

    def arrived_x(step, other):
        along_x[step, other].wait_recv()
        block = block_of(step, other)
        to_core[step, other].append(pass_on(h2_all.at[block], block, far_e, net.core_peer()))

    def whole(step, other):
        for copy in to_core[step, other]:
            copy.wait_recv()

    events = [functools.partial(arrived_y, 0)]
    for step in range(1, high):
        events.append(functools.partial(arrived_z, step))
        events.append(functools.partial(arrived_x, step - 1, True))
        events.append(functools.partial(arrived_y, step))
        events.append(functools.partial(arrived_x, step, False))
    events.append(functools.partial(arrived_x, high - 1, True))
    events = iter(events)

    def pump(count=1):
        for _ in range(count):
            event = next(events, None)
            if event is not None:
                event()

    loads = []
    for e in range(exp_local):
        loads.append(local_copy(w_down.at[e], wd.at[e], 3 * e))
        loads.append(local_copy(w_gate.at[e], wgu.at[e, :, pl.ds(0, hidden)], 3 * e + 1))
        loads.append(local_copy(w_up.at[e], wgu.at[e, :, pl.ds(hidden, hidden)], 3 * e + 2))
    base = 3 * exp_local
    for c in range(cols):
        loads.append(local_copy(w_shared.at[c], ws.at[pl.ds(c * rows_w, rows_w)], base + c))
    base += cols
    keep_own = local_copy(h2, h2_all.at[net.me], base)
    base += 1

    def load_pair(source, step):
        first = local_copy(source.at[block_of(step, False)], hb.at[0], base)
        second = local_copy(source.at[block_of(step, True)], hb.at[1], base + 1)
        first.wait()
        second.wait()

    slot_row = lax.broadcasted_iota(jnp.int32, (capacity, toks), 0).astype(f32) + 1.0
    slot_lane = lax.broadcasted_iota(jnp.int32, (toks, capacity), 1).astype(f32) + 1.0

    def picks(block):
        rows = [
            jnp.where(rank_row[block, e : e + 1, :] == slot_row, 1.0, 0.0).astype(bf16)
            for e in range(exp_local)
        ]
        return jnp.concatenate(rows, axis=0)

    def picks_back(block):
        lanes = [
            jnp.where(rank_col[block, :, e : e + 1] == slot_lane, 1.0, 0.0).astype(bf16)
            for e in range(exp_local)
        ]
        return jnp.concatenate(lanes, axis=1)

    def dispatch(step):
        for b in (0, 1):
            table = picks_back(block_of(step, b == 1))

            def tile(index, b=b, table=table):
                at = tile_at(index, WIDE)
                rows = dot_nn(hb[b, at, :], table).astype(bf16)
                for e in range(exp_local):
                    xbuf[e, at, pl.ds(b * capacity, capacity)] = rows[
                        :, e * capacity : (e + 1) * capacity
                    ]

            each_tile(width // WIDE, tile)

    def save_rows(target, step):
        return [
            local_copy(
                xbuf.at[e], target.at[e, :, pl.ds(step * pair, pair)], base + 2 + e
            )
            for e in range(exp_local)
        ]

    saved = []
    for step in range(high):
        load_pair(grads, step)
        if step == 0:
            for copy in loads:
                copy.wait()

            def turn_tile(index):
                at = tile_at(index, 256)
                for e in range(exp_local):
                    wd_t[e, at, :] = turn(wd[e, :, at])
                    for k in range(2 * hidden // 256):
                        wgu_t[e, k * 256 : (k + 1) * 256, at] = turn(
                            wgu[e, at, k * 256 : (k + 1) * 256]
                        )
                ws_t[:, at] = turn(ws[at, :])

            each_tile(width // 256, turn_tile)
        for copy in saved:
            copy.wait()
        dispatch(step)
        saved = save_rows(cs_all, step)
        cols_at = pl.ds(step * pair, pair)
        for e in range(exp_local):
            dz_all[e, :, cols_at] = dot_nn(wd[e], xbuf[e]).astype(bf16)
        for b in (0, 1):
            sdz_all[block_of(step, b == 1)] = dot_nn(ws_t[2 * third :, :], hb[b]).astype(bf16)
        if step + 2 < high:
            left_z(step + 1)
        if step + 2 <= high - 1:
            start_z(step + 2)
        pump()
    for copy in saved:
        copy.wait()
    for copy in gate_copies:
        copy.wait_recv()
    keep_own.wait()

    across, onward, upward, far_z = {}, {}, {}, {}

    def features(row):
        return pl.ds(pl.multiple_of(row * piece, LANES), piece)

    other_row = 2 * (1 - net.outer) + net.core

    def hand_over(step):
        for b in (1, 0):
            for far in (1, 0):
                outer = 1 - net.outer if far else net.outer
                source = part.at[b, features(2 * outer + 1 - net.core)]
                across[step, b, far] = net.send(
                    source, from_core.at[far, step, b], net.core_peer()
                )

    def sum_cores(step):
        for b in (1, 0):
            for far, row in ((1, other_row), (0, net.row)):
                across[step, b, far].wait_recv()
                slot = from_core.at[far, step, b]
                add_rows(slot, [part.at[b, features(row)], slot])
                if far:
                    onward[step, b] = net.send(slot, from_x.at[step, b], net.x_peer())
        for b in (1, 0):
            for far in (1, 0):
                net.left(across[step, b, far])

    def sum_chips(step):
        for b in (1, 0):
            onward[step, b].wait_recv()
            slot = from_core.at[0, step, b]
            add_rows(slot, [slot, from_x.at[step, b]])
            if b:
                upward[step] = net.send(slot, from_y.at[step], net.y_peer())

    def sum_plane(step):
        upward[step].wait_recv()
        slot = from_core.at[0, step, 0]
        add_rows(slot, [slot, from_y.at[step]])
        if step:
            far_z[step] = net.send(slot, from_z.at[step - 1], net.z_peer(step))

    own_expert = net.me * exp_local
    gate_rows = gates.shape[1]
    gate_at = lax.broadcasted_iota(jnp.int32, (gate_rows, slots), 0)
    gate_of = own_expert + lax.broadcasted_iota(jnp.int32, (gate_rows, slots), 1) // capacity
    dot_at = lax.broadcasted_iota(jnp.int32, (16, slots), 0)
    dot_of = lax.broadcasted_iota(jnp.int32, (16, slots), 1) // capacity
    dots[...] = jnp.zeros_like(dots)
    s_all[2 * third :, :] = jnp.zeros((third, cols * toks), bf16)
    z_all[: 2 * third, :] = jnp.zeros((2 * third, cols * toks), bf16)

    def split(values):
        high_part = values.astype(bf16)
        return high_part, (values - high_part.astype(f32)).astype(bf16)

    saved, out_copies = [], []
    for step in range(high):
        if step:
            whole(step, False)
        whole(step, True)
        for copy in out_copies:
            copy.wait()
        load_pair(h2_all, step)
        for copy in saved:
            copy.wait()
        dispatch(step)
        saved = save_rows(xs_all, step)
        pump()
        slot_gates = []
        for b in (0, 1):
            block = block_of(step, b == 1)
            at = pl.ds(pl.multiple_of(block * toks, toks), toks)
            inner = dot_nn(ws_t[: 2 * third, :], hb[b])
            sa, su = inner[:third], inner[third:]
            sig = 1.0 / (1.0 + jnp.exp(-sa))
            silu = sa * sig
            slope = sig * (1.0 + sa * (1.0 - sig))
            sdz = sdz_all[block].astype(f32)
            s_all[:third, at] = (sdz * su * slope).astype(bf16)
            s_all[third : 2 * third, at] = (sdz * silu).astype(bf16)
            z_all[2 * third :, at] = (silu * su).astype(bf16)
            table = picks_back(block)
            first, second = split(gates[block])
            found = dot_nn(first, table) + dot_nn(second, table)
            slot_gates.append(
                jnp.sum(jnp.where(gate_at == gate_of, found, 0.0), axis=0, keepdims=True)
            )
        if step:
            sum_cores(step - 1)
        cols_at = pl.ds(step * pair, pair)
        slot_dots = []
        for e in range(exp_local):
            pre[...] = dot_nn(wgu_t[e], xbuf[e])
            gate = jnp.concatenate(
                [row[:, e * capacity : (e + 1) * capacity] for row in slot_gates], axis=1
            )

            def gating(index, total, e=e, cols_at=cols_at, gate=gate):
                at = pl.ds(pl.multiple_of(index * 32, 32), 32)
                up_at = pl.ds(pl.multiple_of(hidden + index * 32, 32), 32)
                a, u = pre[at, :], pre[up_at, :]
                dz = dz_all[e, at, cols_at].astype(f32)
                sig = 1.0 / (1.0 + jnp.exp(-a))
                silu = a * sig
                slope = sig * (1.0 + a * (1.0 - sig))
                z = silu * u
                total = total + jnp.sum(z * dz, axis=0, keepdims=True)
                zg_all[e, at, cols_at] = (z * gate).astype(bf16)
                dz = dz * gate
                dgu_all[e, at, cols_at] = (dz * u * slope).astype(bf16)
                dgu_all[e, up_at, cols_at] = (dz * silu).astype(bf16)
                return total

            slot_dots.append(
                lax.fori_loop(0, hidden // 32, gating, jnp.zeros((1, pair), f32))
            )

            def out_tile(index, e=e, cols_at=cols_at):
                at = tile_at(index, WIDE)
                y = dot_nn(wd_t[e, at, :], zg_all[e, :, cols_at]).astype(bf16)
                for b in (0, 1):
                    ybuf[b, at, pl.ds(e * capacity, capacity)] = y[
                        :, b * capacity : (b + 1) * capacity
                    ]

            each_tile(width // WIDE, out_tile)
            pump()
        out_copies = []
        for b in (0, 1):
            block = block_of(step, b == 1)
            at_toks = pl.ds(pl.multiple_of(block * toks, toks), toks)
            table = picks(block)
            row = jnp.concatenate(
                [part_dots[:, b * capacity : (b + 1) * capacity] for part_dots in slot_dots], axis=1
            )
            first, second = split(row)
            both = jnp.where(dot_at == dot_of, first.astype(f32), 0.0)
            both = both + jnp.where(dot_at == dot_of + 8, second.astype(f32), 0.0)
            found = dot_nn(both.astype(bf16), table)
            dots[block] = found[:8] + found[8:]

            def join_tile(index, b=b, table=table, at_toks=at_toks):
                at = tile_at(index, WIDE)
                total = dot_nn(ybuf[b, at, :], table) + dot_nn(ws[at, :], z_all[:, at_toks])
                hb[b, at, :] = total.astype(bf16)

            each_tile(width // WIDE, join_tile)
            out_copies.append(
                local_copy(hb.at[b], out_part.at[block], base + 2 + exp_local + b)
            )
        pump()
        if step:
            sum_chips(step - 1)
        for e in range(exp_local):

            def back_tile(index, e=e, cols_at=cols_at):
                at = tile_at(index, WIDE)
                y = dot_nn(wgu[e, at, :], dgu_all[e, :, cols_at]).astype(bf16)
                for b in (0, 1):
                    ybuf[b, at, pl.ds(e * capacity, capacity)] = y[
                        :, b * capacity : (b + 1) * capacity
                    ]

            each_tile(width // WIDE, back_tile)
        pump()
        for b in (1, 0):
            block = block_of(step, b == 1)
            at_toks = pl.ds(pl.multiple_of(block * toks, toks), toks)
            table = picks(block)

            def back_join(index, b=b, table=table, at_toks=at_toks):
                at = tile_at(index, WIDE)
                total = dot_nn(ybuf[b, at, :], table) + dot_nn(ws[at, :], s_all[:, at_toks])
                part[b, at, :] = total.astype(bf16)

            each_tile(width // WIDE, back_join)
        hand_over(step)
        if step:
            sum_plane(step - 1)
    pump(64)
    last = high - 1
    for copy in saved + out_copies:
        copy.wait()

    load_sem, store_sem = base + 4 + exp_local, base + 6 + exp_local

    def passes(count, load, work, stores):
        def load_copy(j, slot):
            source, target = load(j, slot)
            return pltpu.make_async_copy(source, target, local_sems.at[load_sem + slot])

        def store_copies(j, slot):
            return [
                pltpu.make_async_copy(
                    source, target, local_sems.at[store_sem + 2 * slot + i]
                )
                for i, (source, target) in enumerate(stores(j, slot))
            ]

        load_copy(0, 0).start()

        def body(j):
            slot = lax.rem(j, 2)

            @pl.when(j + 1 < count)
            def _():
                load_copy(j + 1, 1 - slot).start()

            load_copy(j, slot).wait()

            @pl.when(j >= 2)
            def _():
                for copy in store_copies(j - 2, slot):
                    copy.wait()

            work(j, slot)
            for copy in store_copies(j, slot):
                copy.start()

        each_tile(count, body)
        for j in range(max(0, count - 2), count):
            for copy in store_copies(j, j % 2):
                copy.wait()

    depth = cols * capacity
    total_toks = cols * toks
    top, next_top = pl.ds(0, TILE), pl.ds(TILE, TILE)

    def inner_grads(e):
        def work(j, slot):
            found = dot_nt(wgu_t[slot, :TILE, :depth], dgu_all[e]).astype(bf16)
            wd_t[slot, :TILE, :] = found[:, :hidden]
            wd_t[slot, TILE : 2 * TILE, :] = found[:, hidden:]

        passes(
            wide,
            lambda j, slot: (
                xs_all.at[e, tile_at(j)],
                wgu_t.at[slot, top, pl.ds(0, depth)],
            ),
            work,
            lambda j, slot: [
                (wd_t.at[slot, top], g_gate.at[e, tile_at(j)]),
                (wd_t.at[slot, next_top], g_up.at[e, tile_at(j)]),
            ],
        )

    def down_grads(e):
        def work(j, slot):
            found = dot_nt(zg_all[e], wgu_t[slot, :TILE, :depth])
            wd[slot, :, :TILE] = found.astype(bf16)

        passes(
            wide,
            lambda j, slot: (
                cs_all.at[e, tile_at(j)],
                wgu_t.at[slot, top, pl.ds(0, depth)],
            ),
            work,
            lambda j, slot: [
                (wd.at[slot, :, top], g_down.at[e, :, tile_at(j)]),
            ],
        )

    def shared_grads():
        def tile(index):
            at = tile_at(index)
            copies = [
                pltpu.make_async_copy(
                    source.at[c, at],
                    wgu_t.at[slot, top, pl.ds(c * toks, toks)],
                    local_sems.at[slot * cols + c],
                )
                for slot, source in enumerate((h2_all, grads))
                for c in range(cols)
            ]
            for copy in copies:
                copy.start()
            for copy in copies:
                copy.wait()
            found = dot_nt(wgu_t[0, :TILE, :total_toks], s_all[...])
            found = found + dot_nt(wgu_t[1, :TILE, :total_toks], z_all[...])
            stage_low[...] = found.astype(bf16)
            copy = pltpu.make_async_copy(stage_low, g_shared.at[at], local_sems.at[store_sem])
            copy.start()
            copy.wait()

        each_tile(wide, tile)

    first_dots = net.send(dots, dots_core, net.core_peer())
    inner_grads(0)
    sum_cores(last)
    first_dots.wait_recv()
    net.left(first_dots)
    dots[...] = dots[...] + dots_core[...]
    second_dots = net.send(dots, dots_x, net.x_peer())
    inner_grads(1)
    sum_chips(last)
    second_dots.wait_recv()
    dots_core[...] = dots[...] + dots_x[...]
    third_dots = []
    for step in range(1, cols):
        block = lax.rem(net.me + step, cols)
        third_dots.append(
            net.send(dots_core.at[block], gate_dots.at[net.me], net.col_peer(step))
        )
    gate_dots[net.me] = dots_core[net.me]
    down_grads(0)
    sum_plane(last)
    down_grads(1)
    for step in range(1, high):
        far_z[step].wait_recv()
    add_rows(kept, [from_core.at[0, 0, 0], *[from_z.at[step - 1] for step in range(1, high)]])
    own, other = features(net.row), features(other_row)
    back[own, :] = kept[...].astype(bf16)
    far = net.send(back.at[own], back.at[own], net.x_peer())
    near = net.send(back.at[own], back.at[own], net.core_peer())
    shared_grads()
    far.wait_recv()
    crossed = net.send(back.at[other], back.at[other], net.core_peer())
    near.wait_recv()
    crossed.wait_recv()
    for copy in third_dots:
        copy.wait_recv()
    net.finish()


def experts_call(
    cols, collective_id, capacity, h2, grads, w_gate, w_up, w_down, w_shared, rank_row, rank_col, gate
):
    width, toks = h2.shape
    exp_local, _, hidden = w_gate.shape
    high = cols // 2
    packed = w_shared.shape[2]
    piece = width // lax.axis_size("row")
    pair, depth = 2 * capacity, cols * capacity
    any_space = pl.BlockSpec(memory_space=pl.ANY)
    vmem = pl.BlockSpec(memory_space=pltpu.VMEM)
    copies = 160

    def shape(*dims, dtype=bf16):
        return jax.ShapeDtypeStruct(dims, dtype)

    return pl.pallas_call(
        functools.partial(experts_kernel, cols, capacity),
        out_shape=[
            shape(cols, width, toks),
            shape(width, toks),
            shape(exp_local, width, hidden),
            shape(exp_local, width, hidden),
            shape(exp_local, hidden, width),
            shape(width, packed),
            shape(cols, 8, toks, dtype=f32),
            shape(cols, width, toks),
            shape(exp_local, width, depth),
            shape(exp_local, width, depth),
        ],
        in_specs=[any_space] * 6 + [vmem] * 3,
        out_specs=[
            any_space,
            vmem,
            any_space,
            any_space,
            any_space,
            any_space,
            vmem,
            any_space,
            any_space,
            any_space,
        ],
        scratch_shapes=[
            pltpu.VMEM((exp_local, width, 2 * hidden), bf16),
            pltpu.VMEM((exp_local, 2 * hidden, width), bf16),
            pltpu.VMEM((exp_local, hidden, width), bf16),
            pltpu.VMEM((exp_local, width, hidden), bf16),
            pltpu.VMEM((width, packed), bf16),
            pltpu.VMEM((packed, width), bf16),
            pltpu.VMEM((cols, *gate.shape), f32),
            pltpu.VMEM((2, width, toks), bf16),
            pltpu.VMEM((exp_local, width, pair), bf16),
            pltpu.VMEM((2, width, exp_local * capacity), bf16),
            pltpu.VMEM((2, width, toks), bf16),
            pltpu.VMEM((2 * hidden, pair), f32),
            pltpu.VMEM((exp_local, hidden, depth), bf16),
            pltpu.VMEM((exp_local, hidden, depth), bf16),
            pltpu.VMEM((exp_local, 2 * hidden, depth), bf16),
            pltpu.VMEM((cols, packed // 3, toks), bf16),
            pltpu.VMEM((packed, cols * toks), bf16),
            pltpu.VMEM((packed, cols * toks), bf16),
            pltpu.VMEM((TILE, packed), bf16),
            pltpu.VMEM((2, high, 2, piece, toks), bf16),
            pltpu.VMEM((high, 2, piece, toks), bf16),
            pltpu.VMEM((high, piece, toks), bf16),
            pltpu.VMEM((high - 1, piece, toks), bf16),
            pltpu.VMEM((piece, toks), f32),
            pltpu.VMEM((cols, 8, toks), f32),
            pltpu.VMEM((cols, 8, toks), f32),
            pltpu.VMEM((cols, 8, toks), f32),
            pltpu.SemaphoreType.DMA((copies,)),
            pltpu.SemaphoreType.DMA((copies,)),
            pltpu.SemaphoreType.DMA((40,)),
        ],
        compiler_params=pltpu.CompilerParams(
            collective_id=collective_id, has_side_effects=True, vmem_limit_bytes=63 << 20
        ),
        name=f"experts_{collective_id}",
    )(h2, grads, w_gate, w_up, w_down, w_shared, rank_row, rank_col, gate)


def experts_kernels(
    cols, collective_id, capacity, h2, grad_all, w_gate, w_up, w_down, shared_weights, *tables
):
    out_part, back, g_gate, g_up, g_down, g_shared, gate_dots, *_ = experts_call(
        cols, collective_id, capacity, h2, grad_all, w_gate, w_up, w_down, shared_weights, *tables
    )
    wide = (grad.astype(f32) for grad in (g_gate, g_up, g_down))
    return (out_part, back, gate_dots, g_shared, *wide)


def fits(cols, rows, width):
    return cols % 2 == 0 and cols * rows * width * 2 <= 12 << 20


class Sum2D:
    def __init__(self, net, source, start, count, from_y, from_z, out):
        self.net, self.source, self.start, self.count = net, source, start, count
        self.from_y, self.from_z, self.out = from_y, from_z, out
        self.rows = pl.ds(start, count)
        self.order = [*range(1, net.high_count), 0]
        self.along_y, self.along_z = {}, {}

    def mine(self, block):
        return self.source(block, self.start, self.count)

    def send_y(self):
        for step in self.order:
            source = self.mine(self.net.block_ahead(step, True))
            self.along_y[step] = self.net.send(
                source, self.from_y.at[step, self.rows], self.net.y_peer()
            )

    def send_z(self):
        for step in self.order:
            self.along_y[step].wait_recv()
            slot = self.from_y.at[step, self.rows]
            if step:
                add_rows(slot, [self.mine(self.net.block_ahead(step)), slot])
                self.along_z[step] = self.net.send(
                    slot, self.from_z.at[step - 1, self.rows], self.net.z_peer(step)
                )

    def last(self):
        for step in range(1, self.net.high_count):
            self.along_z[step].wait_recv()
        terms = [
            self.from_z.at[step - 1, self.rows] for step in range(1, self.net.high_count)
        ]
        mine = self.mine(self.net.me)
        add_rows(self.out.at[self.rows], [mine, self.from_y.at[0, self.rows], *terms])


def rear_kernel(
    cols,
    experts,
    out_part,
    back,
    gate_dots,
    gate,
    router_probs,
    table_col,
    h1,
    h2,
    tokens,
    attn,
    weights_in,
    out_weights_in,
    grads,
    heads,
    q_low,
    kv_all,
    probs,
    cosine,
    sine,
    out_slice,
    d_tokens,
    share_qkv,
    share_misc,
    share_out,
    weights,
    out_weights,
    misc,
    misc_low,
    grad_turned,
    grad_own,
    gains,
    dots,
    logit_low,
    low,
    dob,
    keys,
    values,
    stacked,
    ds_all,
    kv_grad,
    kv_share,
    dqkv,
    gain_sums,
    own,
    from_core,
    from_x,
    from_y,
    from_z,
    kv_y,
    kv_z,
    out_y,
    out_z,
    qkv_y,
    qkv_z,
    misc_y,
    misc_z,
    row_core,
    row_to,
    row_from,
    send_sems,
    recv_sems,
    local_sems,
):
    net = Net(cols, send_sems, recv_sems)
    width, toks = back.shape
    size = HEAD_DIM
    q_width = q_low.shape[1]
    group = q_width // size
    qkv_width = q_width + 2 * size
    seqs = probs.shape[0]
    local_len = toks // seqs
    rows_w = width // cols
    piece = width // lax.axis_size("row")
    scale = 1.0 / math.sqrt(size)
    other_row = 2 * (1 - net.outer) + net.core

    def local_copy(source, target, index):
        copy = pltpu.make_async_copy(source, target, local_sems.at[index])
        copy.start()
        return copy

    def features(row):
        return pl.ds(pl.multiple_of(row * piece, LANES), piece)

    loads = [
        local_copy(weights_in, weights, 0),
        local_copy(out_weights_in, out_weights, 1),
        local_copy(grads.at[net.me], grad_turned, 2),
    ]
    near_load = local_copy(out_part.at[:, features(net.row)], own.at[0], 3)
    far_load = local_copy(out_part.at[:, features(other_row)], own.at[1], 4)
    net.greet(col_peers(net) + row_peers(net))

    pieces = 4
    count = piece // pieces
    order = [*range(1, net.high_count), 0]
    keys_of = [(step, True) for step in order] + [(step, False) for step in order]
    across, onward, along_y, along_z = {}, {}, {}, {}

    def rows_of(q):
        return pl.ds(q * count, count)

    def out_core(q):
        for far in (1, 0):
            outer = 1 - net.outer if far else net.outer
            for key in keys_of:
                block = net.block_ahead(*key)
                across[q, far, key] = net.send(
                    out_part.at[
                        block,
                        pl.ds(
                            pl.multiple_of(
                                (2 * outer + 1 - net.core) * piece + q * count, 16
                            ),
                            count,
                        ),
                    ],
                    from_core.at[far, block, rows_of(q)],
                    net.core_peer(),
                )

    def out_x(q):
        for key in keys_of:
            across[q, 1, key].wait_recv()
            block = net.block_ahead(*key)
            slot = from_core.at[1, block, rows_of(q)]
            add_rows(slot, [own.at[1, block, rows_of(q)], slot])
            onward[q, key] = net.send(slot, from_x.at[block, rows_of(q)], net.x_peer())

    def out_y_stage(q):
        for key in keys_of:
            across[q, 0, key].wait_recv()
            onward[q, key].wait_recv()
            block = net.block_ahead(*key)
            slot = from_core.at[0, block, rows_of(q)]
            add_rows(slot, [own.at[0, block, rows_of(q)], slot, from_x.at[block, rows_of(q)]])
            if key[1]:
                along_y[q, key[0]] = net.send(
                    slot, from_y.at[key[0], rows_of(q)], net.y_peer()
                )

    def out_z_stage(q):
        for step in order:
            along_y[q, step].wait_recv()
            slot = from_core.at[0, net.block_ahead(step), rows_of(q)]
            add_rows(slot, [slot, from_y.at[step, rows_of(q)]])
            if step:
                along_z[q, step] = net.send(
                    slot, from_z.at[step - 1, rows_of(q)], net.z_peer(step)
                )

    def out_last(q):
        for step in range(1, net.high_count):
            along_z[q, step].wait_recv()
        terms = [from_z.at[step - 1, rows_of(q)] for step in range(1, net.high_count)]
        add_rows(out_slice.at[rows_of(q)], [from_core.at[0, net.me, rows_of(q)], *terms])

    state = {"tick": 0}

    def pump(ticks=1):
        for _ in range(ticks):
            tick = state["tick"]
            state["tick"] += 1
            for lag, stage in enumerate((out_core, out_x, out_y_stage, out_z_stage, out_last)):
                if 0 <= tick - lag < pieces:
                    stage(tick - lag)

    pump()
    for copy in loads:
        copy.wait()

    def chunks(body, rows=32):
        def step(index, carry):
            body(pl.ds(pl.multiple_of(index * rows, rows), rows))
            return carry

        lax.fori_loop(0, toks // rows, step, 0)

    for tile in range(width // TILE):
        at = pl.ds(tile * TILE, TILE)
        turned = jnp.transpose(weights[at, qkv_width : qkv_width + LANES].astype(f32))
        gains[:, at] = turned[experts : experts + 8]
    dots[...] = jnp.zeros_like(dots)
    for c in range(cols):
        dots[2 * c : 2 * c + 2, :] = gate_dots[c, 0:2, :]
    gate_grad = jnp.transpose(dots[...])
    lane = lax.broadcasted_iota(jnp.int32, (toks, LANES), 1)
    mask = (table_col[...] > 0) & (lane < experts)
    chance, gates = router_probs[...], gate[...]
    total = jnp.sum(jnp.where(mask, chance, 0.0), axis=1, keepdims=True)
    gate_grad = jnp.where(mask, gate_grad, 0.0)
    pick_grad = gate_grad - jnp.sum(gates * gate_grad, axis=1, keepdims=True)
    chance_grad = jnp.where(mask, pick_grad / total, 0.0)
    logit_grad = chance * (chance_grad - jnp.sum(chance * chance_grad, axis=1, keepdims=True))
    logit_low[...] = logit_grad.astype(bf16)
    near_load.wait()
    far_load.wait()
    pump()

    for tile in range(width // TILE):
        at = pl.ds(tile * TILE, TILE)
        d_tokens[:, at] = dot_nt(one_hot_square(toks), back[at, :]) + dot_nt(
            logit_low[...], weights[at, qkv_width : qkv_width + LANES]
        )
        grad_own[:, at] = dot_nt(one_hot_square(toks), grad_turned[at, :]).astype(bf16)
    gain_sums[...] = jnp.zeros_like(gain_sums)

    def fold(values, start):
        total = values[0:8]
        for r in range(8, values.shape[0], 8):
            total = total + values[r : r + 8]
        gain_sums[start : start + 8, :] = gain_sums[start : start + 8, :] + total

    def norm_second(at):
        x = tokens[at, :].astype(f32) + attn[at, :].astype(f32)
        inverse = lax.rsqrt(jnp.sum(x * x, axis=1, keepdims=True) / width + norm_eps)
        base = x * inverse
        dh = d_tokens[at, :]
        fold(dh * base, 8)
        scaled = dh * gains[1:2, :]
        mean = jnp.sum(scaled * base, axis=1, keepdims=True) / width
        middle = inverse * (scaled - base * mean) + grad_own[at, :].astype(f32)
        d_tokens[at, :] = middle
        low[at, :] = middle.astype(bf16)

    chunks(norm_second, 16)
    dob[...] = dot_nn(low[...], out_weights[...]).astype(bf16)
    pump()
    for tile in range(width // TILE):
        at = pl.ds(tile * TILE, TILE)
        out_weights[at, :] = dot_tn(low[:, at], heads[...]).astype(bf16)

    def blocks_of(array):
        def source(block, start, count):
            return array.at[pl.ds(pl.multiple_of(block * rows_w + start, 16), count)]

        return source

    out_pieces = 4
    out_count = rows_w // out_pieces
    out_line = [
        Sum2D(net, blocks_of(out_weights), q * out_count, out_count, out_y, out_z, share_out)
        for q in range(out_pieces)
    ]
    out_line[0].send_y()
    out_line[1].send_y()

    kv_line = [
        Sum2D(
            net,
            lambda block, start, count: kv_grad.at[block, pl.ds(start, count)],
            s * local_len,
            local_len,
            kv_y,
            kv_z,
            kv_share,
        )
        for s in range(seqs)
    ]
    for s in range(seqs):
        rows = pl.ds(s * local_len, local_len)
        for c in range(cols):
            at = pl.ds(c * local_len, local_len)
            keys[at, :] = kv_all[c, rows, :size]
            values[at, :] = kv_all[c, rows, size:]

        def attend(g, carry, s=s, rows=rows):
            at = pl.ds(pl.multiple_of(g * size, size), size)
            grow = pl.ds(pl.multiple_of(g * local_len, local_len), local_len)
            dout = dob[rows, at]
            stacked[0, grow, :] = q_low[rows, at]
            stacked[1, grow, :] = dout
            p = probs[s, g]
            p = p.astype(f32)
            dp = dot_nt(dout, values[...])
            delta = jnp.sum(p * dp, axis=1, keepdims=True)
            ds = (p * (dp - delta)).astype(bf16)
            ds_all[grow, :] = ds
            raw = dot_nn(ds, keys[...]) * scale
            dqkv[rows, at] = (
                raw * cosine[rows, :] - pltpu.roll(raw, size // 2, 1) * sine[rows, :]
            ).astype(bf16)
            return carry

        lax.fori_loop(0, group, attend, 0)
        dk = (dot_tn(ds_all[...], stacked[0]) * scale).astype(bf16)
        dv = dot_tn(probs[s].reshape(group * local_len, -1), stacked[1]).astype(bf16)
        for c in range(cols):
            kv_grad[c, rows, :size] = dk[c * local_len : (c + 1) * local_len]
            kv_grad[c, rows, size:] = dv[c * local_len : (c + 1) * local_len]
        kv_line[s].send_y()
        if s == 0:
            out_line[0].send_z()
            pump()
        else:
            kv_line[s - 1].send_z()
    kv_line[seqs - 1].send_z()
    out_line[1].send_z()
    out_line[2].send_y()
    for s in range(seqs):
        kv_line[s].last()
    raw = kv_share[:, :size]
    dqkv[:, q_width : q_width + size] = (
        raw * cosine[...] - pltpu.roll(raw, size // 2, 1) * sine[...]
    ).astype(bf16)
    dqkv[:, q_width + size : qkv_width] = kv_share[:, size:].astype(bf16)

    row_pieces, piece_rows = row_core.shape[0], row_core.shape[1]
    half = row_pieces * piece_rows

    def row_piece(core, i):
        return pl.ds(pl.multiple_of((core * row_pieces + i) * piece_rows, piece_rows), piece_rows)

    over = []
    for core in (1 - net.core, net.core):
        at_rows = pl.ds(pl.multiple_of(core * half, half), half)
        for tile in range(width // TILE):
            at = pl.ds(tile * TILE, TILE)
            low[at_rows, at] = dot_nt(dqkv[at_rows, :], weights[at, :qkv_width]).astype(bf16)
        if not over:
            over = [
                net.send(low.at[row_piece(1 - net.core, i)], row_core.at[i], net.core_peer())
                for i in range(row_pieces)
            ]

    qkv_pieces = 5
    qkv_count = rows_w // qkv_pieces
    for tile in range(width // TILE):
        at = pl.ds(tile * TILE, TILE)
        misc[at, :] = dot_tn(h2[:, at], logit_low[...])
        weights[at, :qkv_width] = dot_tn(h1[:, at], dqkv[...]).astype(bf16)
    qkv_line = [
        Sum2D(
            net,
            lambda block, start, count: weights.at[
                pl.ds(pl.multiple_of(block * rows_w + start, 16), count), pl.ds(0, qkv_width)
            ],
            q * qkv_count,
            qkv_count,
            qkv_y,
            qkv_z,
            share_qkv,
        )
        for q in range(qkv_pieces)
    ]
    qkv_line[0].send_y()
    along, returned = [], []
    for i in range(row_pieces):
        over[i].wait_recv()
        add_rows(row_to.at[i], [low.at[row_piece(net.core, i)], row_core.at[i]])
        along.append(net.send(row_to.at[i], row_from.at[i], net.x_peer()))
    qkv_line[1].send_y()
    for i in range(row_pieces):
        along[i].wait_recv()
        at = row_piece(net.core, i)
        add_rows(grad_own.at[at], [row_to.at[i], row_from.at[i]])
        returned.append(net.send(grad_own.at[at], grad_own.at[at], net.core_peer()))
    qkv_line[0].send_z()
    pump()
    for copy in returned:
        copy.wait_recv()

    def norm_first(at):
        x = tokens[at, :].astype(f32)
        inverse = lax.rsqrt(jnp.sum(x * x, axis=1, keepdims=True) / width + norm_eps)
        base = x * inverse
        dh = grad_own[at, :].astype(f32)
        fold(dh * base, 0)
        scaled = dh * gains[0:1, :]
        mean = jnp.sum(scaled * base, axis=1, keepdims=True) / width
        d_tokens[at, :] = d_tokens[at, :] + inverse * (scaled - base * mean)

    chunks(norm_first, 16)
    total = [jnp.sum(gain_sums[8 * i : 8 * i + 8, :], axis=0, keepdims=True) for i in (0, 1)]
    row_at = lax.broadcasted_iota(jnp.int32, (LANES, TILE), 0)
    for tile in range(width // TILE):
        at = pl.ds(tile * TILE, TILE)
        part = slice(tile * TILE, (tile + 1) * TILE)
        placed = jnp.where(row_at == experts, total[0][:, part], 0.0)
        placed = jnp.where(row_at == experts + 1, total[1][:, part], placed)
        lanes = lax.broadcasted_iota(jnp.int32, (TILE, LANES), 1)
        misc_low[at, :] = jnp.where(lanes < experts, misc[at, :], jnp.transpose(placed)).astype(bf16)
    misc_line = Sum2D(net, blocks_of(misc_low), 0, rows_w, misc_y, misc_z, share_misc)
    misc_line.send_y()
    qkv_line[2].send_y()
    qkv_line[1].send_z()
    out_line[2].send_z()
    out_line[3].send_y()
    pump()
    misc_line.send_z()
    qkv_line[3].send_y()
    qkv_line[2].send_z()
    out_line[3].send_z()
    pump()
    qkv_line[4].send_y()
    qkv_line[3].send_z()
    pump()
    qkv_line[4].send_z()
    pump(8)
    for piece_sum in (*out_line, misc_line, *qkv_line):
        piece_sum.last()
    net.finish()


def rear_call(
    cols, collective_id, experts, out_part, back, gate_dots, gate, router_probs, table_col, h1, h2,
    tokens, attn, weights, out_weights, grads, heads, q_low, kv_all, probs, cosine, sine,
):
    width, toks = back.shape
    q_width = q_low.shape[1]
    size = HEAD_DIM
    qkv_width = q_width + 2 * size
    seqs, group, local_len, full_len = probs.shape
    rows_w, high = width // cols, cols // 2
    piece = width // lax.axis_size("row")
    row_pieces = 4
    row_piece = (row_pieces, toks // 2 // row_pieces, width)
    vmem, any_space = pl.BlockSpec(memory_space=pltpu.VMEM), pl.BlockSpec(memory_space=pl.ANY)

    def shape(*dims, dtype=f32):
        return jax.ShapeDtypeStruct(dims, dtype)

    def sums(rows, columns):
        return [
            pltpu.VMEM((high, rows, columns), bf16),
            pltpu.VMEM((high - 1, rows, columns), bf16),
        ]

    copies = 420
    return pl.pallas_call(
        functools.partial(rear_kernel, cols, experts),
        out_shape=[
            shape(piece, toks),
            shape(toks, width),
            shape(rows_w, qkv_width),
            shape(rows_w, LANES),
            shape(rows_w, q_width),
        ],
        in_specs=[any_space] + [vmem] * 9 + [any_space] * 3 + [vmem] * 6,
        out_specs=[vmem] * 5,
        scratch_shapes=[
            pltpu.VMEM((width, qkv_width + LANES), bf16),
            pltpu.VMEM((width, q_width), bf16),
            pltpu.VMEM((width, LANES), f32),
            pltpu.VMEM((width, LANES), bf16),
            pltpu.VMEM((width, toks), bf16),
            pltpu.VMEM((toks, width), bf16),
            pltpu.VMEM((8, width), f32),
            pltpu.VMEM((LANES, toks), f32),
            pltpu.VMEM((toks, LANES), bf16),
            pltpu.VMEM((toks, width), bf16),
            pltpu.VMEM((toks, q_width), bf16),
            pltpu.VMEM((full_len, size), bf16),
            pltpu.VMEM((full_len, size), bf16),
            pltpu.VMEM((2, group * local_len, size), bf16),
            pltpu.VMEM((group * local_len, full_len), bf16),
            pltpu.VMEM((cols, toks, 2 * size), bf16),
            pltpu.VMEM((toks, 2 * size), f32),
            pltpu.VMEM((toks, qkv_width), bf16),
            pltpu.VMEM((16, width), f32),
            pltpu.VMEM((2, cols, piece, toks), bf16),
            pltpu.VMEM((2, cols, piece, toks), bf16),
            pltpu.VMEM((cols, piece, toks), bf16),
            *sums(piece, toks),
            *sums(toks, 2 * size),
            *sums(rows_w, q_width),
            *sums(rows_w, qkv_width),
            *sums(rows_w, LANES),
            pltpu.VMEM(row_piece, bf16),
            pltpu.VMEM(row_piece, bf16),
            pltpu.VMEM(row_piece, bf16),
            pltpu.SemaphoreType.DMA((copies,)),
            pltpu.SemaphoreType.DMA((copies,)),
            pltpu.SemaphoreType.DMA((8,)),
        ],
        compiler_params=pltpu.CompilerParams(
            collective_id=collective_id, has_side_effects=True, vmem_limit_bytes=62 << 20
        ),
        name=f"rear_{collective_id}",
    )(
        out_part, back, gate_dots, gate, router_probs, table_col, h1, h2, tokens, attn, weights,
        out_weights, grads, heads, q_low, kv_all, probs, cosine, sine,
    )


def experts_plain(
    h2, grad_all, w_gate, w_up, w_down, shared_weights, router, rank_all, capacity, row_width
):
    cols = lax.axis_size("col")
    col_index, row_index = lax.axis_index("col"), lax.axis_index("row")
    toks, width = h2.shape
    exp_local = w_gate.shape[0]
    experts = rank_all.shape[2]
    shared_part = shared_weights.shape[1] // 3
    shared_in_weights = shared_weights[:, : 2 * shared_part]
    shared_down = shared_weights[:, 2 * shared_part :]
    h2_slice = lax.dynamic_slice_in_dim(h2, row_index * row_width, row_width, 1)
    h2_all = gather_all(h2_slice)

    all_mask = (rank_all > 0).astype(f32)
    all_probs = jax.nn.softmax(dot("ctd,de->cte", h2_all, router), axis=-1)
    all_picked = all_probs * all_mask
    all_gate = all_picked / jnp.sum(all_picked, axis=-1, keepdims=True)
    own = col_index * exp_local
    own_gate = lax.dynamic_slice_in_dim(all_gate, own, exp_local, 2)
    own_rank = lax.dynamic_slice_in_dim(rank_all, own, exp_local, 2).astype(jnp.int32)
    slots = jnp.arange(1, capacity + 1, dtype=jnp.int32)
    pick = jnp.swapaxes(own_rank, 1, 2)[:, :, None, :] == slots[:, None]
    slot_gate = jnp.sum(
        jnp.where(pick, jnp.swapaxes(own_gate, 1, 2)[:, :, None, :], 0.0), axis=3
    )[..., None]
    pick_low = pick.astype(bf16).reshape(cols, exp_local * capacity, toks)
    slot_shape = (cols, exp_local, capacity, width)
    slot_rows = dot("cut,ctd->cud", pick_low, h2_all).astype(bf16).reshape(slot_shape)
    slot_grad = dot("cut,ctd->cud", pick_low, grad_all).astype(bf16).reshape(slot_shape)
    gate_pre = dot("necd,edf->necf", slot_rows, w_gate)
    up_pre = dot("necd,edf->necf", slot_rows, w_up)
    silu_gate, slope_gate = silu_parts(gate_pre)
    hidden = silu_gate * up_pre
    gated = (hidden * slot_gate).astype(bf16)
    slot_out = dot("necf,efd->necd", gated, w_down).astype(bf16)
    hidden_grad = dot("necd,efd->necf", slot_grad, w_down)
    slot_dots = jnp.sum(hidden * hidden_grad, axis=-1)
    hidden_grad = hidden_grad * slot_gate
    gate_grad = (hidden_grad * up_pre * slope_gate).astype(bf16)
    up_grad = (hidden_grad * silu_gate).astype(bf16)
    slot_back = dot("necf,edf->necd", gate_grad, w_gate)
    slot_back = (slot_back + dot("necf,edf->necd", up_grad, w_up)).astype(bf16)
    grad_expert_down = dot("necf,necd->efd", gated, slot_grad)
    grad_expert_gate = dot("necd,necf->edf", slot_rows, gate_grad)
    grad_expert_up = dot("necd,necf->edf", slot_rows, up_grad)
    pick_flat = pick_low.reshape(cols, exp_local * capacity, toks)
    slot_out = slot_out.reshape(cols, exp_local * capacity, width)
    slot_back = slot_back.reshape(cols, exp_local * capacity, width)

    shared_pre = dot("ctd,dk->ctk", h2_all, shared_in_weights)
    sgate_pre, sup_pre = shared_pre[:, :, :shared_part], shared_pre[:, :, shared_part:]
    shared_silu, shared_slope = silu_parts(sgate_pre)
    shared_hidden = (shared_silu * sup_pre).astype(bf16)
    part_out = dot("cut,cud->ctd", pick_flat, slot_out) + dot(
        "ctk,dk->ctd", shared_hidden, shared_down
    )
    shared_hgrad = dot("ctd,dk->ctk", grad_all, shared_down)
    shared_grads = jnp.concatenate(
        [shared_hgrad * sup_pre * shared_slope, shared_hgrad * shared_silu], axis=2
    ).astype(bf16)
    part_back = dot("cut,cud->ctd", pick_flat, slot_back) + dot(
        "ctk,dk->ctd", shared_grads, shared_in_weights
    )
    token_dots = jnp.einsum(
        "ceu,ceut->cte", slot_dots, pick.astype(f32), precision=lax.Precision.HIGHEST
    )
    gate_dots = lax.psum(swap_col(token_dots), "row")
    gate_dots = jnp.swapaxes(gate_dots, 0, 1).reshape(toks, experts)

    shared_share = jnp.concatenate(
        [dot("ctd,ctk->dk", h2_all, shared_grads), dot("ctd,ctk->dk", grad_all, shared_hidden)],
        axis=1,
    ).astype(bf16)
    back_full = lax.all_gather(scatter_all(part_back.astype(bf16)), "row", axis=1, tiled=True)
    return (
        part_out.astype(bf16),
        back_full,
        gate_dots,
        shared_share,
        grad_expert_gate,
        grad_expert_up,
        grad_expert_down,
    )


def on_device(
    tokens,
    segments,
    routes,
    attn_gain,
    query_matrix,
    key_matrix,
    value_matrix,
    attention_output_matrix,
    mlp_gain,
    w_router,
    shared_gate_matrix,
    shared_up_matrix,
    shared_down_matrix,
    expert_gate,
    expert_up,
    expert_down,
    cotangent,
):
    local_len, seqs, width = tokens.shape
    cols = lax.axis_size("col")
    col_index = lax.axis_index("col")
    rows_w = query_matrix.shape[0]
    full_len = local_len * cols
    size = HEAD_DIM
    q_width = query_matrix.shape[1]
    kv_width = key_matrix.shape[1]
    kv_local = kv_width // size
    group = q_width // kv_width
    row_width = cotangent.shape[2]
    toks = local_len * seqs
    top = routes.shape[2]
    experts = w_router.shape[1]
    exp_local = expert_gate.shape[0]
    hidden_local = expert_gate.shape[2]
    capacity = max(2, toks * top * 4 // (3 * experts))
    shared_part = shared_gate_matrix.shape[1] // cols
    scale = 1.0 / math.sqrt(size)
    kernels = fits(cols, toks, width) and kv_local == 1 and exp_local == 2

    def seq_major(a):
        return jnp.swapaxes(a, 0, 1).reshape(toks, a.shape[2])

    misc = jnp.concatenate(
        [
            w_router,
            attn_gain[:, None],
            mlp_gain[:, None],
            jnp.zeros((rows_w, LANES - experts - 2), bf16),
        ],
        axis=1,
    )
    shared_weights = jnp.concatenate(
        [
            shared_gate_matrix.reshape(rows_w, cols, shared_part),
            shared_up_matrix.reshape(rows_w, cols, shared_part),
            shared_down_matrix.T.reshape(rows_w, cols, shared_part),
        ],
        axis=2,
    )
    shared_own = jnp.swapaxes(shared_weights, 0, 1)
    grad_own = seq_major(cotangent).astype(bf16)
    cosine, sine = rope_tables(col_index * local_len, local_len, size)
    cosine, sine = jnp.tile(cosine, (seqs, 1)), jnp.tile(sine, (seqs, 1))
    qkv_width = q_width + 2 * kv_width
    flat_routes = seq_major(routes)
    named = flat_routes[:, :, None] == jnp.arange(experts, dtype=jnp.int32)
    mask = jnp.any(named, axis=1)
    order = jnp.arange(toks, dtype=jnp.int32)
    upto = (order[None, :] <= order[:, None]).astype(bf16)
    rank = jnp.where(mask, dot("ij,je->ie", upto, mask.astype(bf16)), 0.0)

    doc = jnp.transpose(segments)
    def to_grid(flat):
        shaped = flat.reshape(seqs, local_len, kv_local, group, size)
        return shaped.transpose(0, 2, 3, 1, 4).reshape(seqs, kv_local, group * local_len, size)

    def from_grid(grid):
        shaped = grid.reshape(seqs, kv_local, group, local_len, size)
        return shaped.transpose(0, 3, 1, 2, 4).reshape(toks, q_width)

    token_rows = seq_major(tokens)
    x = token_rows.astype(f32)
    inv_first = rms_scale(x)
    base_first = x * inv_first
    if kernels:
        table_row = jnp.concatenate([rank.T, doc.reshape(1, toks).astype(f32)], axis=0)
        table_row = jnp.pad(table_row, ((0, -(experts + 1) % 8), (0, 0)))
        table_col = jnp.pad(rank, ((0, 0), (0, LANES - experts))).astype(bf16)
        (
            first_weights,
            out_weights,
            shared_weights,
            grad_all,
            rows_all,
            rank_all,
            h1,
            q_low,
            kv_all,
            probs,
            heads,
            attn,
            h2,
            h2_turned,
            gate,
            probs_router,
        ) = front_call(
            cols,
            0,
            experts,
            token_rows,
            query_matrix,
            key_matrix,
            value_matrix,
            misc,
            attention_output_matrix.T,
            shared_own,
            grad_own.T,
            table_row,
            table_col,
            doc.reshape(toks, 1).astype(f32),
            jnp.concatenate([cosine, cosine], axis=1),
            jnp.concatenate([-sine, sine], axis=1),
            seqs,
        )
    else:
        first_weights = jnp.concatenate([query_matrix, key_matrix, value_matrix, misc], axis=1)
        first_weights = gather_col(first_weights).reshape(width, -1)
        out_weights = gather_col(attention_output_matrix.T).reshape(width, q_width)
        shared_weights, grad_all = swap_col(shared_own), gather_all(grad_own)
        gain_one = first_weights[:, qkv_width + experts].astype(f32)
        h1 = (base_first * gain_one).astype(bf16)
        qkv = dot("tb,bk->tk", h1, first_weights[:, :qkv_width])
        qk = rotate(qkv[:, : q_width + kv_width], cosine, sine).astype(bf16)
        q_low = qk[:, :q_width]
        value_low = qkv[:, q_width + kv_width :].astype(bf16)
        side = jnp.concatenate(
            [
                rank.astype(bf16),
                doc.reshape(toks, 1).astype(bf16),
                jnp.zeros((toks, LANES - experts - 1), bf16),
            ],
            axis=1,
        )
        kv_all = gather_col(jnp.concatenate([qk[:, q_width:], value_low, side], axis=1))
        rank_all = kv_all[:, :, 2 * kv_width : 2 * kv_width + experts]
    if not kernels:
        shared_weights = shared_weights.reshape(width, 3 * shared_part)
    qkv_weights = first_weights[:, :qkv_width]
    router = first_weights[:, qkv_width : qkv_width + experts]
    gain_one = first_weights[:, qkv_width + experts].astype(f32)
    gain_two = first_weights[:, qkv_width + experts + 1].astype(f32)
    kv_seq = jnp.swapaxes(kv_all.reshape(cols, seqs, local_len, -1), 0, 1)
    kv_seq = kv_seq.reshape(seqs, full_len, -1)
    key_all = kv_seq[:, :, :kv_width].reshape(seqs, full_len, kv_local, size)
    value_all = kv_seq[:, :, kv_width : 2 * kv_width].reshape(seqs, full_len, kv_local, size)
    query_grid = to_grid(q_low)
    if not kernels:
        doc_all = kv_seq[:, :, 2 * kv_width + experts]
        place = col_index * local_len + jnp.arange(local_len, dtype=jnp.int32)
        same = doc.astype(bf16)[:, :, None] == doc_all[:, None, :]
        causal = jnp.arange(full_len, dtype=jnp.int32)[None, :] <= place[:, None]
        allowed = jnp.tile(same & causal[None], (1, group, 1))[:, None]
        scores = dot("shrd,skhd->shrk", query_grid, key_all) * scale
        scores = jnp.where(allowed, scores, masked_score)
        weights = jnp.exp(scores - jnp.max(scores, axis=-1, keepdims=True))
        weights = jnp.where(allowed, weights, 0.0)
        probs = (weights / jnp.sum(weights, axis=-1, keepdims=True)).astype(bf16)
        heads = from_grid(dot("shrk,skhd->shrd", probs, value_all)).astype(bf16)
        attn = lax.psum(dot("tk,bk->tb", heads, out_weights).astype(bf16), "row")
    middle = x + attn.astype(f32)

    inv_second = rms_scale(middle)
    base_second = middle * inv_second
    row_index = lax.axis_index("row")
    if not kernels:
        h2 = (base_second * gain_two).astype(bf16)
        probs_router = jax.nn.softmax(dot("td,de->te", h2, router), axis=-1)
        picked = jnp.where(mask, probs_router, 0.0)
        pick_total = jnp.sum(picked, axis=-1, keepdims=True)
        gate = picked / pick_total
    if kernels:
        rank_own = lax.dynamic_slice_in_dim(rank_all, col_index * exp_local, exp_local, 2)
        rank_own = rank_own.astype(f32)
        part_out, back_full, gate_dots, shared_share, *expert_grads = experts_kernels(
            cols,
            3,
            capacity,
            h2_turned,
            grad_all,
            expert_gate,
            expert_up,
            expert_down,
            shared_weights,
            lax.dynamic_slice_in_dim(rows_all, col_index * exp_local, exp_local, 1),
            rank_own,
            gate[:, :experts].T,
        )
    else:
        part_out, back_full, gate_dots, shared_share, *expert_grads = experts_plain(
            h2,
            grad_all,
            expert_gate,
            expert_up,
            expert_down,
            shared_weights,
            router,
            rank_all,
            capacity,
            row_width,
        )
    if not kernels:
        back_full = back_full.astype(f32)
    shared_share = swap_col(shared_share.reshape(cols, rows_w, 3 * shared_part))
    shared_share = jnp.swapaxes(shared_share, 0, 1).astype(f32)
    share_sgate, share_sup, share_sdown = (
        shared_share[:, :, i * shared_part : (i + 1) * shared_part].reshape(rows_w, -1)
        for i in range(3)
    )

    if kernels:
        out_slice, token_grad, share_qkv, share_misc, share_out = rear_call(
            cols,
            5,
            experts,
            part_out,
            back_full,
            gate_dots,
            gate,
            probs_router,
            table_col,
            h1,
            h2,
            token_rows,
            attn,
            first_weights,
            out_weights,
            grad_all,
            heads,
            q_low,
            kv_all,
            probs,
            jnp.concatenate([cosine, cosine], axis=1),
            jnp.concatenate([-sine, sine], axis=1),
        )
    else:
        pick_grad = gate_dots - jnp.sum(gate * gate_dots, axis=-1, keepdims=True)
        prob_grad = jnp.where(mask, pick_grad / pick_total, 0.0)
        logit_grad = probs_router * (
            prob_grad - jnp.sum(probs_router * prob_grad, axis=-1, keepdims=True)
        )
        logit_low = logit_grad.astype(bf16)
        grad_router = dot("td,te->de", h2, logit_low)

        back_full = back_full + dot("te,de->td", logit_low, router)
        grad_own = lax.dynamic_slice_in_dim(grad_all, col_index, 1, 0)[0].astype(f32)
        grad_gain_two = jnp.sum(back_full * base_second, axis=0)
        scaled_two = back_full * gain_two
        middle_grad = (
            inv_second
            * (scaled_two - base_second * jnp.mean(scaled_two * base_second, axis=-1, keepdims=True))
            + grad_own
        )
        attn_grad = middle_grad.astype(bf16)
        grad_out = dot("td,tk->dk", attn_grad, heads).astype(bf16)

        heads_grad = to_grid(dot("td,dk->tk", attn_grad, out_weights).astype(bf16))
        value_grad = dot("shrk,shrd->skhd", probs, heads_grad)
        weight_grad = dot("shrd,skhd->shrk", heads_grad, value_all)
        probs_wide = probs.astype(f32)
        delta = jnp.sum(probs_wide * weight_grad, axis=-1, keepdims=True)
        score_grad = (probs_wide * (weight_grad - delta)).astype(bf16)
        query_grad = from_grid(dot("shrk,skhd->shrd", score_grad, key_all)) * scale
        key_grad = dot("shrk,shrd->skhd", score_grad, query_grid) * scale
        kv_grad = jnp.concatenate(
            [key_grad.reshape(seqs, full_len, kv_width), value_grad.reshape(seqs, full_len, kv_width)],
            axis=2,
        ).astype(bf16)
        kv_grad = jnp.swapaxes(kv_grad.reshape(seqs, cols, local_len, 2 * kv_width), 0, 1)
        kv_share = scatter_col(kv_grad.reshape(cols, toks, 2 * kv_width)).astype(f32)
        qk_grad = rotate(
            jnp.concatenate([query_grad, kv_share[:, :kv_width]], axis=1), cosine, -sine
        )
        qkv_grad = jnp.concatenate([qk_grad, kv_share[:, kv_width:]], axis=1).astype(bf16)
        first_grad = dot("tk,bk->tb", qkv_grad, qkv_weights).astype(bf16)
        first_grad = lax.psum(first_grad, "row").astype(f32)
        grad_gain_one = jnp.sum(first_grad * base_first, axis=0)
        scaled_one = first_grad * gain_one
        token_grad = (
            inv_first
            * (scaled_one - base_first * jnp.mean(scaled_one * base_first, axis=-1, keepdims=True))
            + middle_grad
        )
        grad_first = jnp.concatenate(
            [
                dot("tb,tk->bk", h1, qkv_grad),
                grad_router,
                grad_gain_one[:, None],
                grad_gain_two[:, None],
                jnp.zeros((width, LANES - experts - 2), f32),
            ],
            axis=1,
        ).astype(bf16)
        out_slice = scatter_all(part_out).astype(f32)
        share_out = scatter_col(grad_out.reshape(cols, rows_w, q_width)).astype(f32)
        share_first = scatter_col(grad_first.reshape(cols, rows_w, -1)).astype(f32)
        share_qkv, share_misc = share_first[:, :qkv_width], share_first[:, qkv_width:]
    if kernels:
        out_slice = out_slice.T
    middle_slice = lax.dynamic_slice_in_dim(middle, row_index * row_width, row_width, 1)
    block_out = (middle_slice + out_slice).astype(bf16)

    def tokens_first(a):
        return jnp.swapaxes(a.reshape(seqs, local_len, a.shape[1]), 0, 1)

    return (
        tokens_first(block_out),
        tokens_first(token_grad),
        share_misc[:, experts],
        share_qkv[:, :q_width],
        share_qkv[:, q_width : q_width + kv_width],
        share_qkv[:, q_width + kv_width :],
        share_out.T,
        share_misc[:, experts + 1],
        share_misc[:, :experts],
        share_sgate,
        share_sup,
        share_sdown.T,
        *expert_grads,
    )


def solution(mesh):
    in_specs = (
        P("col", None, None),
        P("col", None),
        P("col", None, None),
        P("col"),
        P("col", "row"),
        P("col", "row"),
        P("col", "row"),
        P("row", "col"),
        P("col"),
        P("col", None),
        P("col", "row"),
        P("col", "row"),
        P("row", "col"),
        P("col", None, "row"),
        P("col", None, "row"),
        P("col", "row", None),
        P("col", None, "row"),
    )
    out_specs = (
        P("col", None, "row"),
        P("col", None, None),
        P("col"),
        P("col", "row"),
        P("col", "row"),
        P("col", "row"),
        P("row", "col"),
        P("col"),
        P("col", None),
        P("col", "row"),
        P("col", "row"),
        P("row", "col"),
        P("col", None, "row"),
        P("col", None, "row"),
        P("col", "row", None),
    )
    return jax.shard_map(
        on_device, mesh=mesh, in_specs=in_specs, out_specs=out_specs, check_vma=False
    )
```

```python
import functools
import math

import jax
import jax.numpy as jnp
from jax import lax
from jax.experimental import pallas as pl
from jax.experimental.pallas import tpu as pltpu
from jax.sharding import PartitionSpec as P

HEAD_DIM = 128
LANES = 128


norm_eps = 1e-05
rope_base = 500000.0
masked_score = -1e30

f32 = jnp.float32
bf16 = jnp.bfloat16
MESH = pl.DeviceIdType.MESH


def dot(form, left, right):
    return jnp.einsum(form, left, right, preferred_element_type=f32)


def rope_tables(start_place, local_len, head_size):
    places = (start_place + jnp.arange(local_len, dtype=jnp.int32)).astype(f32)
    frequency = jnp.power(
        rope_base, -jnp.arange(0, head_size, 2, dtype=jnp.int32).astype(f32) / head_size
    )
    angles = places[:, None] * frequency[None, :]
    return (jnp.cos(angles), jnp.sin(angles))


def rotate(field, cosine, sine):
    half = cosine.shape[1]
    parts = []
    for start in range(0, field.shape[1], 2 * half):
        front = field[:, start : start + half]
        back = field[:, start + half : start + 2 * half]
        parts.append(front * cosine - back * sine)
        parts.append(back * cosine + front * sine)
    return jnp.concatenate(parts, axis=1)


def rms_scale(values_in):
    return lax.rsqrt(jnp.mean(values_in * values_in, axis=-1, keepdims=True) + norm_eps)


def silu_parts(pre_gate):
    sigmoid_gate = jax.nn.sigmoid(pre_gate)
    silu_gate = pre_gate * sigmoid_gate
    slope_gate = sigmoid_gate * (1.0 + pre_gate * (1.0 - sigmoid_gate))
    return (silu_gate, slope_gate)


def gather_col(part):
    return lax.all_gather(part, "col", axis=0, tiled=False)


def scatter_col(blocks):
    flat = blocks.reshape(-1, blocks.shape[-1])
    return lax.psum_scatter(flat, "col", scatter_dimension=0, tiled=True)


def gather_all(part):
    got = lax.all_gather(part, ("col", "row"), axis=0, tiled=False)
    cols, rows = lax.axis_size("col"), lax.axis_size("row")
    got = got.reshape(cols, rows, *part.shape).transpose(0, 2, 1, 3)
    return got.reshape(cols, part.shape[0], rows * part.shape[1])


def scatter_all(blocks):
    flat = blocks.reshape(-1, blocks.shape[-1])
    part = lax.psum_scatter(flat, "row", scatter_dimension=1, tiled=True)
    return lax.psum_scatter(part, "col", scatter_dimension=0, tiled=True)


def swap_col(blocks):
    return lax.all_to_all(blocks, "col", split_axis=0, concat_axis=0, tiled=True)


class Net:
    def __init__(self, cols, send_sems, recv_sems):
        self.send_sems, self.recv_sems, self.used, self.sent = send_sems, recv_sems, 0, []
        self.cols, self.high_count = cols, cols // 2
        self.me = lax.axis_index("col")
        self.high, self.low = self.me // 2, self.me % 2
        self.row = lax.axis_index("row")
        self.outer, self.core = self.row // 2, self.row % 2

    def block(self, step, other=False):
        high = lax.rem(self.high + self.high_count - step, self.high_count)
        return 2 * high + (1 - self.low if other else self.low)

    def block_ahead(self, step, other=False):
        high = lax.rem(self.high + step, self.high_count)
        return 2 * high + (1 - self.low if other else self.low)

    def z_peer(self, step):
        return {"col": self.block_ahead(step)}

    def y_peer(self):
        return {"col": 2 * self.high + 1 - self.low}

    def x_peer(self):
        return {"row": 2 * (1 - self.outer) + self.core}

    def core_peer(self):
        return {"row": 2 * self.outer + 1 - self.core}

    def col_peer(self, step):
        return {"col": lax.rem(self.me + step, self.cols)}

    def greet(self, peers):
        barrier = pltpu.get_barrier_semaphore()
        for peer in peers:
            pl.semaphore_signal(barrier, inc=1, device_id=peer, device_id_type=MESH)
        pl.semaphore_wait(barrier, len(peers))

    def send(self, source, target, peer):
        copy = pltpu.make_async_remote_copy(
            src_ref=source,
            dst_ref=target,
            send_sem=self.send_sems.at[self.used],
            recv_sem=self.recv_sems.at[self.used],
            device_id=peer,
            device_id_type=MESH,
        )
        self.used += 1
        copy.start()
        self.sent.append(copy)
        return copy

    def left(self, copy):
        copy.wait_send()
        self.sent = [other for other in self.sent if other is not copy]

    def finish(self):
        for copy in self.sent:
            copy.wait_send()


def col_peers(net):
    return [net.z_peer(step) for step in range(1, net.high_count)] + [net.y_peer()]


def row_peers(net):
    return [net.x_peer(), net.core_peer()]


def add_rows(target, terms):
    rows = target.shape[0]
    piece = 32 if rows % 32 == 0 else 16

    def body(index, carry):
        at = pl.ds(pl.multiple_of(index * piece, piece), piece)
        total = terms[0][at, :].astype(f32)
        for term in terms[1:]:
            total = total + term[at, :].astype(f32)
        target[at, :] = total.astype(target.dtype)
        return carry

    lax.fori_loop(0, rows // piece, body, 0)


def dot_nn(left, right):
    return lax.dot_general(left, right, (((1,), (0,)), ((), ())), preferred_element_type=f32)


def dot_nt(left, right):
    return lax.dot_general(left, right, (((1,), (1,)), ((), ())), preferred_element_type=f32)


def dot_tn(left, right):
    return lax.dot_general(left, right, (((0,), (0,)), ((), ())), preferred_element_type=f32)


def each_tile(count, body):
    def step(index, carry):
        body(index)
        return carry

    lax.fori_loop(0, count, step, 0)


TILE = 512
WIDE = 1280


def tile_at(index, tile=TILE):
    if isinstance(index, int):
        return pl.ds(index * tile, tile)
    return pl.ds(pl.multiple_of(index * tile, tile), tile)


class Line:
    def __init__(self, net, items, direct=(), direct_from=0):
        self.net, self.items, self.direct, self.direct_from = net, items, list(direct), direct_from
        self.other_row = 2 * (1 - net.outer) + net.core
        self.along_z, self.along_y, self.along_x, self.to_core = {}, {}, {}, {}
        self.moved = []
        self.now = 0

    def in_chip(self, q, step, other, source, slot):
        if self.items[q][2]:
            self.along_x[q, step, other] = self.net.send(source, slot, self.net.x_peer())
            self.to_core[q, step, other] = self.net.send(source, slot, self.net.core_peer())

    def start(self, q):
        net = self.net
        source, slot_of, _ = self.items[q]
        slot = slot_of(net.me, net.row)
        for step in reversed(range(1, net.high_count)):
            self.along_z[q, step] = net.send(source, slot, net.z_peer(step))
        self.along_y[q, 0] = net.send(source, slot, net.y_peer())
        self.in_chip(q, 0, False, source, slot)

    def after_z(self, q):
        net = self.net
        for step in reversed(range(1, net.high_count)):
            self.along_z[q, step].wait_recv()
            slot = self.items[q][1](net.block(step), net.row)
            self.along_y[q, step] = net.send(slot, slot, net.y_peer())
            self.in_chip(q, step, False, slot, slot)

    def after_y(self, q):
        net = self.net
        for step in range(net.high_count):
            self.along_y[q, step].wait_recv()
            slot = self.items[q][1](net.block(step, True), net.row)
            self.in_chip(q, step, True, slot, slot)

    def after_x(self, q):
        net = self.net
        if self.items[q][2]:
            for other in (False, True):
                for step in range(net.high_count):
                    self.along_x[q, step, other].wait_recv()
                    slot = self.items[q][1](net.block(step, other), self.other_row)
                    self.moved.append(net.send(slot, slot, net.core_peer()))

    def tick(self, count=1):
        net = self.net
        for _ in range(count):
            now, self.now = self.now, self.now + 1
            if now < len(self.items):
                if now >= 2:
                    for step in range(1, net.high_count):
                        net.left(self.along_z[now - 2, step])
                self.start(now)
            if now >= self.direct_from and self.direct:
                self.moved.append(net.send(*self.direct.pop(0)))
            for stage, lag in ((self.after_z, 1), (self.after_y, 2), (self.after_x, 3)):
                if 0 <= now - lag < len(self.items):
                    stage(now - lag)

    def drain(self):
        while self.now < len(self.items) + 3 or self.direct:
            self.tick()
        for copy in [*self.moved, *self.to_core.values()]:
            copy.wait_recv()


def front_kernel(
    cols,
    experts,
    tokens,
    query,
    key,
    value,
    misc,
    out_own,
    shared_own,
    grad_own,
    table_row,
    table_col,
    doc_col,
    cosine,
    sine,
    weights,
    out_weights,
    shared_all,
    grad_all,
    rows_all,
    cols_all,
    h1,
    q_low,
    kv_all,
    probs,
    heads,
    attn,
    h2,
    gate,
    router_probs,
    gains,
    inverse,
    kv_low,
    keys,
    values,
    bias,
    partial,
    from_core,
    to_x,
    from_x,
    send_sems,
    recv_sems,
    local_sems,
):
    net = Net(cols, send_sems, recv_sems)
    toks, width = tokens.shape
    size = HEAD_DIM
    q_width = q_low.shape[1]
    group = q_width // size
    rows_w = query.shape[0]
    seqs = probs.shape[0]
    local_len = toks // seqs
    full_len = local_len * cols
    scale = 1.0 / math.sqrt(size)
    mine = pl.ds(pl.multiple_of(net.me * rows_w, 16), rows_w)

    copies = []

    def local_copy(source, target):
        copy = pltpu.make_async_copy(source, target, local_sems.at[len(copies)])
        copy.start()
        copies.append(copy)

    local_copy(query, weights.at[mine, pl.ds(0, q_width)])
    local_copy(key, weights.at[mine, pl.ds(q_width, size)])
    local_copy(value, weights.at[mine, pl.ds(q_width + size, size)])
    local_copy(misc, weights.at[mine, pl.ds(q_width + 2 * size, LANES)])
    first = len(copies)
    local_copy(out_own, out_weights.at[mine])
    local_copy(shared_own.at[net.me], shared_all.at[net.me])
    part = grad_own.shape[1]
    local_copy(
        grad_own, grad_all.at[net.me, :, pl.ds(pl.multiple_of(net.row * part, LANES), part)]
    )
    local_copy(table_row, rows_all.at[net.me])
    local_copy(table_col, cols_all.at[net.me])
    net.greet([net.col_peer(step) for step in range(1, cols)] + row_peers(net))
    for copy in copies[:first]:
        copy.wait()

    def weight_slot(target, start, count):
        def slot(block, row):
            return target.at[pl.ds(pl.multiple_of(block * rows_w + start, 16), count)]

        return slot

    def grad_slot(start, count):
        def slot(block, row):
            return grad_all.at[
                block, pl.ds(start, count), pl.ds(pl.multiple_of(row * part, LANES), part)
            ]

        return slot

    items = [(table_row, lambda block, row: rows_all.at[block], False)]
    pieces, out_pieces, grad_pieces = 5, 4, 4
    count = rows_w // pieces
    for q in range(pieces):
        slot = weight_slot(weights, q * count, count)
        items.append((slot(net.me, net.row), slot, False))
    ready_weights = len(items) + 2
    out_items, grad_items = [], []
    count = rows_w // out_pieces
    for q in range(out_pieces):
        slot = weight_slot(out_weights, q * count, count)
        out_items.append((out_own.at[pl.ds(q * count, count)], slot, False))
    count = toks // grad_pieces
    for q in range(grad_pieces):
        grad_items.append((grad_own.at[pl.ds(q * count, count)], grad_slot(q * count, count), True))
    items += out_items[:2]
    for q in range(2, out_pieces):
        items += [grad_items[q - 2], out_items[q]]
    ready_out = len(items) + 2
    items += grad_items[out_pieces - 2 :]
    items.append((table_col, lambda block, row: cols_all.at[block], False))
    direct = []
    for step in range(1, cols):
        block = lax.rem(net.me + step, cols)
        direct.append((shared_own.at[block], shared_all.at[net.me], net.col_peer(step)))
    line = Line(net, items, direct, ready_weights - 2)

    line.tick(2)
    copies[first + 3].wait()

    def chunks(body, rows=32):
        def step(index, carry):
            body(pl.ds(pl.multiple_of(index * rows, rows), rows))
            return carry

        lax.fori_loop(0, toks // rows, step, 0)

    def measure_first(at):
        x = tokens[at, :].astype(f32)
        total = jnp.sum(x * x, axis=1, keepdims=True)
        inverse[at, :] = jnp.broadcast_to(lax.rsqrt(total / width + norm_eps), (32, LANES))

    chunks(measure_first)
    line.tick(ready_weights - line.now)

    start = q_width + 2 * size
    for tile in range(width // TILE):
        at = pl.ds(tile * TILE, TILE)
        turned = jnp.transpose(weights[at, start : start + LANES].astype(f32))
        gains[:, at] = turned[experts : experts + 8]

    def norm_first(at):
        x = tokens[at, :].astype(f32) * inverse[at, 0:1]
        h1[at, :] = (x * gains[0:1, :]).astype(bf16)

    chunks(norm_first)
    line.tick()
    heads_all = group + 2
    for head in range(heads_all - 1, -1, -1):
        raw = dot_nn(h1[...], weights[:, head * size : (head + 1) * size])
        if head <= group:
            raw = raw * cosine[...] + pltpu.roll(raw, size // 2, 1) * sine[...]
        if head < group:
            q_low[:, head * size : (head + 1) * size] = raw.astype(bf16)
        else:
            kv_low[:, (head - group) * size : (head - group + 1) * size] = raw.astype(bf16)
        if head == group:
            kv_all[net.me] = kv_low[...]

            def kv_slot(s):
                rows = pl.ds(s * local_len, local_len)
                return lambda block, row: kv_all.at[block, rows]

            kv_line = Line(
                net,
                [
                    (kv_low.at[pl.ds(s * local_len, local_len)], kv_slot(s), False)
                    for s in range(seqs)
                ],
            )
            kv_line.tick()
        if head == group // 2:
            kv_line.tick()
    line.tick()
    kv_line.tick()

    for s in range(seqs):
        if s:
            kv_line.tick()
        rows = pl.ds(s * local_len, local_len)
        place = lax.broadcasted_iota(jnp.int32, (local_len, local_len), 0)
        lane = lax.broadcasted_iota(jnp.int32, (local_len, local_len), 1)
        for c in range(cols):
            at = pl.ds(c * local_len, local_len)
            keys[at, :] = kv_all[c, rows, :size]
            values[at, :] = kv_all[c, rows, size:]
            same = doc_col[rows, :] == rows_all[c, experts : experts + 1, rows]
            ahead = (c - net.me) * local_len
            allowed = same & (lane + ahead <= place)
            bias[:, at] = jnp.where(allowed, 0.0, masked_score)

        def attend(g, carry, s=s, rows=rows):
            at = pl.ds(pl.multiple_of(g * size, size), size)
            scores = dot_nt(q_low[rows, at], keys[...]) * scale + bias[...]
            weight = jnp.exp(scores - jnp.max(scores, axis=1, keepdims=True))
            p = (weight / jnp.sum(weight, axis=1, keepdims=True)).astype(bf16)
            probs[s, g] = p
            heads[rows, at] = dot_nn(p, values[...]).astype(bf16)
            return carry

        lax.fori_loop(0, group, attend, 0)
        if line.now < ready_out:
            line.tick()
    line.tick(max(0, ready_out - line.now))
    copies[first].wait()

    pieces = from_core.shape[0]
    piece_rows = from_core.shape[1]

    def row_piece(core, i):
        return pl.ds(
            pl.multiple_of((core * pieces + i) * piece_rows, piece_rows), piece_rows
        )

    half = pieces * piece_rows
    across = []
    for core in (1 - net.core, net.core):
        at_rows = pl.ds(pl.multiple_of(core * half, half), half)
        for tile in range(width // TILE):
            at = pl.ds(tile * TILE, TILE)
            partial[at_rows, at] = dot_nt(heads[at_rows, :], out_weights[at, :]).astype(bf16)
        if not across:
            across = [
                net.send(partial.at[row_piece(1 - net.core, i)], from_core.at[i], net.core_peer())
                for i in range(pieces)
            ]
    along, back = [], []
    for i in range(pieces):
        across[i].wait_recv()
        add_rows(to_x.at[i], [partial.at[row_piece(net.core, i)], from_core.at[i]])
        along.append(net.send(to_x.at[i], from_x.at[i], net.x_peer()))
    line.tick()
    for i in range(pieces):
        along[i].wait_recv()
        at = row_piece(net.core, i)
        add_rows(attn.at[at], [to_x.at[i], from_x.at[i]])
        back.append(net.send(attn.at[at], attn.at[at], net.core_peer()))
    line.tick()
    for copy in back:
        copy.wait_recv()

    def norm_second(at):
        x = tokens[at, :].astype(f32) + attn[at, :].astype(f32)
        total = jnp.sum(x * x, axis=1, keepdims=True)
        h2[at, :] = (x * lax.rsqrt(total / width + norm_eps) * gains[1:2, :]).astype(bf16)

    chunks(norm_second)
    line.tick()
    logits = dot_nn(h2[...], weights[:, start : start + LANES])
    lane = lax.broadcasted_iota(jnp.int32, (toks, LANES), 1)
    logits = jnp.where(lane < experts, logits, masked_score)
    weight = jnp.exp(logits - jnp.max(logits, axis=1, keepdims=True))
    chance = weight / jnp.sum(weight, axis=1, keepdims=True)
    router_probs[...] = chance
    picked = jnp.where((table_col[...] > 0) & (lane < experts), chance, 0.0)
    gate[...] = picked / jnp.sum(picked, axis=1, keepdims=True)
    line.drain()
    kv_line.drain()
    for copy in [*copies[first + 1 : first + 3], copies[first + 4]]:
        copy.wait()
    net.finish()


def front_call(
    cols, collective_id, experts, tokens, query, key, value, misc, out_own, shared_own, grad_own,
    table_row, table_col, doc_col, cosine, sine, seqs,
):
    toks, width = tokens.shape
    q_width = query.shape[1]
    size = HEAD_DIM
    local_len = toks // seqs
    vmem, any_space = pl.BlockSpec(memory_space=pltpu.VMEM), pl.BlockSpec(memory_space=pl.ANY)

    def shape(*dims, dtype=bf16):
        return jax.ShapeDtypeStruct(dims, dtype)

    pieces = 4
    piece = (pieces, toks // 2 // pieces, width)
    copies = 320
    return pl.pallas_call(
        functools.partial(front_kernel, cols, experts),
        out_shape=[
            shape(width, q_width + 2 * size + LANES),
            shape(width, q_width),
            shape(*shared_own.shape),
            shape(cols, toks, width),
            shape(cols, *table_row.shape, dtype=f32),
            shape(cols, *table_col.shape),
            shape(toks, width),
            shape(toks, q_width),
            shape(cols, toks, 2 * size),
            shape(seqs, q_width // size, local_len, cols * local_len),
            shape(toks, q_width),
            shape(toks, width),
            shape(toks, width),
            shape(toks, LANES, dtype=f32),
            shape(toks, LANES, dtype=f32),
        ],
        in_specs=[vmem] + [any_space] * 7 + [vmem] * 5,
        out_specs=[vmem, vmem, any_space, any_space] + [vmem] * 11,
        scratch_shapes=[
            pltpu.VMEM((8, width), f32),
            pltpu.VMEM((toks, LANES), f32),
            pltpu.VMEM((toks, 2 * size), bf16),
            pltpu.VMEM((cols * local_len, size), bf16),
            pltpu.VMEM((cols * local_len, size), bf16),
            pltpu.VMEM((local_len, cols * local_len), f32),
            pltpu.VMEM((toks, width), bf16),
            pltpu.VMEM(piece, bf16),
            pltpu.VMEM(piece, bf16),
            pltpu.VMEM(piece, bf16),
            pltpu.SemaphoreType.DMA((copies,)),
            pltpu.SemaphoreType.DMA((copies,)),
            pltpu.SemaphoreType.DMA((16,)),
        ],
        compiler_params=pltpu.CompilerParams(
            collective_id=collective_id, has_side_effects=True, vmem_limit_bytes=48 << 20
        ),
        name=f"front_{collective_id}",
    )(
        tokens, query, key, value, misc, out_own, shared_own, grad_own,
        table_row, table_col, doc_col, cosine, sine,
    )


def experts_kernel(
    cols,
    capacity,
    h2,
    grads,
    w_gate,
    w_up,
    w_down,
    w_shared,
    rank_row,
    rank_col,
    gate_own,
    out_part,
    back,
    g_gate,
    g_up,
    g_down,
    g_shared,
    gate_dots,
    h2_all,
    xs_all,
    cs_all,
    wgu,
    wd,
    ws,
    gates,
    hb,
    xbuf,
    ybuf,
    obuf,
    part,
    pre,
    gcol,
    dcol,
    dz_all,
    zg_all,
    dgu_all,
    sdz_all,
    sz_all,
    sgu_all,
    from_core,
    from_x,
    from_y,
    from_z,
    kept,
    dots,
    dots_core,
    dots_x,
    tiles,
    tiles_all,
    stage,
    stage_low,
    send_sems,
    recv_sems,
    local_sems,
):
    net = Net(cols, send_sems, recv_sems)
    toks, width = h2.shape
    exp_local, _, hidden = w_gate.shape
    high = net.high_count
    pad = ws.shape[1] // 3
    slots = exp_local * capacity
    pair = 2 * capacity
    piece = width // lax.axis_size("row")
    share = width // LANES // 5 * LANES
    rest = (width - 4 * share) // 2
    wide = width // TILE
    net.greet([net.col_peer(step) for step in range(1, cols)] + row_peers(net))

    def local_copy(source, target, index):
        copy = pltpu.make_async_copy(source, target, local_sems.at[index])
        copy.start()
        return copy

    gate_copies = [
        net.send(gate_own, gates.at[net.me], net.col_peer(step)) for step in range(1, cols)
    ]
    gates[net.me] = gate_own[...]

    def feature_e(row):
        return pl.ds(pl.multiple_of(row * share, LANES), share)

    def feature_r(core):
        return pl.ds(pl.multiple_of(4 * share + core * rest, LANES), rest)

    own_e, own_r = feature_e(net.row), feature_r(net.core)
    far_e = feature_e(2 * (1 - net.outer) + net.core)

    def pass_on(source, block, features, peer):
        return net.send(source.at[..., features], h2_all.at[block, :, features], peer)

    along_z, along_y, along_x, to_core = {}, {}, {}, {}

    def start_z(step):
        along_z[step] = [
            pass_on(h2, net.me, own_e, net.z_peer(high - step)),
            pass_on(h2, net.me, own_r, net.z_peer(high - step)),
        ]

    start_z(1)
    along_y[0] = [
        pass_on(h2, net.me, own_e, net.y_peer()),
        pass_on(h2, net.me, own_r, net.y_peer()),
    ]

    def block_of(step, other):
        return net.block_ahead(step, other)

    def share_in_chip(step, other):
        block = block_of(step, other)
        source = h2_all.at[block]
        along_x[step, other] = pass_on(source, block, own_e, net.x_peer())
        to_core[step, other] = [
            pass_on(source, block, own_e, net.core_peer()),
            pass_on(source, block, own_r, net.core_peer()),
        ]

    def arrived_y(step):
        for copy in along_y[step]:
            copy.wait_recv()
        share_in_chip(step, True)

    def arrived_z(step):
        for copy in along_z[step]:
            copy.wait_recv()
        block = block_of(step, False)
        along_y[step] = [
            pass_on(h2_all.at[block], block, own_e, net.y_peer()),
            pass_on(h2_all.at[block], block, own_r, net.y_peer()),
        ]
        share_in_chip(step, False)

    def arrived_x(step, other):
        along_x[step, other].wait_recv()
        block = block_of(step, other)
        to_core[step, other].append(pass_on(h2_all.at[block], block, far_e, net.core_peer()))

    def whole(step, other):
        for copy in to_core[step, other]:
            copy.wait_recv()

    events = [functools.partial(arrived_y, 0)]
    for step in range(1, high):
        events.append(functools.partial(arrived_z, step))
        events.append(functools.partial(arrived_x, step - 1, True))
        events.append(functools.partial(arrived_y, step))
        events.append(functools.partial(arrived_x, step, False))
    events.append(functools.partial(arrived_x, high - 1, True))
    events = iter(events)

    def pump(count=1):
        for _ in range(count):
            event = next(events, None)
            if event is not None:
                event()

    loads = []
    for e in range(exp_local):
        loads.append(local_copy(w_down.at[e], wd.at[e], 3 * e))
        loads.append(local_copy(w_gate.at[e], wgu.at[e, :, pl.ds(0, hidden)], 3 * e + 1))
        loads.append(local_copy(w_up.at[e], wgu.at[e, :, pl.ds(hidden, hidden)], 3 * e + 2))
    base = 3 * exp_local
    loads.append(local_copy(w_shared, ws, base))
    keep_own = local_copy(h2, h2_all.at[net.me], base + 1)
    base += 2

    def load_pair(source, step):
        first = local_copy(source.at[block_of(step, False)], hb.at[0], base)
        second = local_copy(source.at[block_of(step, True)], hb.at[1], base + 1)
        first.wait()
        second.wait()

    slot_row = lax.broadcasted_iota(jnp.int32, (capacity, toks), 0).astype(f32) + 1.0
    slot_lane = lax.broadcasted_iota(jnp.int32, (toks, capacity), 1).astype(f32) + 1.0

    def chosen(block, e):
        return rank_row[block, e : e + 1, :] == slot_row

    def picks(block):
        rows = [
            jnp.where(chosen(block, e), 1.0, 0.0).astype(bf16) for e in range(exp_local)
        ]
        return jnp.concatenate(rows, axis=0)

    def picks_back(block):
        lanes = [
            jnp.where(rank_col[block, :, e : e + 1] == slot_lane, 1.0, 0.0).astype(bf16)
            for e in range(exp_local)
        ]
        return jnp.concatenate(lanes, axis=1)

    def dispatch(step):
        for b in (0, 1):
            table = picks(block_of(step, b == 1))

            def tile(index, b=b, table=table):
                at = tile_at(index, WIDE)
                rows = dot_nn(table, hb[b, :, at]).astype(bf16)
                for e in range(exp_local):
                    xbuf[e, pl.ds(b * capacity, capacity), at] = rows[
                        e * capacity : (e + 1) * capacity
                    ]

            each_tile(width // WIDE, tile)

    def save_rows(target, step):
        return [
            local_copy(
                xbuf.at[e], target.at[e, pl.ds(step * pair, pair)], base + 2 + e
            )
            for e in range(exp_local)
        ]

    saved = []
    for step in range(high):
        load_pair(grads, step)
        if step == 0:
            for copy in loads:
                copy.wait()
        for copy in saved:
            copy.wait()
        dispatch(step)
        saved = save_rows(cs_all, step)
        for e in range(exp_local):
            dz_all[e, pl.ds(step * pair, pair), :] = dot_nt(xbuf[e], wd[e]).astype(bf16)
        for b in (0, 1):
            sdz_all[block_of(step, b == 1)] = dot_nn(hb[b], ws[:, 2 * pad :]).astype(bf16)
        if step + 2 < high:
            for copy in along_z[step + 1]:
                net.left(copy)
            start_z(step + 2)
        pump()
    for copy in gate_copies:
        copy.wait_recv()
    keep_own.wait()

    across, onward, upward, far_z = {}, {}, {}, {}

    def features(row):
        return pl.ds(pl.multiple_of(row * piece, LANES), piece)

    other_row = 2 * (1 - net.outer) + net.core

    def hand_over(step):
        for b in (1, 0):
            for far in (1, 0):
                outer = 1 - net.outer if far else net.outer
                source = part.at[b, :, features(2 * outer + 1 - net.core)]
                across[step, b, far] = net.send(
                    source, from_core.at[far, step, b], net.core_peer()
                )

    def sum_cores(step):
        for b in (1, 0):
            for far, row in ((1, other_row), (0, net.row)):
                across[step, b, far].wait_recv()
                slot = from_core.at[far, step, b]
                add_rows(slot, [part.at[b, :, features(row)], slot])
                if far:
                    onward[step, b] = net.send(slot, from_x.at[step, b], net.x_peer())
        for b in (1, 0):
            for far in (1, 0):
                net.left(across[step, b, far])

    def sum_chips(step):
        for b in (1, 0):
            onward[step, b].wait_recv()
            slot = from_core.at[0, step, b]
            add_rows(slot, [slot, from_x.at[step, b]])
            if b:
                upward[step] = net.send(slot, from_y.at[step], net.y_peer())

    def sum_plane(step):
        upward[step].wait_recv()
        slot = from_core.at[0, step, 0]
        add_rows(slot, [slot, from_y.at[step]])
        if step:
            far_z[step] = net.send(slot, from_z.at[step - 1], net.z_peer(step))

    own_expert = lax.rem(net.me, cols) * exp_local
    gate_rows = gates.shape[1]
    gate_row = lax.broadcasted_iota(jnp.int32, (gate_rows, toks), 0)
    dots[...] = jnp.zeros_like(dots)
    for step in range(high):
        if step:
            whole(step, False)
        whole(step, True)
        load_pair(h2_all, step)
        for copy in saved:
            copy.wait()
        dispatch(step)
        saved = save_rows(xs_all, step)
        pump()
        for b in (0, 1):
            block = block_of(step, b == 1)
            inner = dot_nn(hb[b], ws[:, : 2 * pad])
            sa, su = inner[:, :pad], inner[:, pad:]
            sig = 1.0 / (1.0 + jnp.exp(-sa))
            silu = sa * sig
            slope = sig * (1.0 + sa * (1.0 - sig))
            sz_all[block] = (silu * su).astype(bf16)
            sdz = sdz_all[block].astype(f32)
            sgu_all[block, :, :pad] = (sdz * su * slope).astype(bf16)
            sgu_all[block, :, pad:] = (sdz * silu).astype(bf16)
        if step:
            sum_cores(step - 1)
        rows = pl.ds(step * pair, pair)
        for e in range(exp_local):
            pre[...] = dot_nn(xbuf[e], wgu[e])
            for b in (0, 1):
                block = block_of(step, b == 1)
                gate = jnp.sum(
                    jnp.where(gate_row == own_expert + e, gates[block], 0.0), axis=0, keepdims=True
                )
                gate = jnp.sum(jnp.where(chosen(block, e), gate, 0.0), axis=1, keepdims=True)
                gcol[pl.ds(b * capacity, capacity), :] = jnp.broadcast_to(gate, (capacity, LANES))

            def gating(index, e=e, step=step):
                at = pl.ds(pl.multiple_of(index * 32, 32), 32)
                saved_at = pl.ds(pl.multiple_of(step * pair + index * 32, 32), 32)
                a, u = pre[at, :hidden], pre[at, hidden:]
                gate = jnp.concatenate([gcol[at, :]] * (hidden // LANES), axis=1)
                dz = dz_all[e, saved_at, :].astype(f32)
                sig = 1.0 / (1.0 + jnp.exp(-a))
                silu = a * sig
                slope = sig * (1.0 + a * (1.0 - sig))
                z = silu * u
                dcol[at, :] = jnp.broadcast_to(
                    jnp.sum(z * dz, axis=1, keepdims=True), (32, LANES)
                )
                zg_all[e, saved_at, :] = (z * gate).astype(bf16)
                dz = dz * gate
                dgu_all[e, saved_at, :hidden] = (dz * u * slope).astype(bf16)
                dgu_all[e, saved_at, hidden:] = (dz * silu).astype(bf16)

            each_tile(pair // 32, gating)
            for b in (0, 1):
                block = block_of(step, b == 1)
                col = dcol[pl.ds(b * capacity, capacity), :]
                col = jnp.concatenate([col] * (toks // LANES), axis=1)
                dots[block, e : e + 1, :] = jnp.sum(
                    jnp.where(chosen(block, e), col, 0.0), axis=0, keepdims=True
                )

            def out_tile(index, e=e):
                at = tile_at(index, WIDE)
                y = dot_nn(zg_all[e, rows, :], wd[e, :, at]).astype(bf16)
                for b in (0, 1):
                    ybuf[b, pl.ds(e * capacity, capacity), at] = y[b * capacity : (b + 1) * capacity]

            each_tile(width // WIDE, out_tile)
            pump()
        if step:
            for copy in out_copies:
                copy.wait()
        out_copies = []
        for b in (0, 1):
            block = block_of(step, b == 1)
            table = picks_back(block)

            def join_tile(index, b=b, table=table, block=block):
                at = tile_at(index, WIDE)
                total = dot_nn(table, ybuf[b, :, at])
                total = total + dot_nt(sz_all[block], ws[at, 2 * pad :])
                obuf[b, :, at] = total.astype(bf16)

            each_tile(width // WIDE, join_tile)
            out_copies.append(
                local_copy(obuf.at[b], out_part.at[block], base + 2 + exp_local + b)
            )
        pump()
        if step:
            sum_chips(step - 1)
        for e in range(exp_local):

            def back_tile(index, e=e):
                at = tile_at(index, WIDE)
                y = dot_nt(dgu_all[e, rows, :], wgu[e, at, :]).astype(bf16)
                for b in (0, 1):
                    ybuf[b, pl.ds(e * capacity, capacity), at] = y[b * capacity : (b + 1) * capacity]

            each_tile(width // WIDE, back_tile)
        pump()
        for b in (1, 0):
            block = block_of(step, b == 1)
            table = picks_back(block)

            def back_join(index, b=b, table=table, block=block):
                at = tile_at(index, WIDE)
                total = dot_nn(table, ybuf[b, :, at])
                total = total + dot_nt(sgu_all[block], ws[at, : 2 * pad])
                part[b, :, at] = total.astype(bf16)

            each_tile(width // WIDE, back_join)
        hand_over(step)
        if step:
            sum_plane(step - 1)
    pump(64)
    last = high - 1
    for copy in saved + out_copies:
        copy.wait()

    load_sem, store_sem = base + 4 + exp_local, base + 6 + exp_local

    def passes(count, load, work, stores):
        def load_copy(j, slot):
            source, target = load(j, slot)
            return pltpu.make_async_copy(source, target, local_sems.at[load_sem + slot])

        def store_copies(j, slot):
            return [
                pltpu.make_async_copy(
                    source, target, local_sems.at[store_sem + 2 * slot + i]
                )
                for i, (source, target) in enumerate(stores(j, slot))
            ]

        load_copy(0, 0).start()

        def body(j):
            slot = lax.rem(j, 2)

            @pl.when(j + 1 < count)
            def _():
                load_copy(j + 1, 1 - slot).start()

            load_copy(j, slot).wait()

            @pl.when(j >= 2)
            def _():
                for copy in store_copies(j - 2, slot):
                    copy.wait()

            work(j, slot)
            for copy in store_copies(j, slot):
                copy.start()

        each_tile(count, body)
        for j in range(max(0, count - 2), count):
            for copy in store_copies(j, j % 2):
                copy.wait()

    def inner_grads(e):
        passes(
            wide,
            lambda j, slot: (
                xs_all.at[e, :, tile_at(j)],
                tiles.at[slot],
            ),
            lambda j, slot: put(stage.at[slot], dot_tn(tiles[slot], dgu_all[e]).astype(bf16)),
            lambda j, slot: [
                (stage.at[slot, :, pl.ds(0, hidden)], g_gate.at[e, tile_at(j)]),
                (stage.at[slot, :, pl.ds(hidden, hidden)], g_up.at[e, tile_at(j)]),
            ],
        )

    def put(target, value):
        target[...] = value

    def down_grads(e):
        passes(
            wide,
            lambda j, slot: (
                cs_all.at[e, :, tile_at(j)],
                tiles.at[slot],
            ),
            lambda j, slot: put(
                stage.at[slot, pl.ds(0, hidden), pl.ds(0, TILE)],
                dot_tn(zg_all[e], tiles[slot]).astype(bf16),
            ),
            lambda j, slot: [
                (
                    stage.at[slot, pl.ds(0, hidden), pl.ds(0, TILE)],
                    g_down.at[e, :, tile_at(j)],
                ),
            ],
        )

    def shared_grads(source, others, start, size):
        def work(j, slot):
            total = dot_tn(tiles_all[slot, 0], others[0])
            for c in range(1, cols):
                total = total + dot_tn(tiles_all[slot, c], others[c])
            stage_low[slot, :, :size] = total.astype(bf16)

        def load(j, slot):
            return (source.at[:, :, tile_at(j)], tiles_all.at[slot])

        passes(
            wide,
            lambda j, slot: load(j, slot),
            work,
            lambda j, slot: [
                (
                    stage_low.at[slot, :, pl.ds(0, size)],
                    g_shared.at[tile_at(j), pl.ds(start, size)],
                ),
            ],
        )

    first_dots = net.send(dots, dots_core, net.core_peer())
    inner_grads(0)
    sum_cores(last)
    first_dots.wait_recv()
    net.left(first_dots)
    dots[...] = dots[...] + dots_core[...]
    second_dots = net.send(dots, dots_x, net.x_peer())
    inner_grads(1)
    sum_chips(last)
    second_dots.wait_recv()
    dots_core[...] = dots[...] + dots_x[...]
    third_dots = []
    for step in range(1, cols):
        block = lax.rem(net.me + step, cols)
        third_dots.append(
            net.send(dots_core.at[block], gate_dots.at[net.me], net.col_peer(step))
        )
    gate_dots[net.me] = dots_core[net.me]
    down_grads(0)
    sum_plane(last)
    down_grads(1)
    for step in range(1, high):
        far_z[step].wait_recv()
    add_rows(kept, [from_core.at[0, 0, 0], *[from_z.at[step - 1] for step in range(1, high)]])
    own, other = features(net.row), features(other_row)
    back[:, own] = kept[...].astype(bf16)
    far = net.send(back.at[:, own], back.at[:, own], net.x_peer())
    near = net.send(back.at[:, own], back.at[:, own], net.core_peer())
    shared_grads(h2_all, sgu_all, 0, 2 * pad)
    far.wait_recv()
    crossed = net.send(back.at[:, other], back.at[:, other], net.core_peer())
    shared_grads(grads, sz_all, 2 * pad, pad)
    near.wait_recv()
    crossed.wait_recv()
    for copy in third_dots:
        copy.wait_recv()
    net.finish()


def experts_call(
    cols, collective_id, capacity, h2, grads, w_gate, w_up, w_down, w_shared, rank_row, rank_col, gate
):
    toks, width = h2.shape
    exp_local, _, hidden = w_gate.shape
    high = cols // 2
    pad = w_shared.shape[1] // 3
    piece = width // lax.axis_size("row")
    pair = 2 * capacity
    any_space = pl.BlockSpec(memory_space=pl.ANY)
    vmem = pl.BlockSpec(memory_space=pltpu.VMEM)
    copies = 160

    def shape(*dims, dtype=bf16):
        return jax.ShapeDtypeStruct(dims, dtype)

    return pl.pallas_call(
        functools.partial(experts_kernel, cols, capacity),
        out_shape=[
            shape(cols, toks, width),
            shape(toks, width),
            shape(exp_local, width, hidden),
            shape(exp_local, width, hidden),
            shape(exp_local, hidden, width),
            shape(width, 3 * pad),
            shape(cols, 8, toks, dtype=f32),
            shape(cols, toks, width),
            shape(exp_local, cols * capacity, width),
            shape(exp_local, cols * capacity, width),
        ],
        in_specs=[any_space] * 6 + [vmem] * 3,
        out_specs=[
            any_space,
            vmem,
            any_space,
            any_space,
            any_space,
            any_space,
            vmem,
            any_space,
            any_space,
            any_space,
        ],
        scratch_shapes=[
            pltpu.VMEM((exp_local, width, 2 * hidden), bf16),
            pltpu.VMEM((exp_local, hidden, width), bf16),
            pltpu.VMEM((width, 3 * pad), bf16),
            pltpu.VMEM((cols, *gate.shape), f32),
            pltpu.VMEM((2, toks, width), bf16),
            pltpu.VMEM((exp_local, pair, width), bf16),
            pltpu.VMEM((2, exp_local * capacity, width), bf16),
            pltpu.VMEM((2, toks, width), bf16),
            pltpu.VMEM((2, toks, width), bf16),
            pltpu.VMEM((pair, 2 * hidden), f32),
            pltpu.VMEM((pair, LANES), f32),
            pltpu.VMEM((pair, LANES), f32),
            pltpu.VMEM((exp_local, cols * capacity, hidden), bf16),
            pltpu.VMEM((exp_local, cols * capacity, hidden), bf16),
            pltpu.VMEM((exp_local, cols * capacity, 2 * hidden), bf16),
            pltpu.VMEM((cols, toks, pad), bf16),
            pltpu.VMEM((cols, toks, pad), bf16),
            pltpu.VMEM((cols, toks, 2 * pad), bf16),
            pltpu.VMEM((2, high, 2, toks, piece), bf16),
            pltpu.VMEM((high, 2, toks, piece), bf16),
            pltpu.VMEM((high, toks, piece), bf16),
            pltpu.VMEM((high - 1, toks, piece), bf16),
            pltpu.VMEM((toks, piece), f32),
            pltpu.VMEM((cols, 8, toks), f32),
            pltpu.VMEM((cols, 8, toks), f32),
            pltpu.VMEM((cols, 8, toks), f32),
            pltpu.VMEM((2, cols * capacity, TILE), bf16),
            pltpu.VMEM((2, cols, toks, TILE), bf16),
            pltpu.VMEM((2, TILE, 2 * hidden), bf16),
            pltpu.VMEM((2, TILE, 2 * pad), bf16),
            pltpu.SemaphoreType.DMA((copies,)),
            pltpu.SemaphoreType.DMA((copies,)),
            pltpu.SemaphoreType.DMA((24,)),
        ],
        compiler_params=pltpu.CompilerParams(
            collective_id=collective_id, has_side_effects=True, vmem_limit_bytes=62 << 20
        ),
        name=f"experts_{collective_id}",
    )(h2, grads, w_gate, w_up, w_down, w_shared, rank_row, rank_col, gate)


def experts_kernels(
    cols, collective_id, capacity, h2, grad_all, w_gate, w_up, w_down, shared_weights, *tables
):
    width, shared_part = shared_weights.shape[0], shared_weights.shape[1] // 3
    pad = -shared_part % LANES
    padded = jnp.pad(shared_weights.reshape(width, 3, shared_part), ((0, 0), (0, 0), (0, pad)))
    padded = padded.reshape(width, -1)
    out_part, back, g_gate, g_up, g_down, g_shared, gate_dots, *_ = experts_call(
        cols, collective_id, capacity, h2, grad_all, w_gate, w_up, w_down, padded, *tables
    )
    g_shared = g_shared.reshape(width, 3, -1)[:, :, :shared_part].reshape(width, -1)
    wide = (grad.astype(f32) for grad in (g_gate, g_up, g_down))
    return (out_part, back, gate_dots, g_shared, *wide)


def fits(cols, rows, width):
    return cols % 2 == 0 and cols * rows * width * 2 <= 12 << 20


class Sum2D:
    def __init__(self, net, source, start, count, from_y, from_z, out):
        self.net, self.source, self.start, self.count = net, source, start, count
        self.from_y, self.from_z, self.out = from_y, from_z, out
        self.rows = pl.ds(start, count)
        self.order = [*range(1, net.high_count), 0]
        self.along_y, self.along_z = {}, {}

    def mine(self, block):
        return self.source(block, self.start, self.count)

    def send_y(self):
        for step in self.order:
            source = self.mine(self.net.block_ahead(step, True))
            self.along_y[step] = self.net.send(
                source, self.from_y.at[step, self.rows], self.net.y_peer()
            )

    def send_z(self):
        for step in self.order:
            self.along_y[step].wait_recv()
            slot = self.from_y.at[step, self.rows]
            if step:
                add_rows(slot, [self.mine(self.net.block_ahead(step)), slot])
                self.along_z[step] = self.net.send(
                    slot, self.from_z.at[step - 1, self.rows], self.net.z_peer(step)
                )

    def last(self):
        for step in range(1, self.net.high_count):
            self.along_z[step].wait_recv()
        terms = [
            self.from_z.at[step - 1, self.rows] for step in range(1, self.net.high_count)
        ]
        mine = self.mine(self.net.me)
        add_rows(self.out.at[self.rows], [mine, self.from_y.at[0, self.rows], *terms])


def rear_kernel(
    cols,
    experts,
    out_part,
    back,
    gate_dots,
    gate,
    router_probs,
    table_col,
    h1,
    h2,
    tokens,
    attn,
    weights_in,
    out_weights_in,
    grads,
    heads,
    q_low,
    kv_all,
    probs,
    cosine,
    sine,
    out_slice,
    d_tokens,
    share_qkv,
    share_misc,
    share_out,
    weights,
    out_weights,
    misc,
    misc_low,
    grad_own,
    gains,
    dots,
    logit_low,
    low,
    dob,
    keys,
    values,
    stacked,
    ds_all,
    kv_grad,
    kv_share,
    dqkv,
    gain_sums,
    own,
    from_core,
    from_x,
    from_y,
    from_z,
    kv_y,
    kv_z,
    out_y,
    out_z,
    qkv_y,
    qkv_z,
    misc_y,
    misc_z,
    row_core,
    row_to,
    row_from,
    send_sems,
    recv_sems,
    local_sems,
):
    net = Net(cols, send_sems, recv_sems)
    toks, width = back.shape
    size = HEAD_DIM
    q_width = q_low.shape[1]
    group = q_width // size
    qkv_width = q_width + 2 * size
    seqs = probs.shape[0]
    local_len = toks // seqs
    rows_w = width // cols
    piece = width // lax.axis_size("row")
    scale = 1.0 / math.sqrt(size)
    other_row = 2 * (1 - net.outer) + net.core

    def local_copy(source, target, index):
        copy = pltpu.make_async_copy(source, target, local_sems.at[index])
        copy.start()
        return copy

    def features(row):
        return pl.ds(pl.multiple_of(row * piece, LANES), piece)

    loads = [
        local_copy(weights_in, weights, 0),
        local_copy(out_weights_in, out_weights, 1),
        local_copy(grads.at[net.me], grad_own, 2),
    ]
    near_load = local_copy(out_part.at[:, :, features(net.row)], own.at[0], 3)
    far_load = local_copy(out_part.at[:, :, features(other_row)], own.at[1], 4)
    net.greet(col_peers(net) + row_peers(net))

    pieces = 4
    count = toks // pieces
    order = [*range(1, net.high_count), 0]
    keys_of = [(step, True) for step in order] + [(step, False) for step in order]
    across, onward, along_y, along_z = {}, {}, {}, {}

    def rows_of(q):
        return pl.ds(q * count, count)

    def out_core(q):
        for far in (1, 0):
            outer = 1 - net.outer if far else net.outer
            for key in keys_of:
                block = net.block_ahead(*key)
                across[q, far, key] = net.send(
                    out_part.at[block, rows_of(q), features(2 * outer + 1 - net.core)],
                    from_core.at[far, block, rows_of(q)],
                    net.core_peer(),
                )

    def out_x(q):
        for key in keys_of:
            across[q, 1, key].wait_recv()
            block = net.block_ahead(*key)
            slot = from_core.at[1, block, rows_of(q)]
            add_rows(slot, [own.at[1, block, rows_of(q)], slot])
            onward[q, key] = net.send(slot, from_x.at[block, rows_of(q)], net.x_peer())

    def out_y_stage(q):
        for key in keys_of:
            across[q, 0, key].wait_recv()
            onward[q, key].wait_recv()
            block = net.block_ahead(*key)
            slot = from_core.at[0, block, rows_of(q)]
            add_rows(slot, [own.at[0, block, rows_of(q)], slot, from_x.at[block, rows_of(q)]])
            if key[1]:
                along_y[q, key[0]] = net.send(
                    slot, from_y.at[key[0], rows_of(q)], net.y_peer()
                )

    def out_z_stage(q):
        for step in order:
            along_y[q, step].wait_recv()
            slot = from_core.at[0, net.block_ahead(step), rows_of(q)]
            add_rows(slot, [slot, from_y.at[step, rows_of(q)]])
            if step:
                along_z[q, step] = net.send(
                    slot, from_z.at[step - 1, rows_of(q)], net.z_peer(step)
                )

    def out_last(q):
        for step in range(1, net.high_count):
            along_z[q, step].wait_recv()
        terms = [from_z.at[step - 1, rows_of(q)] for step in range(1, net.high_count)]
        add_rows(out_slice.at[rows_of(q)], [from_core.at[0, net.me, rows_of(q)], *terms])

    state = {"tick": 0}

    def pump(ticks=1):
        for _ in range(ticks):
            tick = state["tick"]
            state["tick"] += 1
            for lag, stage in enumerate((out_core, out_x, out_y_stage, out_z_stage, out_last)):
                if 0 <= tick - lag < pieces:
                    stage(tick - lag)

    pump()
    for copy in loads:
        copy.wait()

    def chunks(body, rows=32):
        def step(index, carry):
            body(pl.ds(pl.multiple_of(index * rows, rows), rows))
            return carry

        lax.fori_loop(0, toks // rows, step, 0)

    for tile in range(width // TILE):
        at = pl.ds(tile * TILE, TILE)
        turned = jnp.transpose(weights[at, qkv_width : qkv_width + LANES].astype(f32))
        gains[:, at] = turned[experts : experts + 8]
    dots[...] = jnp.zeros_like(dots)
    for c in range(cols):
        dots[2 * c : 2 * c + 2, :] = gate_dots[c, 0:2, :]
    gate_grad = jnp.transpose(dots[...])
    lane = lax.broadcasted_iota(jnp.int32, (toks, LANES), 1)
    mask = (table_col[...] > 0) & (lane < experts)
    chance, gates = router_probs[...], gate[...]
    total = jnp.sum(jnp.where(mask, chance, 0.0), axis=1, keepdims=True)
    gate_grad = jnp.where(mask, gate_grad, 0.0)
    pick_grad = gate_grad - jnp.sum(gates * gate_grad, axis=1, keepdims=True)
    chance_grad = jnp.where(mask, pick_grad / total, 0.0)
    logit_grad = chance * (chance_grad - jnp.sum(chance * chance_grad, axis=1, keepdims=True))
    logit_low[...] = logit_grad.astype(bf16)
    near_load.wait()
    far_load.wait()
    pump()

    for tile in range(width // TILE):
        at = pl.ds(tile * TILE, TILE)
        d_tokens[:, at] = back[:, at].astype(f32) + dot_nt(
            logit_low[...], weights[at, qkv_width : qkv_width + LANES]
        )
    gain_sums[...] = jnp.zeros_like(gain_sums)

    def fold(values, start):
        total = values[0:8]
        for r in range(8, values.shape[0], 8):
            total = total + values[r : r + 8]
        gain_sums[start : start + 8, :] = gain_sums[start : start + 8, :] + total

    def norm_second(at):
        x = tokens[at, :].astype(f32) + attn[at, :].astype(f32)
        inverse = lax.rsqrt(jnp.sum(x * x, axis=1, keepdims=True) / width + norm_eps)
        base = x * inverse
        dh = d_tokens[at, :]
        fold(dh * base, 8)
        scaled = dh * gains[1:2, :]
        mean = jnp.sum(scaled * base, axis=1, keepdims=True) / width
        middle = inverse * (scaled - base * mean) + grad_own[at, :].astype(f32)
        d_tokens[at, :] = middle
        low[at, :] = middle.astype(bf16)

    chunks(norm_second, 16)
    dob[...] = dot_nn(low[...], out_weights[...]).astype(bf16)
    pump()
    for tile in range(width // TILE):
        at = pl.ds(tile * TILE, TILE)
        out_weights[at, :] = dot_tn(low[:, at], heads[...]).astype(bf16)

    def blocks_of(array):
        def source(block, start, count):
            return array.at[pl.ds(pl.multiple_of(block * rows_w + start, 16), count)]

        return source

    out_pieces = 4
    out_count = rows_w // out_pieces
    out_line = [
        Sum2D(net, blocks_of(out_weights), q * out_count, out_count, out_y, out_z, share_out)
        for q in range(out_pieces)
    ]
    out_line[0].send_y()
    out_line[1].send_y()

    kv_line = [
        Sum2D(
            net,
            lambda block, start, count: kv_grad.at[block, pl.ds(start, count)],
            s * local_len,
            local_len,
            kv_y,
            kv_z,
            kv_share,
        )
        for s in range(seqs)
    ]
    for s in range(seqs):
        rows = pl.ds(s * local_len, local_len)
        for c in range(cols):
            at = pl.ds(c * local_len, local_len)
            keys[at, :] = kv_all[c, rows, :size]
            values[at, :] = kv_all[c, rows, size:]

        def attend(g, carry, s=s, rows=rows):
            at = pl.ds(pl.multiple_of(g * size, size), size)
            grow = pl.ds(pl.multiple_of(g * local_len, local_len), local_len)
            dout = dob[rows, at]
            stacked[0, grow, :] = q_low[rows, at]
            stacked[1, grow, :] = dout
            p = probs[s, g]
            p = p.astype(f32)
            dp = dot_nt(dout, values[...])
            delta = jnp.sum(p * dp, axis=1, keepdims=True)
            ds = (p * (dp - delta)).astype(bf16)
            ds_all[grow, :] = ds
            raw = dot_nn(ds, keys[...]) * scale
            dqkv[rows, at] = (
                raw * cosine[rows, :] - pltpu.roll(raw, size // 2, 1) * sine[rows, :]
            ).astype(bf16)
            return carry

        lax.fori_loop(0, group, attend, 0)
        dk = (dot_tn(ds_all[...], stacked[0]) * scale).astype(bf16)
        dv = dot_tn(probs[s].reshape(group * local_len, -1), stacked[1]).astype(bf16)
        for c in range(cols):
            kv_grad[c, rows, :size] = dk[c * local_len : (c + 1) * local_len]
            kv_grad[c, rows, size:] = dv[c * local_len : (c + 1) * local_len]
        kv_line[s].send_y()
        if s == 0:
            out_line[0].send_z()
            pump()
        else:
            kv_line[s - 1].send_z()
    kv_line[seqs - 1].send_z()
    out_line[1].send_z()
    out_line[2].send_y()
    for s in range(seqs):
        kv_line[s].last()
    raw = kv_share[:, :size]
    dqkv[:, q_width : q_width + size] = (
        raw * cosine[...] - pltpu.roll(raw, size // 2, 1) * sine[...]
    ).astype(bf16)
    dqkv[:, q_width + size : qkv_width] = kv_share[:, size:].astype(bf16)

    row_pieces, piece_rows = row_core.shape[0], row_core.shape[1]
    half = row_pieces * piece_rows

    def row_piece(core, i):
        return pl.ds(pl.multiple_of((core * row_pieces + i) * piece_rows, piece_rows), piece_rows)

    over = []
    for core in (1 - net.core, net.core):
        at_rows = pl.ds(pl.multiple_of(core * half, half), half)
        for tile in range(width // TILE):
            at = pl.ds(tile * TILE, TILE)
            low[at_rows, at] = dot_nt(dqkv[at_rows, :], weights[at, :qkv_width]).astype(bf16)
        if not over:
            over = [
                net.send(low.at[row_piece(1 - net.core, i)], row_core.at[i], net.core_peer())
                for i in range(row_pieces)
            ]

    qkv_pieces = 5
    qkv_count = rows_w // qkv_pieces
    for tile in range(width // TILE):
        at = pl.ds(tile * TILE, TILE)
        misc[at, :] = dot_tn(h2[:, at], logit_low[...])
        weights[at, :qkv_width] = dot_tn(h1[:, at], dqkv[...]).astype(bf16)
    qkv_line = [
        Sum2D(
            net,
            lambda block, start, count: weights.at[
                pl.ds(pl.multiple_of(block * rows_w + start, 16), count), pl.ds(0, qkv_width)
            ],
            q * qkv_count,
            qkv_count,
            qkv_y,
            qkv_z,
            share_qkv,
        )
        for q in range(qkv_pieces)
    ]
    qkv_line[0].send_y()
    along, returned = [], []
    for i in range(row_pieces):
        over[i].wait_recv()
        add_rows(row_to.at[i], [low.at[row_piece(net.core, i)], row_core.at[i]])
        along.append(net.send(row_to.at[i], row_from.at[i], net.x_peer()))
    qkv_line[1].send_y()
    for i in range(row_pieces):
        along[i].wait_recv()
        at = row_piece(net.core, i)
        add_rows(grad_own.at[at], [row_to.at[i], row_from.at[i]])
        returned.append(net.send(grad_own.at[at], grad_own.at[at], net.core_peer()))
    qkv_line[0].send_z()
    pump()
    for copy in returned:
        copy.wait_recv()

    def norm_first(at):
        x = tokens[at, :].astype(f32)
        inverse = lax.rsqrt(jnp.sum(x * x, axis=1, keepdims=True) / width + norm_eps)
        base = x * inverse
        dh = grad_own[at, :].astype(f32)
        fold(dh * base, 0)
        scaled = dh * gains[0:1, :]
        mean = jnp.sum(scaled * base, axis=1, keepdims=True) / width
        d_tokens[at, :] = d_tokens[at, :] + inverse * (scaled - base * mean)

    chunks(norm_first, 16)
    total = [jnp.sum(gain_sums[8 * i : 8 * i + 8, :], axis=0, keepdims=True) for i in (0, 1)]
    row_at = lax.broadcasted_iota(jnp.int32, (LANES, TILE), 0)
    for tile in range(width // TILE):
        at = pl.ds(tile * TILE, TILE)
        part = slice(tile * TILE, (tile + 1) * TILE)
        placed = jnp.where(row_at == experts, total[0][:, part], 0.0)
        placed = jnp.where(row_at == experts + 1, total[1][:, part], placed)
        lanes = lax.broadcasted_iota(jnp.int32, (TILE, LANES), 1)
        misc_low[at, :] = jnp.where(lanes < experts, misc[at, :], jnp.transpose(placed)).astype(bf16)
    misc_line = Sum2D(net, blocks_of(misc_low), 0, rows_w, misc_y, misc_z, share_misc)
    misc_line.send_y()
    qkv_line[2].send_y()
    qkv_line[1].send_z()
    out_line[2].send_z()
    out_line[3].send_y()
    pump()
    misc_line.send_z()
    qkv_line[3].send_y()
    qkv_line[2].send_z()
    out_line[3].send_z()
    pump()
    qkv_line[4].send_y()
    qkv_line[3].send_z()
    pump()
    qkv_line[4].send_z()
    pump(8)
    for piece_sum in (*out_line, misc_line, *qkv_line):
        piece_sum.last()
    net.finish()


def rear_call(
    cols, collective_id, experts, out_part, back, gate_dots, gate, router_probs, table_col, h1, h2,
    tokens, attn, weights, out_weights, grads, heads, q_low, kv_all, probs, cosine, sine,
):
    toks, width = back.shape
    q_width = q_low.shape[1]
    size = HEAD_DIM
    qkv_width = q_width + 2 * size
    seqs, group, local_len, full_len = probs.shape
    rows_w, high = width // cols, cols // 2
    piece = width // lax.axis_size("row")
    row_pieces = 4
    row_piece = (row_pieces, toks // 2 // row_pieces, width)
    vmem, any_space = pl.BlockSpec(memory_space=pltpu.VMEM), pl.BlockSpec(memory_space=pl.ANY)

    def shape(*dims, dtype=f32):
        return jax.ShapeDtypeStruct(dims, dtype)

    def sums(rows, columns):
        return [
            pltpu.VMEM((high, rows, columns), bf16),
            pltpu.VMEM((high - 1, rows, columns), bf16),
        ]

    copies = 420
    return pl.pallas_call(
        functools.partial(rear_kernel, cols, experts),
        out_shape=[
            shape(toks, piece),
            shape(toks, width),
            shape(rows_w, qkv_width),
            shape(rows_w, LANES),
            shape(rows_w, q_width),
        ],
        in_specs=[any_space] + [vmem] * 9 + [any_space] * 3 + [vmem] * 6,
        out_specs=[vmem] * 5,
        scratch_shapes=[
            pltpu.VMEM((width, qkv_width + LANES), bf16),
            pltpu.VMEM((width, q_width), bf16),
            pltpu.VMEM((width, LANES), f32),
            pltpu.VMEM((width, LANES), bf16),
            pltpu.VMEM((toks, width), bf16),
            pltpu.VMEM((8, width), f32),
            pltpu.VMEM((LANES, toks), f32),
            pltpu.VMEM((toks, LANES), bf16),
            pltpu.VMEM((toks, width), bf16),
            pltpu.VMEM((toks, q_width), bf16),
            pltpu.VMEM((full_len, size), bf16),
            pltpu.VMEM((full_len, size), bf16),
            pltpu.VMEM((2, group * local_len, size), bf16),
            pltpu.VMEM((group * local_len, full_len), bf16),
            pltpu.VMEM((cols, toks, 2 * size), bf16),
            pltpu.VMEM((toks, 2 * size), f32),
            pltpu.VMEM((toks, qkv_width), bf16),
            pltpu.VMEM((16, width), f32),
            pltpu.VMEM((2, cols, toks, piece), bf16),
            pltpu.VMEM((2, cols, toks, piece), bf16),
            pltpu.VMEM((cols, toks, piece), bf16),
            *sums(toks, piece),
            *sums(toks, 2 * size),
            *sums(rows_w, q_width),
            *sums(rows_w, qkv_width),
            *sums(rows_w, LANES),
            pltpu.VMEM(row_piece, bf16),
            pltpu.VMEM(row_piece, bf16),
            pltpu.VMEM(row_piece, bf16),
            pltpu.SemaphoreType.DMA((copies,)),
            pltpu.SemaphoreType.DMA((copies,)),
            pltpu.SemaphoreType.DMA((8,)),
        ],
        compiler_params=pltpu.CompilerParams(
            collective_id=collective_id, has_side_effects=True, vmem_limit_bytes=62 << 20
        ),
        name=f"rear_{collective_id}",
    )(
        out_part, back, gate_dots, gate, router_probs, table_col, h1, h2, tokens, attn, weights,
        out_weights, grads, heads, q_low, kv_all, probs, cosine, sine,
    )


def experts_plain(
    h2, grad_all, w_gate, w_up, w_down, shared_weights, router, rank_all, capacity, row_width
):
    cols = lax.axis_size("col")
    col_index, row_index = lax.axis_index("col"), lax.axis_index("row")
    toks, width = h2.shape
    exp_local = w_gate.shape[0]
    experts = rank_all.shape[2]
    shared_part = shared_weights.shape[1] // 3
    shared_in_weights = shared_weights[:, : 2 * shared_part]
    shared_down = shared_weights[:, 2 * shared_part :]
    h2_slice = lax.dynamic_slice_in_dim(h2, row_index * row_width, row_width, 1)
    h2_all = gather_all(h2_slice)

    all_mask = (rank_all > 0).astype(f32)
    all_probs = jax.nn.softmax(dot("ctd,de->cte", h2_all, router), axis=-1)
    all_picked = all_probs * all_mask
    all_gate = all_picked / jnp.sum(all_picked, axis=-1, keepdims=True)
    own = col_index * exp_local
    own_gate = lax.dynamic_slice_in_dim(all_gate, own, exp_local, 2)
    own_rank = lax.dynamic_slice_in_dim(rank_all, own, exp_local, 2).astype(jnp.int32)
    slots = jnp.arange(1, capacity + 1, dtype=jnp.int32)
    pick = jnp.swapaxes(own_rank, 1, 2)[:, :, None, :] == slots[:, None]
    slot_gate = jnp.sum(
        jnp.where(pick, jnp.swapaxes(own_gate, 1, 2)[:, :, None, :], 0.0), axis=3
    )[..., None]
    pick_low = pick.astype(bf16).reshape(cols, exp_local * capacity, toks)
    slot_shape = (cols, exp_local, capacity, width)
    slot_rows = dot("cut,ctd->cud", pick_low, h2_all).astype(bf16).reshape(slot_shape)
    slot_grad = dot("cut,ctd->cud", pick_low, grad_all).astype(bf16).reshape(slot_shape)
    gate_pre = dot("necd,edf->necf", slot_rows, w_gate)
    up_pre = dot("necd,edf->necf", slot_rows, w_up)
    silu_gate, slope_gate = silu_parts(gate_pre)
    hidden = silu_gate * up_pre
    gated = (hidden * slot_gate).astype(bf16)
    slot_out = dot("necf,efd->necd", gated, w_down).astype(bf16)
    hidden_grad = dot("necd,efd->necf", slot_grad, w_down)
    slot_dots = jnp.sum(hidden * hidden_grad, axis=-1)
    hidden_grad = hidden_grad * slot_gate
    gate_grad = (hidden_grad * up_pre * slope_gate).astype(bf16)
    up_grad = (hidden_grad * silu_gate).astype(bf16)
    slot_back = dot("necf,edf->necd", gate_grad, w_gate)
    slot_back = (slot_back + dot("necf,edf->necd", up_grad, w_up)).astype(bf16)
    grad_expert_down = dot("necf,necd->efd", gated, slot_grad)
    grad_expert_gate = dot("necd,necf->edf", slot_rows, gate_grad)
    grad_expert_up = dot("necd,necf->edf", slot_rows, up_grad)
    pick_flat = pick_low.reshape(cols, exp_local * capacity, toks)
    slot_out = slot_out.reshape(cols, exp_local * capacity, width)
    slot_back = slot_back.reshape(cols, exp_local * capacity, width)

    shared_pre = dot("ctd,dk->ctk", h2_all, shared_in_weights)
    sgate_pre, sup_pre = shared_pre[:, :, :shared_part], shared_pre[:, :, shared_part:]
    shared_silu, shared_slope = silu_parts(sgate_pre)
    shared_hidden = (shared_silu * sup_pre).astype(bf16)
    part_out = dot("cut,cud->ctd", pick_flat, slot_out) + dot(
        "ctk,dk->ctd", shared_hidden, shared_down
    )
    shared_hgrad = dot("ctd,dk->ctk", grad_all, shared_down)
    shared_grads = jnp.concatenate(
        [shared_hgrad * sup_pre * shared_slope, shared_hgrad * shared_silu], axis=2
    ).astype(bf16)
    part_back = dot("cut,cud->ctd", pick_flat, slot_back) + dot(
        "ctk,dk->ctd", shared_grads, shared_in_weights
    )
    token_dots = jnp.einsum(
        "ceu,ceut->cte", slot_dots, pick.astype(f32), precision=lax.Precision.HIGHEST
    )
    gate_dots = lax.psum(swap_col(token_dots), "row")
    gate_dots = jnp.swapaxes(gate_dots, 0, 1).reshape(toks, experts)

    shared_share = jnp.concatenate(
        [dot("ctd,ctk->dk", h2_all, shared_grads), dot("ctd,ctk->dk", grad_all, shared_hidden)],
        axis=1,
    ).astype(bf16)
    back_full = lax.all_gather(scatter_all(part_back.astype(bf16)), "row", axis=1, tiled=True)
    return (
        part_out.astype(bf16),
        back_full,
        gate_dots,
        shared_share,
        grad_expert_gate,
        grad_expert_up,
        grad_expert_down,
    )


def on_device(
    tokens,
    segments,
    routes,
    attn_gain,
    query_matrix,
    key_matrix,
    value_matrix,
    attention_output_matrix,
    mlp_gain,
    w_router,
    shared_gate_matrix,
    shared_up_matrix,
    shared_down_matrix,
    expert_gate,
    expert_up,
    expert_down,
    cotangent,
):
    local_len, seqs, width = tokens.shape
    cols = lax.axis_size("col")
    col_index = lax.axis_index("col")
    rows_w = query_matrix.shape[0]
    full_len = local_len * cols
    size = HEAD_DIM
    q_width = query_matrix.shape[1]
    kv_width = key_matrix.shape[1]
    kv_local = kv_width // size
    group = q_width // kv_width
    row_width = cotangent.shape[2]
    toks = local_len * seqs
    top = routes.shape[2]
    experts = w_router.shape[1]
    exp_local = expert_gate.shape[0]
    hidden_local = expert_gate.shape[2]
    capacity = max(2, toks * top * 4 // (3 * experts))
    shared_part = shared_gate_matrix.shape[1] // cols
    scale = 1.0 / math.sqrt(size)
    kernels = fits(cols, toks, width) and kv_local == 1 and exp_local == 2

    def seq_major(a):
        return jnp.swapaxes(a, 0, 1).reshape(toks, a.shape[2])

    misc = jnp.concatenate(
        [
            w_router,
            attn_gain[:, None],
            mlp_gain[:, None],
            jnp.zeros((rows_w, LANES - experts - 2), bf16),
        ],
        axis=1,
    )
    shared_weights = jnp.concatenate(
        [
            shared_gate_matrix.reshape(rows_w, cols, shared_part),
            shared_up_matrix.reshape(rows_w, cols, shared_part),
            shared_down_matrix.T.reshape(rows_w, cols, shared_part),
        ],
        axis=2,
    )
    shared_own = jnp.swapaxes(shared_weights, 0, 1)
    grad_own = seq_major(cotangent).astype(bf16)
    cosine, sine = rope_tables(col_index * local_len, local_len, size)
    cosine, sine = jnp.tile(cosine, (seqs, 1)), jnp.tile(sine, (seqs, 1))
    qkv_width = q_width + 2 * kv_width
    flat_routes = seq_major(routes)
    named = flat_routes[:, :, None] == jnp.arange(experts, dtype=jnp.int32)
    mask = jnp.any(named, axis=1)
    order = jnp.arange(toks, dtype=jnp.int32)
    upto = (order[None, :] <= order[:, None]).astype(bf16)
    rank = jnp.where(mask, dot("ij,je->ie", upto, mask.astype(bf16)), 0.0)

    doc = jnp.transpose(segments)
    def to_grid(flat):
        shaped = flat.reshape(seqs, local_len, kv_local, group, size)
        return shaped.transpose(0, 2, 3, 1, 4).reshape(seqs, kv_local, group * local_len, size)

    def from_grid(grid):
        shaped = grid.reshape(seqs, kv_local, group, local_len, size)
        return shaped.transpose(0, 3, 1, 2, 4).reshape(toks, q_width)

    token_rows = seq_major(tokens)
    x = token_rows.astype(f32)
    inv_first = rms_scale(x)
    base_first = x * inv_first
    if kernels:
        table_row = jnp.concatenate([rank.T, doc.reshape(1, toks).astype(f32)], axis=0)
        table_row = jnp.pad(table_row, ((0, -(experts + 1) % 8), (0, 0)))
        table_col = jnp.pad(rank, ((0, 0), (0, LANES - experts))).astype(bf16)
        (
            first_weights,
            out_weights,
            shared_weights,
            grad_all,
            rows_all,
            rank_all,
            h1,
            q_low,
            kv_all,
            probs,
            heads,
            attn,
            h2,
            gate,
            probs_router,
        ) = front_call(
            cols,
            0,
            experts,
            token_rows,
            query_matrix,
            key_matrix,
            value_matrix,
            misc,
            attention_output_matrix.T,
            shared_own,
            grad_own,
            table_row,
            table_col,
            doc.reshape(toks, 1).astype(f32),
            jnp.concatenate([cosine, cosine], axis=1),
            jnp.concatenate([-sine, sine], axis=1),
            seqs,
        )
    else:
        first_weights = jnp.concatenate([query_matrix, key_matrix, value_matrix, misc], axis=1)
        first_weights = gather_col(first_weights).reshape(width, -1)
        out_weights = gather_col(attention_output_matrix.T).reshape(width, q_width)
        shared_weights, grad_all = swap_col(shared_own), gather_all(grad_own)
        gain_one = first_weights[:, qkv_width + experts].astype(f32)
        h1 = (base_first * gain_one).astype(bf16)
        qkv = dot("tb,bk->tk", h1, first_weights[:, :qkv_width])
        qk = rotate(qkv[:, : q_width + kv_width], cosine, sine).astype(bf16)
        q_low = qk[:, :q_width]
        value_low = qkv[:, q_width + kv_width :].astype(bf16)
        side = jnp.concatenate(
            [
                rank.astype(bf16),
                doc.reshape(toks, 1).astype(bf16),
                jnp.zeros((toks, LANES - experts - 1), bf16),
            ],
            axis=1,
        )
        kv_all = gather_col(jnp.concatenate([qk[:, q_width:], value_low, side], axis=1))
        rank_all = kv_all[:, :, 2 * kv_width : 2 * kv_width + experts]
    shared_weights = shared_weights.reshape(width, 3 * shared_part)
    qkv_weights = first_weights[:, :qkv_width]
    router = first_weights[:, qkv_width : qkv_width + experts]
    gain_one = first_weights[:, qkv_width + experts].astype(f32)
    gain_two = first_weights[:, qkv_width + experts + 1].astype(f32)
    kv_seq = jnp.swapaxes(kv_all.reshape(cols, seqs, local_len, -1), 0, 1)
    kv_seq = kv_seq.reshape(seqs, full_len, -1)
    key_all = kv_seq[:, :, :kv_width].reshape(seqs, full_len, kv_local, size)
    value_all = kv_seq[:, :, kv_width : 2 * kv_width].reshape(seqs, full_len, kv_local, size)
    query_grid = to_grid(q_low)
    if not kernels:
        doc_all = kv_seq[:, :, 2 * kv_width + experts]
        place = col_index * local_len + jnp.arange(local_len, dtype=jnp.int32)
        same = doc.astype(bf16)[:, :, None] == doc_all[:, None, :]
        causal = jnp.arange(full_len, dtype=jnp.int32)[None, :] <= place[:, None]
        allowed = jnp.tile(same & causal[None], (1, group, 1))[:, None]
        scores = dot("shrd,skhd->shrk", query_grid, key_all) * scale
        scores = jnp.where(allowed, scores, masked_score)
        weights = jnp.exp(scores - jnp.max(scores, axis=-1, keepdims=True))
        weights = jnp.where(allowed, weights, 0.0)
        probs = (weights / jnp.sum(weights, axis=-1, keepdims=True)).astype(bf16)
        heads = from_grid(dot("shrk,skhd->shrd", probs, value_all)).astype(bf16)
        attn = lax.psum(dot("tk,bk->tb", heads, out_weights).astype(bf16), "row")
    middle = x + attn.astype(f32)

    inv_second = rms_scale(middle)
    base_second = middle * inv_second
    row_index = lax.axis_index("row")
    if not kernels:
        h2 = (base_second * gain_two).astype(bf16)
        probs_router = jax.nn.softmax(dot("td,de->te", h2, router), axis=-1)
        picked = jnp.where(mask, probs_router, 0.0)
        pick_total = jnp.sum(picked, axis=-1, keepdims=True)
        gate = picked / pick_total
    if kernels:
        rank_own = lax.dynamic_slice_in_dim(rank_all, col_index * exp_local, exp_local, 2)
        rank_own = rank_own.astype(f32)
        part_out, back_full, gate_dots, shared_share, *expert_grads = experts_kernels(
            cols,
            3,
            capacity,
            h2,
            grad_all,
            expert_gate,
            expert_up,
            expert_down,
            shared_weights,
            lax.dynamic_slice_in_dim(rows_all, col_index * exp_local, exp_local, 1),
            rank_own,
            gate[:, :experts].T,
        )
    else:
        part_out, back_full, gate_dots, shared_share, *expert_grads = experts_plain(
            h2,
            grad_all,
            expert_gate,
            expert_up,
            expert_down,
            shared_weights,
            router,
            rank_all,
            capacity,
            row_width,
        )
    if not kernels:
        back_full = back_full.astype(f32)
    shared_share = swap_col(shared_share.reshape(cols, rows_w, 3 * shared_part))
    shared_share = jnp.swapaxes(shared_share, 0, 1).astype(f32)
    share_sgate, share_sup, share_sdown = (
        shared_share[:, :, i * shared_part : (i + 1) * shared_part].reshape(rows_w, -1)
        for i in range(3)
    )

    if kernels:
        out_slice, token_grad, share_qkv, share_misc, share_out = rear_call(
            cols,
            5,
            experts,
            part_out,
            back_full,
            gate_dots,
            gate,
            probs_router,
            table_col,
            h1,
            h2,
            token_rows,
            attn,
            first_weights,
            out_weights,
            grad_all,
            heads,
            q_low,
            kv_all,
            probs,
            jnp.concatenate([cosine, cosine], axis=1),
            jnp.concatenate([-sine, sine], axis=1),
        )
    else:
        pick_grad = gate_dots - jnp.sum(gate * gate_dots, axis=-1, keepdims=True)
        prob_grad = jnp.where(mask, pick_grad / pick_total, 0.0)
        logit_grad = probs_router * (
            prob_grad - jnp.sum(probs_router * prob_grad, axis=-1, keepdims=True)
        )
        logit_low = logit_grad.astype(bf16)
        grad_router = dot("td,te->de", h2, logit_low)

        back_full = back_full + dot("te,de->td", logit_low, router)
        grad_own = lax.dynamic_slice_in_dim(grad_all, col_index, 1, 0)[0].astype(f32)
        grad_gain_two = jnp.sum(back_full * base_second, axis=0)
        scaled_two = back_full * gain_two
        middle_grad = (
            inv_second
            * (scaled_two - base_second * jnp.mean(scaled_two * base_second, axis=-1, keepdims=True))
            + grad_own
        )
        attn_grad = middle_grad.astype(bf16)
        grad_out = dot("td,tk->dk", attn_grad, heads).astype(bf16)

        heads_grad = to_grid(dot("td,dk->tk", attn_grad, out_weights).astype(bf16))
        value_grad = dot("shrk,shrd->skhd", probs, heads_grad)
        weight_grad = dot("shrd,skhd->shrk", heads_grad, value_all)
        probs_wide = probs.astype(f32)
        delta = jnp.sum(probs_wide * weight_grad, axis=-1, keepdims=True)
        score_grad = (probs_wide * (weight_grad - delta)).astype(bf16)
        query_grad = from_grid(dot("shrk,skhd->shrd", score_grad, key_all)) * scale
        key_grad = dot("shrk,shrd->skhd", score_grad, query_grid) * scale
        kv_grad = jnp.concatenate(
            [key_grad.reshape(seqs, full_len, kv_width), value_grad.reshape(seqs, full_len, kv_width)],
            axis=2,
        ).astype(bf16)
        kv_grad = jnp.swapaxes(kv_grad.reshape(seqs, cols, local_len, 2 * kv_width), 0, 1)
        kv_share = scatter_col(kv_grad.reshape(cols, toks, 2 * kv_width)).astype(f32)
        qk_grad = rotate(
            jnp.concatenate([query_grad, kv_share[:, :kv_width]], axis=1), cosine, -sine
        )
        qkv_grad = jnp.concatenate([qk_grad, kv_share[:, kv_width:]], axis=1).astype(bf16)
        first_grad = dot("tk,bk->tb", qkv_grad, qkv_weights).astype(bf16)
        first_grad = lax.psum(first_grad, "row").astype(f32)
        grad_gain_one = jnp.sum(first_grad * base_first, axis=0)
        scaled_one = first_grad * gain_one
        token_grad = (
            inv_first
            * (scaled_one - base_first * jnp.mean(scaled_one * base_first, axis=-1, keepdims=True))
            + middle_grad
        )
        grad_first = jnp.concatenate(
            [
                dot("tb,tk->bk", h1, qkv_grad),
                grad_router,
                grad_gain_one[:, None],
                grad_gain_two[:, None],
                jnp.zeros((width, LANES - experts - 2), f32),
            ],
            axis=1,
        ).astype(bf16)
        out_slice = scatter_all(part_out).astype(f32)
        share_out = scatter_col(grad_out.reshape(cols, rows_w, q_width)).astype(f32)
        share_first = scatter_col(grad_first.reshape(cols, rows_w, -1)).astype(f32)
        share_qkv, share_misc = share_first[:, :qkv_width], share_first[:, qkv_width:]
    middle_slice = lax.dynamic_slice_in_dim(middle, row_index * row_width, row_width, 1)
    block_out = (middle_slice + out_slice).astype(bf16)

    def tokens_first(a):
        return jnp.swapaxes(a.reshape(seqs, local_len, a.shape[1]), 0, 1)

    return (
        tokens_first(block_out),
        tokens_first(token_grad),
        share_misc[:, experts],
        share_qkv[:, :q_width],
        share_qkv[:, q_width : q_width + kv_width],
        share_qkv[:, q_width + kv_width :],
        share_out.T,
        share_misc[:, experts + 1],
        share_misc[:, :experts],
        share_sgate,
        share_sup,
        share_sdown.T,
        *expert_grads,
    )


def solution(mesh):
    in_specs = (
        P("col", None, None),
        P("col", None),
        P("col", None, None),
        P("col"),
        P("col", "row"),
        P("col", "row"),
        P("col", "row"),
        P("row", "col"),
        P("col"),
        P("col", None),
        P("col", "row"),
        P("col", "row"),
        P("row", "col"),
        P("col", None, "row"),
        P("col", None, "row"),
        P("col", "row", None),
        P("col", None, "row"),
    )
    out_specs = (
        P("col", None, "row"),
        P("col", None, None),
        P("col"),
        P("col", "row"),
        P("col", "row"),
        P("col", "row"),
        P("row", "col"),
        P("col"),
        P("col", None),
        P("col", "row"),
        P("col", "row"),
        P("row", "col"),
        P("col", None, "row"),
        P("col", None, "row"),
        P("col", "row", None),
    )
    return jax.shard_map(
        on_device, mesh=mesh, in_specs=in_specs, out_specs=out_specs, check_vma=False
    )
```

```python
import functools
import math

import jax
import jax.numpy as jnp
from jax import lax
from jax.experimental import pallas as pl
from jax.experimental.pallas import tpu as pltpu
from jax.sharding import PartitionSpec as P

HEAD_DIM = 128
LANES = 128


norm_eps = 1e-05
rope_base = 500000.0
masked_score = -1e30

f32 = jnp.float32
bf16 = jnp.bfloat16
MESH = pl.DeviceIdType.MESH


def dot(form, left, right):
    return jnp.einsum(form, left, right, preferred_element_type=f32)


def rope_tables(start_place, local_len, head_size):
    places = (start_place + jnp.arange(local_len, dtype=jnp.int32)).astype(f32)
    frequency = jnp.power(
        rope_base, -jnp.arange(0, head_size, 2, dtype=jnp.int32).astype(f32) / head_size
    )
    angles = places[:, None] * frequency[None, :]
    return (jnp.cos(angles), jnp.sin(angles))


def rotate(field, cosine, sine):
    half = cosine.shape[1]
    parts = []
    for start in range(0, field.shape[1], 2 * half):
        front = field[:, start : start + half]
        back = field[:, start + half : start + 2 * half]
        parts.append(front * cosine - back * sine)
        parts.append(back * cosine + front * sine)
    return jnp.concatenate(parts, axis=1)


def rms_scale(values_in):
    return lax.rsqrt(jnp.mean(values_in * values_in, axis=-1, keepdims=True) + norm_eps)


def silu_parts(pre_gate):
    sigmoid_gate = jax.nn.sigmoid(pre_gate)
    silu_gate = pre_gate * sigmoid_gate
    slope_gate = sigmoid_gate * (1.0 + pre_gate * (1.0 - sigmoid_gate))
    return (silu_gate, slope_gate)


def gather_col(part):
    return lax.all_gather(part, "col", axis=0, tiled=False)


def scatter_col(blocks):
    flat = blocks.reshape(-1, blocks.shape[-1])
    return lax.psum_scatter(flat, "col", scatter_dimension=0, tiled=True)


def gather_all(part):
    got = lax.all_gather(part, ("col", "row"), axis=0, tiled=False)
    cols, rows = lax.axis_size("col"), lax.axis_size("row")
    got = got.reshape(cols, rows, *part.shape).transpose(0, 2, 1, 3)
    return got.reshape(cols, part.shape[0], rows * part.shape[1])


def scatter_all(blocks):
    flat = blocks.reshape(-1, blocks.shape[-1])
    part = lax.psum_scatter(flat, "row", scatter_dimension=1, tiled=True)
    return lax.psum_scatter(part, "col", scatter_dimension=0, tiled=True)


def swap_col(blocks):
    return lax.all_to_all(blocks, "col", split_axis=0, concat_axis=0, tiled=True)


class Net:
    def __init__(self, cols, send_sems, recv_sems):
        self.send_sems, self.recv_sems, self.used, self.sent = send_sems, recv_sems, 0, []
        self.cols, self.high_count = cols, cols // 2
        self.me = lax.axis_index("col")
        self.high, self.low = self.me // 2, self.me % 2
        self.row = lax.axis_index("row")
        self.outer, self.core = self.row // 2, self.row % 2

    def block(self, step, other=False):
        high = lax.rem(self.high + self.high_count - step, self.high_count)
        return 2 * high + (1 - self.low if other else self.low)

    def block_ahead(self, step, other=False):
        high = lax.rem(self.high + step, self.high_count)
        return 2 * high + (1 - self.low if other else self.low)

    def z_peer(self, step):
        return {"col": self.block_ahead(step)}

    def y_peer(self):
        return {"col": 2 * self.high + 1 - self.low}

    def x_peer(self):
        return {"row": 2 * (1 - self.outer) + self.core}

    def core_peer(self):
        return {"row": 2 * self.outer + 1 - self.core}

    def col_peer(self, step):
        return {"col": lax.rem(self.me + step, self.cols)}

    def greet(self, peers):
        barrier = pltpu.get_barrier_semaphore()
        for peer in peers:
            pl.semaphore_signal(barrier, inc=1, device_id=peer, device_id_type=MESH)
        pl.semaphore_wait(barrier, len(peers))

    def send(self, source, target, peer):
        copy = pltpu.make_async_remote_copy(
            src_ref=source,
            dst_ref=target,
            send_sem=self.send_sems.at[self.used],
            recv_sem=self.recv_sems.at[self.used],
            device_id=peer,
            device_id_type=MESH,
        )
        self.used += 1
        copy.start()
        self.sent.append(copy)
        return copy

    def left(self, copy):
        copy.wait_send()
        self.sent = [other for other in self.sent if other is not copy]

    def finish(self):
        for copy in self.sent:
            copy.wait_send()


def col_peers(net):
    return [net.z_peer(step) for step in range(1, net.high_count)] + [net.y_peer()]


def row_peers(net):
    return [net.x_peer(), net.core_peer()]


def add_rows(target, terms):
    rows = target.shape[0]
    piece = 32 if rows % 32 == 0 else 16

    def body(index, carry):
        at = pl.ds(pl.multiple_of(index * piece, piece), piece)
        total = terms[0][at, :].astype(f32)
        for term in terms[1:]:
            total = total + term[at, :].astype(f32)
        target[at, :] = total.astype(target.dtype)
        return carry

    lax.fori_loop(0, rows // piece, body, 0)


def dot_nn(left, right):
    return lax.dot_general(left, right, (((1,), (0,)), ((), ())), preferred_element_type=f32)


def dot_nt(left, right):
    return lax.dot_general(left, right, (((1,), (1,)), ((), ())), preferred_element_type=f32)


def dot_tn(left, right):
    return lax.dot_general(left, right, (((0,), (0,)), ((), ())), preferred_element_type=f32)


def each_tile(count, body):
    def step(index, carry):
        body(index)
        return carry

    lax.fori_loop(0, count, step, 0)


TILE = 512
WIDE = 1280


def tile_at(index, tile=TILE):
    if isinstance(index, int):
        return pl.ds(index * tile, tile)
    return pl.ds(pl.multiple_of(index * tile, tile), tile)


class Line:
    def __init__(self, net, items):
        self.net, self.items = net, items
        self.other_row = 2 * (1 - net.outer) + net.core
        self.along_z, self.along_y, self.along_x, self.to_core = {}, {}, {}, {}
        self.moved = []
        self.now = 0

    def in_chip(self, q, step, other, source, slot):
        if self.items[q][2]:
            self.along_x[q, step, other] = self.net.send(source, slot, self.net.x_peer())
            self.to_core[q, step, other] = self.net.send(source, slot, self.net.core_peer())

    def start(self, q):
        net = self.net
        source, slot_of, _ = self.items[q]
        slot = slot_of(net.me, net.row)
        for step in reversed(range(1, net.high_count)):
            self.along_z[q, step] = net.send(source, slot, net.z_peer(step))
        self.along_y[q, 0] = net.send(source, slot, net.y_peer())
        self.in_chip(q, 0, False, source, slot)

    def after_z(self, q):
        net = self.net
        for step in reversed(range(1, net.high_count)):
            self.along_z[q, step].wait_recv()
            slot = self.items[q][1](net.block(step), net.row)
            self.along_y[q, step] = net.send(slot, slot, net.y_peer())
            self.in_chip(q, step, False, slot, slot)

    def after_y(self, q):
        net = self.net
        for step in range(net.high_count):
            self.along_y[q, step].wait_recv()
            slot = self.items[q][1](net.block(step, True), net.row)
            self.in_chip(q, step, True, slot, slot)

    def after_x(self, q):
        net = self.net
        if self.items[q][2]:
            for other in (False, True):
                for step in range(net.high_count):
                    self.along_x[q, step, other].wait_recv()
                    slot = self.items[q][1](net.block(step, other), self.other_row)
                    self.moved.append(net.send(slot, slot, net.core_peer()))

    def tick(self, count=1):
        net = self.net
        for _ in range(count):
            now, self.now = self.now, self.now + 1
            if now < len(self.items):
                if now >= 2:
                    for step in range(1, net.high_count):
                        net.left(self.along_z[now - 2, step])
                self.start(now)
            for stage, lag in ((self.after_z, 1), (self.after_y, 2), (self.after_x, 3)):
                if 0 <= now - lag < len(self.items):
                    stage(now - lag)

    def drain(self):
        while self.now < len(self.items) + 3:
            self.tick()
        for copy in [*self.moved, *self.to_core.values()]:
            copy.wait_recv()


def front_kernel(
    cols,
    experts,
    tokens,
    query,
    key,
    value,
    misc,
    out_own,
    grad_own,
    table_row,
    table_col,
    doc_col,
    cosine,
    sine,
    weights,
    out_weights,
    grad_all,
    rows_all,
    cols_all,
    h1,
    q_low,
    kv_all,
    probs,
    heads,
    attn,
    h2,
    gate,
    router_probs,
    gains,
    inverse,
    kv_low,
    keys,
    values,
    bias,
    partial,
    from_core,
    to_x,
    from_x,
    send_sems,
    recv_sems,
    local_sems,
):
    net = Net(cols, send_sems, recv_sems)
    toks, width = tokens.shape
    size = HEAD_DIM
    q_width = q_low.shape[1]
    group = q_width // size
    rows_w = query.shape[0]
    seqs = probs.shape[0]
    local_len = toks // seqs
    full_len = local_len * cols
    scale = 1.0 / math.sqrt(size)
    mine = pl.ds(pl.multiple_of(net.me * rows_w, 16), rows_w)

    copies = []

    def local_copy(source, target):
        copy = pltpu.make_async_copy(source, target, local_sems.at[len(copies)])
        copy.start()
        copies.append(copy)

    local_copy(query, weights.at[mine, pl.ds(0, q_width)])
    local_copy(key, weights.at[mine, pl.ds(q_width, size)])
    local_copy(value, weights.at[mine, pl.ds(q_width + size, size)])
    local_copy(misc, weights.at[mine, pl.ds(q_width + 2 * size, LANES)])
    first = len(copies)
    local_copy(out_own, out_weights.at[mine])
    part = grad_own.shape[1]
    local_copy(
        grad_own, grad_all.at[net.me, :, pl.ds(pl.multiple_of(net.row * part, LANES), part)]
    )
    local_copy(table_row, rows_all.at[net.me])
    local_copy(table_col, cols_all.at[net.me])
    net.greet([net.col_peer(step) for step in range(1, cols)] + row_peers(net))
    for copy in copies[:first]:
        copy.wait()

    def weight_slot(target, start, count):
        def slot(block, row):
            return target.at[pl.ds(pl.multiple_of(block * rows_w + start, 16), count)]

        return slot

    def grad_slot(start, count):
        def slot(block, row):
            return grad_all.at[
                block, pl.ds(start, count), pl.ds(pl.multiple_of(row * part, LANES), part)
            ]

        return slot

    items = [(table_row, lambda block, row: rows_all.at[block], False)]
    pieces, out_pieces, grad_pieces = 5, 4, 4
    count = rows_w // pieces
    for q in range(pieces):
        slot = weight_slot(weights, q * count, count)
        items.append((slot(net.me, net.row), slot, False))
    ready_weights = len(items) + 2
    out_items, grad_items = [], []
    count = rows_w // out_pieces
    for q in range(out_pieces):
        slot = weight_slot(out_weights, q * count, count)
        out_items.append((out_own.at[pl.ds(q * count, count)], slot, False))
    count = toks // grad_pieces
    for q in range(grad_pieces):
        grad_items.append((grad_own.at[pl.ds(q * count, count)], grad_slot(q * count, count), True))
    items += out_items[:2]
    for q in range(2, out_pieces):
        items += [grad_items[q - 2], out_items[q]]
    ready_out = len(items) + 2
    items += grad_items[out_pieces - 2 :]
    items.append((table_col, lambda block, row: cols_all.at[block], False))
    line = Line(net, items)

    line.tick(2)
    copies[first + 2].wait()

    def chunks(body, rows=32):
        def step(index, carry):
            body(pl.ds(pl.multiple_of(index * rows, rows), rows))
            return carry

        lax.fori_loop(0, toks // rows, step, 0)

    def measure_first(at):
        x = tokens[at, :].astype(f32)
        total = jnp.sum(x * x, axis=1, keepdims=True)
        inverse[at, :] = jnp.broadcast_to(lax.rsqrt(total / width + norm_eps), (32, LANES))

    chunks(measure_first)
    line.tick(ready_weights - line.now)

    start = q_width + 2 * size
    for tile in range(width // TILE):
        at = pl.ds(tile * TILE, TILE)
        turned = jnp.transpose(weights[at, start : start + LANES].astype(f32))
        gains[:, at] = turned[experts : experts + 8]

    def norm_first(at):
        x = tokens[at, :].astype(f32) * inverse[at, 0:1]
        h1[at, :] = (x * gains[0:1, :]).astype(bf16)

    chunks(norm_first)
    line.tick()
    heads_all = group + 2
    for head in range(heads_all - 1, -1, -1):
        raw = dot_nn(h1[...], weights[:, head * size : (head + 1) * size])
        if head <= group:
            raw = raw * cosine[...] + pltpu.roll(raw, size // 2, 1) * sine[...]
        if head < group:
            q_low[:, head * size : (head + 1) * size] = raw.astype(bf16)
        else:
            kv_low[:, (head - group) * size : (head - group + 1) * size] = raw.astype(bf16)
        if head == group:
            kv_all[net.me] = kv_low[...]

            def kv_slot(s):
                rows = pl.ds(s * local_len, local_len)
                return lambda block, row: kv_all.at[block, rows]

            kv_line = Line(
                net,
                [
                    (kv_low.at[pl.ds(s * local_len, local_len)], kv_slot(s), False)
                    for s in range(seqs)
                ],
            )
            kv_line.tick()
        if head == group // 2:
            kv_line.tick()
    line.tick()
    kv_line.tick()

    for s in range(seqs):
        if s:
            kv_line.tick()
        rows = pl.ds(s * local_len, local_len)
        place = lax.broadcasted_iota(jnp.int32, (local_len, local_len), 0)
        lane = lax.broadcasted_iota(jnp.int32, (local_len, local_len), 1)
        for c in range(cols):
            at = pl.ds(c * local_len, local_len)
            keys[at, :] = kv_all[c, rows, :size]
            values[at, :] = kv_all[c, rows, size:]
            same = doc_col[rows, :] == rows_all[c, experts : experts + 1, rows]
            ahead = (c - net.me) * local_len
            allowed = same & (lane + ahead <= place)
            bias[:, at] = jnp.where(allowed, 0.0, masked_score)

        def attend(g, carry, s=s, rows=rows):
            at = pl.ds(pl.multiple_of(g * size, size), size)
            scores = dot_nt(q_low[rows, at], keys[...]) * scale + bias[...]
            weight = jnp.exp(scores - jnp.max(scores, axis=1, keepdims=True))
            p = (weight / jnp.sum(weight, axis=1, keepdims=True)).astype(bf16)
            probs[s, g] = p
            heads[rows, at] = dot_nn(p, values[...]).astype(bf16)
            return carry

        lax.fori_loop(0, group, attend, 0)
        if line.now < ready_out:
            line.tick()
    line.tick(max(0, ready_out - line.now))
    copies[first].wait()

    pieces = from_core.shape[0]
    piece_rows = from_core.shape[1]

    def row_piece(core, i):
        return pl.ds(
            pl.multiple_of((core * pieces + i) * piece_rows, piece_rows), piece_rows
        )

    half = pieces * piece_rows
    across = []
    for core in (1 - net.core, net.core):
        at_rows = pl.ds(pl.multiple_of(core * half, half), half)
        for tile in range(width // TILE):
            at = pl.ds(tile * TILE, TILE)
            partial[at_rows, at] = dot_nt(heads[at_rows, :], out_weights[at, :]).astype(bf16)
        if not across:
            across = [
                net.send(partial.at[row_piece(1 - net.core, i)], from_core.at[i], net.core_peer())
                for i in range(pieces)
            ]
    along, back = [], []
    for i in range(pieces):
        across[i].wait_recv()
        add_rows(to_x.at[i], [partial.at[row_piece(net.core, i)], from_core.at[i]])
        along.append(net.send(to_x.at[i], from_x.at[i], net.x_peer()))
    line.tick()
    for i in range(pieces):
        along[i].wait_recv()
        at = row_piece(net.core, i)
        add_rows(attn.at[at], [to_x.at[i], from_x.at[i]])
        back.append(net.send(attn.at[at], attn.at[at], net.core_peer()))
    line.tick()
    for copy in back:
        copy.wait_recv()

    def norm_second(at):
        x = tokens[at, :].astype(f32) + attn[at, :].astype(f32)
        total = jnp.sum(x * x, axis=1, keepdims=True)
        h2[at, :] = (x * lax.rsqrt(total / width + norm_eps) * gains[1:2, :]).astype(bf16)

    chunks(norm_second)
    line.tick()
    logits = dot_nn(h2[...], weights[:, start : start + LANES])
    lane = lax.broadcasted_iota(jnp.int32, (toks, LANES), 1)
    logits = jnp.where(lane < experts, logits, masked_score)
    weight = jnp.exp(logits - jnp.max(logits, axis=1, keepdims=True))
    chance = weight / jnp.sum(weight, axis=1, keepdims=True)
    router_probs[...] = chance
    picked = jnp.where((table_col[...] > 0) & (lane < experts), chance, 0.0)
    gate[...] = picked / jnp.sum(picked, axis=1, keepdims=True)
    line.drain()
    kv_line.drain()
    for copy in (copies[first + 1], copies[first + 3]):
        copy.wait()
    net.finish()


def front_call(
    cols, collective_id, experts, tokens, query, key, value, misc, out_own, grad_own, table_row,
    table_col, doc_col, cosine, sine, seqs,
):
    toks, width = tokens.shape
    q_width = query.shape[1]
    size = HEAD_DIM
    local_len = toks // seqs
    vmem, any_space = pl.BlockSpec(memory_space=pltpu.VMEM), pl.BlockSpec(memory_space=pl.ANY)

    def shape(*dims, dtype=bf16):
        return jax.ShapeDtypeStruct(dims, dtype)

    pieces = 4
    piece = (pieces, toks // 2 // pieces, width)
    copies = 320
    return pl.pallas_call(
        functools.partial(front_kernel, cols, experts),
        out_shape=[
            shape(width, q_width + 2 * size + LANES),
            shape(width, q_width),
            shape(cols, toks, width),
            shape(cols, *table_row.shape, dtype=f32),
            shape(cols, *table_col.shape),
            shape(toks, width),
            shape(toks, q_width),
            shape(cols, toks, 2 * size),
            shape(seqs, q_width // size, local_len, cols * local_len),
            shape(toks, q_width),
            shape(toks, width),
            shape(toks, width),
            shape(toks, LANES, dtype=f32),
            shape(toks, LANES, dtype=f32),
        ],
        in_specs=[vmem] + [any_space] * 6 + [vmem] * 5,
        out_specs=[vmem, vmem, any_space] + [vmem] * 11,
        scratch_shapes=[
            pltpu.VMEM((8, width), f32),
            pltpu.VMEM((toks, LANES), f32),
            pltpu.VMEM((toks, 2 * size), bf16),
            pltpu.VMEM((cols * local_len, size), bf16),
            pltpu.VMEM((cols * local_len, size), bf16),
            pltpu.VMEM((local_len, cols * local_len), f32),
            pltpu.VMEM((toks, width), bf16),
            pltpu.VMEM(piece, bf16),
            pltpu.VMEM(piece, bf16),
            pltpu.VMEM(piece, bf16),
            pltpu.SemaphoreType.DMA((copies,)),
            pltpu.SemaphoreType.DMA((copies,)),
            pltpu.SemaphoreType.DMA((16,)),
        ],
        compiler_params=pltpu.CompilerParams(
            collective_id=collective_id, has_side_effects=True, vmem_limit_bytes=48 << 20
        ),
        name=f"front_{collective_id}",
    )(
        tokens, query, key, value, misc, out_own, grad_own,
        table_row, table_col, doc_col, cosine, sine,
    )


def experts_kernel(
    cols,
    capacity,
    h2,
    grads,
    w_gate,
    w_up,
    w_down,
    w_shared,
    rank_row,
    rank_col,
    gate_own,
    out_part,
    back,
    g_gate,
    g_up,
    g_down,
    g_shared,
    shared_back,
    gate_dots,
    h2_all,
    xs_all,
    cs_all,
    wgu,
    wd,
    ws,
    gates,
    hb,
    xbuf,
    ybuf,
    obuf,
    part,
    pre,
    gcol,
    dcol,
    dz_all,
    zg_all,
    dgu_all,
    sz_all,
    sgu_all,
    from_core,
    from_x,
    from_y,
    from_z,
    kept,
    dots,
    dots_core,
    dots_x,
    tiles,
    tiles_all,
    stage,
    stage_low,
    send_sems,
    recv_sems,
    local_sems,
):
    net = Net(cols, send_sems, recv_sems)
    toks, width = h2.shape
    exp_local, _, hidden = w_gate.shape
    high = net.high_count
    pad = ws.shape[1] // 3
    rows_w = w_shared.shape[1]
    slots = exp_local * capacity
    pair = 2 * capacity
    piece = width // lax.axis_size("row")
    share = width // LANES // 5 * LANES
    rest = (width - 4 * share) // 2
    wide = width // TILE
    net.greet([net.col_peer(step) for step in range(1, cols)] + row_peers(net))

    def local_copy(source, target, index):
        copy = pltpu.make_async_copy(source, target, local_sems.at[index])
        copy.start()
        return copy

    gate_copies = [
        net.send(gate_own, gates.at[net.me], net.col_peer(step)) for step in range(1, cols)
    ]
    gates[net.me] = gate_own[...]

    def feature_e(row):
        return pl.ds(pl.multiple_of(row * share, LANES), share)

    def feature_r(core):
        return pl.ds(pl.multiple_of(4 * share + core * rest, LANES), rest)

    own_e, own_r = feature_e(net.row), feature_r(net.core)
    far_e = feature_e(2 * (1 - net.outer) + net.core)

    def pass_on(source, block, features, peer):
        return net.send(source.at[..., features], h2_all.at[block, :, features], peer)

    along_z, along_y, along_x, to_core = {}, {}, {}, {}

    def start_z(step):
        along_z[step] = [
            pass_on(h2, net.me, own_e, net.z_peer(high - step)),
            pass_on(h2, net.me, own_r, net.z_peer(high - step)),
        ]

    start_z(1)
    along_y[0] = [
        pass_on(h2, net.me, own_e, net.y_peer()),
        pass_on(h2, net.me, own_r, net.y_peer()),
    ]

    def block_of(step, other):
        return net.block_ahead(step, other)

    def share_in_chip(step, other):
        block = block_of(step, other)
        source = h2_all.at[block]
        along_x[step, other] = pass_on(source, block, own_e, net.x_peer())
        to_core[step, other] = [
            pass_on(source, block, own_e, net.core_peer()),
            pass_on(source, block, own_r, net.core_peer()),
        ]

    def arrived_y(step):
        for copy in along_y[step]:
            copy.wait_recv()
        share_in_chip(step, True)

    def arrived_z(step):
        for copy in along_z[step]:
            copy.wait_recv()
        block = block_of(step, False)
        along_y[step] = [
            pass_on(h2_all.at[block], block, own_e, net.y_peer()),
            pass_on(h2_all.at[block], block, own_r, net.y_peer()),
        ]
        share_in_chip(step, False)

    def arrived_x(step, other):
        along_x[step, other].wait_recv()
        block = block_of(step, other)
        to_core[step, other].append(pass_on(h2_all.at[block], block, far_e, net.core_peer()))

    def whole(step, other):
        for copy in to_core[step, other]:
            copy.wait_recv()

    events = [functools.partial(arrived_y, 0)]
    for step in range(1, high):
        events.append(functools.partial(arrived_z, step))
        events.append(functools.partial(arrived_x, step - 1, True))
        events.append(functools.partial(arrived_y, step))
        events.append(functools.partial(arrived_x, step, False))
    events.append(functools.partial(arrived_x, high - 1, True))
    events = iter(events)

    def pump(count=1):
        for _ in range(count):
            event = next(events, None)
            if event is not None:
                event()

    loads = []
    for e in range(exp_local):
        loads.append(local_copy(w_down.at[e], wd.at[e], 3 * e))
        loads.append(local_copy(w_gate.at[e], wgu.at[e, :, pl.ds(0, hidden)], 3 * e + 1))
        loads.append(local_copy(w_up.at[e], wgu.at[e, :, pl.ds(hidden, hidden)], 3 * e + 2))
    base = 3 * exp_local
    own_rows = pl.ds(pl.multiple_of(net.me * rows_w, 16), rows_w)
    loads.append(local_copy(w_shared.at[net.me], ws.at[own_rows], base))
    swaps = []

    def swap_next(count):
        for _ in range(count):
            step = len(swaps) + 1
            if step < cols:
                block = lax.rem(net.me + step, cols)
                swaps.append(net.send(w_shared.at[block], ws.at[own_rows], net.col_peer(step)))

    keep_own = local_copy(h2, h2_all.at[net.me], base + 1)
    base += 2

    def load_pair(source, step):
        first = local_copy(source.at[block_of(step, False)], hb.at[0], base)
        second = local_copy(source.at[block_of(step, True)], hb.at[1], base + 1)
        first.wait()
        second.wait()

    slot_row = lax.broadcasted_iota(jnp.int32, (capacity, toks), 0).astype(f32) + 1.0
    slot_lane = lax.broadcasted_iota(jnp.int32, (toks, capacity), 1).astype(f32) + 1.0

    def chosen(block, e):
        return rank_row[block, e : e + 1, :] == slot_row

    def picks(block):
        rows = [
            jnp.where(chosen(block, e), 1.0, 0.0).astype(bf16) for e in range(exp_local)
        ]
        return jnp.concatenate(rows, axis=0)

    def picks_back(block):
        lanes = [
            jnp.where(rank_col[block, :, e : e + 1] == slot_lane, 1.0, 0.0).astype(bf16)
            for e in range(exp_local)
        ]
        return jnp.concatenate(lanes, axis=1)

    def dispatch(step):
        for b in (0, 1):
            table = picks(block_of(step, b == 1))

            def tile(index, b=b, table=table):
                at = tile_at(index, WIDE)
                rows = dot_nn(table, hb[b, :, at]).astype(bf16)
                for e in range(exp_local):
                    xbuf[e, pl.ds(b * capacity, capacity), at] = rows[
                        e * capacity : (e + 1) * capacity
                    ]

            each_tile(width // WIDE, tile)

    def save_rows(target, step):
        return [
            local_copy(
                xbuf.at[e], target.at[e, pl.ds(step * pair, pair)], base + 2 + e
            )
            for e in range(exp_local)
        ]

    saved = []
    for step in range(high):
        load_pair(grads, step)
        if step == 0:
            for copy in loads:
                copy.wait()
        for copy in saved:
            copy.wait()
        dispatch(step)
        saved = save_rows(cs_all, step)
        for e in range(exp_local):
            dz_all[e, pl.ds(step * pair, pair), :] = dot_nt(xbuf[e], wd[e]).astype(bf16)
        swap_next(2)
        pump()
    for copy in gate_copies:
        copy.wait_recv()
    keep_own.wait()

    across, onward, upward, far_z = {}, {}, {}, {}

    def features(row):
        return pl.ds(pl.multiple_of(row * piece, LANES), piece)

    other_row = 2 * (1 - net.outer) + net.core

    def hand_over(step):
        for b in (1, 0):
            for far in (1, 0):
                outer = 1 - net.outer if far else net.outer
                source = part.at[b, :, features(2 * outer + 1 - net.core)]
                across[step, b, far] = net.send(
                    source, from_core.at[far, step, b], net.core_peer()
                )

    def sum_cores(step):
        for b in (1, 0):
            for far, row in ((1, other_row), (0, net.row)):
                across[step, b, far].wait_recv()
                slot = from_core.at[far, step, b]
                add_rows(slot, [part.at[b, :, features(row)], slot])
                if far:
                    onward[step, b] = net.send(slot, from_x.at[step, b], net.x_peer())
        for b in (1, 0):
            for far in (1, 0):
                net.left(across[step, b, far])

    def sum_chips(step):
        for b in (1, 0):
            onward[step, b].wait_recv()
            slot = from_core.at[0, step, b]
            add_rows(slot, [slot, from_x.at[step, b]])
            if b:
                upward[step] = net.send(slot, from_y.at[step], net.y_peer())

    def sum_plane(step):
        upward[step].wait_recv()
        slot = from_core.at[0, step, 0]
        add_rows(slot, [slot, from_y.at[step]])
        if step:
            far_z[step] = net.send(slot, from_z.at[step - 1], net.z_peer(step))

    own_expert = lax.rem(net.me, cols) * exp_local
    gate_rows = gates.shape[1]
    gate_row = lax.broadcasted_iota(jnp.int32, (gate_rows, toks), 0)
    dots[...] = jnp.zeros_like(dots)
    for step in range(high):
        if step:
            whole(step, False)
        whole(step, True)
        load_pair(h2_all, step)
        for copy in saved:
            copy.wait()
        dispatch(step)
        saved = save_rows(xs_all, step)
        if step + 2 < high:
            for copy in along_z[step + 1]:
                net.left(copy)
            start_z(step + 2)
        pump()
        if step:
            for copy in out_copies:
                copy.wait()
        grad_copies = [
            local_copy(grads.at[block_of(step, b == 1)], obuf.at[b], base + 2 + exp_local + b)
            for b in (0, 1)
        ]
        if step:
            sum_cores(step - 1)
        rows = pl.ds(step * pair, pair)
        for e in range(exp_local):
            pre[...] = dot_nn(xbuf[e], wgu[e])
            for b in (0, 1):
                block = block_of(step, b == 1)
                gate = jnp.sum(
                    jnp.where(gate_row == own_expert + e, gates[block], 0.0), axis=0, keepdims=True
                )
                gate = jnp.sum(jnp.where(chosen(block, e), gate, 0.0), axis=1, keepdims=True)
                gcol[pl.ds(b * capacity, capacity), :] = jnp.broadcast_to(gate, (capacity, LANES))

            def gating(index, e=e, step=step):
                at = pl.ds(pl.multiple_of(index * 32, 32), 32)
                saved_at = pl.ds(pl.multiple_of(step * pair + index * 32, 32), 32)
                a, u = pre[at, :hidden], pre[at, hidden:]
                gate = jnp.concatenate([gcol[at, :]] * (hidden // LANES), axis=1)
                dz = dz_all[e, saved_at, :].astype(f32)
                sig = 1.0 / (1.0 + jnp.exp(-a))
                silu = a * sig
                slope = sig * (1.0 + a * (1.0 - sig))
                z = silu * u
                dcol[at, :] = jnp.broadcast_to(
                    jnp.sum(z * dz, axis=1, keepdims=True), (32, LANES)
                )
                zg_all[e, saved_at, :] = (z * gate).astype(bf16)
                dz = dz * gate
                dgu_all[e, saved_at, :hidden] = (dz * u * slope).astype(bf16)
                dgu_all[e, saved_at, hidden:] = (dz * silu).astype(bf16)

            each_tile(pair // 32, gating)
            for b in (0, 1):
                block = block_of(step, b == 1)
                col = dcol[pl.ds(b * capacity, capacity), :]
                col = jnp.concatenate([col] * (toks // LANES), axis=1)
                dots[block, e : e + 1, :] = jnp.sum(
                    jnp.where(chosen(block, e), col, 0.0), axis=0, keepdims=True
                )

            def out_tile(index, e=e):
                at = tile_at(index, WIDE)
                y = dot_nn(zg_all[e, rows, :], wd[e, :, at]).astype(bf16)
                for b in (0, 1):
                    ybuf[b, pl.ds(e * capacity, capacity), at] = y[b * capacity : (b + 1) * capacity]

            each_tile(width // WIDE, out_tile)
            pump()
        if step == 0:
            for copy in swaps:
                copy.wait_recv()
        for copy in grad_copies:
            copy.wait()
        inner = dot_nn(hb[...].reshape(2 * toks, width), ws[:, : 2 * pad])
        sdz_both = dot_nn(obuf[...].reshape(2 * toks, width), ws[:, 2 * pad :])
        for b in (0, 1):
            block = block_of(step, b == 1)
            sa, su = inner[b * toks : (b + 1) * toks, :pad], inner[b * toks : (b + 1) * toks, pad:]
            sdz = sdz_both[b * toks : (b + 1) * toks]
            sig = 1.0 / (1.0 + jnp.exp(-sa))
            silu = sa * sig
            slope = sig * (1.0 + sa * (1.0 - sig))
            sz_all[block] = (silu * su).astype(bf16)
            sgu_all[block, :, :pad] = (sdz * su * slope).astype(bf16)
            sgu_all[block, :, pad:] = (sdz * silu).astype(bf16)
        out_copies = []
        for b in (0, 1):
            block = block_of(step, b == 1)
            table = picks_back(block)

            def join_tile(index, b=b, table=table, block=block):
                at = tile_at(index, WIDE)
                total = dot_nn(table, ybuf[b, :, at])
                total = total + dot_nt(sz_all[block], ws[at, 2 * pad :])
                obuf[b, :, at] = total.astype(bf16)

            each_tile(width // WIDE, join_tile)
            out_copies.append(
                local_copy(obuf.at[b], out_part.at[block], base + 2 + exp_local + b)
            )
        pump()
        if step:
            sum_chips(step - 1)
        for e in range(exp_local):

            def back_tile(index, e=e):
                at = tile_at(index, WIDE)
                y = dot_nt(dgu_all[e, rows, :], wgu[e, at, :]).astype(bf16)
                for b in (0, 1):
                    ybuf[b, pl.ds(e * capacity, capacity), at] = y[b * capacity : (b + 1) * capacity]

            each_tile(width // WIDE, back_tile)
        pump()
        for b in (1, 0):
            block = block_of(step, b == 1)
            table = picks_back(block)

            def back_join(index, b=b, table=table, block=block):
                at = tile_at(index, WIDE)
                total = dot_nn(table, ybuf[b, :, at])
                total = total + dot_nt(sgu_all[block], ws[at, : 2 * pad])
                part[b, :, at] = total.astype(bf16)

            each_tile(width // WIDE, back_join)
        hand_over(step)
        if step:
            sum_plane(step - 1)
    pump(64)
    last = high - 1
    for copy in saved + out_copies:
        copy.wait()

    load_sem, store_sem = base + 4 + exp_local, base + 6 + exp_local

    def passes(count, load, work, stores):
        def load_copy(j, slot):
            source, target = load(j, slot)
            return pltpu.make_async_copy(source, target, local_sems.at[load_sem + slot])

        def store_copies(j, slot):
            return [
                pltpu.make_async_copy(
                    source, target, local_sems.at[store_sem + 2 * slot + i]
                )
                for i, (source, target) in enumerate(stores(j, slot))
            ]

        load_copy(0, 0).start()

        def body(j):
            slot = lax.rem(j, 2)

            @pl.when(j + 1 < count)
            def _():
                load_copy(j + 1, 1 - slot).start()

            load_copy(j, slot).wait()

            @pl.when(j >= 2)
            def _():
                for copy in store_copies(j - 2, slot):
                    copy.wait()

            work(j, slot)
            for copy in store_copies(j, slot):
                copy.start()

        each_tile(count, body)
        for j in range(max(0, count - 2), count):
            for copy in store_copies(j, j % 2):
                copy.wait()

    def inner_grads(e):
        passes(
            wide,
            lambda j, slot: (
                xs_all.at[e, :, tile_at(j)],
                tiles.at[slot],
            ),
            lambda j, slot: put(stage.at[slot], dot_tn(tiles[slot], dgu_all[e]).astype(bf16)),
            lambda j, slot: [
                (stage.at[slot, :, pl.ds(0, hidden)], g_gate.at[e, tile_at(j)]),
                (stage.at[slot, :, pl.ds(hidden, hidden)], g_up.at[e, tile_at(j)]),
            ],
        )

    def put(target, value):
        target[...] = value

    def down_grads(e):
        passes(
            wide,
            lambda j, slot: (
                cs_all.at[e, :, tile_at(j)],
                tiles.at[slot],
            ),
            lambda j, slot: put(
                stage.at[slot, pl.ds(0, hidden), pl.ds(0, TILE)],
                dot_tn(zg_all[e], tiles[slot]).astype(bf16),
            ),
            lambda j, slot: [
                (
                    stage.at[slot, pl.ds(0, hidden), pl.ds(0, TILE)],
                    g_down.at[e, :, tile_at(j)],
                ),
            ],
        )

    def shared_grads(source, others, start, size):
        def work(j, slot):
            total = dot_tn(tiles_all[slot, 0], others[0])
            for c in range(1, cols):
                total = total + dot_tn(tiles_all[slot, c], others[c])
            stage_low[slot, :, :size] = total.astype(bf16)

        def load(j, slot):
            return (source.at[:, :, tile_at(j)], tiles_all.at[slot])

        passes(
            wide,
            lambda j, slot: load(j, slot),
            work,
            lambda j, slot: [
                (
                    stage_low.at[slot, :, pl.ds(0, size)],
                    g_shared.at[tile_at(j), pl.ds(start, size)],
                ),
            ],
        )

    first_dots = net.send(dots, dots_core, net.core_peer())
    shared_grads(h2_all, sgu_all, 0, 2 * pad)
    sum_cores(last)
    shared_grads(grads, sz_all, 2 * pad, pad)
    keep_own = local_copy(g_shared.at[own_rows], shared_back.at[net.me], base)
    returns = []
    for step in range(1, cols):
        block = lax.rem(net.me + step, cols)
        rows = pl.ds(pl.multiple_of(block * rows_w, 16), rows_w)
        returns.append(net.send(g_shared.at[rows], shared_back.at[net.me], net.col_peer(step)))
    inner_grads(0)
    first_dots.wait_recv()
    net.left(first_dots)
    dots[...] = dots[...] + dots_core[...]
    second_dots = net.send(dots, dots_x, net.x_peer())
    inner_grads(1)
    sum_chips(last)
    second_dots.wait_recv()
    dots_core[...] = dots[...] + dots_x[...]
    third_dots = []
    for step in range(1, cols):
        block = lax.rem(net.me + step, cols)
        third_dots.append(
            net.send(dots_core.at[block], gate_dots.at[net.me], net.col_peer(step))
        )
    gate_dots[net.me] = dots_core[net.me]
    down_grads(0)
    sum_plane(last)
    for step in range(1, high):
        far_z[step].wait_recv()
    add_rows(kept, [from_core.at[0, 0, 0], *[from_z.at[step - 1] for step in range(1, high)]])
    own, other = features(net.row), features(other_row)
    back[:, own] = kept[...].astype(bf16)
    far = net.send(back.at[:, own], back.at[:, own], net.x_peer())
    near = net.send(back.at[:, own], back.at[:, own], net.core_peer())
    far.wait_recv()
    crossed = net.send(back.at[:, other], back.at[:, other], net.core_peer())
    down_grads(1)
    keep_own.wait()
    for copy in returns:
        copy.wait_recv()
    near.wait_recv()
    crossed.wait_recv()
    for copy in third_dots:
        copy.wait_recv()
    net.finish()


def experts_call(
    cols, collective_id, capacity, h2, grads, w_gate, w_up, w_down, w_shared, rank_row, rank_col, gate
):
    toks, width = h2.shape
    exp_local, _, hidden = w_gate.shape
    high = cols // 2
    pad = w_shared.shape[2] // 3
    piece = width // lax.axis_size("row")
    pair = 2 * capacity
    any_space = pl.BlockSpec(memory_space=pl.ANY)
    vmem = pl.BlockSpec(memory_space=pltpu.VMEM)
    copies = 160

    def shape(*dims, dtype=bf16):
        return jax.ShapeDtypeStruct(dims, dtype)

    return pl.pallas_call(
        functools.partial(experts_kernel, cols, capacity),
        out_shape=[
            shape(cols, toks, width),
            shape(toks, width),
            shape(exp_local, width, hidden),
            shape(exp_local, width, hidden),
            shape(exp_local, hidden, width),
            shape(width, 3 * pad),
            shape(*w_shared.shape),
            shape(cols, 8, toks, dtype=f32),
            shape(cols, toks, width),
            shape(exp_local, cols * capacity, width),
            shape(exp_local, cols * capacity, width),
        ],
        in_specs=[any_space] * 6 + [vmem] * 3,
        out_specs=[
            any_space,
            vmem,
            any_space,
            any_space,
            any_space,
            any_space,
            any_space,
            vmem,
            any_space,
            any_space,
            any_space,
        ],
        scratch_shapes=[
            pltpu.VMEM((exp_local, width, 2 * hidden), bf16),
            pltpu.VMEM((exp_local, hidden, width), bf16),
            pltpu.VMEM((width, 3 * pad), bf16),
            pltpu.VMEM((cols, *gate.shape), f32),
            pltpu.VMEM((2, toks, width), bf16),
            pltpu.VMEM((exp_local, pair, width), bf16),
            pltpu.VMEM((2, exp_local * capacity, width), bf16),
            pltpu.VMEM((2, toks, width), bf16),
            pltpu.VMEM((2, toks, width), bf16),
            pltpu.VMEM((pair, 2 * hidden), f32),
            pltpu.VMEM((pair, LANES), f32),
            pltpu.VMEM((pair, LANES), f32),
            pltpu.VMEM((exp_local, cols * capacity, hidden), bf16),
            pltpu.VMEM((exp_local, cols * capacity, hidden), bf16),
            pltpu.VMEM((exp_local, cols * capacity, 2 * hidden), bf16),
            pltpu.VMEM((cols, toks, pad), bf16),
            pltpu.VMEM((cols, toks, 2 * pad), bf16),
            pltpu.VMEM((2, high, 2, toks, piece), bf16),
            pltpu.VMEM((high, 2, toks, piece), bf16),
            pltpu.VMEM((high, toks, piece), bf16),
            pltpu.VMEM((high - 1, toks, piece), bf16),
            pltpu.VMEM((toks, piece), f32),
            pltpu.VMEM((cols, 8, toks), f32),
            pltpu.VMEM((cols, 8, toks), f32),
            pltpu.VMEM((cols, 8, toks), f32),
            pltpu.VMEM((2, cols * capacity, TILE), bf16),
            pltpu.VMEM((2, cols, toks, TILE), bf16),
            pltpu.VMEM((2, TILE, 2 * hidden), bf16),
            pltpu.VMEM((2, TILE, 2 * pad), bf16),
            pltpu.SemaphoreType.DMA((copies,)),
            pltpu.SemaphoreType.DMA((copies,)),
            pltpu.SemaphoreType.DMA((24,)),
        ],
        compiler_params=pltpu.CompilerParams(
            collective_id=collective_id, has_side_effects=True, vmem_limit_bytes=62 << 20
        ),
        name=f"experts_{collective_id}",
    )(h2, grads, w_gate, w_up, w_down, w_shared, rank_row, rank_col, gate)


def experts_kernels(
    cols, collective_id, capacity, h2, grad_all, w_gate, w_up, w_down, shared_own, *tables
):
    rows_w, shared_part = shared_own.shape[1], shared_own.shape[2] // 3
    pad = -shared_part % LANES
    padded = jnp.pad(
        shared_own.reshape(cols, rows_w, 3, shared_part), ((0, 0), (0, 0), (0, 0), (0, pad))
    )
    padded = padded.reshape(cols, rows_w, -1)
    out_part, back, g_gate, g_up, g_down, _, shared_back, gate_dots, *_ = experts_call(
        cols, collective_id, capacity, h2, grad_all, w_gate, w_up, w_down, padded, *tables
    )
    shared_back = shared_back.reshape(cols, rows_w, 3, -1)[..., :shared_part]
    wide = (grad.astype(f32) for grad in (g_gate, g_up, g_down))
    return (out_part, back, gate_dots, shared_back.reshape(cols, rows_w, -1), *wide)


def fits(cols, rows, width):
    return cols % 2 == 0 and cols * rows * width * 2 <= 12 << 20


class Sum2D:
    def __init__(self, net, source, start, count, from_y, from_z, out):
        self.net, self.source, self.start, self.count = net, source, start, count
        self.from_y, self.from_z, self.out = from_y, from_z, out
        self.rows = pl.ds(start, count)
        self.order = [*range(1, net.high_count), 0]
        self.along_y, self.along_z = {}, {}

    def mine(self, block):
        return self.source(block, self.start, self.count)

    def send_y(self):
        for step in self.order:
            source = self.mine(self.net.block_ahead(step, True))
            self.along_y[step] = self.net.send(
                source, self.from_y.at[step, self.rows], self.net.y_peer()
            )

    def send_z(self):
        for step in self.order:
            self.along_y[step].wait_recv()
            slot = self.from_y.at[step, self.rows]
            if step:
                add_rows(slot, [self.mine(self.net.block_ahead(step)), slot])
                self.along_z[step] = self.net.send(
                    slot, self.from_z.at[step - 1, self.rows], self.net.z_peer(step)
                )

    def last(self):
        for step in range(1, self.net.high_count):
            self.along_z[step].wait_recv()
        terms = [
            self.from_z.at[step - 1, self.rows] for step in range(1, self.net.high_count)
        ]
        mine = self.mine(self.net.me)
        add_rows(self.out.at[self.rows], [mine, self.from_y.at[0, self.rows], *terms])


def rear_kernel(
    cols,
    experts,
    out_part,
    back,
    gate_dots,
    gate,
    router_probs,
    table_col,
    h1,
    h2,
    tokens,
    attn,
    weights_in,
    out_weights_in,
    grads,
    heads,
    q_low,
    kv_all,
    probs,
    cosine,
    sine,
    out_slice,
    d_tokens,
    share_qkv,
    share_misc,
    share_out,
    weights,
    out_weights,
    misc,
    misc_low,
    grad_own,
    gains,
    dots,
    logit_low,
    low,
    dob,
    keys,
    values,
    stacked,
    ds_all,
    kv_grad,
    kv_share,
    dqkv,
    gain_sums,
    own,
    from_core,
    from_x,
    from_y,
    from_z,
    kv_y,
    kv_z,
    out_y,
    out_z,
    qkv_y,
    qkv_z,
    misc_y,
    misc_z,
    row_core,
    row_to,
    row_from,
    send_sems,
    recv_sems,
    local_sems,
):
    net = Net(cols, send_sems, recv_sems)
    toks, width = back.shape
    size = HEAD_DIM
    q_width = q_low.shape[1]
    group = q_width // size
    qkv_width = q_width + 2 * size
    seqs = probs.shape[0]
    local_len = toks // seqs
    rows_w = width // cols
    piece = width // lax.axis_size("row")
    scale = 1.0 / math.sqrt(size)
    other_row = 2 * (1 - net.outer) + net.core

    def local_copy(source, target, index):
        copy = pltpu.make_async_copy(source, target, local_sems.at[index])
        copy.start()
        return copy

    def features(row):
        return pl.ds(pl.multiple_of(row * piece, LANES), piece)

    loads = [
        local_copy(weights_in, weights, 0),
        local_copy(out_weights_in, out_weights, 1),
        local_copy(grads.at[net.me], grad_own, 2),
    ]
    near_load = local_copy(out_part.at[:, :, features(net.row)], own.at[0], 3)
    far_load = local_copy(out_part.at[:, :, features(other_row)], own.at[1], 4)
    net.greet(col_peers(net) + row_peers(net))

    pieces = 4
    count = toks // pieces
    order = [*range(1, net.high_count), 0]
    keys_of = [(step, True) for step in order] + [(step, False) for step in order]
    across, onward, along_y, along_z = {}, {}, {}, {}

    def rows_of(q):
        return pl.ds(q * count, count)

    def out_core(q):
        for far in (1, 0):
            outer = 1 - net.outer if far else net.outer
            for key in keys_of:
                block = net.block_ahead(*key)
                across[q, far, key] = net.send(
                    out_part.at[block, rows_of(q), features(2 * outer + 1 - net.core)],
                    from_core.at[far, block, rows_of(q)],
                    net.core_peer(),
                )

    def out_x(q):
        for key in keys_of:
            across[q, 1, key].wait_recv()
            block = net.block_ahead(*key)
            slot = from_core.at[1, block, rows_of(q)]
            add_rows(slot, [own.at[1, block, rows_of(q)], slot])
            onward[q, key] = net.send(slot, from_x.at[block, rows_of(q)], net.x_peer())

    def out_y_stage(q):
        for key in keys_of:
            across[q, 0, key].wait_recv()
            onward[q, key].wait_recv()
            block = net.block_ahead(*key)
            slot = from_core.at[0, block, rows_of(q)]
            add_rows(slot, [own.at[0, block, rows_of(q)], slot, from_x.at[block, rows_of(q)]])
            if key[1]:
                along_y[q, key[0]] = net.send(
                    slot, from_y.at[key[0], rows_of(q)], net.y_peer()
                )

    def out_z_stage(q):
        for step in order:
            along_y[q, step].wait_recv()
            slot = from_core.at[0, net.block_ahead(step), rows_of(q)]
            add_rows(slot, [slot, from_y.at[step, rows_of(q)]])
            if step:
                along_z[q, step] = net.send(
                    slot, from_z.at[step - 1, rows_of(q)], net.z_peer(step)
                )

    def out_last(q):
        for step in range(1, net.high_count):
            along_z[q, step].wait_recv()
        terms = [from_z.at[step - 1, rows_of(q)] for step in range(1, net.high_count)]
        add_rows(out_slice.at[rows_of(q)], [from_core.at[0, net.me, rows_of(q)], *terms])

    state = {"tick": 0}

    def pump(ticks=1):
        for _ in range(ticks):
            tick = state["tick"]
            state["tick"] += 1
            for lag, stage in enumerate((out_core, out_x, out_y_stage, out_z_stage, out_last)):
                if 0 <= tick - lag < pieces:
                    stage(tick - lag)

    pump()
    for copy in loads:
        copy.wait()

    def chunks(body, rows=32):
        def step(index, carry):
            body(pl.ds(pl.multiple_of(index * rows, rows), rows))
            return carry

        lax.fori_loop(0, toks // rows, step, 0)

    for tile in range(width // TILE):
        at = pl.ds(tile * TILE, TILE)
        turned = jnp.transpose(weights[at, qkv_width : qkv_width + LANES].astype(f32))
        gains[:, at] = turned[experts : experts + 8]
    dots[...] = jnp.zeros_like(dots)
    for c in range(cols):
        dots[2 * c : 2 * c + 2, :] = gate_dots[c, 0:2, :]
    gate_grad = jnp.transpose(dots[...])
    lane = lax.broadcasted_iota(jnp.int32, (toks, LANES), 1)
    mask = (table_col[...] > 0) & (lane < experts)
    chance, gates = router_probs[...], gate[...]
    total = jnp.sum(jnp.where(mask, chance, 0.0), axis=1, keepdims=True)
    gate_grad = jnp.where(mask, gate_grad, 0.0)
    pick_grad = gate_grad - jnp.sum(gates * gate_grad, axis=1, keepdims=True)
    chance_grad = jnp.where(mask, pick_grad / total, 0.0)
    logit_grad = chance * (chance_grad - jnp.sum(chance * chance_grad, axis=1, keepdims=True))
    logit_low[...] = logit_grad.astype(bf16)
    near_load.wait()
    far_load.wait()
    pump()

    for tile in range(width // TILE):
        at = pl.ds(tile * TILE, TILE)
        d_tokens[:, at] = back[:, at].astype(f32) + dot_nt(
            logit_low[...], weights[at, qkv_width : qkv_width + LANES]
        )
    gain_sums[...] = jnp.zeros_like(gain_sums)

    def fold(values, start):
        total = values[0:8]
        for r in range(8, values.shape[0], 8):
            total = total + values[r : r + 8]
        gain_sums[start : start + 8, :] = gain_sums[start : start + 8, :] + total

    def norm_second(at):
        x = tokens[at, :].astype(f32) + attn[at, :].astype(f32)
        inverse = lax.rsqrt(jnp.sum(x * x, axis=1, keepdims=True) / width + norm_eps)
        base = x * inverse
        dh = d_tokens[at, :]
        fold(dh * base, 8)
        scaled = dh * gains[1:2, :]
        mean = jnp.sum(scaled * base, axis=1, keepdims=True) / width
        middle = inverse * (scaled - base * mean) + grad_own[at, :].astype(f32)
        d_tokens[at, :] = middle
        low[at, :] = middle.astype(bf16)

    chunks(norm_second, 16)
    dob[...] = dot_nn(low[...], out_weights[...]).astype(bf16)
    pump()
    for tile in range(width // TILE):
        at = pl.ds(tile * TILE, TILE)
        out_weights[at, :] = dot_tn(low[:, at], heads[...]).astype(bf16)

    def blocks_of(array):
        def source(block, start, count):
            return array.at[pl.ds(pl.multiple_of(block * rows_w + start, 16), count)]

        return source

    out_pieces = 4
    out_count = rows_w // out_pieces
    out_line = [
        Sum2D(net, blocks_of(out_weights), q * out_count, out_count, out_y, out_z, share_out)
        for q in range(out_pieces)
    ]
    out_line[0].send_y()
    out_line[1].send_y()

    kv_line = [
        Sum2D(
            net,
            lambda block, start, count: kv_grad.at[block, pl.ds(start, count)],
            s * local_len,
            local_len,
            kv_y,
            kv_z,
            kv_share,
        )
        for s in range(seqs)
    ]
    for s in range(seqs):
        rows = pl.ds(s * local_len, local_len)
        for c in range(cols):
            at = pl.ds(c * local_len, local_len)
            keys[at, :] = kv_all[c, rows, :size]
            values[at, :] = kv_all[c, rows, size:]

        def attend(g, carry, s=s, rows=rows):
            at = pl.ds(pl.multiple_of(g * size, size), size)
            grow = pl.ds(pl.multiple_of(g * local_len, local_len), local_len)
            dout = dob[rows, at]
            stacked[0, grow, :] = q_low[rows, at]
            stacked[1, grow, :] = dout
            p = probs[s, g]
            p = p.astype(f32)
            dp = dot_nt(dout, values[...])
            delta = jnp.sum(p * dp, axis=1, keepdims=True)
            ds = (p * (dp - delta)).astype(bf16)
            ds_all[grow, :] = ds
            raw = dot_nn(ds, keys[...]) * scale
            dqkv[rows, at] = (
                raw * cosine[rows, :] - pltpu.roll(raw, size // 2, 1) * sine[rows, :]
            ).astype(bf16)
            return carry

        lax.fori_loop(0, group, attend, 0)
        dk = (dot_tn(ds_all[...], stacked[0]) * scale).astype(bf16)
        dv = dot_tn(probs[s].reshape(group * local_len, -1), stacked[1]).astype(bf16)
        for c in range(cols):
            kv_grad[c, rows, :size] = dk[c * local_len : (c + 1) * local_len]
            kv_grad[c, rows, size:] = dv[c * local_len : (c + 1) * local_len]
        kv_line[s].send_y()
        if s == 0:
            out_line[0].send_z()
            pump()
        else:
            kv_line[s - 1].send_z()
    kv_line[seqs - 1].send_z()
    out_line[1].send_z()
    out_line[2].send_y()
    for s in range(seqs):
        kv_line[s].last()
    raw = kv_share[:, :size]
    dqkv[:, q_width : q_width + size] = (
        raw * cosine[...] - pltpu.roll(raw, size // 2, 1) * sine[...]
    ).astype(bf16)
    dqkv[:, q_width + size : qkv_width] = kv_share[:, size:].astype(bf16)

    row_pieces, piece_rows = row_core.shape[0], row_core.shape[1]
    half = row_pieces * piece_rows

    def row_piece(core, i):
        return pl.ds(pl.multiple_of((core * row_pieces + i) * piece_rows, piece_rows), piece_rows)

    over = []
    for core in (1 - net.core, net.core):
        at_rows = pl.ds(pl.multiple_of(core * half, half), half)
        for tile in range(width // TILE):
            at = pl.ds(tile * TILE, TILE)
            low[at_rows, at] = dot_nt(dqkv[at_rows, :], weights[at, :qkv_width]).astype(bf16)
        if not over:
            over = [
                net.send(low.at[row_piece(1 - net.core, i)], row_core.at[i], net.core_peer())
                for i in range(row_pieces)
            ]

    qkv_pieces = 5
    qkv_count = rows_w // qkv_pieces
    for tile in range(width // TILE):
        at = pl.ds(tile * TILE, TILE)
        misc[at, :] = dot_tn(h2[:, at], logit_low[...])
        weights[at, :qkv_width] = dot_tn(h1[:, at], dqkv[...]).astype(bf16)
    qkv_line = [
        Sum2D(
            net,
            lambda block, start, count: weights.at[
                pl.ds(pl.multiple_of(block * rows_w + start, 16), count), pl.ds(0, qkv_width)
            ],
            q * qkv_count,
            qkv_count,
            qkv_y,
            qkv_z,
            share_qkv,
        )
        for q in range(qkv_pieces)
    ]
    qkv_line[0].send_y()
    along, returned = [], []
    for i in range(row_pieces):
        over[i].wait_recv()
        add_rows(row_to.at[i], [low.at[row_piece(net.core, i)], row_core.at[i]])
        along.append(net.send(row_to.at[i], row_from.at[i], net.x_peer()))
    qkv_line[1].send_y()
    for i in range(row_pieces):
        along[i].wait_recv()
        at = row_piece(net.core, i)
        add_rows(grad_own.at[at], [row_to.at[i], row_from.at[i]])
        returned.append(net.send(grad_own.at[at], grad_own.at[at], net.core_peer()))
    qkv_line[0].send_z()
    pump()
    for copy in returned:
        copy.wait_recv()

    def norm_first(at):
        x = tokens[at, :].astype(f32)
        inverse = lax.rsqrt(jnp.sum(x * x, axis=1, keepdims=True) / width + norm_eps)
        base = x * inverse
        dh = grad_own[at, :].astype(f32)
        fold(dh * base, 0)
        scaled = dh * gains[0:1, :]
        mean = jnp.sum(scaled * base, axis=1, keepdims=True) / width
        d_tokens[at, :] = d_tokens[at, :] + inverse * (scaled - base * mean)

    chunks(norm_first, 16)
    total = [jnp.sum(gain_sums[8 * i : 8 * i + 8, :], axis=0, keepdims=True) for i in (0, 1)]
    row_at = lax.broadcasted_iota(jnp.int32, (LANES, TILE), 0)
    for tile in range(width // TILE):
        at = pl.ds(tile * TILE, TILE)
        part = slice(tile * TILE, (tile + 1) * TILE)
        placed = jnp.where(row_at == experts, total[0][:, part], 0.0)
        placed = jnp.where(row_at == experts + 1, total[1][:, part], placed)
        lanes = lax.broadcasted_iota(jnp.int32, (TILE, LANES), 1)
        misc_low[at, :] = jnp.where(lanes < experts, misc[at, :], jnp.transpose(placed)).astype(bf16)
    misc_line = Sum2D(net, blocks_of(misc_low), 0, rows_w, misc_y, misc_z, share_misc)
    misc_line.send_y()
    qkv_line[2].send_y()
    qkv_line[1].send_z()
    out_line[2].send_z()
    out_line[3].send_y()
    pump()
    misc_line.send_z()
    qkv_line[3].send_y()
    qkv_line[2].send_z()
    out_line[3].send_z()
    pump()
    qkv_line[4].send_y()
    qkv_line[3].send_z()
    pump()
    qkv_line[4].send_z()
    pump(8)
    for piece_sum in (*out_line, misc_line, *qkv_line):
        piece_sum.last()
    net.finish()


def rear_call(
    cols, collective_id, experts, out_part, back, gate_dots, gate, router_probs, table_col, h1, h2,
    tokens, attn, weights, out_weights, grads, heads, q_low, kv_all, probs, cosine, sine,
):
    toks, width = back.shape
    q_width = q_low.shape[1]
    size = HEAD_DIM
    qkv_width = q_width + 2 * size
    seqs, group, local_len, full_len = probs.shape
    rows_w, high = width // cols, cols // 2
    piece = width // lax.axis_size("row")
    row_pieces = 4
    row_piece = (row_pieces, toks // 2 // row_pieces, width)
    vmem, any_space = pl.BlockSpec(memory_space=pltpu.VMEM), pl.BlockSpec(memory_space=pl.ANY)

    def shape(*dims, dtype=f32):
        return jax.ShapeDtypeStruct(dims, dtype)

    def sums(rows, columns):
        return [
            pltpu.VMEM((high, rows, columns), bf16),
            pltpu.VMEM((high - 1, rows, columns), bf16),
        ]

    copies = 420
    return pl.pallas_call(
        functools.partial(rear_kernel, cols, experts),
        out_shape=[
            shape(toks, piece),
            shape(toks, width),
            shape(rows_w, qkv_width),
            shape(rows_w, LANES),
            shape(rows_w, q_width),
        ],
        in_specs=[any_space] + [vmem] * 9 + [any_space] * 3 + [vmem] * 6,
        out_specs=[vmem] * 5,
        scratch_shapes=[
            pltpu.VMEM((width, qkv_width + LANES), bf16),
            pltpu.VMEM((width, q_width), bf16),
            pltpu.VMEM((width, LANES), f32),
            pltpu.VMEM((width, LANES), bf16),
            pltpu.VMEM((toks, width), bf16),
            pltpu.VMEM((8, width), f32),
            pltpu.VMEM((LANES, toks), f32),
            pltpu.VMEM((toks, LANES), bf16),
            pltpu.VMEM((toks, width), bf16),
            pltpu.VMEM((toks, q_width), bf16),
            pltpu.VMEM((full_len, size), bf16),
            pltpu.VMEM((full_len, size), bf16),
            pltpu.VMEM((2, group * local_len, size), bf16),
            pltpu.VMEM((group * local_len, full_len), bf16),
            pltpu.VMEM((cols, toks, 2 * size), bf16),
            pltpu.VMEM((toks, 2 * size), f32),
            pltpu.VMEM((toks, qkv_width), bf16),
            pltpu.VMEM((16, width), f32),
            pltpu.VMEM((2, cols, toks, piece), bf16),
            pltpu.VMEM((2, cols, toks, piece), bf16),
            pltpu.VMEM((cols, toks, piece), bf16),
            *sums(toks, piece),
            *sums(toks, 2 * size),
            *sums(rows_w, q_width),
            *sums(rows_w, qkv_width),
            *sums(rows_w, LANES),
            pltpu.VMEM(row_piece, bf16),
            pltpu.VMEM(row_piece, bf16),
            pltpu.VMEM(row_piece, bf16),
            pltpu.SemaphoreType.DMA((copies,)),
            pltpu.SemaphoreType.DMA((copies,)),
            pltpu.SemaphoreType.DMA((8,)),
        ],
        compiler_params=pltpu.CompilerParams(
            collective_id=collective_id, has_side_effects=True, vmem_limit_bytes=62 << 20
        ),
        name=f"rear_{collective_id}",
    )(
        out_part, back, gate_dots, gate, router_probs, table_col, h1, h2, tokens, attn, weights,
        out_weights, grads, heads, q_low, kv_all, probs, cosine, sine,
    )


def experts_plain(
    h2, grad_all, w_gate, w_up, w_down, shared_weights, router, rank_all, capacity, row_width
):
    cols = lax.axis_size("col")
    col_index, row_index = lax.axis_index("col"), lax.axis_index("row")
    toks, width = h2.shape
    exp_local = w_gate.shape[0]
    experts = rank_all.shape[2]
    shared_part = shared_weights.shape[1] // 3
    shared_in_weights = shared_weights[:, : 2 * shared_part]
    shared_down = shared_weights[:, 2 * shared_part :]
    h2_slice = lax.dynamic_slice_in_dim(h2, row_index * row_width, row_width, 1)
    h2_all = gather_all(h2_slice)

    all_mask = (rank_all > 0).astype(f32)
    all_probs = jax.nn.softmax(dot("ctd,de->cte", h2_all, router), axis=-1)
    all_picked = all_probs * all_mask
    all_gate = all_picked / jnp.sum(all_picked, axis=-1, keepdims=True)
    own = col_index * exp_local
    own_gate = lax.dynamic_slice_in_dim(all_gate, own, exp_local, 2)
    own_rank = lax.dynamic_slice_in_dim(rank_all, own, exp_local, 2).astype(jnp.int32)
    slots = jnp.arange(1, capacity + 1, dtype=jnp.int32)
    pick = jnp.swapaxes(own_rank, 1, 2)[:, :, None, :] == slots[:, None]
    slot_gate = jnp.sum(
        jnp.where(pick, jnp.swapaxes(own_gate, 1, 2)[:, :, None, :], 0.0), axis=3
    )[..., None]
    pick_low = pick.astype(bf16).reshape(cols, exp_local * capacity, toks)
    slot_shape = (cols, exp_local, capacity, width)
    slot_rows = dot("cut,ctd->cud", pick_low, h2_all).astype(bf16).reshape(slot_shape)
    slot_grad = dot("cut,ctd->cud", pick_low, grad_all).astype(bf16).reshape(slot_shape)
    gate_pre = dot("necd,edf->necf", slot_rows, w_gate)
    up_pre = dot("necd,edf->necf", slot_rows, w_up)
    silu_gate, slope_gate = silu_parts(gate_pre)
    hidden = silu_gate * up_pre
    gated = (hidden * slot_gate).astype(bf16)
    slot_out = dot("necf,efd->necd", gated, w_down).astype(bf16)
    hidden_grad = dot("necd,efd->necf", slot_grad, w_down)
    slot_dots = jnp.sum(hidden * hidden_grad, axis=-1)
    hidden_grad = hidden_grad * slot_gate
    gate_grad = (hidden_grad * up_pre * slope_gate).astype(bf16)
    up_grad = (hidden_grad * silu_gate).astype(bf16)
    slot_back = dot("necf,edf->necd", gate_grad, w_gate)
    slot_back = (slot_back + dot("necf,edf->necd", up_grad, w_up)).astype(bf16)
    grad_expert_down = dot("necf,necd->efd", gated, slot_grad)
    grad_expert_gate = dot("necd,necf->edf", slot_rows, gate_grad)
    grad_expert_up = dot("necd,necf->edf", slot_rows, up_grad)
    pick_flat = pick_low.reshape(cols, exp_local * capacity, toks)
    slot_out = slot_out.reshape(cols, exp_local * capacity, width)
    slot_back = slot_back.reshape(cols, exp_local * capacity, width)

    shared_pre = dot("ctd,dk->ctk", h2_all, shared_in_weights)
    sgate_pre, sup_pre = shared_pre[:, :, :shared_part], shared_pre[:, :, shared_part:]
    shared_silu, shared_slope = silu_parts(sgate_pre)
    shared_hidden = (shared_silu * sup_pre).astype(bf16)
    part_out = dot("cut,cud->ctd", pick_flat, slot_out) + dot(
        "ctk,dk->ctd", shared_hidden, shared_down
    )
    shared_hgrad = dot("ctd,dk->ctk", grad_all, shared_down)
    shared_grads = jnp.concatenate(
        [shared_hgrad * sup_pre * shared_slope, shared_hgrad * shared_silu], axis=2
    ).astype(bf16)
    part_back = dot("cut,cud->ctd", pick_flat, slot_back) + dot(
        "ctk,dk->ctd", shared_grads, shared_in_weights
    )
    token_dots = jnp.einsum(
        "ceu,ceut->cte", slot_dots, pick.astype(f32), precision=lax.Precision.HIGHEST
    )
    gate_dots = lax.psum(swap_col(token_dots), "row")
    gate_dots = jnp.swapaxes(gate_dots, 0, 1).reshape(toks, experts)

    shared_share = jnp.concatenate(
        [dot("ctd,ctk->dk", h2_all, shared_grads), dot("ctd,ctk->dk", grad_all, shared_hidden)],
        axis=1,
    ).astype(bf16)
    back_full = lax.all_gather(scatter_all(part_back.astype(bf16)), "row", axis=1, tiled=True)
    return (
        part_out.astype(bf16),
        back_full,
        gate_dots,
        shared_share,
        grad_expert_gate,
        grad_expert_up,
        grad_expert_down,
    )


def on_device(
    tokens,
    segments,
    routes,
    attn_gain,
    query_matrix,
    key_matrix,
    value_matrix,
    attention_output_matrix,
    mlp_gain,
    w_router,
    shared_gate_matrix,
    shared_up_matrix,
    shared_down_matrix,
    expert_gate,
    expert_up,
    expert_down,
    cotangent,
):
    local_len, seqs, width = tokens.shape
    cols = lax.axis_size("col")
    col_index = lax.axis_index("col")
    rows_w = query_matrix.shape[0]
    full_len = local_len * cols
    size = HEAD_DIM
    q_width = query_matrix.shape[1]
    kv_width = key_matrix.shape[1]
    kv_local = kv_width // size
    group = q_width // kv_width
    row_width = cotangent.shape[2]
    toks = local_len * seqs
    top = routes.shape[2]
    experts = w_router.shape[1]
    exp_local = expert_gate.shape[0]
    hidden_local = expert_gate.shape[2]
    capacity = max(2, toks * top * 4 // (3 * experts))
    shared_part = shared_gate_matrix.shape[1] // cols
    scale = 1.0 / math.sqrt(size)
    kernels = fits(cols, toks, width) and kv_local == 1 and exp_local == 2

    def seq_major(a):
        return jnp.swapaxes(a, 0, 1).reshape(toks, a.shape[2])

    misc = jnp.concatenate(
        [
            w_router,
            attn_gain[:, None],
            mlp_gain[:, None],
            jnp.zeros((rows_w, LANES - experts - 2), bf16),
        ],
        axis=1,
    )
    shared_weights = jnp.concatenate(
        [
            shared_gate_matrix.reshape(rows_w, cols, shared_part),
            shared_up_matrix.reshape(rows_w, cols, shared_part),
            shared_down_matrix.T.reshape(rows_w, cols, shared_part),
        ],
        axis=2,
    )
    shared_own = jnp.swapaxes(shared_weights, 0, 1)
    grad_own = seq_major(cotangent).astype(bf16)
    cosine, sine = rope_tables(col_index * local_len, local_len, size)
    cosine, sine = jnp.tile(cosine, (seqs, 1)), jnp.tile(sine, (seqs, 1))
    qkv_width = q_width + 2 * kv_width
    flat_routes = seq_major(routes)
    named = flat_routes[:, :, None] == jnp.arange(experts, dtype=jnp.int32)
    mask = jnp.any(named, axis=1)
    order = jnp.arange(toks, dtype=jnp.int32)
    upto = (order[None, :] <= order[:, None]).astype(bf16)
    rank = jnp.where(mask, dot("ij,je->ie", upto, mask.astype(bf16)), 0.0)

    doc = jnp.transpose(segments)
    def to_grid(flat):
        shaped = flat.reshape(seqs, local_len, kv_local, group, size)
        return shaped.transpose(0, 2, 3, 1, 4).reshape(seqs, kv_local, group * local_len, size)

    def from_grid(grid):
        shaped = grid.reshape(seqs, kv_local, group, local_len, size)
        return shaped.transpose(0, 3, 1, 2, 4).reshape(toks, q_width)

    token_rows = seq_major(tokens)
    x = token_rows.astype(f32)
    inv_first = rms_scale(x)
    base_first = x * inv_first
    if kernels:
        table_row = jnp.concatenate([rank.T, doc.reshape(1, toks).astype(f32)], axis=0)
        table_row = jnp.pad(table_row, ((0, -(experts + 1) % 8), (0, 0)))
        table_col = jnp.pad(rank, ((0, 0), (0, LANES - experts))).astype(bf16)
        (
            first_weights,
            out_weights,
            grad_all,
            rows_all,
            rank_all,
            h1,
            q_low,
            kv_all,
            probs,
            heads,
            attn,
            h2,
            gate,
            probs_router,
        ) = front_call(
            cols,
            0,
            experts,
            token_rows,
            query_matrix,
            key_matrix,
            value_matrix,
            misc,
            attention_output_matrix.T,
            grad_own,
            table_row,
            table_col,
            doc.reshape(toks, 1).astype(f32),
            jnp.concatenate([cosine, cosine], axis=1),
            jnp.concatenate([-sine, sine], axis=1),
            seqs,
        )
    else:
        first_weights = jnp.concatenate([query_matrix, key_matrix, value_matrix, misc], axis=1)
        first_weights = gather_col(first_weights).reshape(width, -1)
        out_weights = gather_col(attention_output_matrix.T).reshape(width, q_width)
        shared_weights = swap_col(shared_own).reshape(width, 3 * shared_part)
        grad_all = gather_all(grad_own)
        gain_one = first_weights[:, qkv_width + experts].astype(f32)
        h1 = (base_first * gain_one).astype(bf16)
        qkv = dot("tb,bk->tk", h1, first_weights[:, :qkv_width])
        qk = rotate(qkv[:, : q_width + kv_width], cosine, sine).astype(bf16)
        q_low = qk[:, :q_width]
        value_low = qkv[:, q_width + kv_width :].astype(bf16)
        side = jnp.concatenate(
            [
                rank.astype(bf16),
                doc.reshape(toks, 1).astype(bf16),
                jnp.zeros((toks, LANES - experts - 1), bf16),
            ],
            axis=1,
        )
        kv_all = gather_col(jnp.concatenate([qk[:, q_width:], value_low, side], axis=1))
        rank_all = kv_all[:, :, 2 * kv_width : 2 * kv_width + experts]
    qkv_weights = first_weights[:, :qkv_width]
    router = first_weights[:, qkv_width : qkv_width + experts]
    gain_one = first_weights[:, qkv_width + experts].astype(f32)
    gain_two = first_weights[:, qkv_width + experts + 1].astype(f32)
    kv_seq = jnp.swapaxes(kv_all.reshape(cols, seqs, local_len, -1), 0, 1)
    kv_seq = kv_seq.reshape(seqs, full_len, -1)
    key_all = kv_seq[:, :, :kv_width].reshape(seqs, full_len, kv_local, size)
    value_all = kv_seq[:, :, kv_width : 2 * kv_width].reshape(seqs, full_len, kv_local, size)
    query_grid = to_grid(q_low)
    if not kernels:
        doc_all = kv_seq[:, :, 2 * kv_width + experts]
        place = col_index * local_len + jnp.arange(local_len, dtype=jnp.int32)
        same = doc.astype(bf16)[:, :, None] == doc_all[:, None, :]
        causal = jnp.arange(full_len, dtype=jnp.int32)[None, :] <= place[:, None]
        allowed = jnp.tile(same & causal[None], (1, group, 1))[:, None]
        scores = dot("shrd,skhd->shrk", query_grid, key_all) * scale
        scores = jnp.where(allowed, scores, masked_score)
        weights = jnp.exp(scores - jnp.max(scores, axis=-1, keepdims=True))
        weights = jnp.where(allowed, weights, 0.0)
        probs = (weights / jnp.sum(weights, axis=-1, keepdims=True)).astype(bf16)
        heads = from_grid(dot("shrk,skhd->shrd", probs, value_all)).astype(bf16)
        attn = lax.psum(dot("tk,bk->tb", heads, out_weights).astype(bf16), "row")
    middle = x + attn.astype(f32)

    inv_second = rms_scale(middle)
    base_second = middle * inv_second
    row_index = lax.axis_index("row")
    if not kernels:
        h2 = (base_second * gain_two).astype(bf16)
        probs_router = jax.nn.softmax(dot("td,de->te", h2, router), axis=-1)
        picked = jnp.where(mask, probs_router, 0.0)
        pick_total = jnp.sum(picked, axis=-1, keepdims=True)
        gate = picked / pick_total
    if kernels:
        rank_own = lax.dynamic_slice_in_dim(rank_all, col_index * exp_local, exp_local, 2)
        rank_own = rank_own.astype(f32)
        part_out, back_full, gate_dots, shared_share, *expert_grads = experts_kernels(
            cols,
            3,
            capacity,
            h2,
            grad_all,
            expert_gate,
            expert_up,
            expert_down,
            shared_own,
            lax.dynamic_slice_in_dim(rows_all, col_index * exp_local, exp_local, 1),
            rank_own,
            gate[:, :experts].T,
        )
    else:
        part_out, back_full, gate_dots, shared_share, *expert_grads = experts_plain(
            h2,
            grad_all,
            expert_gate,
            expert_up,
            expert_down,
            shared_weights,
            router,
            rank_all,
            capacity,
            row_width,
        )
    if not kernels:
        back_full = back_full.astype(f32)
    if not kernels:
        shared_share = swap_col(shared_share.reshape(cols, rows_w, 3 * shared_part))
    shared_share = jnp.swapaxes(shared_share, 0, 1).astype(f32)
    share_sgate, share_sup, share_sdown = (
        shared_share[:, :, i * shared_part : (i + 1) * shared_part].reshape(rows_w, -1)
        for i in range(3)
    )

    if kernels:
        out_slice, token_grad, share_qkv, share_misc, share_out = rear_call(
            cols,
            5,
            experts,
            part_out,
            back_full,
            gate_dots,
            gate,
            probs_router,
            table_col,
            h1,
            h2,
            token_rows,
            attn,
            first_weights,
            out_weights,
            grad_all,
            heads,
            q_low,
            kv_all,
            probs,
            jnp.concatenate([cosine, cosine], axis=1),
            jnp.concatenate([-sine, sine], axis=1),
        )
    else:
        pick_grad = gate_dots - jnp.sum(gate * gate_dots, axis=-1, keepdims=True)
        prob_grad = jnp.where(mask, pick_grad / pick_total, 0.0)
        logit_grad = probs_router * (
            prob_grad - jnp.sum(probs_router * prob_grad, axis=-1, keepdims=True)
        )
        logit_low = logit_grad.astype(bf16)
        grad_router = dot("td,te->de", h2, logit_low)

        back_full = back_full + dot("te,de->td", logit_low, router)
        grad_own = lax.dynamic_slice_in_dim(grad_all, col_index, 1, 0)[0].astype(f32)
        grad_gain_two = jnp.sum(back_full * base_second, axis=0)
        scaled_two = back_full * gain_two
        middle_grad = (
            inv_second
            * (scaled_two - base_second * jnp.mean(scaled_two * base_second, axis=-1, keepdims=True))
            + grad_own
        )
        attn_grad = middle_grad.astype(bf16)
        grad_out = dot("td,tk->dk", attn_grad, heads).astype(bf16)

        heads_grad = to_grid(dot("td,dk->tk", attn_grad, out_weights).astype(bf16))
        value_grad = dot("shrk,shrd->skhd", probs, heads_grad)
        weight_grad = dot("shrd,skhd->shrk", heads_grad, value_all)
        probs_wide = probs.astype(f32)
        delta = jnp.sum(probs_wide * weight_grad, axis=-1, keepdims=True)
        score_grad = (probs_wide * (weight_grad - delta)).astype(bf16)
        query_grad = from_grid(dot("shrk,skhd->shrd", score_grad, key_all)) * scale
        key_grad = dot("shrk,shrd->skhd", score_grad, query_grid) * scale
        kv_grad = jnp.concatenate(
            [key_grad.reshape(seqs, full_len, kv_width), value_grad.reshape(seqs, full_len, kv_width)],
            axis=2,
        ).astype(bf16)
        kv_grad = jnp.swapaxes(kv_grad.reshape(seqs, cols, local_len, 2 * kv_width), 0, 1)
        kv_share = scatter_col(kv_grad.reshape(cols, toks, 2 * kv_width)).astype(f32)
        qk_grad = rotate(
            jnp.concatenate([query_grad, kv_share[:, :kv_width]], axis=1), cosine, -sine
        )
        qkv_grad = jnp.concatenate([qk_grad, kv_share[:, kv_width:]], axis=1).astype(bf16)
        first_grad = dot("tk,bk->tb", qkv_grad, qkv_weights).astype(bf16)
        first_grad = lax.psum(first_grad, "row").astype(f32)
        grad_gain_one = jnp.sum(first_grad * base_first, axis=0)
        scaled_one = first_grad * gain_one
        token_grad = (
            inv_first
            * (scaled_one - base_first * jnp.mean(scaled_one * base_first, axis=-1, keepdims=True))
            + middle_grad
        )
        grad_first = jnp.concatenate(
            [
                dot("tb,tk->bk", h1, qkv_grad),
                grad_router,
                grad_gain_one[:, None],
                grad_gain_two[:, None],
                jnp.zeros((width, LANES - experts - 2), f32),
            ],
            axis=1,
        ).astype(bf16)
        out_slice = scatter_all(part_out).astype(f32)
        share_out = scatter_col(grad_out.reshape(cols, rows_w, q_width)).astype(f32)
        share_first = scatter_col(grad_first.reshape(cols, rows_w, -1)).astype(f32)
        share_qkv, share_misc = share_first[:, :qkv_width], share_first[:, qkv_width:]
    middle_slice = lax.dynamic_slice_in_dim(middle, row_index * row_width, row_width, 1)
    block_out = (middle_slice + out_slice).astype(bf16)

    def tokens_first(a):
        return jnp.swapaxes(a.reshape(seqs, local_len, a.shape[1]), 0, 1)

    return (
        tokens_first(block_out),
        tokens_first(token_grad),
        share_misc[:, experts],
        share_qkv[:, :q_width],
        share_qkv[:, q_width : q_width + kv_width],
        share_qkv[:, q_width + kv_width :],
        share_out.T,
        share_misc[:, experts + 1],
        share_misc[:, :experts],
        share_sgate,
        share_sup,
        share_sdown.T,
        *expert_grads,
    )


def solution(mesh):
    in_specs = (
        P("col", None, None),
        P("col", None),
        P("col", None, None),
        P("col"),
        P("col", "row"),
        P("col", "row"),
        P("col", "row"),
        P("row", "col"),
        P("col"),
        P("col", None),
        P("col", "row"),
        P("col", "row"),
        P("row", "col"),
        P("col", None, "row"),
        P("col", None, "row"),
        P("col", "row", None),
        P("col", None, "row"),
    )
    out_specs = (
        P("col", None, "row"),
        P("col", None, None),
        P("col"),
        P("col", "row"),
        P("col", "row"),
        P("col", "row"),
        P("row", "col"),
        P("col"),
        P("col", None),
        P("col", "row"),
        P("col", "row"),
        P("row", "col"),
        P("col", None, "row"),
        P("col", None, "row"),
        P("col", "row", None),
    )
    return jax.shard_map(
        on_device, mesh=mesh, in_specs=in_specs, out_specs=out_specs, check_vma=False
    )
```

```python
import functools
import math

import jax
import jax.numpy as jnp
from jax import lax
from jax.experimental import pallas as pl
from jax.experimental.pallas import tpu as pltpu
from jax.sharding import PartitionSpec as P

HEAD_DIM = 128
LANES = 128


norm_eps = 1e-05
rope_base = 500000.0
masked_score = -1e30

f32 = jnp.float32
bf16 = jnp.bfloat16
MESH = pl.DeviceIdType.MESH


def dot(form, left, right):
    return jnp.einsum(form, left, right, preferred_element_type=f32)


def rope_tables(start_place, local_len, head_size):
    places = (start_place + jnp.arange(local_len, dtype=jnp.int32)).astype(f32)
    frequency = jnp.power(
        rope_base, -jnp.arange(0, head_size, 2, dtype=jnp.int32).astype(f32) / head_size
    )
    angles = places[:, None] * frequency[None, :]
    return (jnp.cos(angles), jnp.sin(angles))


def rotate(field, cosine, sine):
    half = cosine.shape[1]
    parts = []
    for start in range(0, field.shape[1], 2 * half):
        front = field[:, start : start + half]
        back = field[:, start + half : start + 2 * half]
        parts.append(front * cosine - back * sine)
        parts.append(back * cosine + front * sine)
    return jnp.concatenate(parts, axis=1)


def rms_scale(values_in):
    return lax.rsqrt(jnp.mean(values_in * values_in, axis=-1, keepdims=True) + norm_eps)


def silu_parts(pre_gate):
    sigmoid_gate = jax.nn.sigmoid(pre_gate)
    silu_gate = pre_gate * sigmoid_gate
    slope_gate = sigmoid_gate * (1.0 + pre_gate * (1.0 - sigmoid_gate))
    return (silu_gate, slope_gate)


def gather_col(part):
    return lax.all_gather(part, "col", axis=0, tiled=False)


def scatter_col(blocks):
    flat = blocks.reshape(-1, blocks.shape[-1])
    return lax.psum_scatter(flat, "col", scatter_dimension=0, tiled=True)


def gather_all(part):
    got = lax.all_gather(part, ("col", "row"), axis=0, tiled=False)
    cols, rows = lax.axis_size("col"), lax.axis_size("row")
    got = got.reshape(cols, rows, *part.shape).transpose(0, 2, 1, 3)
    return got.reshape(cols, part.shape[0], rows * part.shape[1])


def scatter_all(blocks):
    flat = blocks.reshape(-1, blocks.shape[-1])
    part = lax.psum_scatter(flat, "row", scatter_dimension=1, tiled=True)
    return lax.psum_scatter(part, "col", scatter_dimension=0, tiled=True)


def swap_col(blocks):
    return lax.all_to_all(blocks, "col", split_axis=0, concat_axis=0, tiled=True)


class Net:
    def __init__(self, cols, send_sems, recv_sems):
        self.send_sems, self.recv_sems, self.used, self.sent = send_sems, recv_sems, 0, []
        self.cols, self.high_count = cols, cols // 2
        self.me = lax.axis_index("col")
        self.high, self.low = self.me // 2, self.me % 2
        self.row = lax.axis_index("row")
        self.outer, self.core = self.row // 2, self.row % 2

    def block(self, step, other=False):
        high = lax.rem(self.high + self.high_count - step, self.high_count)
        return 2 * high + (1 - self.low if other else self.low)

    def block_ahead(self, step, other=False):
        high = lax.rem(self.high + step, self.high_count)
        return 2 * high + (1 - self.low if other else self.low)

    def z_peer(self, step):
        return {"col": self.block_ahead(step)}

    def y_peer(self):
        return {"col": 2 * self.high + 1 - self.low}

    def x_peer(self):
        return {"row": 2 * (1 - self.outer) + self.core}

    def core_peer(self):
        return {"row": 2 * self.outer + 1 - self.core}

    def col_peer(self, step):
        return {"col": lax.rem(self.me + step, self.cols)}

    def greet(self, peers):
        barrier = pltpu.get_barrier_semaphore()
        for peer in peers:
            pl.semaphore_signal(barrier, inc=1, device_id=peer, device_id_type=MESH)
        pl.semaphore_wait(barrier, len(peers))

    def send(self, source, target, peer):
        copy = pltpu.make_async_remote_copy(
            src_ref=source,
            dst_ref=target,
            send_sem=self.send_sems.at[self.used],
            recv_sem=self.recv_sems.at[self.used],
            device_id=peer,
            device_id_type=MESH,
        )
        self.used += 1
        copy.start()
        self.sent.append(copy)
        return copy

    def left(self, copy):
        copy.wait_send()
        self.sent = [other for other in self.sent if other is not copy]

    def finish(self):
        for copy in self.sent:
            copy.wait_send()


def col_peers(net):
    return [net.z_peer(step) for step in range(1, net.high_count)] + [net.y_peer()]


def row_peers(net):
    return [net.x_peer(), net.core_peer()]


def add_rows(target, terms):
    rows = target.shape[0]
    piece = 32 if rows % 32 == 0 else 16

    def body(index, carry):
        at = pl.ds(pl.multiple_of(index * piece, piece), piece)
        total = terms[0][at, :].astype(f32)
        for term in terms[1:]:
            total = total + term[at, :].astype(f32)
        target[at, :] = total.astype(target.dtype)
        return carry

    lax.fori_loop(0, rows // piece, body, 0)


def dot_nn(left, right):
    return lax.dot_general(left, right, (((1,), (0,)), ((), ())), preferred_element_type=f32)


def dot_nt(left, right):
    return lax.dot_general(left, right, (((1,), (1,)), ((), ())), preferred_element_type=f32)


def dot_tn(left, right):
    return lax.dot_general(left, right, (((0,), (0,)), ((), ())), preferred_element_type=f32)


def each_tile(count, body):
    def step(index, carry):
        body(index)
        return carry

    lax.fori_loop(0, count, step, 0)


TILE = 512
WIDE = 1280


def tile_at(index, tile=TILE):
    if isinstance(index, int):
        return pl.ds(index * tile, tile)
    return pl.ds(pl.multiple_of(index * tile, tile), tile)


class Line:
    def __init__(self, net, items):
        self.net, self.items = net, items
        self.other_row = 2 * (1 - net.outer) + net.core
        self.along_z, self.along_y, self.along_x, self.to_core = {}, {}, {}, {}
        self.moved = []
        self.now = 0

    def in_chip(self, q, step, other, source, slot):
        if self.items[q][2]:
            self.along_x[q, step, other] = self.net.send(source, slot, self.net.x_peer())
            self.to_core[q, step, other] = self.net.send(source, slot, self.net.core_peer())

    def start(self, q):
        net = self.net
        source, slot_of, _ = self.items[q]
        slot = slot_of(net.me, net.row)
        for step in reversed(range(1, net.high_count)):
            self.along_z[q, step] = net.send(source, slot, net.z_peer(step))
        self.along_y[q, 0] = net.send(source, slot, net.y_peer())
        self.in_chip(q, 0, False, source, slot)

    def after_z(self, q):
        net = self.net
        for step in reversed(range(1, net.high_count)):
            self.along_z[q, step].wait_recv()
            slot = self.items[q][1](net.block(step), net.row)
            self.along_y[q, step] = net.send(slot, slot, net.y_peer())
            self.in_chip(q, step, False, slot, slot)

    def after_y(self, q):
        net = self.net
        for step in range(net.high_count):
            self.along_y[q, step].wait_recv()
            slot = self.items[q][1](net.block(step, True), net.row)
            self.in_chip(q, step, True, slot, slot)

    def after_x(self, q):
        net = self.net
        if self.items[q][2]:
            for other in (False, True):
                for step in range(net.high_count):
                    self.along_x[q, step, other].wait_recv()
                    slot = self.items[q][1](net.block(step, other), self.other_row)
                    self.moved.append(net.send(slot, slot, net.core_peer()))

    def tick(self, count=1):
        net = self.net
        for _ in range(count):
            now, self.now = self.now, self.now + 1
            if now < len(self.items):
                if now >= 2:
                    for step in range(1, net.high_count):
                        net.left(self.along_z[now - 2, step])
                self.start(now)
            for stage, lag in ((self.after_z, 1), (self.after_y, 2), (self.after_x, 3)):
                if 0 <= now - lag < len(self.items):
                    stage(now - lag)

    def drain(self):
        while self.now < len(self.items) + 3:
            self.tick()
        for copy in [*self.moved, *self.to_core.values()]:
            copy.wait_recv()


def front_kernel(
    cols,
    experts,
    tokens,
    query,
    key,
    value,
    misc,
    out_own,
    grad_own,
    shared_own,
    table_row,
    table_col,
    doc_col,
    cosine,
    sine,
    weights,
    out_weights,
    grad_all,
    shared_all,
    rows_all,
    cols_all,
    h1,
    q_low,
    kv_all,
    probs,
    heads,
    attn,
    h2,
    gate,
    router_probs,
    gains,
    inverse,
    kv_low,
    keys,
    values,
    bias,
    partial,
    from_core,
    to_x,
    from_x,
    send_sems,
    recv_sems,
    local_sems,
):
    net = Net(cols, send_sems, recv_sems)
    toks, width = tokens.shape
    size = HEAD_DIM
    q_width = q_low.shape[1]
    group = q_width // size
    rows_w = query.shape[0]
    seqs = probs.shape[0]
    local_len = toks // seqs
    full_len = local_len * cols
    scale = 1.0 / math.sqrt(size)
    mine = pl.ds(pl.multiple_of(net.me * rows_w, 16), rows_w)

    copies = []

    def local_copy(source, target):
        copy = pltpu.make_async_copy(source, target, local_sems.at[len(copies)])
        copy.start()
        copies.append(copy)

    local_copy(query, weights.at[mine, pl.ds(0, q_width)])
    local_copy(key, weights.at[mine, pl.ds(q_width, size)])
    local_copy(value, weights.at[mine, pl.ds(q_width + size, size)])
    local_copy(misc, weights.at[mine, pl.ds(q_width + 2 * size, LANES)])
    first = len(copies)
    local_copy(out_own, out_weights.at[mine])
    part = grad_own.shape[1]
    local_copy(
        grad_own, grad_all.at[net.me, :, pl.ds(pl.multiple_of(net.row * part, LANES), part)]
    )
    local_copy(table_row, rows_all.at[net.me])
    local_copy(table_col, cols_all.at[net.me])
    local_copy(shared_own.at[net.me], shared_all.at[net.me])
    net.greet([net.col_peer(step) for step in range(1, cols)] + row_peers(net))
    for copy in copies[:first]:
        copy.wait()

    def weight_slot(target, start, count):
        def slot(block, row):
            return target.at[pl.ds(pl.multiple_of(block * rows_w + start, 16), count)]

        return slot

    def grad_slot(start, count):
        def slot(block, row):
            return grad_all.at[
                block, pl.ds(start, count), pl.ds(pl.multiple_of(row * part, LANES), part)
            ]

        return slot

    items = [(table_row, lambda block, row: rows_all.at[block], False)]
    pieces, out_pieces, grad_pieces = 5, 4, 4
    count = rows_w // pieces
    for q in range(pieces):
        slot = weight_slot(weights, q * count, count)
        items.append((slot(net.me, net.row), slot, False))
    ready_weights = len(items) + 2
    out_items, grad_items = [], []
    count = rows_w // out_pieces
    for q in range(out_pieces):
        slot = weight_slot(out_weights, q * count, count)
        out_items.append((out_own.at[pl.ds(q * count, count)], slot, False))
    count = toks // grad_pieces
    for q in range(grad_pieces):
        grad_items.append((grad_own.at[pl.ds(q * count, count)], grad_slot(q * count, count), True))
    items += out_items[:2]
    for q in range(2, out_pieces):
        items += [grad_items[q - 2], out_items[q]]
    ready_out = len(items) + 2
    items += grad_items[out_pieces - 2 :]
    items.append((table_col, lambda block, row: cols_all.at[block], False))
    line = Line(net, items)
    swaps = []

    def swap_next(count):
        for _ in range(count):
            step = len(swaps) + 1
            if step < cols:
                block = lax.rem(net.me + step, cols)
                swaps.append(
                    net.send(shared_own.at[block], shared_all.at[net.me], net.col_peer(step))
                )

    line.tick(2)
    copies[first + 2].wait()

    def chunks(body, rows=32):
        def step(index, carry):
            body(pl.ds(pl.multiple_of(index * rows, rows), rows))
            return carry

        lax.fori_loop(0, toks // rows, step, 0)

    def measure_first(at):
        x = tokens[at, :].astype(f32)
        total = jnp.sum(x * x, axis=1, keepdims=True)
        inverse[at, :] = jnp.broadcast_to(lax.rsqrt(total / width + norm_eps), (32, LANES))

    chunks(measure_first)
    line.tick(ready_weights - line.now)

    start = q_width + 2 * size
    for tile in range(width // TILE):
        at = pl.ds(tile * TILE, TILE)
        turned = jnp.transpose(weights[at, start : start + LANES].astype(f32))
        gains[:, at] = turned[experts : experts + 8]

    def norm_first(at):
        x = tokens[at, :].astype(f32) * inverse[at, 0:1]
        h1[at, :] = (x * gains[0:1, :]).astype(bf16)

    chunks(norm_first)
    line.tick()

    def rotated(raw):
        return raw * cosine[...] + pltpu.roll(raw, size // 2, 1) * sine[...]

    raw = dot_nn(h1[...], weights[:, q_width : q_width + 2 * size])
    kv_low[:, :size] = rotated(raw[:, :size]).astype(bf16)
    kv_low[:, size:] = raw[:, size:].astype(bf16)
    kv_all[net.me] = kv_low[...]

    def kv_slot(s):
        rows = pl.ds(s * local_len, local_len)
        return lambda block, row: kv_all.at[block, rows]

    kv_line = Line(
        net,
        [(kv_low.at[pl.ds(s * local_len, local_len)], kv_slot(s), False) for s in range(seqs)],
    )
    kv_line.tick()
    raw = dot_nn(h1[...], weights[:, :q_width])
    for head in range(group):
        at = slice(head * size, (head + 1) * size)
        q_low[:, at] = rotated(raw[:, at]).astype(bf16)
    kv_line.tick()
    line.tick()
    kv_line.tick()

    for s in range(seqs):
        if s:
            kv_line.tick()
        rows = pl.ds(s * local_len, local_len)
        place = lax.broadcasted_iota(jnp.int32, (local_len, local_len), 0)
        lane = lax.broadcasted_iota(jnp.int32, (local_len, local_len), 1)
        for c in range(cols):
            at = pl.ds(c * local_len, local_len)
            keys[at, :] = kv_all[c, rows, :size]
            values[at, :] = kv_all[c, rows, size:]
            same = doc_col[rows, :] == rows_all[c, experts : experts + 1, rows]
            ahead = (c - net.me) * local_len
            allowed = same & (lane + ahead <= place)
            bias[:, at] = jnp.where(allowed, 0.0, masked_score)

        def attend(g, carry, s=s, rows=rows):
            at = pl.ds(pl.multiple_of(g * size, size), size)
            scores = dot_nt(q_low[rows, at], keys[...]) * scale + bias[...]
            weight = jnp.exp(scores - jnp.max(scores, axis=1, keepdims=True))
            p = (weight / jnp.sum(weight, axis=1, keepdims=True)).astype(bf16)
            probs[s, g] = p
            heads[rows, at] = dot_nn(p, values[...]).astype(bf16)
            return carry

        lax.fori_loop(0, group, attend, 0)
        if line.now < ready_out:
            line.tick()
    line.tick(max(0, ready_out - line.now))
    swap_next(3)
    copies[first].wait()

    pieces = from_core.shape[0]
    piece_rows = from_core.shape[1]

    def row_piece(core, i):
        return pl.ds(
            pl.multiple_of((core * pieces + i) * piece_rows, piece_rows), piece_rows
        )

    half = pieces * piece_rows
    across = []
    for core in (1 - net.core, net.core):
        at_rows = pl.ds(pl.multiple_of(core * half, half), half)
        for tile in range(width // TILE):
            at = pl.ds(tile * TILE, TILE)
            partial[at_rows, at] = dot_nt(heads[at_rows, :], out_weights[at, :]).astype(bf16)
        if not across:
            across = [
                net.send(partial.at[row_piece(1 - net.core, i)], from_core.at[i], net.core_peer())
                for i in range(pieces)
            ]
    along, back = [], []
    for i in range(pieces):
        across[i].wait_recv()
        add_rows(to_x.at[i], [partial.at[row_piece(net.core, i)], from_core.at[i]])
        along.append(net.send(to_x.at[i], from_x.at[i], net.x_peer()))
    line.tick()
    swap_next(cols)
    for i in range(pieces):
        along[i].wait_recv()
        at = row_piece(net.core, i)
        add_rows(attn.at[at], [to_x.at[i], from_x.at[i]])
        back.append(net.send(attn.at[at], attn.at[at], net.core_peer()))
    line.tick()
    for copy in back:
        copy.wait_recv()

    def norm_second(at):
        x = tokens[at, :].astype(f32) + attn[at, :].astype(f32)
        total = jnp.sum(x * x, axis=1, keepdims=True)
        h2[at, :] = (x * lax.rsqrt(total / width + norm_eps) * gains[1:2, :]).astype(bf16)

    chunks(norm_second)
    line.tick()
    logits = dot_nn(h2[...], weights[:, start : start + LANES])
    lane = lax.broadcasted_iota(jnp.int32, (toks, LANES), 1)
    logits = jnp.where(lane < experts, logits, masked_score)
    weight = jnp.exp(logits - jnp.max(logits, axis=1, keepdims=True))
    chance = weight / jnp.sum(weight, axis=1, keepdims=True)
    router_probs[...] = chance
    picked = jnp.where((table_col[...] > 0) & (lane < experts), chance, 0.0)
    gate[...] = picked / jnp.sum(picked, axis=1, keepdims=True)
    line.drain()
    kv_line.drain()
    for copy in swaps:
        copy.wait_recv()
    for copy in (copies[first + 1], *copies[first + 3 :]):
        copy.wait()
    net.finish()


def front_call(
    cols, collective_id, experts, tokens, query, key, value, misc, out_own, grad_own, shared_own,
    table_row, table_col, doc_col, cosine, sine, seqs,
):
    toks, width = tokens.shape
    q_width = query.shape[1]
    size = HEAD_DIM
    local_len = toks // seqs
    vmem, any_space = pl.BlockSpec(memory_space=pltpu.VMEM), pl.BlockSpec(memory_space=pl.ANY)

    def shape(*dims, dtype=bf16):
        return jax.ShapeDtypeStruct(dims, dtype)

    pieces = 4
    piece = (pieces, toks // 2 // pieces, width)
    copies = 320
    return pl.pallas_call(
        functools.partial(front_kernel, cols, experts),
        out_shape=[
            shape(width, q_width + 2 * size + LANES),
            shape(width, q_width),
            shape(cols, toks, width),
            shape(*shared_own.shape),
            shape(cols, *table_row.shape, dtype=f32),
            shape(cols, *table_col.shape),
            shape(toks, width),
            shape(toks, q_width),
            shape(cols, toks, 2 * size),
            shape(seqs, q_width // size, local_len, cols * local_len),
            shape(toks, q_width),
            shape(toks, width),
            shape(toks, width),
            shape(toks, LANES, dtype=f32),
            shape(toks, LANES, dtype=f32),
        ],
        in_specs=[vmem] + [any_space] * 7 + [vmem] * 5,
        out_specs=[vmem, vmem, any_space, any_space] + [vmem] * 11,
        scratch_shapes=[
            pltpu.VMEM((8, width), f32),
            pltpu.VMEM((toks, LANES), f32),
            pltpu.VMEM((toks, 2 * size), bf16),
            pltpu.VMEM((cols * local_len, size), bf16),
            pltpu.VMEM((cols * local_len, size), bf16),
            pltpu.VMEM((local_len, cols * local_len), f32),
            pltpu.VMEM((toks, width), bf16),
            pltpu.VMEM(piece, bf16),
            pltpu.VMEM(piece, bf16),
            pltpu.VMEM(piece, bf16),
            pltpu.SemaphoreType.DMA((copies,)),
            pltpu.SemaphoreType.DMA((copies,)),
            pltpu.SemaphoreType.DMA((16,)),
        ],
        compiler_params=pltpu.CompilerParams(
            collective_id=collective_id, has_side_effects=True, vmem_limit_bytes=48 << 20
        ),
        name=f"front_{collective_id}",
    )(
        tokens, query, key, value, misc, out_own, grad_own, shared_own,
        table_row, table_col, doc_col, cosine, sine,
    )


def experts_kernel(
    cols,
    capacity,
    h2,
    grads,
    w_gate,
    w_up,
    w_down,
    w_shared,
    rank_row,
    rank_col,
    gate_own,
    out_part,
    back,
    g_gate,
    g_up,
    g_down,
    g_shared,
    gate_dots,
    h2_all,
    xs_all,
    cs_all,
    wgu,
    wd,
    ws,
    gates,
    hb,
    xbuf,
    ybuf,
    obuf,
    part,
    pre,
    gcol,
    dcol,
    dz_all,
    zg_all,
    dgu_all,
    sz_all,
    sgu_all,
    from_core,
    from_x,
    from_y,
    from_z,
    kept,
    dots,
    dots_core,
    dots_x,
    tiles,
    tiles_all,
    stage,
    stage_low,
    send_sems,
    recv_sems,
    local_sems,
):
    net = Net(cols, send_sems, recv_sems)
    toks, width = h2.shape
    exp_local, _, hidden = w_gate.shape
    high = net.high_count
    pad = ws.shape[1] // 3
    rows_w = w_shared.shape[1]
    slots = exp_local * capacity
    pair = 2 * capacity
    piece = width // lax.axis_size("row")
    share = width // LANES // 5 * LANES
    rest = (width - 4 * share) // 2
    wide = width // TILE
    net.greet([net.col_peer(step) for step in range(1, cols)] + row_peers(net))

    def local_copy(source, target, index):
        copy = pltpu.make_async_copy(source, target, local_sems.at[index])
        copy.start()
        return copy

    gate_copies = [
        net.send(gate_own, gates.at[net.me], net.col_peer(step)) for step in range(1, cols)
    ]
    gates[net.me] = gate_own[...]

    def feature_e(row):
        return pl.ds(pl.multiple_of(row * share, LANES), share)

    def feature_r(core):
        return pl.ds(pl.multiple_of(4 * share + core * rest, LANES), rest)

    own_e, own_r = feature_e(net.row), feature_r(net.core)
    far_e = feature_e(2 * (1 - net.outer) + net.core)

    def pass_on(source, block, features, peer):
        return net.send(source.at[..., features], h2_all.at[block, :, features], peer)

    along_z, along_y, along_x, to_core = {}, {}, {}, {}

    def start_z(step):
        along_z[step] = [
            pass_on(h2, net.me, own_e, net.z_peer(high - step)),
            pass_on(h2, net.me, own_r, net.z_peer(high - step)),
        ]

    start_z(1)
    along_y[0] = [
        pass_on(h2, net.me, own_e, net.y_peer()),
        pass_on(h2, net.me, own_r, net.y_peer()),
    ]

    def block_of(step, other):
        return net.block_ahead(step, other)

    def share_in_chip(step, other):
        block = block_of(step, other)
        source = h2_all.at[block]
        along_x[step, other] = pass_on(source, block, own_e, net.x_peer())
        to_core[step, other] = [
            pass_on(source, block, own_e, net.core_peer()),
            pass_on(source, block, own_r, net.core_peer()),
        ]

    def arrived_y(step):
        for copy in along_y[step]:
            copy.wait_recv()
        share_in_chip(step, True)

    def arrived_z(step):
        for copy in along_z[step]:
            copy.wait_recv()
        block = block_of(step, False)
        along_y[step] = [
            pass_on(h2_all.at[block], block, own_e, net.y_peer()),
            pass_on(h2_all.at[block], block, own_r, net.y_peer()),
        ]
        share_in_chip(step, False)

    def arrived_x(step, other):
        along_x[step, other].wait_recv()
        block = block_of(step, other)
        to_core[step, other].append(pass_on(h2_all.at[block], block, far_e, net.core_peer()))

    def whole(step, other):
        for copy in to_core[step, other]:
            copy.wait_recv()

    events = [functools.partial(arrived_y, 0)]
    for step in range(1, high):
        events.append(functools.partial(arrived_z, step))
        events.append(functools.partial(arrived_x, step - 1, True))
        events.append(functools.partial(arrived_y, step))
        events.append(functools.partial(arrived_x, step, False))
    events.append(functools.partial(arrived_x, high - 1, True))
    events = iter(events)

    def pump(count=1):
        for _ in range(count):
            event = next(events, None)
            if event is not None:
                event()

    loads = []
    for e in range(exp_local):
        loads.append(local_copy(w_down.at[e], wd.at[e], 3 * e))
        loads.append(local_copy(w_gate.at[e], wgu.at[e, :, pl.ds(0, hidden)], 3 * e + 1))
        loads.append(local_copy(w_up.at[e], wgu.at[e, :, pl.ds(hidden, hidden)], 3 * e + 2))
    base = 3 * exp_local
    for c in range(cols):
        loads.append(local_copy(w_shared.at[c], ws.at[pl.ds(c * rows_w, rows_w)], base + c))
    base += cols - 1
    keep_own = local_copy(h2, h2_all.at[net.me], base + 1)
    base += 2

    def load_pair(source, step):
        first = local_copy(source.at[block_of(step, False)], hb.at[0], base)
        second = local_copy(source.at[block_of(step, True)], hb.at[1], base + 1)
        first.wait()
        second.wait()

    slot_row = lax.broadcasted_iota(jnp.int32, (capacity, toks), 0).astype(f32) + 1.0
    slot_lane = lax.broadcasted_iota(jnp.int32, (toks, capacity), 1).astype(f32) + 1.0

    def chosen(block, e):
        return rank_row[block, e : e + 1, :] == slot_row

    def picks(block):
        rows = [
            jnp.where(chosen(block, e), 1.0, 0.0).astype(bf16) for e in range(exp_local)
        ]
        return jnp.concatenate(rows, axis=0)

    def picks_back(block):
        lanes = [
            jnp.where(rank_col[block, :, e : e + 1] == slot_lane, 1.0, 0.0).astype(bf16)
            for e in range(exp_local)
        ]
        return jnp.concatenate(lanes, axis=1)

    def dispatch(step):
        for b in (0, 1):
            table = picks(block_of(step, b == 1))

            def tile(index, b=b, table=table):
                at = tile_at(index, WIDE)
                rows = dot_nn(table, hb[b, :, at]).astype(bf16)
                for e in range(exp_local):
                    xbuf[e, pl.ds(b * capacity, capacity), at] = rows[
                        e * capacity : (e + 1) * capacity
                    ]

            each_tile(width // WIDE, tile)

    def save_rows(target, step):
        return [
            local_copy(
                xbuf.at[e], target.at[e, pl.ds(step * pair, pair)], base + 2 + e
            )
            for e in range(exp_local)
        ]

    saved = []
    for step in range(high):
        load_pair(grads, step)
        if step == 0:
            for copy in loads:
                copy.wait()
        for copy in saved:
            copy.wait()
        dispatch(step)
        saved = save_rows(cs_all, step)
        for e in range(exp_local):
            dz_all[e, pl.ds(step * pair, pair), :] = dot_nt(xbuf[e], wd[e]).astype(bf16)
        pump()
    for copy in gate_copies:
        copy.wait_recv()
    keep_own.wait()

    across, onward, upward, far_z = {}, {}, {}, {}

    def features(row):
        return pl.ds(pl.multiple_of(row * piece, LANES), piece)

    other_row = 2 * (1 - net.outer) + net.core

    def hand_over(step):
        for b in (1, 0):
            for far in (1, 0):
                outer = 1 - net.outer if far else net.outer
                source = part.at[b, :, features(2 * outer + 1 - net.core)]
                across[step, b, far] = net.send(
                    source, from_core.at[far, step, b], net.core_peer()
                )

    def sum_cores(step):
        for b in (1, 0):
            for far, row in ((1, other_row), (0, net.row)):
                across[step, b, far].wait_recv()
                slot = from_core.at[far, step, b]
                add_rows(slot, [part.at[b, :, features(row)], slot])
                if far:
                    onward[step, b] = net.send(slot, from_x.at[step, b], net.x_peer())
        for b in (1, 0):
            for far in (1, 0):
                net.left(across[step, b, far])

    def sum_chips(step):
        for b in (1, 0):
            onward[step, b].wait_recv()
            slot = from_core.at[0, step, b]
            add_rows(slot, [slot, from_x.at[step, b]])
            if b:
                upward[step] = net.send(slot, from_y.at[step], net.y_peer())

    def sum_plane(step):
        upward[step].wait_recv()
        slot = from_core.at[0, step, 0]
        add_rows(slot, [slot, from_y.at[step]])
        if step:
            far_z[step] = net.send(slot, from_z.at[step - 1], net.z_peer(step))

    own_expert = lax.rem(net.me, cols) * exp_local
    gate_rows = gates.shape[1]
    gate_row = lax.broadcasted_iota(jnp.int32, (gate_rows, toks), 0)
    dots[...] = jnp.zeros_like(dots)
    for step in range(high):
        if step:
            whole(step, False)
        whole(step, True)
        load_pair(h2_all, step)
        for copy in saved:
            copy.wait()
        dispatch(step)
        saved = save_rows(xs_all, step)
        if step + 2 < high:
            for copy in along_z[step + 1]:
                net.left(copy)
            start_z(step + 2)
        pump()
        if step:
            for copy in out_copies:
                copy.wait()
        grad_copies = [
            local_copy(grads.at[block_of(step, b == 1)], obuf.at[b], base + 2 + exp_local + b)
            for b in (0, 1)
        ]
        if step:
            sum_cores(step - 1)
        rows = pl.ds(step * pair, pair)
        for e in range(exp_local):
            pre[...] = dot_nn(xbuf[e], wgu[e])
            for b in (0, 1):
                block = block_of(step, b == 1)
                gate = jnp.sum(
                    jnp.where(gate_row == own_expert + e, gates[block], 0.0), axis=0, keepdims=True
                )
                gate = jnp.sum(jnp.where(chosen(block, e), gate, 0.0), axis=1, keepdims=True)
                gcol[pl.ds(b * capacity, capacity), :] = jnp.broadcast_to(gate, (capacity, LANES))

            def gating(index, e=e, step=step):
                at = pl.ds(pl.multiple_of(index * 32, 32), 32)
                saved_at = pl.ds(pl.multiple_of(step * pair + index * 32, 32), 32)
                a, u = pre[at, :hidden], pre[at, hidden:]
                gate = jnp.concatenate([gcol[at, :]] * (hidden // LANES), axis=1)
                dz = dz_all[e, saved_at, :].astype(f32)
                sig = 1.0 / (1.0 + jnp.exp(-a))
                silu = a * sig
                slope = sig * (1.0 + a * (1.0 - sig))
                z = silu * u
                dcol[at, :] = jnp.broadcast_to(
                    jnp.sum(z * dz, axis=1, keepdims=True), (32, LANES)
                )
                zg_all[e, saved_at, :] = (z * gate).astype(bf16)
                dz = dz * gate
                dgu_all[e, saved_at, :hidden] = (dz * u * slope).astype(bf16)
                dgu_all[e, saved_at, hidden:] = (dz * silu).astype(bf16)

            each_tile(pair // 32, gating)
            for b in (0, 1):
                block = block_of(step, b == 1)
                col = dcol[pl.ds(b * capacity, capacity), :]
                col = jnp.concatenate([col] * (toks // LANES), axis=1)
                dots[block, e : e + 1, :] = jnp.sum(
                    jnp.where(chosen(block, e), col, 0.0), axis=0, keepdims=True
                )

            def out_tile(index, e=e):
                at = tile_at(index, WIDE)
                y = dot_nn(zg_all[e, rows, :], wd[e, :, at]).astype(bf16)
                for b in (0, 1):
                    ybuf[b, pl.ds(e * capacity, capacity), at] = y[b * capacity : (b + 1) * capacity]

            each_tile(width // WIDE, out_tile)
            pump()
        for copy in grad_copies:
            copy.wait()
        inner = dot_nn(hb[...].reshape(2 * toks, width), ws[:, : 2 * pad])
        sdz_both = dot_nn(obuf[...].reshape(2 * toks, width), ws[:, 2 * pad :])
        for b in (0, 1):
            block = block_of(step, b == 1)
            sa, su = inner[b * toks : (b + 1) * toks, :pad], inner[b * toks : (b + 1) * toks, pad:]
            sdz = sdz_both[b * toks : (b + 1) * toks]
            sig = 1.0 / (1.0 + jnp.exp(-sa))
            silu = sa * sig
            slope = sig * (1.0 + sa * (1.0 - sig))
            sz_all[block] = (silu * su).astype(bf16)
            sgu_all[block, :, :pad] = (sdz * su * slope).astype(bf16)
            sgu_all[block, :, pad:] = (sdz * silu).astype(bf16)
        out_copies = []
        for b in (0, 1):
            block = block_of(step, b == 1)
            table = picks_back(block)

            def join_tile(index, b=b, table=table, block=block):
                at = tile_at(index, WIDE)
                total = dot_nn(table, ybuf[b, :, at])
                total = total + dot_nt(sz_all[block], ws[at, 2 * pad :])
                obuf[b, :, at] = total.astype(bf16)

            each_tile(width // WIDE, join_tile)
            out_copies.append(
                local_copy(obuf.at[b], out_part.at[block], base + 2 + exp_local + b)
            )
        pump()
        if step:
            sum_chips(step - 1)
        for e in range(exp_local):

            def back_tile(index, e=e):
                at = tile_at(index, WIDE)
                y = dot_nt(dgu_all[e, rows, :], wgu[e, at, :]).astype(bf16)
                for b in (0, 1):
                    ybuf[b, pl.ds(e * capacity, capacity), at] = y[b * capacity : (b + 1) * capacity]

            each_tile(width // WIDE, back_tile)
        pump()
        for b in (1, 0):
            block = block_of(step, b == 1)
            table = picks_back(block)

            def back_join(index, b=b, table=table, block=block):
                at = tile_at(index, WIDE)
                total = dot_nn(table, ybuf[b, :, at])
                total = total + dot_nt(sgu_all[block], ws[at, : 2 * pad])
                part[b, :, at] = total.astype(bf16)

            each_tile(width // WIDE, back_join)
        hand_over(step)
        if step:
            sum_plane(step - 1)
    pump(64)
    last = high - 1
    for copy in saved + out_copies:
        copy.wait()

    load_sem, store_sem = base + 4 + exp_local, base + 6 + exp_local

    def passes(count, load, work, stores):
        def load_copy(j, slot):
            source, target = load(j, slot)
            return pltpu.make_async_copy(source, target, local_sems.at[load_sem + slot])

        def store_copies(j, slot):
            return [
                pltpu.make_async_copy(
                    source, target, local_sems.at[store_sem + 2 * slot + i]
                )
                for i, (source, target) in enumerate(stores(j, slot))
            ]

        load_copy(0, 0).start()

        def body(j):
            slot = lax.rem(j, 2)

            @pl.when(j + 1 < count)
            def _():
                load_copy(j + 1, 1 - slot).start()

            load_copy(j, slot).wait()

            @pl.when(j >= 2)
            def _():
                for copy in store_copies(j - 2, slot):
                    copy.wait()

            work(j, slot)
            for copy in store_copies(j, slot):
                copy.start()

        each_tile(count, body)
        for j in range(max(0, count - 2), count):
            for copy in store_copies(j, j % 2):
                copy.wait()

    def inner_grads(e):
        passes(
            wide,
            lambda j, slot: (
                xs_all.at[e, :, tile_at(j)],
                tiles.at[slot],
            ),
            lambda j, slot: put(stage.at[slot], dot_tn(tiles[slot], dgu_all[e]).astype(bf16)),
            lambda j, slot: [
                (stage.at[slot, :, pl.ds(0, hidden)], g_gate.at[e, tile_at(j)]),
                (stage.at[slot, :, pl.ds(hidden, hidden)], g_up.at[e, tile_at(j)]),
            ],
        )

    def put(target, value):
        target[...] = value

    def down_grads(e):
        passes(
            wide,
            lambda j, slot: (
                cs_all.at[e, :, tile_at(j)],
                tiles.at[slot],
            ),
            lambda j, slot: put(
                stage.at[slot, pl.ds(0, hidden), pl.ds(0, TILE)],
                dot_tn(zg_all[e], tiles[slot]).astype(bf16),
            ),
            lambda j, slot: [
                (
                    stage.at[slot, pl.ds(0, hidden), pl.ds(0, TILE)],
                    g_down.at[e, :, tile_at(j)],
                ),
            ],
        )

    def shared_grads(source, others, start, size):
        def work(j, slot):
            total = dot_tn(tiles_all[slot, 0], others[0])
            for c in range(1, cols):
                total = total + dot_tn(tiles_all[slot, c], others[c])
            stage_low[slot, :, :size] = total.astype(bf16)

        def load(j, slot):
            return (source.at[:, :, tile_at(j)], tiles_all.at[slot])

        passes(
            wide,
            lambda j, slot: load(j, slot),
            work,
            lambda j, slot: [
                (
                    stage_low.at[slot, :, pl.ds(0, size)],
                    g_shared.at[tile_at(j), pl.ds(start, size)],
                ),
            ],
        )

    first_dots = net.send(dots, dots_core, net.core_peer())
    shared_grads(h2_all, sgu_all, 0, 2 * pad)
    sum_cores(last)
    shared_grads(grads, sz_all, 2 * pad, pad)
    inner_grads(0)
    first_dots.wait_recv()
    net.left(first_dots)
    dots[...] = dots[...] + dots_core[...]
    second_dots = net.send(dots, dots_x, net.x_peer())
    inner_grads(1)
    sum_chips(last)
    second_dots.wait_recv()
    dots_core[...] = dots[...] + dots_x[...]
    third_dots = []
    for step in range(1, cols):
        block = lax.rem(net.me + step, cols)
        third_dots.append(
            net.send(dots_core.at[block], gate_dots.at[net.me], net.col_peer(step))
        )
    gate_dots[net.me] = dots_core[net.me]
    down_grads(0)
    sum_plane(last)
    for step in range(1, high):
        far_z[step].wait_recv()
    add_rows(kept, [from_core.at[0, 0, 0], *[from_z.at[step - 1] for step in range(1, high)]])
    own, other = features(net.row), features(other_row)
    back[:, own] = kept[...].astype(bf16)
    far = net.send(back.at[:, own], back.at[:, own], net.x_peer())
    near = net.send(back.at[:, own], back.at[:, own], net.core_peer())
    far.wait_recv()
    crossed = net.send(back.at[:, other], back.at[:, other], net.core_peer())
    down_grads(1)
    near.wait_recv()
    crossed.wait_recv()
    for copy in third_dots:
        copy.wait_recv()
    net.finish()


def experts_call(
    cols, collective_id, capacity, h2, grads, w_gate, w_up, w_down, w_shared, rank_row, rank_col, gate
):
    toks, width = h2.shape
    exp_local, _, hidden = w_gate.shape
    high = cols // 2
    pad = w_shared.shape[2] // 3
    piece = width // lax.axis_size("row")
    pair = 2 * capacity
    any_space = pl.BlockSpec(memory_space=pl.ANY)
    vmem = pl.BlockSpec(memory_space=pltpu.VMEM)
    copies = 160

    def shape(*dims, dtype=bf16):
        return jax.ShapeDtypeStruct(dims, dtype)

    return pl.pallas_call(
        functools.partial(experts_kernel, cols, capacity),
        out_shape=[
            shape(cols, toks, width),
            shape(toks, width),
            shape(exp_local, width, hidden),
            shape(exp_local, width, hidden),
            shape(exp_local, hidden, width),
            shape(width, 3 * pad),
            shape(cols, 8, toks, dtype=f32),
            shape(cols, toks, width),
            shape(exp_local, cols * capacity, width),
            shape(exp_local, cols * capacity, width),
        ],
        in_specs=[any_space] * 6 + [vmem] * 3,
        out_specs=[
            any_space,
            vmem,
            any_space,
            any_space,
            any_space,
            any_space,
            vmem,
            any_space,
            any_space,
            any_space,
        ],
        scratch_shapes=[
            pltpu.VMEM((exp_local, width, 2 * hidden), bf16),
            pltpu.VMEM((exp_local, hidden, width), bf16),
            pltpu.VMEM((width, 3 * pad), bf16),
            pltpu.VMEM((cols, *gate.shape), f32),
            pltpu.VMEM((2, toks, width), bf16),
            pltpu.VMEM((exp_local, pair, width), bf16),
            pltpu.VMEM((2, exp_local * capacity, width), bf16),
            pltpu.VMEM((2, toks, width), bf16),
            pltpu.VMEM((2, toks, width), bf16),
            pltpu.VMEM((pair, 2 * hidden), f32),
            pltpu.VMEM((pair, LANES), f32),
            pltpu.VMEM((pair, LANES), f32),
            pltpu.VMEM((exp_local, cols * capacity, hidden), bf16),
            pltpu.VMEM((exp_local, cols * capacity, hidden), bf16),
            pltpu.VMEM((exp_local, cols * capacity, 2 * hidden), bf16),
            pltpu.VMEM((cols, toks, pad), bf16),
            pltpu.VMEM((cols, toks, 2 * pad), bf16),
            pltpu.VMEM((2, high, 2, toks, piece), bf16),
            pltpu.VMEM((high, 2, toks, piece), bf16),
            pltpu.VMEM((high, toks, piece), bf16),
            pltpu.VMEM((high - 1, toks, piece), bf16),
            pltpu.VMEM((toks, piece), f32),
            pltpu.VMEM((cols, 8, toks), f32),
            pltpu.VMEM((cols, 8, toks), f32),
            pltpu.VMEM((cols, 8, toks), f32),
            pltpu.VMEM((2, cols * capacity, TILE), bf16),
            pltpu.VMEM((2, cols, toks, TILE), bf16),
            pltpu.VMEM((2, TILE, 2 * hidden), bf16),
            pltpu.VMEM((2, TILE, 2 * pad), bf16),
            pltpu.SemaphoreType.DMA((copies,)),
            pltpu.SemaphoreType.DMA((copies,)),
            pltpu.SemaphoreType.DMA((32,)),
        ],
        compiler_params=pltpu.CompilerParams(
            collective_id=collective_id, has_side_effects=True, vmem_limit_bytes=62 << 20
        ),
        name=f"experts_{collective_id}",
    )(h2, grads, w_gate, w_up, w_down, w_shared, rank_row, rank_col, gate)


def padded_thirds(packed):
    third = packed.shape[-1] // 3
    parts = packed.reshape(*packed.shape[:-1], 3, third)
    parts = jnp.pad(parts, ((0, 0),) * (parts.ndim - 1) + ((0, -third % LANES),))
    return parts.reshape(*packed.shape[:-1], -1)


def fits(cols, rows, width):
    return cols % 2 == 0 and cols * rows * width * 2 <= 12 << 20


class Sum2D:
    def __init__(self, net, source, start, count, from_y, from_z, out):
        self.net, self.source, self.start, self.count = net, source, start, count
        self.from_y, self.from_z, self.out = from_y, from_z, out
        self.rows = pl.ds(start, count)
        self.order = [*range(1, net.high_count), 0]
        self.along_y, self.along_z = {}, {}

    def mine(self, block):
        return self.source(block, self.start, self.count)

    def send_y(self):
        for step in self.order:
            source = self.mine(self.net.block_ahead(step, True))
            self.along_y[step] = self.net.send(
                source, self.from_y.at[step, self.rows], self.net.y_peer()
            )

    def send_z(self):
        for step in self.order:
            self.along_y[step].wait_recv()
            slot = self.from_y.at[step, self.rows]
            if step:
                add_rows(slot, [self.mine(self.net.block_ahead(step)), slot])
                self.along_z[step] = self.net.send(
                    slot, self.from_z.at[step - 1, self.rows], self.net.z_peer(step)
                )

    def last(self):
        for step in range(1, self.net.high_count):
            self.along_z[step].wait_recv()
        terms = [
            self.from_z.at[step - 1, self.rows] for step in range(1, self.net.high_count)
        ]
        mine = self.mine(self.net.me)
        add_rows(self.out.at[self.rows], [mine, self.from_y.at[0, self.rows], *terms])


def rear_kernel(
    cols,
    experts,
    out_part,
    g_shared,
    back,
    gate_dots,
    gate,
    router_probs,
    table_col,
    h1,
    h2,
    tokens,
    attn,
    weights_in,
    out_weights_in,
    grads,
    heads,
    q_low,
    kv_all,
    probs,
    cosine,
    sine,
    out_slice,
    d_tokens,
    share_qkv,
    share_misc,
    share_out,
    shared_back,
    weights,
    out_weights,
    misc,
    misc_low,
    grad_own,
    gains,
    dots,
    logit_low,
    low,
    dob,
    keys,
    values,
    stacked,
    ds_all,
    kv_grad,
    kv_share,
    dqkv,
    gain_sums,
    own,
    from_core,
    from_x,
    from_y,
    from_z,
    kv_y,
    kv_z,
    out_y,
    out_z,
    qkv_y,
    qkv_z,
    misc_y,
    misc_z,
    row_core,
    row_to,
    row_from,
    send_sems,
    recv_sems,
    local_sems,
):
    net = Net(cols, send_sems, recv_sems)
    toks, width = back.shape
    size = HEAD_DIM
    q_width = q_low.shape[1]
    group = q_width // size
    qkv_width = q_width + 2 * size
    seqs = probs.shape[0]
    local_len = toks // seqs
    rows_w = width // cols
    piece = width // lax.axis_size("row")
    scale = 1.0 / math.sqrt(size)
    other_row = 2 * (1 - net.outer) + net.core

    def local_copy(source, target, index):
        copy = pltpu.make_async_copy(source, target, local_sems.at[index])
        copy.start()
        return copy

    def features(row):
        return pl.ds(pl.multiple_of(row * piece, LANES), piece)

    loads = [
        local_copy(weights_in, weights, 0),
        local_copy(out_weights_in, out_weights, 1),
        local_copy(grads.at[net.me], grad_own, 2),
    ]
    near_load = local_copy(out_part.at[:, :, features(net.row)], own.at[0], 3)
    far_load = local_copy(out_part.at[:, :, features(other_row)], own.at[1], 4)
    own_rows = pl.ds(pl.multiple_of(net.me * rows_w, 16), rows_w)
    keep_own = local_copy(g_shared.at[own_rows], shared_back.at[net.me], 5)
    net.greet([net.col_peer(step) for step in range(1, cols)] + row_peers(net))
    swaps = []
    for step in range(1, cols):
        block = lax.rem(net.me + step, cols)
        rows = pl.ds(pl.multiple_of(block * rows_w, 16), rows_w)
        swaps.append(net.send(g_shared.at[rows], shared_back.at[net.me], net.col_peer(step)))

    pieces = 4
    count = toks // pieces
    order = [*range(1, net.high_count), 0]
    keys_of = [(step, True) for step in order] + [(step, False) for step in order]
    across, onward, along_y, along_z = {}, {}, {}, {}

    def rows_of(q):
        return pl.ds(q * count, count)

    def out_core(q):
        for far in (1, 0):
            outer = 1 - net.outer if far else net.outer
            for key in keys_of:
                block = net.block_ahead(*key)
                across[q, far, key] = net.send(
                    out_part.at[block, rows_of(q), features(2 * outer + 1 - net.core)],
                    from_core.at[far, block, rows_of(q)],
                    net.core_peer(),
                )

    def out_x(q):
        for key in keys_of:
            across[q, 1, key].wait_recv()
            block = net.block_ahead(*key)
            slot = from_core.at[1, block, rows_of(q)]
            add_rows(slot, [own.at[1, block, rows_of(q)], slot])
            onward[q, key] = net.send(slot, from_x.at[block, rows_of(q)], net.x_peer())

    def out_y_stage(q):
        for key in keys_of:
            across[q, 0, key].wait_recv()
            onward[q, key].wait_recv()
            block = net.block_ahead(*key)
            slot = from_core.at[0, block, rows_of(q)]
            add_rows(slot, [own.at[0, block, rows_of(q)], slot, from_x.at[block, rows_of(q)]])
            if key[1]:
                along_y[q, key[0]] = net.send(
                    slot, from_y.at[key[0], rows_of(q)], net.y_peer()
                )

    def out_z_stage(q):
        for step in order:
            along_y[q, step].wait_recv()
            slot = from_core.at[0, net.block_ahead(step), rows_of(q)]
            add_rows(slot, [slot, from_y.at[step, rows_of(q)]])
            if step:
                along_z[q, step] = net.send(
                    slot, from_z.at[step - 1, rows_of(q)], net.z_peer(step)
                )

    def out_last(q):
        for step in range(1, net.high_count):
            along_z[q, step].wait_recv()
        terms = [from_z.at[step - 1, rows_of(q)] for step in range(1, net.high_count)]
        add_rows(out_slice.at[rows_of(q)], [from_core.at[0, net.me, rows_of(q)], *terms])

    state = {"tick": 0}

    def pump(ticks=1):
        for _ in range(ticks):
            tick = state["tick"]
            state["tick"] += 1
            for lag, stage in enumerate((out_core, out_x, out_y_stage, out_z_stage, out_last)):
                if 0 <= tick - lag < pieces:
                    stage(tick - lag)

    pump()
    for copy in loads:
        copy.wait()

    def chunks(body, rows=32):
        def step(index, carry):
            body(pl.ds(pl.multiple_of(index * rows, rows), rows))
            return carry

        lax.fori_loop(0, toks // rows, step, 0)

    for tile in range(width // TILE):
        at = pl.ds(tile * TILE, TILE)
        turned = jnp.transpose(weights[at, qkv_width : qkv_width + LANES].astype(f32))
        gains[:, at] = turned[experts : experts + 8]
    dots[...] = jnp.zeros_like(dots)
    for c in range(cols):
        dots[2 * c : 2 * c + 2, :] = gate_dots[c, 0:2, :]
    gate_grad = jnp.transpose(dots[...])
    lane = lax.broadcasted_iota(jnp.int32, (toks, LANES), 1)
    mask = (table_col[...] > 0) & (lane < experts)
    chance, gates = router_probs[...], gate[...]
    total = jnp.sum(jnp.where(mask, chance, 0.0), axis=1, keepdims=True)
    gate_grad = jnp.where(mask, gate_grad, 0.0)
    pick_grad = gate_grad - jnp.sum(gates * gate_grad, axis=1, keepdims=True)
    chance_grad = jnp.where(mask, pick_grad / total, 0.0)
    logit_grad = chance * (chance_grad - jnp.sum(chance * chance_grad, axis=1, keepdims=True))
    logit_low[...] = logit_grad.astype(bf16)
    near_load.wait()
    far_load.wait()
    pump()

    for tile in range(width // TILE):
        at = pl.ds(tile * TILE, TILE)
        d_tokens[:, at] = back[:, at].astype(f32) + dot_nt(
            logit_low[...], weights[at, qkv_width : qkv_width + LANES]
        )
    gain_sums[...] = jnp.zeros_like(gain_sums)

    def fold(values, start):
        total = values[0:8]
        for r in range(8, values.shape[0], 8):
            total = total + values[r : r + 8]
        gain_sums[start : start + 8, :] = gain_sums[start : start + 8, :] + total

    def norm_second(at):
        x = tokens[at, :].astype(f32) + attn[at, :].astype(f32)
        inverse = lax.rsqrt(jnp.sum(x * x, axis=1, keepdims=True) / width + norm_eps)
        base = x * inverse
        dh = d_tokens[at, :]
        fold(dh * base, 8)
        scaled = dh * gains[1:2, :]
        mean = jnp.sum(scaled * base, axis=1, keepdims=True) / width
        middle = inverse * (scaled - base * mean) + grad_own[at, :].astype(f32)
        d_tokens[at, :] = middle
        low[at, :] = middle.astype(bf16)

    chunks(norm_second, 16)
    dob[...] = dot_nn(low[...], out_weights[...]).astype(bf16)
    pump()
    for tile in range(width // TILE):
        at = pl.ds(tile * TILE, TILE)
        out_weights[at, :] = dot_tn(low[:, at], heads[...]).astype(bf16)

    def blocks_of(array):
        def source(block, start, count):
            return array.at[pl.ds(pl.multiple_of(block * rows_w + start, 16), count)]

        return source

    out_pieces = 4
    out_count = rows_w // out_pieces
    out_line = [
        Sum2D(net, blocks_of(out_weights), q * out_count, out_count, out_y, out_z, share_out)
        for q in range(out_pieces)
    ]
    out_line[0].send_y()
    out_line[1].send_y()

    kv_line = [
        Sum2D(
            net,
            lambda block, start, count: kv_grad.at[block, pl.ds(start, count)],
            s * local_len,
            local_len,
            kv_y,
            kv_z,
            kv_share,
        )
        for s in range(seqs)
    ]
    for s in range(seqs):
        rows = pl.ds(s * local_len, local_len)
        for c in range(cols):
            at = pl.ds(c * local_len, local_len)
            keys[at, :] = kv_all[c, rows, :size]
            values[at, :] = kv_all[c, rows, size:]

        def attend(g, carry, s=s, rows=rows):
            at = pl.ds(pl.multiple_of(g * size, size), size)
            grow = pl.ds(pl.multiple_of(g * local_len, local_len), local_len)
            dout = dob[rows, at]
            stacked[0, grow, :] = q_low[rows, at]
            stacked[1, grow, :] = dout
            p = probs[s, g]
            p = p.astype(f32)
            dp = dot_nt(dout, values[...])
            delta = jnp.sum(p * dp, axis=1, keepdims=True)
            ds = (p * (dp - delta)).astype(bf16)
            ds_all[grow, :] = ds
            raw = dot_nn(ds, keys[...]) * scale
            dqkv[rows, at] = (
                raw * cosine[rows, :] - pltpu.roll(raw, size // 2, 1) * sine[rows, :]
            ).astype(bf16)
            return carry

        lax.fori_loop(0, group, attend, 0)
        dk = (dot_tn(ds_all[...], stacked[0]) * scale).astype(bf16)
        dv = dot_tn(probs[s].reshape(group * local_len, -1), stacked[1]).astype(bf16)
        for c in range(cols):
            kv_grad[c, rows, :size] = dk[c * local_len : (c + 1) * local_len]
            kv_grad[c, rows, size:] = dv[c * local_len : (c + 1) * local_len]
        kv_line[s].send_y()
        if s == 0:
            out_line[2].send_y()
            out_line[0].send_z()
            pump()
        else:
            out_line[3].send_y()
            kv_line[s - 1].send_z()
    kv_line[seqs - 1].send_z()
    out_line[1].send_z()
    for s in range(seqs):
        kv_line[s].last()
    raw = kv_share[:, :size]
    dqkv[:, q_width : q_width + size] = (
        raw * cosine[...] - pltpu.roll(raw, size // 2, 1) * sine[...]
    ).astype(bf16)
    dqkv[:, q_width + size : qkv_width] = kv_share[:, size:].astype(bf16)

    row_pieces, piece_rows = row_core.shape[0], row_core.shape[1]
    half = row_pieces * piece_rows

    def row_piece(core, i):
        return pl.ds(pl.multiple_of((core * row_pieces + i) * piece_rows, piece_rows), piece_rows)

    over = []
    for core in (1 - net.core, net.core):
        at_rows = pl.ds(pl.multiple_of(core * half, half), half)
        for tile in range(width // TILE):
            at = pl.ds(tile * TILE, TILE)
            low[at_rows, at] = dot_nt(dqkv[at_rows, :], weights[at, :qkv_width]).astype(bf16)
        if not over:
            over = [
                net.send(low.at[row_piece(1 - net.core, i)], row_core.at[i], net.core_peer())
                for i in range(row_pieces)
            ]

    qkv_pieces = 5
    qkv_count = rows_w // qkv_pieces
    for tile in range(width // TILE):
        at = pl.ds(tile * TILE, TILE)
        misc[at, :] = dot_tn(h2[:, at], logit_low[...])
        weights[at, :qkv_width] = dot_tn(h1[:, at], dqkv[...]).astype(bf16)
    qkv_line = [
        Sum2D(
            net,
            lambda block, start, count: weights.at[
                pl.ds(pl.multiple_of(block * rows_w + start, 16), count), pl.ds(0, qkv_width)
            ],
            q * qkv_count,
            qkv_count,
            qkv_y,
            qkv_z,
            share_qkv,
        )
        for q in range(qkv_pieces)
    ]
    qkv_line[0].send_y()
    along, returned = [], []
    for i in range(row_pieces):
        over[i].wait_recv()
        add_rows(row_to.at[i], [low.at[row_piece(net.core, i)], row_core.at[i]])
        along.append(net.send(row_to.at[i], row_from.at[i], net.x_peer()))
    qkv_line[1].send_y()
    for i in range(row_pieces):
        along[i].wait_recv()
        at = row_piece(net.core, i)
        add_rows(grad_own.at[at], [row_to.at[i], row_from.at[i]])
        returned.append(net.send(grad_own.at[at], grad_own.at[at], net.core_peer()))
    qkv_line[0].send_z()
    pump()
    for copy in returned:
        copy.wait_recv()

    def norm_first(at):
        x = tokens[at, :].astype(f32)
        inverse = lax.rsqrt(jnp.sum(x * x, axis=1, keepdims=True) / width + norm_eps)
        base = x * inverse
        dh = grad_own[at, :].astype(f32)
        fold(dh * base, 0)
        scaled = dh * gains[0:1, :]
        mean = jnp.sum(scaled * base, axis=1, keepdims=True) / width
        d_tokens[at, :] = d_tokens[at, :] + inverse * (scaled - base * mean)

    chunks(norm_first, 16)
    total = [jnp.sum(gain_sums[8 * i : 8 * i + 8, :], axis=0, keepdims=True) for i in (0, 1)]
    row_at = lax.broadcasted_iota(jnp.int32, (LANES, TILE), 0)
    for tile in range(width // TILE):
        at = pl.ds(tile * TILE, TILE)
        part = slice(tile * TILE, (tile + 1) * TILE)
        placed = jnp.where(row_at == experts, total[0][:, part], 0.0)
        placed = jnp.where(row_at == experts + 1, total[1][:, part], placed)
        lanes = lax.broadcasted_iota(jnp.int32, (TILE, LANES), 1)
        misc_low[at, :] = jnp.where(lanes < experts, misc[at, :], jnp.transpose(placed)).astype(bf16)
    misc_line = Sum2D(net, blocks_of(misc_low), 0, rows_w, misc_y, misc_z, share_misc)
    misc_line.send_y()
    qkv_line[2].send_y()
    qkv_line[1].send_z()
    out_line[2].send_z()
    pump()
    misc_line.send_z()
    qkv_line[3].send_y()
    qkv_line[2].send_z()
    out_line[3].send_z()
    pump()
    qkv_line[4].send_y()
    qkv_line[3].send_z()
    pump()
    qkv_line[4].send_z()
    pump(8)
    for piece_sum in (*out_line, misc_line, *qkv_line):
        piece_sum.last()
    keep_own.wait()
    for copy in swaps:
        copy.wait_recv()
    net.finish()


def rear_call(
    cols, collective_id, experts, out_part, g_shared, back, gate_dots, gate, router_probs, table_col, h1, h2,
    tokens, attn, weights, out_weights, grads, heads, q_low, kv_all, probs, cosine, sine,
):
    toks, width = back.shape
    q_width = q_low.shape[1]
    size = HEAD_DIM
    qkv_width = q_width + 2 * size
    seqs, group, local_len, full_len = probs.shape
    rows_w, high = width // cols, cols // 2
    piece = width // lax.axis_size("row")
    row_pieces = 4
    row_piece = (row_pieces, toks // 2 // row_pieces, width)
    vmem, any_space = pl.BlockSpec(memory_space=pltpu.VMEM), pl.BlockSpec(memory_space=pl.ANY)

    def shape(*dims, dtype=f32):
        return jax.ShapeDtypeStruct(dims, dtype)

    def sums(rows, columns):
        return [
            pltpu.VMEM((high, rows, columns), bf16),
            pltpu.VMEM((high - 1, rows, columns), bf16),
        ]

    copies = 420
    return pl.pallas_call(
        functools.partial(rear_kernel, cols, experts),
        out_shape=[
            shape(toks, piece),
            shape(toks, width),
            shape(rows_w, qkv_width),
            shape(rows_w, LANES),
            shape(rows_w, q_width),
            shape(cols, rows_w, g_shared.shape[1], dtype=bf16),
        ],
        in_specs=[any_space] * 2 + [vmem] * 9 + [any_space] * 3 + [vmem] * 6,
        out_specs=[vmem] * 5 + [any_space],
        scratch_shapes=[
            pltpu.VMEM((width, qkv_width + LANES), bf16),
            pltpu.VMEM((width, q_width), bf16),
            pltpu.VMEM((width, LANES), f32),
            pltpu.VMEM((width, LANES), bf16),
            pltpu.VMEM((toks, width), bf16),
            pltpu.VMEM((8, width), f32),
            pltpu.VMEM((LANES, toks), f32),
            pltpu.VMEM((toks, LANES), bf16),
            pltpu.VMEM((toks, width), bf16),
            pltpu.VMEM((toks, q_width), bf16),
            pltpu.VMEM((full_len, size), bf16),
            pltpu.VMEM((full_len, size), bf16),
            pltpu.VMEM((2, group * local_len, size), bf16),
            pltpu.VMEM((group * local_len, full_len), bf16),
            pltpu.VMEM((cols, toks, 2 * size), bf16),
            pltpu.VMEM((toks, 2 * size), f32),
            pltpu.VMEM((toks, qkv_width), bf16),
            pltpu.VMEM((16, width), f32),
            pltpu.VMEM((2, cols, toks, piece), bf16),
            pltpu.VMEM((2, cols, toks, piece), bf16),
            pltpu.VMEM((cols, toks, piece), bf16),
            *sums(toks, piece),
            *sums(toks, 2 * size),
            *sums(rows_w, q_width),
            *sums(rows_w, qkv_width),
            *sums(rows_w, LANES),
            pltpu.VMEM(row_piece, bf16),
            pltpu.VMEM(row_piece, bf16),
            pltpu.VMEM(row_piece, bf16),
            pltpu.SemaphoreType.DMA((copies,)),
            pltpu.SemaphoreType.DMA((copies,)),
            pltpu.SemaphoreType.DMA((8,)),
        ],
        compiler_params=pltpu.CompilerParams(
            collective_id=collective_id, has_side_effects=True, vmem_limit_bytes=62 << 20
        ),
        name=f"rear_{collective_id}",
    )(
        out_part, g_shared, back, gate_dots, gate, router_probs, table_col, h1, h2, tokens, attn, weights,
        out_weights, grads, heads, q_low, kv_all, probs, cosine, sine,
    )


def experts_plain(
    h2, grad_all, w_gate, w_up, w_down, shared_weights, router, rank_all, capacity, row_width
):
    cols = lax.axis_size("col")
    col_index, row_index = lax.axis_index("col"), lax.axis_index("row")
    toks, width = h2.shape
    exp_local = w_gate.shape[0]
    experts = rank_all.shape[2]
    shared_part = shared_weights.shape[1] // 3
    shared_in_weights = shared_weights[:, : 2 * shared_part]
    shared_down = shared_weights[:, 2 * shared_part :]
    h2_slice = lax.dynamic_slice_in_dim(h2, row_index * row_width, row_width, 1)
    h2_all = gather_all(h2_slice)

    all_mask = (rank_all > 0).astype(f32)
    all_probs = jax.nn.softmax(dot("ctd,de->cte", h2_all, router), axis=-1)
    all_picked = all_probs * all_mask
    all_gate = all_picked / jnp.sum(all_picked, axis=-1, keepdims=True)
    own = col_index * exp_local
    own_gate = lax.dynamic_slice_in_dim(all_gate, own, exp_local, 2)
    own_rank = lax.dynamic_slice_in_dim(rank_all, own, exp_local, 2).astype(jnp.int32)
    slots = jnp.arange(1, capacity + 1, dtype=jnp.int32)
    pick = jnp.swapaxes(own_rank, 1, 2)[:, :, None, :] == slots[:, None]
    slot_gate = jnp.sum(
        jnp.where(pick, jnp.swapaxes(own_gate, 1, 2)[:, :, None, :], 0.0), axis=3
    )[..., None]
    pick_low = pick.astype(bf16).reshape(cols, exp_local * capacity, toks)
    slot_shape = (cols, exp_local, capacity, width)
    slot_rows = dot("cut,ctd->cud", pick_low, h2_all).astype(bf16).reshape(slot_shape)
    slot_grad = dot("cut,ctd->cud", pick_low, grad_all).astype(bf16).reshape(slot_shape)
    gate_pre = dot("necd,edf->necf", slot_rows, w_gate)
    up_pre = dot("necd,edf->necf", slot_rows, w_up)
    silu_gate, slope_gate = silu_parts(gate_pre)
    hidden = silu_gate * up_pre
    gated = (hidden * slot_gate).astype(bf16)
    slot_out = dot("necf,efd->necd", gated, w_down).astype(bf16)
    hidden_grad = dot("necd,efd->necf", slot_grad, w_down)
    slot_dots = jnp.sum(hidden * hidden_grad, axis=-1)
    hidden_grad = hidden_grad * slot_gate
    gate_grad = (hidden_grad * up_pre * slope_gate).astype(bf16)
    up_grad = (hidden_grad * silu_gate).astype(bf16)
    slot_back = dot("necf,edf->necd", gate_grad, w_gate)
    slot_back = (slot_back + dot("necf,edf->necd", up_grad, w_up)).astype(bf16)
    grad_expert_down = dot("necf,necd->efd", gated, slot_grad)
    grad_expert_gate = dot("necd,necf->edf", slot_rows, gate_grad)
    grad_expert_up = dot("necd,necf->edf", slot_rows, up_grad)
    pick_flat = pick_low.reshape(cols, exp_local * capacity, toks)
    slot_out = slot_out.reshape(cols, exp_local * capacity, width)
    slot_back = slot_back.reshape(cols, exp_local * capacity, width)

    shared_pre = dot("ctd,dk->ctk", h2_all, shared_in_weights)
    sgate_pre, sup_pre = shared_pre[:, :, :shared_part], shared_pre[:, :, shared_part:]
    shared_silu, shared_slope = silu_parts(sgate_pre)
    shared_hidden = (shared_silu * sup_pre).astype(bf16)
    part_out = dot("cut,cud->ctd", pick_flat, slot_out) + dot(
        "ctk,dk->ctd", shared_hidden, shared_down
    )
    shared_hgrad = dot("ctd,dk->ctk", grad_all, shared_down)
    shared_grads = jnp.concatenate(
        [shared_hgrad * sup_pre * shared_slope, shared_hgrad * shared_silu], axis=2
    ).astype(bf16)
    part_back = dot("cut,cud->ctd", pick_flat, slot_back) + dot(
        "ctk,dk->ctd", shared_grads, shared_in_weights
    )
    token_dots = jnp.einsum(
        "ceu,ceut->cte", slot_dots, pick.astype(f32), precision=lax.Precision.HIGHEST
    )
    gate_dots = lax.psum(swap_col(token_dots), "row")
    gate_dots = jnp.swapaxes(gate_dots, 0, 1).reshape(toks, experts)

    shared_share = jnp.concatenate(
        [dot("ctd,ctk->dk", h2_all, shared_grads), dot("ctd,ctk->dk", grad_all, shared_hidden)],
        axis=1,
    ).astype(bf16)
    back_full = lax.all_gather(scatter_all(part_back.astype(bf16)), "row", axis=1, tiled=True)
    return (
        part_out.astype(bf16),
        back_full,
        gate_dots,
        shared_share,
        grad_expert_gate,
        grad_expert_up,
        grad_expert_down,
    )


def on_device(
    tokens,
    segments,
    routes,
    attn_gain,
    query_matrix,
    key_matrix,
    value_matrix,
    attention_output_matrix,
    mlp_gain,
    w_router,
    shared_gate_matrix,
    shared_up_matrix,
    shared_down_matrix,
    expert_gate,
    expert_up,
    expert_down,
    cotangent,
):
    local_len, seqs, width = tokens.shape
    cols = lax.axis_size("col")
    col_index = lax.axis_index("col")
    rows_w = query_matrix.shape[0]
    full_len = local_len * cols
    size = HEAD_DIM
    q_width = query_matrix.shape[1]
    kv_width = key_matrix.shape[1]
    kv_local = kv_width // size
    group = q_width // kv_width
    row_width = cotangent.shape[2]
    toks = local_len * seqs
    top = routes.shape[2]
    experts = w_router.shape[1]
    exp_local = expert_gate.shape[0]
    hidden_local = expert_gate.shape[2]
    capacity = max(2, toks * top * 4 // (3 * experts))
    shared_part = shared_gate_matrix.shape[1] // cols
    scale = 1.0 / math.sqrt(size)
    kernels = fits(cols, toks, width) and kv_local == 1 and exp_local == 2

    def seq_major(a):
        return jnp.swapaxes(a, 0, 1).reshape(toks, a.shape[2])

    misc = jnp.concatenate(
        [
            w_router,
            attn_gain[:, None],
            mlp_gain[:, None],
            jnp.zeros((rows_w, LANES - experts - 2), bf16),
        ],
        axis=1,
    )
    shared_weights = jnp.concatenate(
        [
            shared_gate_matrix.reshape(rows_w, cols, shared_part),
            shared_up_matrix.reshape(rows_w, cols, shared_part),
            shared_down_matrix.T.reshape(rows_w, cols, shared_part),
        ],
        axis=2,
    )
    shared_own = jnp.swapaxes(shared_weights, 0, 1)
    grad_own = seq_major(cotangent).astype(bf16)
    cosine, sine = rope_tables(col_index * local_len, local_len, size)
    cosine, sine = jnp.tile(cosine, (seqs, 1)), jnp.tile(sine, (seqs, 1))
    qkv_width = q_width + 2 * kv_width
    flat_routes = seq_major(routes)
    named = flat_routes[:, :, None] == jnp.arange(experts, dtype=jnp.int32)
    mask = jnp.any(named, axis=1)
    order = jnp.arange(toks, dtype=jnp.int32)
    upto = (order[None, :] <= order[:, None]).astype(bf16)
    rank = jnp.where(mask, dot("ij,je->ie", upto, mask.astype(bf16)), 0.0)

    doc = jnp.transpose(segments)
    def to_grid(flat):
        shaped = flat.reshape(seqs, local_len, kv_local, group, size)
        return shaped.transpose(0, 2, 3, 1, 4).reshape(seqs, kv_local, group * local_len, size)

    def from_grid(grid):
        shaped = grid.reshape(seqs, kv_local, group, local_len, size)
        return shaped.transpose(0, 3, 1, 2, 4).reshape(toks, q_width)

    token_rows = seq_major(tokens)
    x = token_rows.astype(f32)
    inv_first = rms_scale(x)
    base_first = x * inv_first
    if kernels:
        table_row = jnp.concatenate([rank.T, doc.reshape(1, toks).astype(f32)], axis=0)
        table_row = jnp.pad(table_row, ((0, -(experts + 1) % 8), (0, 0)))
        table_col = jnp.pad(rank, ((0, 0), (0, LANES - experts))).astype(bf16)
        (
            first_weights,
            out_weights,
            grad_all,
            shared_weights,
            rows_all,
            rank_all,
            h1,
            q_low,
            kv_all,
            probs,
            heads,
            attn,
            h2,
            gate,
            probs_router,
        ) = front_call(
            cols,
            0,
            experts,
            token_rows,
            query_matrix,
            key_matrix,
            value_matrix,
            misc,
            attention_output_matrix.T,
            grad_own,
            padded_thirds(shared_own),
            table_row,
            table_col,
            doc.reshape(toks, 1).astype(f32),
            jnp.concatenate([cosine, cosine], axis=1),
            jnp.concatenate([-sine, sine], axis=1),
            seqs,
        )
    else:
        first_weights = jnp.concatenate([query_matrix, key_matrix, value_matrix, misc], axis=1)
        first_weights = gather_col(first_weights).reshape(width, -1)
        out_weights = gather_col(attention_output_matrix.T).reshape(width, q_width)
        shared_weights = swap_col(shared_own).reshape(width, 3 * shared_part)
        grad_all = gather_all(grad_own)
        gain_one = first_weights[:, qkv_width + experts].astype(f32)
        h1 = (base_first * gain_one).astype(bf16)
        qkv = dot("tb,bk->tk", h1, first_weights[:, :qkv_width])
        qk = rotate(qkv[:, : q_width + kv_width], cosine, sine).astype(bf16)
        q_low = qk[:, :q_width]
        value_low = qkv[:, q_width + kv_width :].astype(bf16)
        side = jnp.concatenate(
            [
                rank.astype(bf16),
                doc.reshape(toks, 1).astype(bf16),
                jnp.zeros((toks, LANES - experts - 1), bf16),
            ],
            axis=1,
        )
        kv_all = gather_col(jnp.concatenate([qk[:, q_width:], value_low, side], axis=1))
        rank_all = kv_all[:, :, 2 * kv_width : 2 * kv_width + experts]
    qkv_weights = first_weights[:, :qkv_width]
    router = first_weights[:, qkv_width : qkv_width + experts]
    gain_one = first_weights[:, qkv_width + experts].astype(f32)
    gain_two = first_weights[:, qkv_width + experts + 1].astype(f32)
    kv_seq = jnp.swapaxes(kv_all.reshape(cols, seqs, local_len, -1), 0, 1)
    kv_seq = kv_seq.reshape(seqs, full_len, -1)
    key_all = kv_seq[:, :, :kv_width].reshape(seqs, full_len, kv_local, size)
    value_all = kv_seq[:, :, kv_width : 2 * kv_width].reshape(seqs, full_len, kv_local, size)
    query_grid = to_grid(q_low)
    if not kernels:
        doc_all = kv_seq[:, :, 2 * kv_width + experts]
        place = col_index * local_len + jnp.arange(local_len, dtype=jnp.int32)
        same = doc.astype(bf16)[:, :, None] == doc_all[:, None, :]
        causal = jnp.arange(full_len, dtype=jnp.int32)[None, :] <= place[:, None]
        allowed = jnp.tile(same & causal[None], (1, group, 1))[:, None]
        scores = dot("shrd,skhd->shrk", query_grid, key_all) * scale
        scores = jnp.where(allowed, scores, masked_score)
        weights = jnp.exp(scores - jnp.max(scores, axis=-1, keepdims=True))
        weights = jnp.where(allowed, weights, 0.0)
        probs = (weights / jnp.sum(weights, axis=-1, keepdims=True)).astype(bf16)
        heads = from_grid(dot("shrk,skhd->shrd", probs, value_all)).astype(bf16)
        attn = lax.psum(dot("tk,bk->tb", heads, out_weights).astype(bf16), "row")
    middle = x + attn.astype(f32)

    inv_second = rms_scale(middle)
    base_second = middle * inv_second
    row_index = lax.axis_index("row")
    if not kernels:
        h2 = (base_second * gain_two).astype(bf16)
        probs_router = jax.nn.softmax(dot("td,de->te", h2, router), axis=-1)
        picked = jnp.where(mask, probs_router, 0.0)
        pick_total = jnp.sum(picked, axis=-1, keepdims=True)
        gate = picked / pick_total
    if kernels:
        rank_own = lax.dynamic_slice_in_dim(rank_all, col_index * exp_local, exp_local, 2)
        rank_own = rank_own.astype(f32)
        part_out, back_full, *expert_grads, g_shared, gate_dots, _, _, _ = experts_call(
            cols,
            3,
            capacity,
            h2,
            grad_all,
            expert_gate,
            expert_up,
            expert_down,
            shared_weights,
            lax.dynamic_slice_in_dim(rows_all, col_index * exp_local, exp_local, 1),
            rank_own,
            gate[:, :experts].T,
        )
        expert_grads = [grad.astype(f32) for grad in expert_grads]
    else:
        part_out, back_full, gate_dots, shared_share, *expert_grads = experts_plain(
            h2,
            grad_all,
            expert_gate,
            expert_up,
            expert_down,
            shared_weights,
            router,
            rank_all,
            capacity,
            row_width,
        )
    if not kernels:
        back_full = back_full.astype(f32)
    if kernels:
        out_slice, token_grad, share_qkv, share_misc, share_out, shared_share = rear_call(
            cols,
            5,
            experts,
            part_out,
            g_shared,
            back_full,
            gate_dots,
            gate,
            probs_router,
            table_col,
            h1,
            h2,
            token_rows,
            attn,
            first_weights,
            out_weights,
            grad_all,
            heads,
            q_low,
            kv_all,
            probs,
            jnp.concatenate([cosine, cosine], axis=1),
            jnp.concatenate([-sine, sine], axis=1),
        )
    else:
        pick_grad = gate_dots - jnp.sum(gate * gate_dots, axis=-1, keepdims=True)
        prob_grad = jnp.where(mask, pick_grad / pick_total, 0.0)
        logit_grad = probs_router * (
            prob_grad - jnp.sum(probs_router * prob_grad, axis=-1, keepdims=True)
        )
        logit_low = logit_grad.astype(bf16)
        grad_router = dot("td,te->de", h2, logit_low)

        back_full = back_full + dot("te,de->td", logit_low, router)
        grad_own = lax.dynamic_slice_in_dim(grad_all, col_index, 1, 0)[0].astype(f32)
        grad_gain_two = jnp.sum(back_full * base_second, axis=0)
        scaled_two = back_full * gain_two
        middle_grad = (
            inv_second
            * (scaled_two - base_second * jnp.mean(scaled_two * base_second, axis=-1, keepdims=True))
            + grad_own
        )
        attn_grad = middle_grad.astype(bf16)
        grad_out = dot("td,tk->dk", attn_grad, heads).astype(bf16)

        heads_grad = to_grid(dot("td,dk->tk", attn_grad, out_weights).astype(bf16))
        value_grad = dot("shrk,shrd->skhd", probs, heads_grad)
        weight_grad = dot("shrd,skhd->shrk", heads_grad, value_all)
        probs_wide = probs.astype(f32)
        delta = jnp.sum(probs_wide * weight_grad, axis=-1, keepdims=True)
        score_grad = (probs_wide * (weight_grad - delta)).astype(bf16)
        query_grad = from_grid(dot("shrk,skhd->shrd", score_grad, key_all)) * scale
        key_grad = dot("shrk,shrd->skhd", score_grad, query_grid) * scale
        kv_grad = jnp.concatenate(
            [key_grad.reshape(seqs, full_len, kv_width), value_grad.reshape(seqs, full_len, kv_width)],
            axis=2,
        ).astype(bf16)
        kv_grad = jnp.swapaxes(kv_grad.reshape(seqs, cols, local_len, 2 * kv_width), 0, 1)
        kv_share = scatter_col(kv_grad.reshape(cols, toks, 2 * kv_width)).astype(f32)
        qk_grad = rotate(
            jnp.concatenate([query_grad, kv_share[:, :kv_width]], axis=1), cosine, -sine
        )
        qkv_grad = jnp.concatenate([qk_grad, kv_share[:, kv_width:]], axis=1).astype(bf16)
        first_grad = dot("tk,bk->tb", qkv_grad, qkv_weights).astype(bf16)
        first_grad = lax.psum(first_grad, "row").astype(f32)
        grad_gain_one = jnp.sum(first_grad * base_first, axis=0)
        scaled_one = first_grad * gain_one
        token_grad = (
            inv_first
            * (scaled_one - base_first * jnp.mean(scaled_one * base_first, axis=-1, keepdims=True))
            + middle_grad
        )
        grad_first = jnp.concatenate(
            [
                dot("tb,tk->bk", h1, qkv_grad),
                grad_router,
                grad_gain_one[:, None],
                grad_gain_two[:, None],
                jnp.zeros((width, LANES - experts - 2), f32),
            ],
            axis=1,
        ).astype(bf16)
        out_slice = scatter_all(part_out).astype(f32)
        share_out = scatter_col(grad_out.reshape(cols, rows_w, q_width)).astype(f32)
        share_first = scatter_col(grad_first.reshape(cols, rows_w, -1)).astype(f32)
        share_qkv, share_misc = share_first[:, :qkv_width], share_first[:, qkv_width:]
    if kernels:
        shared_share = shared_share.reshape(cols, rows_w, 3, -1)[..., :shared_part]
        shared_share = shared_share.reshape(cols, rows_w, -1)
    else:
        shared_share = swap_col(shared_share.reshape(cols, rows_w, 3 * shared_part))
    shared_share = jnp.swapaxes(shared_share, 0, 1).astype(f32)
    share_sgate, share_sup, share_sdown = (
        shared_share[:, :, i * shared_part : (i + 1) * shared_part].reshape(rows_w, -1)
        for i in range(3)
    )

    middle_slice = lax.dynamic_slice_in_dim(middle, row_index * row_width, row_width, 1)
    block_out = (middle_slice + out_slice).astype(bf16)

    def tokens_first(a):
        return jnp.swapaxes(a.reshape(seqs, local_len, a.shape[1]), 0, 1)

    return (
        tokens_first(block_out),
        tokens_first(token_grad),
        share_misc[:, experts],
        share_qkv[:, :q_width],
        share_qkv[:, q_width : q_width + kv_width],
        share_qkv[:, q_width + kv_width :],
        share_out.T,
        share_misc[:, experts + 1],
        share_misc[:, :experts],
        share_sgate,
        share_sup,
        share_sdown.T,
        *expert_grads,
    )


def solution(mesh):
    in_specs = (
        P("col", None, None),
        P("col", None),
        P("col", None, None),
        P("col"),
        P("col", "row"),
        P("col", "row"),
        P("col", "row"),
        P("row", "col"),
        P("col"),
        P("col", None),
        P("col", "row"),
        P("col", "row"),
        P("row", "col"),
        P("col", None, "row"),
        P("col", None, "row"),
        P("col", "row", None),
        P("col", None, "row"),
    )
    out_specs = (
        P("col", None, "row"),
        P("col", None, None),
        P("col"),
        P("col", "row"),
        P("col", "row"),
        P("col", "row"),
        P("row", "col"),
        P("col"),
        P("col", None),
        P("col", "row"),
        P("col", "row"),
        P("row", "col"),
        P("col", None, "row"),
        P("col", None, "row"),
        P("col", "row", None),
    )
    return jax.shard_map(
        on_device, mesh=mesh, in_specs=in_specs, out_specs=out_specs, check_vma=False
    )
```

```python
import functools
import math

import jax
import jax.numpy as jnp
from jax import lax
from jax.experimental import pallas as pl
from jax.experimental.pallas import tpu as pltpu
from jax.sharding import PartitionSpec as P

HEAD_DIM = 128
LANES = 128


norm_eps = 1e-05
rope_base = 500000.0
masked_score = -1e30

f32 = jnp.float32
bf16 = jnp.bfloat16
MESH = pl.DeviceIdType.MESH


def dot(form, left, right):
    return jnp.einsum(form, left, right, preferred_element_type=f32)


def rope_tables(start_place, local_len, head_size):
    places = (start_place + jnp.arange(local_len, dtype=jnp.int32)).astype(f32)
    frequency = jnp.power(
        rope_base, -jnp.arange(0, head_size, 2, dtype=jnp.int32).astype(f32) / head_size
    )
    angles = places[:, None] * frequency[None, :]
    return (jnp.cos(angles), jnp.sin(angles))


def rotate(field, cosine, sine):
    half = cosine.shape[1]
    parts = []
    for start in range(0, field.shape[1], 2 * half):
        front = field[:, start : start + half]
        back = field[:, start + half : start + 2 * half]
        parts.append(front * cosine - back * sine)
        parts.append(back * cosine + front * sine)
    return jnp.concatenate(parts, axis=1)


def rms_scale(values_in):
    return lax.rsqrt(jnp.mean(values_in * values_in, axis=-1, keepdims=True) + norm_eps)


def silu_parts(pre_gate):
    sigmoid_gate = jax.nn.sigmoid(pre_gate)
    silu_gate = pre_gate * sigmoid_gate
    slope_gate = sigmoid_gate * (1.0 + pre_gate * (1.0 - sigmoid_gate))
    return (silu_gate, slope_gate)


def gather_col(part):
    return lax.all_gather(part, "col", axis=0, tiled=False)


def scatter_col(blocks):
    flat = blocks.reshape(-1, blocks.shape[-1])
    return lax.psum_scatter(flat, "col", scatter_dimension=0, tiled=True)


def gather_all(part):
    got = lax.all_gather(part, ("col", "row"), axis=0, tiled=False)
    cols, rows = lax.axis_size("col"), lax.axis_size("row")
    got = got.reshape(cols, rows, *part.shape).transpose(0, 2, 1, 3)
    return got.reshape(cols, part.shape[0], rows * part.shape[1])


def scatter_all(blocks):
    flat = blocks.reshape(-1, blocks.shape[-1])
    part = lax.psum_scatter(flat, "row", scatter_dimension=1, tiled=True)
    return lax.psum_scatter(part, "col", scatter_dimension=0, tiled=True)


def swap_col(blocks):
    return lax.all_to_all(blocks, "col", split_axis=0, concat_axis=0, tiled=True)


class Net:
    def __init__(self, cols, send_sems, recv_sems):
        self.send_sems, self.recv_sems, self.used, self.sent = send_sems, recv_sems, 0, []
        self.cols, self.high_count = cols, cols // 2
        self.me = lax.axis_index("col")
        self.high, self.low = self.me // 2, self.me % 2
        self.row = lax.axis_index("row")
        self.outer, self.core = self.row // 2, self.row % 2

    def block(self, step, other=False):
        high = lax.rem(self.high + self.high_count - step, self.high_count)
        return 2 * high + (1 - self.low if other else self.low)

    def block_ahead(self, step, other=False):
        high = lax.rem(self.high + step, self.high_count)
        return 2 * high + (1 - self.low if other else self.low)

    def z_peer(self, step):
        return {"col": self.block_ahead(step)}

    def y_peer(self):
        return {"col": 2 * self.high + 1 - self.low}

    def x_peer(self):
        return {"row": 2 * (1 - self.outer) + self.core}

    def core_peer(self):
        return {"row": 2 * self.outer + 1 - self.core}

    def col_peer(self, step):
        return {"col": lax.rem(self.me + step, self.cols)}

    def greet(self, peers):
        barrier = pltpu.get_barrier_semaphore()
        for peer in peers:
            pl.semaphore_signal(barrier, inc=1, device_id=peer, device_id_type=MESH)
        pl.semaphore_wait(barrier, len(peers))

    def send(self, source, target, peer):
        copy = pltpu.make_async_remote_copy(
            src_ref=source,
            dst_ref=target,
            send_sem=self.send_sems.at[self.used],
            recv_sem=self.recv_sems.at[self.used],
            device_id=peer,
            device_id_type=MESH,
        )
        self.used += 1
        copy.start()
        self.sent.append(copy)
        return copy

    def left(self, copy):
        copy.wait_send()
        self.sent = [other for other in self.sent if other is not copy]

    def finish(self):
        for copy in self.sent:
            copy.wait_send()


def col_peers(net):
    return [net.z_peer(step) for step in range(1, net.high_count)] + [net.y_peer()]


def row_peers(net):
    return [net.x_peer(), net.core_peer()]


def add_rows(target, terms):
    rows = target.shape[0]
    piece = 32 if rows % 32 == 0 else 16

    def body(index, carry):
        at = pl.ds(pl.multiple_of(index * piece, piece), piece)
        total = terms[0][at, :].astype(f32)
        for term in terms[1:]:
            total = total + term[at, :].astype(f32)
        target[at, :] = total.astype(target.dtype)
        return carry

    lax.fori_loop(0, rows // piece, body, 0)


def dot_nn(left, right):
    return lax.dot_general(left, right, (((1,), (0,)), ((), ())), preferred_element_type=f32)


def dot_nt(left, right):
    return lax.dot_general(left, right, (((1,), (1,)), ((), ())), preferred_element_type=f32)


def dot_tn(left, right):
    return lax.dot_general(left, right, (((0,), (0,)), ((), ())), preferred_element_type=f32)


def each_tile(count, body):
    def step(index, carry):
        body(index)
        return carry

    lax.fori_loop(0, count, step, 0)


TILE = 512
WIDE = 1280


def tile_at(index, tile=TILE):
    if isinstance(index, int):
        return pl.ds(index * tile, tile)
    return pl.ds(pl.multiple_of(index * tile, tile), tile)


class Line:
    def __init__(self, net, items):
        self.net, self.items = net, items
        self.other_row = 2 * (1 - net.outer) + net.core
        self.along_z, self.along_y, self.along_x, self.to_core = {}, {}, {}, {}
        self.moved = []
        self.now = 0

    def in_chip(self, q, step, other, source, slot):
        if self.items[q][2]:
            self.along_x[q, step, other] = self.net.send(source, slot, self.net.x_peer())
            self.to_core[q, step, other] = self.net.send(source, slot, self.net.core_peer())

    def start(self, q):
        net = self.net
        source, slot_of, _ = self.items[q]
        slot = slot_of(net.me, net.row)
        for step in reversed(range(1, net.high_count)):
            self.along_z[q, step] = net.send(source, slot, net.z_peer(step))
        self.along_y[q, 0] = net.send(source, slot, net.y_peer())
        self.in_chip(q, 0, False, source, slot)

    def after_z(self, q):
        net = self.net
        for step in reversed(range(1, net.high_count)):
            self.along_z[q, step].wait_recv()
            slot = self.items[q][1](net.block(step), net.row)
            self.along_y[q, step] = net.send(slot, slot, net.y_peer())
            self.in_chip(q, step, False, slot, slot)

    def after_y(self, q):
        net = self.net
        for step in range(net.high_count):
            self.along_y[q, step].wait_recv()
            slot = self.items[q][1](net.block(step, True), net.row)
            self.in_chip(q, step, True, slot, slot)

    def after_x(self, q):
        net = self.net
        if self.items[q][2]:
            for other in (False, True):
                for step in range(net.high_count):
                    self.along_x[q, step, other].wait_recv()
                    slot = self.items[q][1](net.block(step, other), self.other_row)
                    self.moved.append(net.send(slot, slot, net.core_peer()))

    def tick(self, count=1):
        net = self.net
        for _ in range(count):
            now, self.now = self.now, self.now + 1
            if now < len(self.items):
                if now >= 2:
                    for step in range(1, net.high_count):
                        net.left(self.along_z[now - 2, step])
                self.start(now)
            for stage, lag in ((self.after_z, 1), (self.after_y, 2), (self.after_x, 3)):
                if 0 <= now - lag < len(self.items):
                    stage(now - lag)

    def drain(self):
        while self.now < len(self.items) + 3:
            self.tick()
        for copy in [*self.moved, *self.to_core.values()]:
            copy.wait_recv()


def front_kernel(
    cols,
    experts,
    tokens,
    query,
    key,
    value,
    misc,
    out_own,
    grad_own,
    shared_own,
    table_row,
    table_col,
    doc_col,
    cosine,
    sine,
    weights,
    out_weights,
    grad_all,
    shared_all,
    rows_all,
    cols_all,
    h1,
    q_low,
    kv_all,
    probs,
    heads,
    attn,
    h2,
    gate,
    router_probs,
    gains,
    inverse,
    kv_low,
    keys,
    values,
    bias,
    partial,
    from_core,
    to_x,
    from_x,
    send_sems,
    recv_sems,
    local_sems,
):
    net = Net(cols, send_sems, recv_sems)
    toks, width = tokens.shape
    size = HEAD_DIM
    q_width = q_low.shape[1]
    group = q_width // size
    rows_w = query.shape[0]
    seqs = probs.shape[0]
    local_len = toks // seqs
    full_len = local_len * cols
    scale = 1.0 / math.sqrt(size)
    mine = pl.ds(pl.multiple_of(net.me * rows_w, 16), rows_w)

    copies = []

    def local_copy(source, target):
        copy = pltpu.make_async_copy(source, target, local_sems.at[len(copies)])
        copy.start()
        copies.append(copy)

    local_copy(query, weights.at[mine, pl.ds(0, q_width)])
    local_copy(key, weights.at[mine, pl.ds(q_width, size)])
    local_copy(value, weights.at[mine, pl.ds(q_width + size, size)])
    local_copy(misc, weights.at[mine, pl.ds(q_width + 2 * size, LANES)])
    first = len(copies)
    local_copy(out_own, out_weights.at[mine])
    part = grad_own.shape[1]
    local_copy(
        grad_own, grad_all.at[net.me, :, pl.ds(pl.multiple_of(net.row * part, LANES), part)]
    )
    local_copy(table_row, rows_all.at[net.me])
    local_copy(table_col, cols_all.at[net.me])
    local_copy(shared_own.at[net.me], shared_all.at[net.me])
    net.greet([net.col_peer(step) for step in range(1, cols)] + row_peers(net))
    for copy in copies[:first]:
        copy.wait()

    def weight_slot(target, start, count):
        def slot(block, row):
            return target.at[pl.ds(pl.multiple_of(block * rows_w + start, 16), count)]

        return slot

    def grad_slot(start, count):
        def slot(block, row):
            return grad_all.at[
                block, pl.ds(start, count), pl.ds(pl.multiple_of(row * part, LANES), part)
            ]

        return slot

    items = [(table_row, lambda block, row: rows_all.at[block], False)]
    pieces, out_pieces, grad_pieces = 5, 4, 4
    count = rows_w // pieces
    for q in range(pieces):
        slot = weight_slot(weights, q * count, count)
        items.append((slot(net.me, net.row), slot, False))
    ready_weights = len(items) + 2
    out_items, grad_items = [], []
    count = rows_w // out_pieces
    for q in range(out_pieces):
        slot = weight_slot(out_weights, q * count, count)
        out_items.append((out_own.at[pl.ds(q * count, count)], slot, False))
    count = toks // grad_pieces
    for q in range(grad_pieces):
        grad_items.append((grad_own.at[pl.ds(q * count, count)], grad_slot(q * count, count), True))
    items += out_items[:2]
    for q in range(2, out_pieces):
        items += [grad_items[q - 2], out_items[q]]
    ready_out = len(items) + 2
    items += grad_items[out_pieces - 2 :]
    items.append((table_col, lambda block, row: cols_all.at[block], False))
    line = Line(net, items)
    swaps = []

    def swap_next(count):
        for _ in range(count):
            step = len(swaps) + 1
            if step < cols:
                block = lax.rem(net.me + step, cols)
                swaps.append(
                    net.send(shared_own.at[block], shared_all.at[net.me], net.col_peer(step))
                )

    line.tick(2)
    copies[first + 2].wait()

    def chunks(body, rows=32):
        def step(index, carry):
            body(pl.ds(pl.multiple_of(index * rows, rows), rows))
            return carry

        lax.fori_loop(0, toks // rows, step, 0)

    def measure_first(at):
        x = tokens[at, :].astype(f32)
        total = jnp.sum(x * x, axis=1, keepdims=True)
        inverse[at, :] = jnp.broadcast_to(lax.rsqrt(total / width + norm_eps), (32, LANES))

    chunks(measure_first)
    line.tick(ready_weights - line.now)

    start = q_width + 2 * size
    for tile in range(width // TILE):
        at = pl.ds(tile * TILE, TILE)
        turned = jnp.transpose(weights[at, start : start + LANES].astype(f32))
        gains[:, at] = turned[experts : experts + 8]

    def norm_first(at):
        x = tokens[at, :].astype(f32) * inverse[at, 0:1]
        h1[at, :] = (x * gains[0:1, :]).astype(bf16)

    chunks(norm_first)
    line.tick()

    def rotated(raw):
        return raw * cosine[...] + pltpu.roll(raw, size // 2, 1) * sine[...]

    raw = dot_nn(h1[...], weights[:, q_width : q_width + 2 * size])
    kv_low[:, :size] = rotated(raw[:, :size]).astype(bf16)
    kv_low[:, size:] = raw[:, size:].astype(bf16)
    kv_all[net.me] = kv_low[...]

    def kv_slot(s):
        rows = pl.ds(s * local_len, local_len)
        return lambda block, row: kv_all.at[block, rows]

    kv_line = Line(
        net,
        [(kv_low.at[pl.ds(s * local_len, local_len)], kv_slot(s), False) for s in range(seqs)],
    )
    kv_line.tick()
    raw = dot_nn(h1[...], weights[:, :q_width])
    for head in range(group):
        at = slice(head * size, (head + 1) * size)
        q_low[:, at] = rotated(raw[:, at]).astype(bf16)
    kv_line.tick()
    line.tick()
    kv_line.tick()

    for s in range(seqs):
        if s:
            kv_line.tick()
        rows = pl.ds(s * local_len, local_len)
        place = lax.broadcasted_iota(jnp.int32, (local_len, local_len), 0)
        lane = lax.broadcasted_iota(jnp.int32, (local_len, local_len), 1)
        for c in range(cols):
            at = pl.ds(c * local_len, local_len)
            keys[at, :] = kv_all[c, rows, :size]
            values[at, :] = kv_all[c, rows, size:]
            same = doc_col[rows, :] == rows_all[c, experts : experts + 1, rows]
            ahead = (c - net.me) * local_len
            allowed = same & (lane + ahead <= place)
            bias[:, at] = jnp.where(allowed, 0.0, masked_score)

        def attend(g, carry, s=s, rows=rows):
            at = pl.ds(pl.multiple_of(g * size, size), size)
            scores = dot_nt(q_low[rows, at], keys[...]) * scale + bias[...]
            weight = jnp.exp(scores - jnp.max(scores, axis=1, keepdims=True))
            p = (weight / jnp.sum(weight, axis=1, keepdims=True)).astype(bf16)
            probs[s, g] = p
            heads[rows, at] = dot_nn(p, values[...]).astype(bf16)
            return carry

        lax.fori_loop(0, group, attend, 0)
        if line.now < ready_out:
            line.tick()
    line.tick(max(0, ready_out - line.now))
    swap_next(3)
    copies[first].wait()

    pieces = from_core.shape[0]
    piece_rows = from_core.shape[1]

    def row_piece(core, i):
        return pl.ds(
            pl.multiple_of((core * pieces + i) * piece_rows, piece_rows), piece_rows
        )

    half = pieces * piece_rows
    across = []
    for core in (1 - net.core, net.core):
        at_rows = pl.ds(pl.multiple_of(core * half, half), half)
        for tile in range(width // TILE):
            at = pl.ds(tile * TILE, TILE)
            partial[at_rows, at] = dot_nt(heads[at_rows, :], out_weights[at, :]).astype(bf16)
        if not across:
            across = [
                net.send(partial.at[row_piece(1 - net.core, i)], from_core.at[i], net.core_peer())
                for i in range(pieces)
            ]
    along, back = [], []
    for i in range(pieces):
        across[i].wait_recv()
        add_rows(to_x.at[i], [partial.at[row_piece(net.core, i)], from_core.at[i]])
        along.append(net.send(to_x.at[i], from_x.at[i], net.x_peer()))
    line.tick()
    swap_next(cols)
    for i in range(pieces):
        along[i].wait_recv()
        at = row_piece(net.core, i)
        add_rows(attn.at[at], [to_x.at[i], from_x.at[i]])
        back.append(net.send(attn.at[at], attn.at[at], net.core_peer()))
    line.tick()
    for copy in back:
        copy.wait_recv()

    def norm_second(at):
        x = tokens[at, :].astype(f32) + attn[at, :].astype(f32)
        total = jnp.sum(x * x, axis=1, keepdims=True)
        h2[at, :] = (x * lax.rsqrt(total / width + norm_eps) * gains[1:2, :]).astype(bf16)

    chunks(norm_second)
    line.tick()
    logits = dot_nn(h2[...], weights[:, start : start + LANES])
    lane = lax.broadcasted_iota(jnp.int32, (toks, LANES), 1)
    logits = jnp.where(lane < experts, logits, masked_score)
    weight = jnp.exp(logits - jnp.max(logits, axis=1, keepdims=True))
    chance = weight / jnp.sum(weight, axis=1, keepdims=True)
    router_probs[...] = chance
    picked = jnp.where((table_col[...] > 0) & (lane < experts), chance, 0.0)
    gate[...] = picked / jnp.sum(picked, axis=1, keepdims=True)
    line.drain()
    kv_line.drain()
    for copy in swaps:
        copy.wait_recv()
    for copy in (copies[first + 1], *copies[first + 3 :]):
        copy.wait()
    net.finish()


def front_call(
    cols, collective_id, experts, tokens, query, key, value, misc, out_own, grad_own, shared_own,
    table_row, table_col, doc_col, cosine, sine, seqs,
):
    toks, width = tokens.shape
    q_width = query.shape[1]
    size = HEAD_DIM
    local_len = toks // seqs
    vmem, any_space = pl.BlockSpec(memory_space=pltpu.VMEM), pl.BlockSpec(memory_space=pl.ANY)

    def shape(*dims, dtype=bf16):
        return jax.ShapeDtypeStruct(dims, dtype)

    pieces = 4
    piece = (pieces, toks // 2 // pieces, width)
    copies = 320
    return pl.pallas_call(
        functools.partial(front_kernel, cols, experts),
        out_shape=[
            shape(width, q_width + 2 * size + LANES),
            shape(width, q_width),
            shape(cols, toks, width),
            shape(*shared_own.shape),
            shape(cols, *table_row.shape, dtype=f32),
            shape(cols, *table_col.shape),
            shape(toks, width),
            shape(toks, q_width),
            shape(cols, toks, 2 * size),
            shape(seqs, q_width // size, local_len, cols * local_len),
            shape(toks, q_width),
            shape(toks, width),
            shape(toks, width),
            shape(toks, LANES, dtype=f32),
            shape(toks, LANES, dtype=f32),
        ],
        in_specs=[vmem] + [any_space] * 7 + [vmem] * 5,
        out_specs=[vmem, vmem, any_space, any_space] + [vmem] * 11,
        scratch_shapes=[
            pltpu.VMEM((8, width), f32),
            pltpu.VMEM((toks, LANES), f32),
            pltpu.VMEM((toks, 2 * size), bf16),
            pltpu.VMEM((cols * local_len, size), bf16),
            pltpu.VMEM((cols * local_len, size), bf16),
            pltpu.VMEM((local_len, cols * local_len), f32),
            pltpu.VMEM((toks, width), bf16),
            pltpu.VMEM(piece, bf16),
            pltpu.VMEM(piece, bf16),
            pltpu.VMEM(piece, bf16),
            pltpu.SemaphoreType.DMA((copies,)),
            pltpu.SemaphoreType.DMA((copies,)),
            pltpu.SemaphoreType.DMA((16,)),
        ],
        compiler_params=pltpu.CompilerParams(
            collective_id=collective_id, has_side_effects=True, vmem_limit_bytes=48 << 20
        ),
        name=f"front_{collective_id}",
    )(
        tokens, query, key, value, misc, out_own, grad_own, shared_own,
        table_row, table_col, doc_col, cosine, sine,
    )


def experts_kernel(
    cols,
    capacity,
    h2,
    grads,
    w_gate,
    w_up,
    w_down,
    w_shared,
    rank_row,
    rank_col,
    gate_own,
    out_part,
    back,
    g_gate,
    g_up,
    g_down,
    g_shared,
    shared_back,
    gate_dots,
    h2_all,
    xs_all,
    cs_all,
    wgu,
    wd,
    ws,
    gates,
    hb,
    xbuf,
    ybuf,
    obuf,
    part,
    pre,
    gcol,
    dcol,
    dz_all,
    zg_all,
    dgu_all,
    sdz_all,
    sz_all,
    sgu_all,
    from_core,
    from_x,
    from_y,
    from_z,
    kept,
    dots,
    dots_core,
    dots_x,
    tiles,
    tiles_all,
    stage,
    stage_low,
    send_sems,
    recv_sems,
    local_sems,
):
    net = Net(cols, send_sems, recv_sems)
    toks, width = h2.shape
    exp_local, _, hidden = w_gate.shape
    high = net.high_count
    pad = ws.shape[1] // 3
    rows_w = w_shared.shape[1]
    slots = exp_local * capacity
    pair = 2 * capacity
    piece = width // lax.axis_size("row")
    share = width // LANES // 5 * LANES
    rest = (width - 4 * share) // 2
    wide = width // TILE
    net.greet([net.col_peer(step) for step in range(1, cols)] + row_peers(net))

    def local_copy(source, target, index):
        copy = pltpu.make_async_copy(source, target, local_sems.at[index])
        copy.start()
        return copy

    gate_copies = [
        net.send(gate_own, gates.at[net.me], net.col_peer(step)) for step in range(1, cols)
    ]
    gates[net.me] = gate_own[...]

    def feature_e(row):
        return pl.ds(pl.multiple_of(row * share, LANES), share)

    def feature_r(core):
        return pl.ds(pl.multiple_of(4 * share + core * rest, LANES), rest)

    own_e, own_r = feature_e(net.row), feature_r(net.core)
    far_e = feature_e(2 * (1 - net.outer) + net.core)

    def pass_on(source, block, features, peer):
        return net.send(source.at[..., features], h2_all.at[block, :, features], peer)

    along_z, along_y, along_x, to_core = {}, {}, {}, {}

    def start_z(step):
        along_z[step] = [
            pass_on(h2, net.me, own_e, net.z_peer(high - step)),
            pass_on(h2, net.me, own_r, net.z_peer(high - step)),
        ]

    start_z(1)
    along_y[0] = [
        pass_on(h2, net.me, own_e, net.y_peer()),
        pass_on(h2, net.me, own_r, net.y_peer()),
    ]

    def block_of(step, other):
        return net.block_ahead(step, other)

    def share_in_chip(step, other):
        block = block_of(step, other)
        source = h2_all.at[block]
        along_x[step, other] = pass_on(source, block, own_e, net.x_peer())
        to_core[step, other] = [
            pass_on(source, block, own_e, net.core_peer()),
            pass_on(source, block, own_r, net.core_peer()),
        ]

    def arrived_y(step):
        for copy in along_y[step]:
            copy.wait_recv()
        share_in_chip(step, True)

    def arrived_z(step):
        for copy in along_z[step]:
            copy.wait_recv()
        block = block_of(step, False)
        along_y[step] = [
            pass_on(h2_all.at[block], block, own_e, net.y_peer()),
            pass_on(h2_all.at[block], block, own_r, net.y_peer()),
        ]
        share_in_chip(step, False)

    def arrived_x(step, other):
        along_x[step, other].wait_recv()
        block = block_of(step, other)
        to_core[step, other].append(pass_on(h2_all.at[block], block, far_e, net.core_peer()))

    def whole(step, other):
        for copy in to_core[step, other]:
            copy.wait_recv()

    events = [functools.partial(arrived_y, 0)]
    for step in range(1, high):
        events.append(functools.partial(arrived_z, step))
        events.append(functools.partial(arrived_x, step - 1, True))
        events.append(functools.partial(arrived_y, step))
        events.append(functools.partial(arrived_x, step, False))
    events.append(functools.partial(arrived_x, high - 1, True))
    events = iter(events)

    def pump(count=1):
        for _ in range(count):
            event = next(events, None)
            if event is not None:
                event()

    loads = []
    for e in range(exp_local):
        loads.append(local_copy(w_down.at[e], wd.at[e], 3 * e))
        loads.append(local_copy(w_gate.at[e], wgu.at[e, :, pl.ds(0, hidden)], 3 * e + 1))
        loads.append(local_copy(w_up.at[e], wgu.at[e, :, pl.ds(hidden, hidden)], 3 * e + 2))
    base = 3 * exp_local
    for c in range(cols):
        loads.append(local_copy(w_shared.at[c], ws.at[pl.ds(c * rows_w, rows_w)], base + c))
    base += cols - 1
    keep_own = local_copy(h2, h2_all.at[net.me], base + 1)
    base += 2

    def load_pair(source, step):
        first = local_copy(source.at[block_of(step, False)], hb.at[0], base)
        second = local_copy(source.at[block_of(step, True)], hb.at[1], base + 1)
        first.wait()
        second.wait()

    slot_row = lax.broadcasted_iota(jnp.int32, (capacity, toks), 0).astype(f32) + 1.0
    slot_lane = lax.broadcasted_iota(jnp.int32, (toks, capacity), 1).astype(f32) + 1.0

    def chosen(block, e):
        return rank_row[block, e : e + 1, :] == slot_row

    def picks(block):
        rows = [
            jnp.where(chosen(block, e), 1.0, 0.0).astype(bf16) for e in range(exp_local)
        ]
        return jnp.concatenate(rows, axis=0)

    def picks_back(block):
        lanes = [
            jnp.where(rank_col[block, :, e : e + 1] == slot_lane, 1.0, 0.0).astype(bf16)
            for e in range(exp_local)
        ]
        return jnp.concatenate(lanes, axis=1)

    def dispatch(step):
        for b in (0, 1):
            table = picks(block_of(step, b == 1))

            def tile(index, b=b, table=table):
                at = tile_at(index, WIDE)
                rows = dot_nn(table, hb[b, :, at]).astype(bf16)
                for e in range(exp_local):
                    xbuf[e, pl.ds(b * capacity, capacity), at] = rows[
                        e * capacity : (e + 1) * capacity
                    ]

            each_tile(width // WIDE, tile)

    def save_rows(target, step):
        return [
            local_copy(
                xbuf.at[e], target.at[e, pl.ds(step * pair, pair)], base + 2 + e
            )
            for e in range(exp_local)
        ]

    saved = []
    for step in range(high):
        load_pair(grads, step)
        if step == 0:
            for copy in loads:
                copy.wait()
        for copy in saved:
            copy.wait()
        dispatch(step)
        saved = save_rows(cs_all, step)
        for e in range(exp_local):
            dz_all[e, pl.ds(step * pair, pair), :] = dot_nt(xbuf[e], wd[e]).astype(bf16)
        for b in (0, 1):
            sdz_all[block_of(step, b == 1)] = dot_nn(hb[b], ws[:, 2 * pad :]).astype(bf16)
        if step + 2 < high:
            for copy in along_z[step + 1]:
                net.left(copy)
            start_z(step + 2)
        pump()
    for copy in gate_copies:
        copy.wait_recv()
    keep_own.wait()

    across, onward, upward, far_z = {}, {}, {}, {}

    def features(row):
        return pl.ds(pl.multiple_of(row * piece, LANES), piece)

    other_row = 2 * (1 - net.outer) + net.core

    def hand_over(step):
        for b in (1, 0):
            for far in (1, 0):
                outer = 1 - net.outer if far else net.outer
                source = part.at[b, :, features(2 * outer + 1 - net.core)]
                across[step, b, far] = net.send(
                    source, from_core.at[far, step, b], net.core_peer()
                )

    def sum_cores(step):
        for b in (1, 0):
            for far, row in ((1, other_row), (0, net.row)):
                across[step, b, far].wait_recv()
                slot = from_core.at[far, step, b]
                add_rows(slot, [part.at[b, :, features(row)], slot])
                if far:
                    onward[step, b] = net.send(slot, from_x.at[step, b], net.x_peer())
        for b in (1, 0):
            for far in (1, 0):
                net.left(across[step, b, far])

    def sum_chips(step):
        for b in (1, 0):
            onward[step, b].wait_recv()
            slot = from_core.at[0, step, b]
            add_rows(slot, [slot, from_x.at[step, b]])
            if b:
                upward[step] = net.send(slot, from_y.at[step], net.y_peer())

    def sum_plane(step):
        upward[step].wait_recv()
        slot = from_core.at[0, step, 0]
        add_rows(slot, [slot, from_y.at[step]])
        if step:
            far_z[step] = net.send(slot, from_z.at[step - 1], net.z_peer(step))

    own_expert = lax.rem(net.me, cols) * exp_local
    gate_rows = gates.shape[1]
    gate_row = lax.broadcasted_iota(jnp.int32, (gate_rows, toks), 0)
    dots[...] = jnp.zeros_like(dots)
    for step in range(high):
        if step:
            whole(step, False)
        whole(step, True)
        load_pair(h2_all, step)
        for copy in saved:
            copy.wait()
        dispatch(step)
        saved = save_rows(xs_all, step)
        pump()
        for b in (0, 1):
            block = block_of(step, b == 1)
            inner = dot_nn(hb[b], ws[:, : 2 * pad])
            sa, su = inner[:, :pad], inner[:, pad:]
            sig = 1.0 / (1.0 + jnp.exp(-sa))
            silu = sa * sig
            slope = sig * (1.0 + sa * (1.0 - sig))
            sz_all[block] = (silu * su).astype(bf16)
            sdz = sdz_all[block].astype(f32)
            sgu_all[block, :, :pad] = (sdz * su * slope).astype(bf16)
            sgu_all[block, :, pad:] = (sdz * silu).astype(bf16)
        if step:
            sum_cores(step - 1)
        rows = pl.ds(step * pair, pair)
        for e in range(exp_local):
            pre[...] = dot_nn(xbuf[e], wgu[e])
            for b in (0, 1):
                block = block_of(step, b == 1)
                gate = jnp.sum(
                    jnp.where(gate_row == own_expert + e, gates[block], 0.0), axis=0, keepdims=True
                )
                gate = jnp.sum(jnp.where(chosen(block, e), gate, 0.0), axis=1, keepdims=True)
                gcol[pl.ds(b * capacity, capacity), :] = jnp.broadcast_to(gate, (capacity, LANES))

            def gating(index, e=e, step=step):
                at = pl.ds(pl.multiple_of(index * 32, 32), 32)
                saved_at = pl.ds(pl.multiple_of(step * pair + index * 32, 32), 32)
                a, u = pre[at, :hidden], pre[at, hidden:]
                gate = jnp.concatenate([gcol[at, :]] * (hidden // LANES), axis=1)
                dz = dz_all[e, saved_at, :].astype(f32)
                sig = 1.0 / (1.0 + jnp.exp(-a))
                silu = a * sig
                slope = sig * (1.0 + a * (1.0 - sig))
                z = silu * u
                dcol[at, :] = jnp.broadcast_to(
                    jnp.sum(z * dz, axis=1, keepdims=True), (32, LANES)
                )
                zg_all[e, saved_at, :] = (z * gate).astype(bf16)
                dz = dz * gate
                dgu_all[e, saved_at, :hidden] = (dz * u * slope).astype(bf16)
                dgu_all[e, saved_at, hidden:] = (dz * silu).astype(bf16)

            each_tile(pair // 32, gating)
            for b in (0, 1):
                block = block_of(step, b == 1)
                col = dcol[pl.ds(b * capacity, capacity), :]
                col = jnp.concatenate([col] * (toks // LANES), axis=1)
                dots[block, e : e + 1, :] = jnp.sum(
                    jnp.where(chosen(block, e), col, 0.0), axis=0, keepdims=True
                )

            def out_tile(index, e=e):
                at = tile_at(index, WIDE)
                y = dot_nn(zg_all[e, rows, :], wd[e, :, at]).astype(bf16)
                for b in (0, 1):
                    ybuf[b, pl.ds(e * capacity, capacity), at] = y[b * capacity : (b + 1) * capacity]

            each_tile(width // WIDE, out_tile)
            pump()
        if step:
            for copy in out_copies:
                copy.wait()
        out_copies = []
        for b in (0, 1):
            block = block_of(step, b == 1)
            table = picks_back(block)

            def join_tile(index, b=b, table=table, block=block):
                at = tile_at(index, WIDE)
                total = dot_nn(table, ybuf[b, :, at])
                total = total + dot_nt(sz_all[block], ws[at, 2 * pad :])
                obuf[b, :, at] = total.astype(bf16)

            each_tile(width // WIDE, join_tile)
            out_copies.append(
                local_copy(obuf.at[b], out_part.at[block], base + 2 + exp_local + b)
            )
        pump()
        if step:
            sum_chips(step - 1)
        for e in range(exp_local):

            def back_tile(index, e=e):
                at = tile_at(index, WIDE)
                y = dot_nt(dgu_all[e, rows, :], wgu[e, at, :]).astype(bf16)
                for b in (0, 1):
                    ybuf[b, pl.ds(e * capacity, capacity), at] = y[b * capacity : (b + 1) * capacity]

            each_tile(width // WIDE, back_tile)
        pump()
        for b in (1, 0):
            block = block_of(step, b == 1)
            table = picks_back(block)

            def back_join(index, b=b, table=table, block=block):
                at = tile_at(index, WIDE)
                total = dot_nn(table, ybuf[b, :, at])
                total = total + dot_nt(sgu_all[block], ws[at, : 2 * pad])
                part[b, :, at] = total.astype(bf16)

            each_tile(width // WIDE, back_join)
        hand_over(step)
        if step:
            sum_plane(step - 1)
    pump(64)
    last = high - 1
    for copy in saved + out_copies:
        copy.wait()

    load_sem, store_sem = base + 4 + exp_local, base + 6 + exp_local

    def passes(count, load, work, stores):
        def load_copy(j, slot):
            source, target = load(j, slot)
            return pltpu.make_async_copy(source, target, local_sems.at[load_sem + slot])

        def store_copies(j, slot):
            return [
                pltpu.make_async_copy(
                    source, target, local_sems.at[store_sem + 2 * slot + i]
                )
                for i, (source, target) in enumerate(stores(j, slot))
            ]

        load_copy(0, 0).start()

        def body(j):
            slot = lax.rem(j, 2)

            @pl.when(j + 1 < count)
            def _():
                load_copy(j + 1, 1 - slot).start()

            load_copy(j, slot).wait()

            @pl.when(j >= 2)
            def _():
                for copy in store_copies(j - 2, slot):
                    copy.wait()

            work(j, slot)
            for copy in store_copies(j, slot):
                copy.start()

        each_tile(count, body)
        for j in range(max(0, count - 2), count):
            for copy in store_copies(j, j % 2):
                copy.wait()

    def inner_grads(e):
        passes(
            wide,
            lambda j, slot: (
                xs_all.at[e, :, tile_at(j)],
                tiles.at[slot],
            ),
            lambda j, slot: put(stage.at[slot], dot_tn(tiles[slot], dgu_all[e]).astype(bf16)),
            lambda j, slot: [
                (stage.at[slot, :, pl.ds(0, hidden)], g_gate.at[e, tile_at(j)]),
                (stage.at[slot, :, pl.ds(hidden, hidden)], g_up.at[e, tile_at(j)]),
            ],
        )

    def put(target, value):
        target[...] = value

    def down_grads(e):
        passes(
            wide,
            lambda j, slot: (
                cs_all.at[e, :, tile_at(j)],
                tiles.at[slot],
            ),
            lambda j, slot: put(
                stage.at[slot, pl.ds(0, hidden), pl.ds(0, TILE)],
                dot_tn(zg_all[e], tiles[slot]).astype(bf16),
            ),
            lambda j, slot: [
                (
                    stage.at[slot, pl.ds(0, hidden), pl.ds(0, TILE)],
                    g_down.at[e, :, tile_at(j)],
                ),
            ],
        )

    def shared_grads(source, others, start, size):
        def work(j, slot):
            total = dot_tn(tiles_all[slot, 0], others[0])
            for c in range(1, cols):
                total = total + dot_tn(tiles_all[slot, c], others[c])
            stage_low[slot, :, :size] = total.astype(bf16)

        def load(j, slot):
            return (source.at[:, :, tile_at(j)], tiles_all.at[slot])

        passes(
            wide,
            lambda j, slot: load(j, slot),
            work,
            lambda j, slot: [
                (
                    stage_low.at[slot, :, pl.ds(0, size)],
                    g_shared.at[tile_at(j), pl.ds(start, size)],
                ),
            ],
        )

    first_dots = net.send(dots, dots_core, net.core_peer())
    shared_grads(h2_all, sgu_all, 0, 2 * pad)
    sum_cores(last)
    first_dots.wait_recv()
    net.left(first_dots)
    dots[...] = dots[...] + dots_core[...]
    second_dots = net.send(dots, dots_x, net.x_peer())
    shared_grads(grads, sz_all, 2 * pad, pad)
    own_rows = pl.ds(pl.multiple_of(net.me * rows_w, 16), rows_w)
    keep_own = local_copy(g_shared.at[own_rows], shared_back.at[net.me], base)
    returns = []
    for step in range(1, cols):
        block = lax.rem(net.me + step, cols)
        rows = pl.ds(pl.multiple_of(block * rows_w, 16), rows_w)
        returns.append(net.send(g_shared.at[rows], shared_back.at[net.me], net.col_peer(step)))
    inner_grads(0)
    sum_chips(last)
    second_dots.wait_recv()
    dots_core[...] = dots[...] + dots_x[...]
    third_dots = []
    for step in range(1, cols):
        block = lax.rem(net.me + step, cols)
        third_dots.append(
            net.send(dots_core.at[block], gate_dots.at[net.me], net.col_peer(step))
        )
    gate_dots[net.me] = dots_core[net.me]
    inner_grads(1)
    sum_plane(last)
    down_grads(0)
    for step in range(1, high):
        far_z[step].wait_recv()
    add_rows(kept, [from_core.at[0, 0, 0], *[from_z.at[step - 1] for step in range(1, high)]])
    own, other = features(net.row), features(other_row)
    back[:, own] = kept[...].astype(bf16)
    far = net.send(back.at[:, own], back.at[:, own], net.x_peer())
    near = net.send(back.at[:, own], back.at[:, own], net.core_peer())
    down_grads(1)
    far.wait_recv()
    crossed = net.send(back.at[:, other], back.at[:, other], net.core_peer())
    keep_own.wait()
    for copy in returns:
        copy.wait_recv()
    near.wait_recv()
    crossed.wait_recv()
    for copy in third_dots:
        copy.wait_recv()
    net.finish()


def experts_call(
    cols, collective_id, capacity, h2, grads, w_gate, w_up, w_down, w_shared, rank_row, rank_col, gate
):
    toks, width = h2.shape
    exp_local, _, hidden = w_gate.shape
    high = cols // 2
    pad = w_shared.shape[2] // 3
    piece = width // lax.axis_size("row")
    pair = 2 * capacity
    any_space = pl.BlockSpec(memory_space=pl.ANY)
    vmem = pl.BlockSpec(memory_space=pltpu.VMEM)
    copies = 160

    def shape(*dims, dtype=bf16):
        return jax.ShapeDtypeStruct(dims, dtype)

    return pl.pallas_call(
        functools.partial(experts_kernel, cols, capacity),
        out_shape=[
            shape(cols, toks, width),
            shape(toks, width),
            shape(exp_local, width, hidden),
            shape(exp_local, width, hidden),
            shape(exp_local, hidden, width),
            shape(width, 3 * pad),
            shape(*w_shared.shape),
            shape(cols, 8, toks, dtype=f32),
            shape(cols, toks, width),
            shape(exp_local, cols * capacity, width),
            shape(exp_local, cols * capacity, width),
        ],
        in_specs=[any_space] * 6 + [vmem] * 3,
        out_specs=[
            any_space,
            vmem,
            any_space,
            any_space,
            any_space,
            any_space,
            any_space,
            vmem,
            any_space,
            any_space,
            any_space,
        ],
        scratch_shapes=[
            pltpu.VMEM((exp_local, width, 2 * hidden), bf16),
            pltpu.VMEM((exp_local, hidden, width), bf16),
            pltpu.VMEM((width, 3 * pad), bf16),
            pltpu.VMEM((cols, *gate.shape), f32),
            pltpu.VMEM((2, toks, width), bf16),
            pltpu.VMEM((exp_local, pair, width), bf16),
            pltpu.VMEM((2, exp_local * capacity, width), bf16),
            pltpu.VMEM((2, toks, width), bf16),
            pltpu.VMEM((2, toks, width), bf16),
            pltpu.VMEM((pair, 2 * hidden), f32),
            pltpu.VMEM((pair, LANES), f32),
            pltpu.VMEM((pair, LANES), f32),
            pltpu.VMEM((exp_local, cols * capacity, hidden), bf16),
            pltpu.VMEM((exp_local, cols * capacity, hidden), bf16),
            pltpu.VMEM((exp_local, cols * capacity, 2 * hidden), bf16),
            pltpu.VMEM((cols, toks, pad), bf16),
            pltpu.VMEM((cols, toks, pad), bf16),
            pltpu.VMEM((cols, toks, 2 * pad), bf16),
            pltpu.VMEM((2, high, 2, toks, piece), bf16),
            pltpu.VMEM((high, 2, toks, piece), bf16),
            pltpu.VMEM((high, toks, piece), bf16),
            pltpu.VMEM((high - 1, toks, piece), bf16),
            pltpu.VMEM((toks, piece), f32),
            pltpu.VMEM((cols, 8, toks), f32),
            pltpu.VMEM((cols, 8, toks), f32),
            pltpu.VMEM((cols, 8, toks), f32),
            pltpu.VMEM((2, cols * capacity, TILE), bf16),
            pltpu.VMEM((2, cols, toks, TILE), bf16),
            pltpu.VMEM((2, TILE, 2 * hidden), bf16),
            pltpu.VMEM((2, TILE, 2 * pad), bf16),
            pltpu.SemaphoreType.DMA((copies,)),
            pltpu.SemaphoreType.DMA((copies,)),
            pltpu.SemaphoreType.DMA((32,)),
        ],
        compiler_params=pltpu.CompilerParams(
            collective_id=collective_id, has_side_effects=True, vmem_limit_bytes=62 << 20
        ),
        name=f"experts_{collective_id}",
    )(h2, grads, w_gate, w_up, w_down, w_shared, rank_row, rank_col, gate)


def padded_thirds(packed):
    third = packed.shape[-1] // 3
    parts = packed.reshape(*packed.shape[:-1], 3, third)
    parts = jnp.pad(parts, ((0, 0),) * (parts.ndim - 1) + ((0, -third % LANES),))
    return parts.reshape(*packed.shape[:-1], -1)


def fits(cols, rows, width):
    return cols % 2 == 0 and cols * rows * width * 2 <= 12 << 20


class Sum2D:
    def __init__(self, net, source, start, count, from_y, from_z, out):
        self.net, self.source, self.start, self.count = net, source, start, count
        self.from_y, self.from_z, self.out = from_y, from_z, out
        self.rows = pl.ds(start, count)
        self.order = [*range(1, net.high_count), 0]
        self.along_y, self.along_z = {}, {}

    def mine(self, block):
        return self.source(block, self.start, self.count)

    def send_y(self):
        for step in self.order:
            source = self.mine(self.net.block_ahead(step, True))
            self.along_y[step] = self.net.send(
                source, self.from_y.at[step, self.rows], self.net.y_peer()
            )

    def send_z(self):
        for step in self.order:
            self.along_y[step].wait_recv()
            slot = self.from_y.at[step, self.rows]
            if step:
                add_rows(slot, [self.mine(self.net.block_ahead(step)), slot])
                self.along_z[step] = self.net.send(
                    slot, self.from_z.at[step - 1, self.rows], self.net.z_peer(step)
                )

    def last(self):
        for step in range(1, self.net.high_count):
            self.along_z[step].wait_recv()
        terms = [
            self.from_z.at[step - 1, self.rows] for step in range(1, self.net.high_count)
        ]
        mine = self.mine(self.net.me)
        add_rows(self.out.at[self.rows], [mine, self.from_y.at[0, self.rows], *terms])


def rear_kernel(
    cols,
    experts,
    out_part,
    back,
    gate_dots,
    gate,
    router_probs,
    table_col,
    h1,
    h2,
    tokens,
    attn,
    weights_in,
    out_weights_in,
    grads,
    heads,
    q_low,
    kv_all,
    probs,
    cosine,
    sine,
    out_slice,
    d_tokens,
    share_qkv,
    share_misc,
    share_out,
    weights,
    out_weights,
    misc,
    misc_low,
    grad_own,
    gains,
    dots,
    logit_low,
    low,
    dob,
    keys,
    values,
    stacked,
    ds_all,
    kv_grad,
    kv_share,
    dqkv,
    gain_sums,
    own,
    from_core,
    from_x,
    from_y,
    from_z,
    kv_y,
    kv_z,
    out_y,
    out_z,
    qkv_y,
    qkv_z,
    misc_y,
    misc_z,
    row_core,
    row_to,
    row_from,
    send_sems,
    recv_sems,
    local_sems,
):
    net = Net(cols, send_sems, recv_sems)
    toks, width = back.shape
    size = HEAD_DIM
    q_width = q_low.shape[1]
    group = q_width // size
    qkv_width = q_width + 2 * size
    seqs = probs.shape[0]
    local_len = toks // seqs
    rows_w = width // cols
    piece = width // lax.axis_size("row")
    scale = 1.0 / math.sqrt(size)
    other_row = 2 * (1 - net.outer) + net.core

    def local_copy(source, target, index):
        copy = pltpu.make_async_copy(source, target, local_sems.at[index])
        copy.start()
        return copy

    def features(row):
        return pl.ds(pl.multiple_of(row * piece, LANES), piece)

    loads = [
        local_copy(weights_in, weights, 0),
        local_copy(out_weights_in, out_weights, 1),
        local_copy(grads.at[net.me], grad_own, 2),
    ]
    near_load = local_copy(out_part.at[:, :, features(net.row)], own.at[0], 3)
    far_load = local_copy(out_part.at[:, :, features(other_row)], own.at[1], 4)
    net.greet(col_peers(net) + row_peers(net))

    pieces = 4
    count = toks // pieces
    order = [*range(1, net.high_count), 0]
    keys_of = [(step, True) for step in order] + [(step, False) for step in order]
    across, onward, along_y, along_z = {}, {}, {}, {}

    def rows_of(q):
        return pl.ds(q * count, count)

    def out_core(q):
        for far in (1, 0):
            outer = 1 - net.outer if far else net.outer
            for key in keys_of:
                block = net.block_ahead(*key)
                across[q, far, key] = net.send(
                    out_part.at[block, rows_of(q), features(2 * outer + 1 - net.core)],
                    from_core.at[far, block, rows_of(q)],
                    net.core_peer(),
                )

    def out_x(q):
        for key in keys_of:
            across[q, 1, key].wait_recv()
            block = net.block_ahead(*key)
            slot = from_core.at[1, block, rows_of(q)]
            add_rows(slot, [own.at[1, block, rows_of(q)], slot])
            onward[q, key] = net.send(slot, from_x.at[block, rows_of(q)], net.x_peer())

    def out_y_stage(q):
        for key in keys_of:
            across[q, 0, key].wait_recv()
            onward[q, key].wait_recv()
            block = net.block_ahead(*key)
            slot = from_core.at[0, block, rows_of(q)]
            add_rows(slot, [own.at[0, block, rows_of(q)], slot, from_x.at[block, rows_of(q)]])
            if key[1]:
                along_y[q, key[0]] = net.send(
                    slot, from_y.at[key[0], rows_of(q)], net.y_peer()
                )

    def out_z_stage(q):
        for step in order:
            along_y[q, step].wait_recv()
            slot = from_core.at[0, net.block_ahead(step), rows_of(q)]
            add_rows(slot, [slot, from_y.at[step, rows_of(q)]])
            if step:
                along_z[q, step] = net.send(
                    slot, from_z.at[step - 1, rows_of(q)], net.z_peer(step)
                )

    def out_last(q):
        for step in range(1, net.high_count):
            along_z[q, step].wait_recv()
        terms = [from_z.at[step - 1, rows_of(q)] for step in range(1, net.high_count)]
        add_rows(out_slice.at[rows_of(q)], [from_core.at[0, net.me, rows_of(q)], *terms])

    state = {"tick": 0}

    def pump(ticks=1):
        for _ in range(ticks):
            tick = state["tick"]
            state["tick"] += 1
            for lag, stage in enumerate((out_core, out_x, out_y_stage, out_z_stage, out_last)):
                if 0 <= tick - lag < pieces:
                    stage(tick - lag)

    pump()
    for copy in loads:
        copy.wait()

    def chunks(body, rows=32):
        def step(index, carry):
            body(pl.ds(pl.multiple_of(index * rows, rows), rows))
            return carry

        lax.fori_loop(0, toks // rows, step, 0)

    for tile in range(width // TILE):
        at = pl.ds(tile * TILE, TILE)
        turned = jnp.transpose(weights[at, qkv_width : qkv_width + LANES].astype(f32))
        gains[:, at] = turned[experts : experts + 8]
    dots[...] = jnp.zeros_like(dots)
    for c in range(cols):
        dots[2 * c : 2 * c + 2, :] = gate_dots[c, 0:2, :]
    gate_grad = jnp.transpose(dots[...])
    lane = lax.broadcasted_iota(jnp.int32, (toks, LANES), 1)
    mask = (table_col[...] > 0) & (lane < experts)
    chance, gates = router_probs[...], gate[...]
    total = jnp.sum(jnp.where(mask, chance, 0.0), axis=1, keepdims=True)
    gate_grad = jnp.where(mask, gate_grad, 0.0)
    pick_grad = gate_grad - jnp.sum(gates * gate_grad, axis=1, keepdims=True)
    chance_grad = jnp.where(mask, pick_grad / total, 0.0)
    logit_grad = chance * (chance_grad - jnp.sum(chance * chance_grad, axis=1, keepdims=True))
    logit_low[...] = logit_grad.astype(bf16)
    near_load.wait()
    far_load.wait()
    pump()

    for tile in range(width // TILE):
        at = pl.ds(tile * TILE, TILE)
        d_tokens[:, at] = back[:, at].astype(f32) + dot_nt(
            logit_low[...], weights[at, qkv_width : qkv_width + LANES]
        )
    gain_sums[...] = jnp.zeros_like(gain_sums)

    def fold(values, start):
        total = values[0:8]
        for r in range(8, values.shape[0], 8):
            total = total + values[r : r + 8]
        gain_sums[start : start + 8, :] = gain_sums[start : start + 8, :] + total

    def norm_second(at):
        x = tokens[at, :].astype(f32) + attn[at, :].astype(f32)
        inverse = lax.rsqrt(jnp.sum(x * x, axis=1, keepdims=True) / width + norm_eps)
        base = x * inverse
        dh = d_tokens[at, :]
        fold(dh * base, 8)
        scaled = dh * gains[1:2, :]
        mean = jnp.sum(scaled * base, axis=1, keepdims=True) / width
        middle = inverse * (scaled - base * mean) + grad_own[at, :].astype(f32)
        d_tokens[at, :] = middle
        low[at, :] = middle.astype(bf16)

    chunks(norm_second, 16)
    dob[...] = dot_nn(low[...], out_weights[...]).astype(bf16)
    pump()
    for tile in range(width // TILE):
        at = pl.ds(tile * TILE, TILE)
        out_weights[at, :] = dot_tn(low[:, at], heads[...]).astype(bf16)

    def blocks_of(array):
        def source(block, start, count):
            return array.at[pl.ds(pl.multiple_of(block * rows_w + start, 16), count)]

        return source

    out_pieces = 4
    out_count = rows_w // out_pieces
    out_line = [
        Sum2D(net, blocks_of(out_weights), q * out_count, out_count, out_y, out_z, share_out)
        for q in range(out_pieces)
    ]
    out_line[0].send_y()
    out_line[1].send_y()

    kv_line = [
        Sum2D(
            net,
            lambda block, start, count: kv_grad.at[block, pl.ds(start, count)],
            s * local_len,
            local_len,
            kv_y,
            kv_z,
            kv_share,
        )
        for s in range(seqs)
    ]
    for s in range(seqs):
        rows = pl.ds(s * local_len, local_len)
        for c in range(cols):
            at = pl.ds(c * local_len, local_len)
            keys[at, :] = kv_all[c, rows, :size]
            values[at, :] = kv_all[c, rows, size:]

        def attend(g, carry, s=s, rows=rows):
            at = pl.ds(pl.multiple_of(g * size, size), size)
            grow = pl.ds(pl.multiple_of(g * local_len, local_len), local_len)
            dout = dob[rows, at]
            stacked[0, grow, :] = q_low[rows, at]
            stacked[1, grow, :] = dout
            p = probs[s, g]
            p = p.astype(f32)
            dp = dot_nt(dout, values[...])
            delta = jnp.sum(p * dp, axis=1, keepdims=True)
            ds = (p * (dp - delta)).astype(bf16)
            ds_all[grow, :] = ds
            raw = dot_nn(ds, keys[...]) * scale
            dqkv[rows, at] = (
                raw * cosine[rows, :] - pltpu.roll(raw, size // 2, 1) * sine[rows, :]
            ).astype(bf16)
            return carry

        lax.fori_loop(0, group, attend, 0)
        dk = (dot_tn(ds_all[...], stacked[0]) * scale).astype(bf16)
        dv = dot_tn(probs[s].reshape(group * local_len, -1), stacked[1]).astype(bf16)
        for c in range(cols):
            kv_grad[c, rows, :size] = dk[c * local_len : (c + 1) * local_len]
            kv_grad[c, rows, size:] = dv[c * local_len : (c + 1) * local_len]
        kv_line[s].send_y()
        if s == 0:
            out_line[0].send_z()
            pump()
        else:
            kv_line[s - 1].send_z()
    kv_line[seqs - 1].send_z()
    out_line[1].send_z()
    out_line[2].send_y()
    for s in range(seqs):
        kv_line[s].last()
    raw = kv_share[:, :size]
    dqkv[:, q_width : q_width + size] = (
        raw * cosine[...] - pltpu.roll(raw, size // 2, 1) * sine[...]
    ).astype(bf16)
    dqkv[:, q_width + size : qkv_width] = kv_share[:, size:].astype(bf16)

    row_pieces, piece_rows = row_core.shape[0], row_core.shape[1]
    half = row_pieces * piece_rows

    def row_piece(core, i):
        return pl.ds(pl.multiple_of((core * row_pieces + i) * piece_rows, piece_rows), piece_rows)

    over = []
    for core in (1 - net.core, net.core):
        at_rows = pl.ds(pl.multiple_of(core * half, half), half)
        for tile in range(width // TILE):
            at = pl.ds(tile * TILE, TILE)
            low[at_rows, at] = dot_nt(dqkv[at_rows, :], weights[at, :qkv_width]).astype(bf16)
        if not over:
            over = [
                net.send(low.at[row_piece(1 - net.core, i)], row_core.at[i], net.core_peer())
                for i in range(row_pieces)
            ]

    qkv_pieces = 5
    qkv_count = rows_w // qkv_pieces
    for tile in range(width // TILE):
        at = pl.ds(tile * TILE, TILE)
        misc[at, :] = dot_tn(h2[:, at], logit_low[...])
        weights[at, :qkv_width] = dot_tn(h1[:, at], dqkv[...]).astype(bf16)
    qkv_line = [
        Sum2D(
            net,
            lambda block, start, count: weights.at[
                pl.ds(pl.multiple_of(block * rows_w + start, 16), count), pl.ds(0, qkv_width)
            ],
            q * qkv_count,
            qkv_count,
            qkv_y,
            qkv_z,
            share_qkv,
        )
        for q in range(qkv_pieces)
    ]
    qkv_line[0].send_y()
    along, returned = [], []
    for i in range(row_pieces):
        over[i].wait_recv()
        add_rows(row_to.at[i], [low.at[row_piece(net.core, i)], row_core.at[i]])
        along.append(net.send(row_to.at[i], row_from.at[i], net.x_peer()))
    qkv_line[1].send_y()
    for i in range(row_pieces):
        along[i].wait_recv()
        at = row_piece(net.core, i)
        add_rows(grad_own.at[at], [row_to.at[i], row_from.at[i]])
        returned.append(net.send(grad_own.at[at], grad_own.at[at], net.core_peer()))
    qkv_line[0].send_z()
    pump()
    for copy in returned:
        copy.wait_recv()

    def norm_first(at):
        x = tokens[at, :].astype(f32)
        inverse = lax.rsqrt(jnp.sum(x * x, axis=1, keepdims=True) / width + norm_eps)
        base = x * inverse
        dh = grad_own[at, :].astype(f32)
        fold(dh * base, 0)
        scaled = dh * gains[0:1, :]
        mean = jnp.sum(scaled * base, axis=1, keepdims=True) / width
        d_tokens[at, :] = d_tokens[at, :] + inverse * (scaled - base * mean)

    chunks(norm_first, 16)
    total = [jnp.sum(gain_sums[8 * i : 8 * i + 8, :], axis=0, keepdims=True) for i in (0, 1)]
    row_at = lax.broadcasted_iota(jnp.int32, (LANES, TILE), 0)
    for tile in range(width // TILE):
        at = pl.ds(tile * TILE, TILE)
        part = slice(tile * TILE, (tile + 1) * TILE)
        placed = jnp.where(row_at == experts, total[0][:, part], 0.0)
        placed = jnp.where(row_at == experts + 1, total[1][:, part], placed)
        lanes = lax.broadcasted_iota(jnp.int32, (TILE, LANES), 1)
        misc_low[at, :] = jnp.where(lanes < experts, misc[at, :], jnp.transpose(placed)).astype(bf16)
    misc_line = Sum2D(net, blocks_of(misc_low), 0, rows_w, misc_y, misc_z, share_misc)
    misc_line.send_y()
    qkv_line[2].send_y()
    qkv_line[1].send_z()
    out_line[2].send_z()
    out_line[3].send_y()
    pump()
    misc_line.send_z()
    qkv_line[3].send_y()
    qkv_line[2].send_z()
    out_line[3].send_z()
    pump()
    qkv_line[4].send_y()
    qkv_line[3].send_z()
    pump()
    qkv_line[4].send_z()
    pump(8)
    for piece_sum in (*out_line, misc_line, *qkv_line):
        piece_sum.last()
    net.finish()


def rear_call(
    cols, collective_id, experts, out_part, back, gate_dots, gate, router_probs, table_col, h1, h2,
    tokens, attn, weights, out_weights, grads, heads, q_low, kv_all, probs, cosine, sine,
):
    toks, width = back.shape
    q_width = q_low.shape[1]
    size = HEAD_DIM
    qkv_width = q_width + 2 * size
    seqs, group, local_len, full_len = probs.shape
    rows_w, high = width // cols, cols // 2
    piece = width // lax.axis_size("row")
    row_pieces = 4
    row_piece = (row_pieces, toks // 2 // row_pieces, width)
    vmem, any_space = pl.BlockSpec(memory_space=pltpu.VMEM), pl.BlockSpec(memory_space=pl.ANY)

    def shape(*dims, dtype=f32):
        return jax.ShapeDtypeStruct(dims, dtype)

    def sums(rows, columns):
        return [
            pltpu.VMEM((high, rows, columns), bf16),
            pltpu.VMEM((high - 1, rows, columns), bf16),
        ]

    copies = 420
    return pl.pallas_call(
        functools.partial(rear_kernel, cols, experts),
        out_shape=[
            shape(toks, piece),
            shape(toks, width),
            shape(rows_w, qkv_width),
            shape(rows_w, LANES),
            shape(rows_w, q_width),
        ],
        in_specs=[any_space] + [vmem] * 9 + [any_space] * 3 + [vmem] * 6,
        out_specs=[vmem] * 5,
        scratch_shapes=[
            pltpu.VMEM((width, qkv_width + LANES), bf16),
            pltpu.VMEM((width, q_width), bf16),
            pltpu.VMEM((width, LANES), f32),
            pltpu.VMEM((width, LANES), bf16),
            pltpu.VMEM((toks, width), bf16),
            pltpu.VMEM((8, width), f32),
            pltpu.VMEM((LANES, toks), f32),
            pltpu.VMEM((toks, LANES), bf16),
            pltpu.VMEM((toks, width), bf16),
            pltpu.VMEM((toks, q_width), bf16),
            pltpu.VMEM((full_len, size), bf16),
            pltpu.VMEM((full_len, size), bf16),
            pltpu.VMEM((2, group * local_len, size), bf16),
            pltpu.VMEM((group * local_len, full_len), bf16),
            pltpu.VMEM((cols, toks, 2 * size), bf16),
            pltpu.VMEM((toks, 2 * size), f32),
            pltpu.VMEM((toks, qkv_width), bf16),
            pltpu.VMEM((16, width), f32),
            pltpu.VMEM((2, cols, toks, piece), bf16),
            pltpu.VMEM((2, cols, toks, piece), bf16),
            pltpu.VMEM((cols, toks, piece), bf16),
            *sums(toks, piece),
            *sums(toks, 2 * size),
            *sums(rows_w, q_width),
            *sums(rows_w, qkv_width),
            *sums(rows_w, LANES),
            pltpu.VMEM(row_piece, bf16),
            pltpu.VMEM(row_piece, bf16),
            pltpu.VMEM(row_piece, bf16),
            pltpu.SemaphoreType.DMA((copies,)),
            pltpu.SemaphoreType.DMA((copies,)),
            pltpu.SemaphoreType.DMA((8,)),
        ],
        compiler_params=pltpu.CompilerParams(
            collective_id=collective_id, has_side_effects=True, vmem_limit_bytes=62 << 20
        ),
        name=f"rear_{collective_id}",
    )(
        out_part, back, gate_dots, gate, router_probs, table_col, h1, h2, tokens, attn, weights,
        out_weights, grads, heads, q_low, kv_all, probs, cosine, sine,
    )


def experts_plain(
    h2, grad_all, w_gate, w_up, w_down, shared_weights, router, rank_all, capacity, row_width
):
    cols = lax.axis_size("col")
    col_index, row_index = lax.axis_index("col"), lax.axis_index("row")
    toks, width = h2.shape
    exp_local = w_gate.shape[0]
    experts = rank_all.shape[2]
    shared_part = shared_weights.shape[1] // 3
    shared_in_weights = shared_weights[:, : 2 * shared_part]
    shared_down = shared_weights[:, 2 * shared_part :]
    h2_slice = lax.dynamic_slice_in_dim(h2, row_index * row_width, row_width, 1)
    h2_all = gather_all(h2_slice)

    all_mask = (rank_all > 0).astype(f32)
    all_probs = jax.nn.softmax(dot("ctd,de->cte", h2_all, router), axis=-1)
    all_picked = all_probs * all_mask
    all_gate = all_picked / jnp.sum(all_picked, axis=-1, keepdims=True)
    own = col_index * exp_local
    own_gate = lax.dynamic_slice_in_dim(all_gate, own, exp_local, 2)
    own_rank = lax.dynamic_slice_in_dim(rank_all, own, exp_local, 2).astype(jnp.int32)
    slots = jnp.arange(1, capacity + 1, dtype=jnp.int32)
    pick = jnp.swapaxes(own_rank, 1, 2)[:, :, None, :] == slots[:, None]
    slot_gate = jnp.sum(
        jnp.where(pick, jnp.swapaxes(own_gate, 1, 2)[:, :, None, :], 0.0), axis=3
    )[..., None]
    pick_low = pick.astype(bf16).reshape(cols, exp_local * capacity, toks)
    slot_shape = (cols, exp_local, capacity, width)
    slot_rows = dot("cut,ctd->cud", pick_low, h2_all).astype(bf16).reshape(slot_shape)
    slot_grad = dot("cut,ctd->cud", pick_low, grad_all).astype(bf16).reshape(slot_shape)
    gate_pre = dot("necd,edf->necf", slot_rows, w_gate)
    up_pre = dot("necd,edf->necf", slot_rows, w_up)
    silu_gate, slope_gate = silu_parts(gate_pre)
    hidden = silu_gate * up_pre
    gated = (hidden * slot_gate).astype(bf16)
    slot_out = dot("necf,efd->necd", gated, w_down).astype(bf16)
    hidden_grad = dot("necd,efd->necf", slot_grad, w_down)
    slot_dots = jnp.sum(hidden * hidden_grad, axis=-1)
    hidden_grad = hidden_grad * slot_gate
    gate_grad = (hidden_grad * up_pre * slope_gate).astype(bf16)
    up_grad = (hidden_grad * silu_gate).astype(bf16)
    slot_back = dot("necf,edf->necd", gate_grad, w_gate)
    slot_back = (slot_back + dot("necf,edf->necd", up_grad, w_up)).astype(bf16)
    grad_expert_down = dot("necf,necd->efd", gated, slot_grad)
    grad_expert_gate = dot("necd,necf->edf", slot_rows, gate_grad)
    grad_expert_up = dot("necd,necf->edf", slot_rows, up_grad)
    pick_flat = pick_low.reshape(cols, exp_local * capacity, toks)
    slot_out = slot_out.reshape(cols, exp_local * capacity, width)
    slot_back = slot_back.reshape(cols, exp_local * capacity, width)

    shared_pre = dot("ctd,dk->ctk", h2_all, shared_in_weights)
    sgate_pre, sup_pre = shared_pre[:, :, :shared_part], shared_pre[:, :, shared_part:]
    shared_silu, shared_slope = silu_parts(sgate_pre)
    shared_hidden = (shared_silu * sup_pre).astype(bf16)
    part_out = dot("cut,cud->ctd", pick_flat, slot_out) + dot(
        "ctk,dk->ctd", shared_hidden, shared_down
    )
    shared_hgrad = dot("ctd,dk->ctk", grad_all, shared_down)
    shared_grads = jnp.concatenate(
        [shared_hgrad * sup_pre * shared_slope, shared_hgrad * shared_silu], axis=2
    ).astype(bf16)
    part_back = dot("cut,cud->ctd", pick_flat, slot_back) + dot(
        "ctk,dk->ctd", shared_grads, shared_in_weights
    )
    token_dots = jnp.einsum(
        "ceu,ceut->cte", slot_dots, pick.astype(f32), precision=lax.Precision.HIGHEST
    )
    gate_dots = lax.psum(swap_col(token_dots), "row")
    gate_dots = jnp.swapaxes(gate_dots, 0, 1).reshape(toks, experts)

    shared_share = jnp.concatenate(
        [dot("ctd,ctk->dk", h2_all, shared_grads), dot("ctd,ctk->dk", grad_all, shared_hidden)],
        axis=1,
    ).astype(bf16)
    back_full = lax.all_gather(scatter_all(part_back.astype(bf16)), "row", axis=1, tiled=True)
    return (
        part_out.astype(bf16),
        back_full,
        gate_dots,
        shared_share,
        grad_expert_gate,
        grad_expert_up,
        grad_expert_down,
    )


def on_device(
    tokens,
    segments,
    routes,
    attn_gain,
    query_matrix,
    key_matrix,
    value_matrix,
    attention_output_matrix,
    mlp_gain,
    w_router,
    shared_gate_matrix,
    shared_up_matrix,
    shared_down_matrix,
    expert_gate,
    expert_up,
    expert_down,
    cotangent,
):
    local_len, seqs, width = tokens.shape
    cols = lax.axis_size("col")
    col_index = lax.axis_index("col")
    rows_w = query_matrix.shape[0]
    full_len = local_len * cols
    size = HEAD_DIM
    q_width = query_matrix.shape[1]
    kv_width = key_matrix.shape[1]
    kv_local = kv_width // size
    group = q_width // kv_width
    row_width = cotangent.shape[2]
    toks = local_len * seqs
    top = routes.shape[2]
    experts = w_router.shape[1]
    exp_local = expert_gate.shape[0]
    hidden_local = expert_gate.shape[2]
    capacity = max(2, toks * top * 4 // (3 * experts))
    shared_part = shared_gate_matrix.shape[1] // cols
    scale = 1.0 / math.sqrt(size)
    kernels = fits(cols, toks, width) and kv_local == 1 and exp_local == 2

    def seq_major(a):
        return jnp.swapaxes(a, 0, 1).reshape(toks, a.shape[2])

    misc = jnp.concatenate(
        [
            w_router,
            attn_gain[:, None],
            mlp_gain[:, None],
            jnp.zeros((rows_w, LANES - experts - 2), bf16),
        ],
        axis=1,
    )
    shared_weights = jnp.concatenate(
        [
            shared_gate_matrix.reshape(rows_w, cols, shared_part),
            shared_up_matrix.reshape(rows_w, cols, shared_part),
            shared_down_matrix.T.reshape(rows_w, cols, shared_part),
        ],
        axis=2,
    )
    shared_own = jnp.swapaxes(shared_weights, 0, 1)
    grad_own = seq_major(cotangent).astype(bf16)
    cosine, sine = rope_tables(col_index * local_len, local_len, size)
    cosine, sine = jnp.tile(cosine, (seqs, 1)), jnp.tile(sine, (seqs, 1))
    qkv_width = q_width + 2 * kv_width
    flat_routes = seq_major(routes)
    named = flat_routes[:, :, None] == jnp.arange(experts, dtype=jnp.int32)
    mask = jnp.any(named, axis=1)
    order = jnp.arange(toks, dtype=jnp.int32)
    upto = (order[None, :] <= order[:, None]).astype(bf16)
    rank = jnp.where(mask, dot("ij,je->ie", upto, mask.astype(bf16)), 0.0)

    doc = jnp.transpose(segments)
    def to_grid(flat):
        shaped = flat.reshape(seqs, local_len, kv_local, group, size)
        return shaped.transpose(0, 2, 3, 1, 4).reshape(seqs, kv_local, group * local_len, size)

    def from_grid(grid):
        shaped = grid.reshape(seqs, kv_local, group, local_len, size)
        return shaped.transpose(0, 3, 1, 2, 4).reshape(toks, q_width)

    token_rows = seq_major(tokens)
    x = token_rows.astype(f32)
    inv_first = rms_scale(x)
    base_first = x * inv_first
    if kernels:
        table_row = jnp.concatenate([rank.T, doc.reshape(1, toks).astype(f32)], axis=0)
        table_row = jnp.pad(table_row, ((0, -(experts + 1) % 8), (0, 0)))
        table_col = jnp.pad(rank, ((0, 0), (0, LANES - experts))).astype(bf16)
        (
            first_weights,
            out_weights,
            grad_all,
            shared_weights,
            rows_all,
            rank_all,
            h1,
            q_low,
            kv_all,
            probs,
            heads,
            attn,
            h2,
            gate,
            probs_router,
        ) = front_call(
            cols,
            0,
            experts,
            token_rows,
            query_matrix,
            key_matrix,
            value_matrix,
            misc,
            attention_output_matrix.T,
            grad_own,
            padded_thirds(shared_own),
            table_row,
            table_col,
            doc.reshape(toks, 1).astype(f32),
            jnp.concatenate([cosine, cosine], axis=1),
            jnp.concatenate([-sine, sine], axis=1),
            seqs,
        )
    else:
        first_weights = jnp.concatenate([query_matrix, key_matrix, value_matrix, misc], axis=1)
        first_weights = gather_col(first_weights).reshape(width, -1)
        out_weights = gather_col(attention_output_matrix.T).reshape(width, q_width)
        shared_weights = swap_col(shared_own).reshape(width, 3 * shared_part)
        grad_all = gather_all(grad_own)
        gain_one = first_weights[:, qkv_width + experts].astype(f32)
        h1 = (base_first * gain_one).astype(bf16)
        qkv = dot("tb,bk->tk", h1, first_weights[:, :qkv_width])
        qk = rotate(qkv[:, : q_width + kv_width], cosine, sine).astype(bf16)
        q_low = qk[:, :q_width]
        value_low = qkv[:, q_width + kv_width :].astype(bf16)
        side = jnp.concatenate(
            [
                rank.astype(bf16),
                doc.reshape(toks, 1).astype(bf16),
                jnp.zeros((toks, LANES - experts - 1), bf16),
            ],
            axis=1,
        )
        kv_all = gather_col(jnp.concatenate([qk[:, q_width:], value_low, side], axis=1))
        rank_all = kv_all[:, :, 2 * kv_width : 2 * kv_width + experts]
    qkv_weights = first_weights[:, :qkv_width]
    router = first_weights[:, qkv_width : qkv_width + experts]
    gain_one = first_weights[:, qkv_width + experts].astype(f32)
    gain_two = first_weights[:, qkv_width + experts + 1].astype(f32)
    kv_seq = jnp.swapaxes(kv_all.reshape(cols, seqs, local_len, -1), 0, 1)
    kv_seq = kv_seq.reshape(seqs, full_len, -1)
    key_all = kv_seq[:, :, :kv_width].reshape(seqs, full_len, kv_local, size)
    value_all = kv_seq[:, :, kv_width : 2 * kv_width].reshape(seqs, full_len, kv_local, size)
    query_grid = to_grid(q_low)
    if not kernels:
        doc_all = kv_seq[:, :, 2 * kv_width + experts]
        place = col_index * local_len + jnp.arange(local_len, dtype=jnp.int32)
        same = doc.astype(bf16)[:, :, None] == doc_all[:, None, :]
        causal = jnp.arange(full_len, dtype=jnp.int32)[None, :] <= place[:, None]
        allowed = jnp.tile(same & causal[None], (1, group, 1))[:, None]
        scores = dot("shrd,skhd->shrk", query_grid, key_all) * scale
        scores = jnp.where(allowed, scores, masked_score)
        weights = jnp.exp(scores - jnp.max(scores, axis=-1, keepdims=True))
        weights = jnp.where(allowed, weights, 0.0)
        probs = (weights / jnp.sum(weights, axis=-1, keepdims=True)).astype(bf16)
        heads = from_grid(dot("shrk,skhd->shrd", probs, value_all)).astype(bf16)
        attn = lax.psum(dot("tk,bk->tb", heads, out_weights).astype(bf16), "row")
    middle = x + attn.astype(f32)

    inv_second = rms_scale(middle)
    base_second = middle * inv_second
    row_index = lax.axis_index("row")
    if not kernels:
        h2 = (base_second * gain_two).astype(bf16)
        probs_router = jax.nn.softmax(dot("td,de->te", h2, router), axis=-1)
        picked = jnp.where(mask, probs_router, 0.0)
        pick_total = jnp.sum(picked, axis=-1, keepdims=True)
        gate = picked / pick_total
    if kernels:
        rank_own = lax.dynamic_slice_in_dim(rank_all, col_index * exp_local, exp_local, 2)
        rank_own = rank_own.astype(f32)
        part_out, back_full, *expert_grads, _, shared_share, gate_dots, _, _, _ = experts_call(
            cols,
            3,
            capacity,
            h2,
            grad_all,
            expert_gate,
            expert_up,
            expert_down,
            shared_weights,
            lax.dynamic_slice_in_dim(rows_all, col_index * exp_local, exp_local, 1),
            rank_own,
            gate[:, :experts].T,
        )
        expert_grads = [grad.astype(f32) for grad in expert_grads]
    else:
        part_out, back_full, gate_dots, shared_share, *expert_grads = experts_plain(
            h2,
            grad_all,
            expert_gate,
            expert_up,
            expert_down,
            shared_weights,
            router,
            rank_all,
            capacity,
            row_width,
        )
    if not kernels:
        back_full = back_full.astype(f32)
    if kernels:
        shared_share = shared_share.reshape(cols, rows_w, 3, -1)[..., :shared_part]
        shared_share = shared_share.reshape(cols, rows_w, -1)
    else:
        shared_share = swap_col(shared_share.reshape(cols, rows_w, 3 * shared_part))
    shared_share = jnp.swapaxes(shared_share, 0, 1).astype(f32)
    share_sgate, share_sup, share_sdown = (
        shared_share[:, :, i * shared_part : (i + 1) * shared_part].reshape(rows_w, -1)
        for i in range(3)
    )

    if kernels:
        out_slice, token_grad, share_qkv, share_misc, share_out = rear_call(
            cols,
            5,
            experts,
            part_out,
            back_full,
            gate_dots,
            gate,
            probs_router,
            table_col,
            h1,
            h2,
            token_rows,
            attn,
            first_weights,
            out_weights,
            grad_all,
            heads,
            q_low,
            kv_all,
            probs,
            jnp.concatenate([cosine, cosine], axis=1),
            jnp.concatenate([-sine, sine], axis=1),
        )
    else:
        pick_grad = gate_dots - jnp.sum(gate * gate_dots, axis=-1, keepdims=True)
        prob_grad = jnp.where(mask, pick_grad / pick_total, 0.0)
        logit_grad = probs_router * (
            prob_grad - jnp.sum(probs_router * prob_grad, axis=-1, keepdims=True)
        )
        logit_low = logit_grad.astype(bf16)
        grad_router = dot("td,te->de", h2, logit_low)

        back_full = back_full + dot("te,de->td", logit_low, router)
        grad_own = lax.dynamic_slice_in_dim(grad_all, col_index, 1, 0)[0].astype(f32)
        grad_gain_two = jnp.sum(back_full * base_second, axis=0)
        scaled_two = back_full * gain_two
        middle_grad = (
            inv_second
            * (scaled_two - base_second * jnp.mean(scaled_two * base_second, axis=-1, keepdims=True))
            + grad_own
        )
        attn_grad = middle_grad.astype(bf16)
        grad_out = dot("td,tk->dk", attn_grad, heads).astype(bf16)

        heads_grad = to_grid(dot("td,dk->tk", attn_grad, out_weights).astype(bf16))
        value_grad = dot("shrk,shrd->skhd", probs, heads_grad)
        weight_grad = dot("shrd,skhd->shrk", heads_grad, value_all)
        probs_wide = probs.astype(f32)
        delta = jnp.sum(probs_wide * weight_grad, axis=-1, keepdims=True)
        score_grad = (probs_wide * (weight_grad - delta)).astype(bf16)
        query_grad = from_grid(dot("shrk,skhd->shrd", score_grad, key_all)) * scale
        key_grad = dot("shrk,shrd->skhd", score_grad, query_grid) * scale
        kv_grad = jnp.concatenate(
            [key_grad.reshape(seqs, full_len, kv_width), value_grad.reshape(seqs, full_len, kv_width)],
            axis=2,
        ).astype(bf16)
        kv_grad = jnp.swapaxes(kv_grad.reshape(seqs, cols, local_len, 2 * kv_width), 0, 1)
        kv_share = scatter_col(kv_grad.reshape(cols, toks, 2 * kv_width)).astype(f32)
        qk_grad = rotate(
            jnp.concatenate([query_grad, kv_share[:, :kv_width]], axis=1), cosine, -sine
        )
        qkv_grad = jnp.concatenate([qk_grad, kv_share[:, kv_width:]], axis=1).astype(bf16)
        first_grad = dot("tk,bk->tb", qkv_grad, qkv_weights).astype(bf16)
        first_grad = lax.psum(first_grad, "row").astype(f32)
        grad_gain_one = jnp.sum(first_grad * base_first, axis=0)
        scaled_one = first_grad * gain_one
        token_grad = (
            inv_first
            * (scaled_one - base_first * jnp.mean(scaled_one * base_first, axis=-1, keepdims=True))
            + middle_grad
        )
        grad_first = jnp.concatenate(
            [
                dot("tb,tk->bk", h1, qkv_grad),
                grad_router,
                grad_gain_one[:, None],
                grad_gain_two[:, None],
                jnp.zeros((width, LANES - experts - 2), f32),
            ],
            axis=1,
        ).astype(bf16)
        out_slice = scatter_all(part_out).astype(f32)
        share_out = scatter_col(grad_out.reshape(cols, rows_w, q_width)).astype(f32)
        share_first = scatter_col(grad_first.reshape(cols, rows_w, -1)).astype(f32)
        share_qkv, share_misc = share_first[:, :qkv_width], share_first[:, qkv_width:]
    middle_slice = lax.dynamic_slice_in_dim(middle, row_index * row_width, row_width, 1)
    block_out = (middle_slice + out_slice).astype(bf16)

    def tokens_first(a):
        return jnp.swapaxes(a.reshape(seqs, local_len, a.shape[1]), 0, 1)

    return (
        tokens_first(block_out),
        tokens_first(token_grad),
        share_misc[:, experts],
        share_qkv[:, :q_width],
        share_qkv[:, q_width : q_width + kv_width],
        share_qkv[:, q_width + kv_width :],
        share_out.T,
        share_misc[:, experts + 1],
        share_misc[:, :experts],
        share_sgate,
        share_sup,
        share_sdown.T,
        *expert_grads,
    )


def solution(mesh):
    in_specs = (
        P("col", None, None),
        P("col", None),
        P("col", None, None),
        P("col"),
        P("col", "row"),
        P("col", "row"),
        P("col", "row"),
        P("row", "col"),
        P("col"),
        P("col", None),
        P("col", "row"),
        P("col", "row"),
        P("row", "col"),
        P("col", None, "row"),
        P("col", None, "row"),
        P("col", "row", None),
        P("col", None, "row"),
    )
    out_specs = (
        P("col", None, "row"),
        P("col", None, None),
        P("col"),
        P("col", "row"),
        P("col", "row"),
        P("col", "row"),
        P("row", "col"),
        P("col"),
        P("col", None),
        P("col", "row"),
        P("col", "row"),
        P("row", "col"),
        P("col", None, "row"),
        P("col", None, "row"),
        P("col", "row", None),
    )
    return jax.shard_map(
        on_device, mesh=mesh, in_specs=in_specs, out_specs=out_specs, check_vma=False
    )
```
